32 devices in a mesh: node: 8 (over y, x, core), expert: 4 (over z).
Axes of the slice: x: 2, y: 2, z: 4, core: 2. Of those that a mesh axis runs over, the one named last changes fastest.
Arguments:
- tokens: bfloat16 [16384, 1024], P(('node', 'expert')), may hold values from -6 to 6
- gain_attn: bfloat16 [1024], P(('node', 'expert')), may hold values from 0.5 to 1.5
- w_qkv: bfloat16 [1024, 3072], P(('node', 'expert')), may hold values from -0.1875 to 0.1875
- w_out: bfloat16 [1024, 1024], P(('node', 'expert')), may hold values from -1.5 to 1.5
- gain_mix: bfloat16 [1024], P(('node', 'expert')), may hold values from 0.5 to 1.5
- w_fc: bfloat16 [1024, 4096], P(('node', 'expert')), may hold values from -0.1875 to 0.1875
- w_proj: bfloat16 [4096, 1024], P(('node', 'expert')), may hold values from -0.1875 to 0.1875
- w_router: bfloat16 [1024, 4], P(('node', 'expert')), may hold values from -0.1875 to 0.1875
- w_coef: bfloat16 [1024, 2], P(('node', 'expert')), may hold values from -0.1875 to 0.1875
- expert_in: bfloat16 [4, 1024, 4096], P('expert', None, 'node'), may hold values from -0.1875 to 0.1875
- expert_out: bfloat16 [4, 4096, 1024], P('expert', 'node'), may hold values from -2 to 2
- routes: int32 [16384, 1], P(('node', 'expert')), may hold values from 0 to 3; in each aligned block of 512 rows (0 to 511, 512 to 1023, ...) at most 160 rows name the same one
- dropped: int32 [16384], P(('node', 'expert')), may hold values 0 or 1
- cotangent: bfloat16 [16384, 1024], P(('node', 'expert')), may hold values from -6 to 6
Outputs:
- mixed: bfloat16 [16384, 1024], P(('node', 'expert'))
- tokens_grad: float32 [16384, 1024], P(('node', 'expert'))
- gain_attn_grad: float32 [1024], P(('node', 'expert'))
- w_qkv_grad: float32 [1024, 3072], P(('node', 'expert'))
- w_out_grad: float32 [1024, 1024], P(('node', 'expert'))
- gain_mix_grad: float32 [1024], P(('node', 'expert'))
- w_fc_grad: float32 [1024, 4096], P(('node', 'expert'))
- w_proj_grad: float32 [4096, 1024], P(('node', 'expert'))
- w_router_grad: float32 [1024, 4], P(('node', 'expert'))
- w_coef_grad: float32 [1024, 2], P(('node', 'expert'))
- expert_in_grad: float32 [4, 1024, 4096], P('expert', None, 'node')
- expert_out_grad: float32 [4, 4096, 1024], P('expert', 'node')
The draws below stay inside these ranges and needn't reach their ends.
Inputs may be any that keep to these rules, and one draw needn't show every extreme that they name: `routes`: the rows of one device name one expert at most 160 times, and in some devices an expert is named exactly 160 times.
All inputs are finite; a program needn't handle non-finite values. No bound on the sum of `dropped` on one device may be relied on, other than what follows from the above.
Results may differ from the reference program's by a relative error of at most 0.015.
Values may be sent and summed in bfloat16 or wider, within the bound.
A program may use at most 192 MiB of HBM per device.

```python
import math
import jax
import jax.numpy as jnp
import numpy as np
from jax import lax

D = 1024
H = 16
HD = 64
FF = 4096
SEQ = 512
TOK_DEV = 512
TOKENS = 16384
EXPERTS = 4
CAP = 160
N_NODE = 8
N_EXPERT = 4


def plant(values, rng, smallest, largest):
    extent = values.shape
    place = [jax.random.randint(jax.random.fold_in(rng, axis), (), 0, extent[axis]) for axis in range(len(extent))]
    values = values.at[tuple(place)].set(smallest)
    longest = extent.index(max(extent))
    place[longest] = (place[longest] + 1) % extent[longest]
    return values.at[tuple(place)].set(largest)


def level_of(stream_key, dims, split, low, largest):
    gain = 1.0
    for dim, blocks in split:
        heights = jax.random.uniform(jax.random.fold_in(jax.random.fold_in(stream_key, 6), dim), (blocks,), jnp.float32, low / len(split), largest / len(split))
        gain = gain * jnp.repeat(jnp.exp(heights), dims[dim] // blocks).reshape((-1,) + (1,) * (len(dims) - 1 - dim))
    return gain


def deal_out(rng, own, number, rows, number_of, top, most, skew):
    order = jax.random.permutation(rng, number_of)
    packed, ordinary = load_shares(number_of, rows * top, most, skew, True), load_shares(number_of, rows * top, most, skew, False)
    places = jnp.arange(number_of)

    def named(sizes, turn):
        used = int((sizes > 0).sum())
        fixed = max(1, used // 4)
        passed = fixed + (places - fixed + turn * (used - fixed)) % max(1, number_of - fixed)
        return jnp.zeros((number_of,), jnp.int32).at[order[jnp.where(places < fixed, places, passed)]].set(jnp.asarray(sizes, jnp.int32))

    sizes = jnp.where(number % 4 == 0, named(packed, number // 4), named(ordinary, number - number // 4 - 1))
    mixed = jax.random.permutation(jax.random.fold_in(own, 3), number_of)
    giver, receiver = mixed[0:number_of // 2 * 2:2], mixed[1:number_of // 2 * 2:2]
    slack = jnp.minimum(sizes[giver] - 1, most - sizes[receiver]) // 2
    slack = jnp.where((giver == order[0]) | (receiver == order[0]) | (sizes[receiver] == 0), 0, jnp.maximum(slack, 0))
    passed = jax.random.randint(jax.random.fold_in(own, 4), (number_of // 2,), 0, 1 << 20) % (slack + 1)
    sizes = sizes.at[giver].add(-passed).at[receiver].add(passed)
    labels = jnp.searchsorted(jnp.cumsum(sizes), jnp.arange(rows * top), side="right").astype(jnp.int32)
    listing = labels.reshape(top, rows).T
    listing = listing[jax.random.permutation(jax.random.fold_in(own, 1), rows)]
    turn = jax.random.randint(jax.random.fold_in(own, 2), (rows, 1), 0, top)
    return jnp.take_along_axis(listing, (jnp.arange(top)[None, :] + turn) % top, axis=1)


def load_shares(number_of, total, reach, skew, full):
    loads = [(1 << 20) // math.isqrt(standing ** skew) + 1 for standing in range(1, number_of + 1)]
    largest = reach if full else min(reach, max(-(-total // number_of), total * loads[0] // sum(loads)))
    least = 1 if total - largest >= number_of - 1 else 0
    counts, surplus = [largest] + [least] * (number_of - 1), total - largest - least * (number_of - 1)
    while surplus > 0:
        movable = [i for i in range(1, number_of) if counts[i] < largest] or [i for i in range(1, number_of) if counts[i] < reach]
        mass, left = sum([loads[i] for i in movable]), surplus
        for i in movable:
            extra = min(reach - counts[i], max(1, left * loads[i] // mass), surplus)
            counts[i] = counts[i] + extra
            surplus = surplus - extra
    return np.array(counts)


def gaussian(rng, dims, width, limit, split=(), kind=jnp.bfloat16):
    entries = width * jax.random.normal(rng, dims, jnp.float32)
    if split:
        entries = entries * level_of(rng, dims, split, -0.22, 0.18)
    return jnp.clip(entries, -limit, limit).astype(kind)


def setup_inputs(seed: int = 0) -> dict:
    key_list = jax.random.split(jax.random.key(seed), 15)
    tokens = gaussian(key_list[0], (TOKENS, D), 1.0, 6.0, ((0, 32),))
    gain_attn = jnp.clip(1.0 + 0.1 * jax.random.normal(key_list[1], (D,), jnp.float32), 0.5, 1.5).astype(jnp.bfloat16)
    w_qkv = gaussian(key_list[2], (D, 3 * D), D ** -0.5, 0.1875, ((0, 32),))
    w_out = gaussian(key_list[3], (D, D), (D // 64) ** -0.5, 1.5, ((0, 32),))
    gain_mix = jnp.clip(1.0 + 0.1 * jax.random.normal(key_list[4], (D,), jnp.float32), 0.5, 1.5).astype(jnp.bfloat16)
    w_fc = gaussian(key_list[5], (D, FF), D ** -0.5, 0.1875, ((0, 32),))
    w_proj = gaussian(key_list[6], (FF, D), (FF // 4) ** -0.5, 0.1875, ((0, 32),))
    w_router = gaussian(key_list[7], (D, EXPERTS), (0.75 * D ** -0.5), 0.1875, ((0, 32),))
    w_coef = gaussian(key_list[8], (D, 2), (D ** -0.5), 0.1875, ((0, 32),))
    expert_in = gaussian(key_list[9], (EXPERTS, D, FF), D ** -0.5, 0.1875, ((0, 4), (2, 8)))
    expert_out = gaussian(key_list[10], (EXPERTS, FF, D), (max(FF // 512, 1)) ** -0.5, 2.0, ((0, 4), (1, 8)))
    routes_keys = jax.random.split(jax.random.fold_in(key_list[11], 1), TOKENS // TOK_DEV)
    routes_turns = jax.random.permutation(jax.random.fold_in(key_list[11], 3), TOKENS // TOK_DEV)
    routes = jax.vmap(lambda own, number: deal_out(jax.random.fold_in(key_list[11], 2), own, number, TOK_DEV, EXPERTS, 1, CAP, 2))(routes_keys, routes_turns).reshape((TOKENS, 1))
    dropped = plant((jax.random.randint(key_list[12], (TOKENS,), 0, 8) < 1).astype(jnp.int32), jax.random.fold_in(key_list[12], 1), 0, 1)
    cotangent = gaussian(key_list[13], (TOKENS, D), 1.0, 6.0, ((0, 32),))
    return {"tokens": tokens, "gain_attn": gain_attn, "w_qkv": w_qkv, "w_out": w_out, "gain_mix": gain_mix, "w_fc": w_fc, "w_proj": w_proj, "w_router": w_router, "w_coef": w_coef, "expert_in": expert_in, "expert_out": expert_out, "routes": routes, "dropped": dropped, "cotangent": cotangent}


@jax.custom_vjp
def low(v):
    return lax.optimization_barrier(v.astype(jnp.bfloat16)).astype(jnp.float32)

@jax.custom_vjp
def low_back(v):
    return v

def low_keep(v):
    return (low(v), None)

def low_pass(kept, grad):
    return (grad,)

def back_keep(v):
    return (v, None)

def back_low(kept, grad):
    return (low(grad),)
low.defvjp(low_keep, low_pass)
low_back.defvjp(back_keep, back_low)
highest = lax.Precision.HIGHEST
epsilon = 1e-05

def matmul(left_op, right_op):
    return jnp.dot(left_op, right_op, precision=highest)

def gelu_tanh(values):
    return jax.nn.gelu(values, approximate=True)

def normalize(values):
    centered = values - lax.optimization_barrier(jnp.mean(values, axis=-1, keepdims=True))
    return centered * lax.rsqrt(lax.optimization_barrier(jnp.mean(centered * centered, axis=-1, keepdims=True)) + epsilon)

def attend(qkv_seq):
    queries = qkv_seq[:, :D].reshape(SEQ, H, HD)
    keys_all = qkv_seq[:, D:2 * D].reshape(SEQ, H, HD)
    value_rows = qkv_seq[:, 2 * D:].reshape(SEQ, H, HD)
    scores = jnp.einsum('qhd,khd->hqk', queries, keys_all, precision=highest) * (1.0 / math.sqrt(HD))
    scores = low_back(scores)
    causal = lax.broadcasted_iota(jnp.int32, (SEQ, SEQ), 0) >= lax.broadcasted_iota(jnp.int32, (SEQ, SEQ), 1)
    scores = jnp.where(causal[None], scores, -jnp.inf)
    attn_probs = jax.nn.softmax(scores, axis=-1)
    output = jnp.einsum('hqk,khd->qhd', low(attn_probs), value_rows, precision=highest)
    return output.reshape(SEQ, D)

def expert(seq_items):
    row_block, weight_in, weight_out = seq_items
    hidden = low(gelu_tanh(low_back(matmul(row_block, weight_in))))
    return low(low_back(matmul(hidden, weight_out)))

def reference(tokens, gain_attn, w_qkv, w_out, gain_mix, w_fc, w_proj, w_router, w_coef, expert_in, expert_out, routes, dropped, cotangent):
    devices = N_NODE * N_EXPERT
    route_tok = routes[:, 0].astype(jnp.int32)
    per_device = route_tok.reshape(devices, TOK_DEV)
    chosen_int = (per_device[:, :, None] == jnp.arange(EXPERTS, dtype=jnp.int32)[None, None, :]).astype(jnp.int32)
    position = lax.optimization_barrier(jnp.sum(chosen_int * (jnp.cumsum(chosen_int, axis=1) - 1), axis=2))
    owner_dev = jnp.arange(devices, dtype=jnp.int32)[:, None]
    target = ((per_device * devices + owner_dev) * CAP + position).reshape(TOKENS).astype(jnp.int32)
    source = jnp.zeros((EXPERTS * devices * CAP,), jnp.int32).at[target].set(jnp.arange(TOKENS, dtype=jnp.int32))
    chosen = chosen_int.reshape(TOKENS, EXPERTS).astype(jnp.float32)
    kept_tok = (1 - dropped).astype(jnp.float32)

    def forward(residual, gain_one, qkv_weight, out_weight, gain_two, fc_weight, proj_weight, router_weight, coef_weight, weight_in, weight_out):
        attn_in = low(normalize(residual) * gain_one)
        qkv_rows = low(low_back(matmul(attn_in, qkv_weight)))
        attended = lax.map(jax.checkpoint(attend), qkv_rows.reshape(TOKENS // SEQ, SEQ, 3 * D)).reshape(TOKENS, D)
        attended = low(low_back(attended))
        after_attn = residual + low_back(matmul(attended, out_weight))
        mixed_in = low(normalize(after_attn) * gain_two)
        hidden = low(gelu_tanh(low_back(matmul(mixed_in, fc_weight))))
        dense_out = low_back(matmul(hidden, proj_weight))
        router_probs = jax.nn.softmax(matmul(mixed_in, router_weight), axis=-1)
        gate_tok = lax.optimization_barrier(jnp.sum(router_probs * chosen, axis=1)) * kept_tok
        coef_tok = jax.nn.softmax(matmul(mixed_in, coef_weight), axis=-1)
        sent_rows = low_back(mixed_in)[source].reshape(EXPERTS, devices * CAP, D)
        returned = lax.map(jax.checkpoint(expert), (sent_rows, weight_in, weight_out))
        returned = returned.reshape(EXPERTS * devices * CAP, D)[target]
        return after_attn + coef_tok[:, :1] * dense_out + coef_tok[:, 1:] * gate_tok[:, None] * returned
    floats = (tokens, gain_attn, w_qkv, w_out, gain_mix, w_fc, w_proj, w_router, w_coef, expert_in, expert_out)
    floats = tuple((item.astype(jnp.float32) for item in floats))
    mixed, pullback = jax.vjp(forward, *floats)
    grads = pullback(cotangent.astype(jnp.float32))
    return (mixed.astype(jnp.bfloat16), grads[0], grads[1], grads[2], grads[3], grads[4], grads[5], grads[6], grads[7], grads[8], grads[9], grads[10])
```

```python
import functools
import math

import jax
import jax.numpy as jnp
from jax import lax
from jax.experimental import pallas as pl
from jax.experimental.pallas import tpu as pltpu
from jax.sharding import PartitionSpec as P

HD = 64
PAIR = 2 * HD
SEQ = 512
QB = 256
BLOCK = 512
MIB = 1 << 20
AXES = ("node", "expert")
MESH = pl.DeviceIdType.MESH
highest = lax.Precision.HIGHEST
epsilon = 1e-05
f32 = jnp.float32
bf16 = jnp.bfloat16


def normalize(values):
    centered = values - jnp.mean(values, axis=-1, keepdims=True)
    inv_scale = lax.rsqrt(jnp.mean(centered * centered, axis=-1, keepdims=True) + epsilon)
    return (centered * inv_scale, inv_scale)


def norm_back(grad_norm, normed, inv_scale):
    mean_grad = jnp.mean(grad_norm, axis=-1, keepdims=True)
    mean_cross = jnp.mean(grad_norm * normed, axis=-1, keepdims=True)
    return inv_scale * (grad_norm - mean_grad - normed * mean_cross)


def contract(left_op, right_op, left_dim, right_dim):
    return lax.dot_general(
        left_op, right_op, (((left_dim,), (right_dim,)), ((), ())), preferred_element_type=f32
    )


def matmul(left_op, right_op):
    return contract(left_op, right_op, 1, 0)


def product_tn(left_op, right_op):
    return contract(left_op, right_op, 0, 0)


def outer_nt(left_op, right_op):
    return contract(left_op, right_op, 1, 1)


class Transfer:
    pass


def gather_kernel(experts, plans, n_args, *refs):
    src, dst = refs[:n_args], refs[n_args : 2 * n_args]
    send, recv, loc = refs[2 * n_args :]
    n, e = lax.axis_index("node"), lax.axis_index("expert")
    k, x, y = lax.rem(n, 2), lax.rem(n // 2, 2), n // 4
    nx, ny = y * 4 + (1 - x) * 2 + k, (1 - y) * 4 + x * 2 + k
    nd, nc = (1 - y) * 4 + (1 - x) * 2 + k, y * 4 + x * 2 + 1 - k
    barrier = pltpu.get_barrier_semaphore()
    peers = [(nx, e), (ny, e), (nc, e)] + [(n, lax.rem(e + j, experts)) for j in range(1, experts)]
    for peer in peers:
        pl.semaphore_signal(barrier, inc=1, device_id=peer, device_id_type=MESH)
    pl.semaphore_wait(barrier, len(peers))

    def remote(source, target, item, kind, device):
        return pltpu.make_async_remote_copy(
            src_ref=source,
            dst_ref=target,
            send_sem=send.at[item, kind],
            recv_sem=recv.at[item, kind],
            device_id=device,
            device_id_type=MESH,
        )

    items = []
    for i, (arg, dense, start, size) in enumerate(plans):
        t = Transfer()
        items.append(t)
        cols = pl.ds(start, size)
        shard, whole = src[arg], dst[arg]
        rows = shard.shape[0]
        per = experts if dense else 1
        own = n * per + (e if dense else 0)

        def bundle(m, whole=whole, per=per, cols=cols):
            return whole.at[pl.ds(m * per, per), :, cols]

        def half(m, h, whole=whole, per=per, cols=cols, dense=dense, rows=rows):
            if dense:
                return whole.at[pl.ds(m * per + h * (per // 2), per // 2), :, cols]
            return whole.at[m, pl.ds(h * (rows // 2), rows // 2), cols]

        mine = shard.at[:, cols]
        t.local = pltpu.make_async_copy(mine, whole.at[own, :, cols], loc.at[i])
        t.z = []
        if dense:
            t.z = [
                remote(mine, whole.at[own, :, cols], i, j - 1, (n, lax.rem(e + j, experts)))
                for j in range(1, experts)
            ]
            first, land = bundle(n), bundle(n)
        else:
            first, land = mine, whole.at[n, :, cols]
        b = experts - 1
        t.xy = [remote(first, land, i, b, (nx, e)), remote(first, land, i, b + 1, (ny, e))]
        t.diag = [
            remote(half(nx, 0), half(nx, 0), i, b + 2, (ny, e)),
            remote(half(ny, 1), half(ny, 1), i, b + 3, (nx, e)),
        ]
        t.core = [remote(first, land, i, b + 4, (nc, e))] + [
            remote(bundle(m), bundle(m), i, b + 5 + j, (nc, e)) for j, m in enumerate((nx, ny, nd))
        ]

    def step_z(t):
        t.local.start()
        for copy in t.z:
            copy.start()

    def step_xy(t):
        for copy in t.z:
            copy.wait()
        t.local.wait()
        t.xy[0].start()
        t.xy[1].start()
        t.core[0].start()

    def step_diag(t):
        for i in range(2):
            t.xy[i].wait()
            t.diag[i].start()
            t.core[1 + i].start()

    def step_core(t):
        t.diag[0].wait()
        t.diag[1].wait()
        t.core[3].start()

    def step_end(t):
        for copy in t.core:
            copy.wait()

    steps = (step_z, step_xy, step_diag, step_core, step_end)
    for turn in range(len(items) + len(steps) - 1):
        for late, step in enumerate(steps):
            if 0 <= turn - late < len(items):
                step(items[turn - late])


def gather(args, dense, plans, nodes, experts, collective_id, name):
    m = len(plans)
    outs = [
        jax.ShapeDtypeStruct(((nodes * experts if d else nodes),) + a.shape, a.dtype)
        for a, d in zip(args, dense)
    ]
    plans = [(arg, dense[arg], start, size) for arg, start, size in plans]
    hbm = pl.BlockSpec(memory_space=pltpu.HBM)
    return pl.pallas_call(
        functools.partial(gather_kernel, experts, plans, len(args)),
        out_shape=outs,
        in_specs=[hbm] * len(args),
        out_specs=[hbm] * len(args),
        scratch_shapes=[
            pltpu.SemaphoreType.DMA((m, experts + 7)),
            pltpu.SemaphoreType.DMA((m, experts + 7)),
            pltpu.SemaphoreType.DMA((m,)),
        ],
        compiler_params=pltpu.CompilerParams(collective_id=collective_id, has_side_effects=True),
        name=name,
    )(*args)


def masks():
    lanes = lax.broadcasted_iota(jnp.int32, (1, PAIR), 1)
    return [(lanes // HD == h).astype(bf16) for h in range(2)]


def causal(scores_t, start):
    keys = lax.broadcasted_iota(jnp.int32, scores_t.shape, 0)
    queries = lax.broadcasted_iota(jnp.int32, scores_t.shape, 1) + start
    return jnp.where(keys <= queries, scores_t, -jnp.inf)


def attend_forward_kernel(q_ref, k_ref, v_ref, o_ref, lse_ref):
    q = q_ref[...] * (1.0 / math.sqrt(HD))
    k = k_ref[...]
    vt = v_ref[...].T
    length = q.shape[0]
    outs = []
    for h, mask in enumerate(masks()):
        kh = k * mask
        row = []
        for start in range(0, length, QB):
            end = start + QB
            scores = causal(outer_nt(kh[:end], q[start:end]), start)
            top = jnp.max(scores, axis=0, keepdims=True)
            expd = jnp.exp(scores - top)
            total = jnp.sum(expd, axis=0, keepdims=True)
            probs = (expd / total).astype(bf16)
            row.append(matmul(vt[h * HD : (h + 1) * HD, :end], probs))
            lse_ref[0, h : h + 1, start:end] = top + jnp.log(total)
        outs.append(jnp.concatenate(row, axis=1))
    o_ref[...] = jnp.concatenate(outs, axis=0).T.astype(bf16)


def attend_forward(qkv, width):
    length = qkv.shape[0]
    pairs = width // PAIR
    part = lambda p: pl.BlockSpec((SEQ, PAIR), lambda s, i: (s, p * pairs + i))
    return pl.pallas_call(
        attend_forward_kernel,
        grid=(length // SEQ, pairs),
        out_shape=[
            jax.ShapeDtypeStruct((length, width), bf16),
            jax.ShapeDtypeStruct((length // SEQ * pairs, 2, SEQ), f32),
        ],
        in_specs=[part(0), part(1), part(2)],
        out_specs=[
            pl.BlockSpec((SEQ, PAIR), lambda s, i: (s, i)),
            pl.BlockSpec((1, 2, SEQ), lambda s, i: (s * pairs + i, 0, 0)),
        ],
        cost_estimate=pl.CostEstimate(
            flops=4 * length * SEQ * width, bytes_accessed=10 * length * width, transcendentals=0
        ),
        compiler_params=pltpu.CompilerParams(vmem_limit_bytes=48 * MIB),
        name="attend_forward",
    )(qkv, qkv, qkv)


def attend_backward_kernel(q_ref, k_ref, v_ref, g_ref, lse_ref, d_ref):
    scaling = 1.0 / math.sqrt(HD)
    q, k, v, g = q_ref[...], k_ref[...], v_ref[...], g_ref[...]
    qs = q * scaling
    kt = k.T
    length = q.shape[0]
    grad_k = [0.0] * (length // QB)
    grad_v = [0.0] * (length // QB)
    grad_q = []
    for h, mask in enumerate(masks()):
        kh, vh, qh, gh = k * mask, v * mask, q * mask, g * mask
        row = []
        for c, start in enumerate(range(0, length, QB)):
            end = start + QB
            scores = causal(outer_nt(kh[:end], qs[start:end]), start)
            probs = jnp.exp(scores - lse_ref[0, h : h + 1, start:end])
            grad_probs = outer_nt(vh[:end], g[start:end])
            delta = jnp.sum(probs * grad_probs, axis=0, keepdims=True)
            grad_scores = (probs * (grad_probs - delta)).astype(bf16)
            more_v = matmul(probs.astype(bf16), gh[start:end])
            more_k = matmul(grad_scores, qh[start:end])
            for b in range(c + 1):
                rows = slice(b * QB, (b + 1) * QB)
                grad_v[b] = grad_v[b] + more_v[rows]
                grad_k[b] = grad_k[b] + more_k[rows]
            row.append(matmul(kt[h * HD : (h + 1) * HD, :end], grad_scores))
        grad_q.append(jnp.concatenate(row, axis=1))
    d_ref[0] = (jnp.concatenate(grad_q, axis=0).T * scaling).astype(bf16)
    for b in range(length // QB):
        d_ref[1, b * QB : (b + 1) * QB] = (grad_k[b] * scaling).astype(bf16)
        d_ref[2, b * QB : (b + 1) * QB] = grad_v[b].astype(bf16)


def attend_backward(qkv, lse, grad, width):
    length = qkv.shape[0]
    pairs = width // PAIR
    part = lambda p: pl.BlockSpec((SEQ, PAIR), lambda s, i: (s, p * pairs + i))
    return pl.pallas_call(
        attend_backward_kernel,
        grid=(length // SEQ, pairs),
        out_shape=jax.ShapeDtypeStruct((3, length, width), bf16),
        in_specs=[
            part(0),
            part(1),
            part(2),
            part(0),
            pl.BlockSpec((1, 2, SEQ), lambda s, i: (s * pairs + i, 0, 0)),
        ],
        out_specs=pl.BlockSpec((3, SEQ, PAIR), lambda s, i: (0, s, i)),
        cost_estimate=pl.CostEstimate(
            flops=10 * length * SEQ * width, bytes_accessed=16 * length * width, transcendentals=0
        ),
        compiler_params=pltpu.CompilerParams(vmem_limit_bytes=48 * MIB),
        name="attend_backward",
    )(qkv, qkv, qkv, grad, lse)


def gelu_both(v):
    c = math.sqrt(2.0 / math.pi)
    square = v * v
    t = jnp.tanh(c * (v + 0.044715 * (square * v)))
    half = 0.5 * (1.0 + t)
    slope = half + 0.5 * v * (1.0 - t * t) * (c * (1.0 + (3 * 0.044715) * square))
    return v * half, slope


def mlp_kernel(x_ref, g_ref, w1_ref, w2_ref, out_ref, back_ref, d1_ref, d2_ref, xt, gt, out_sum, back_sum):
    j = pl.program_id(0)

    @pl.when(j == 0)
    def _():
        xt[...] = x_ref[...].T
        gt[...] = g_ref[...].T
        out_sum[...] = jnp.zeros_like(out_sum)
        back_sum[...] = jnp.zeros_like(back_sum)

    w1 = w1_ref[...].reshape(w1_ref.shape[-2:])
    w2 = w2_ref[...].reshape(w2_ref.shape[-2:])
    hidden, slope = gelu_both(matmul(x_ref[...], w1))
    hidden = hidden.astype(bf16)
    grad_pre = (slope * outer_nt(g_ref[...], w2)).astype(bf16)
    out_sum[...] += matmul(hidden, w2)
    back_sum[...] += outer_nt(grad_pre, w1)
    d1_ref[...] = matmul(xt[...], grad_pre).astype(bf16).reshape(d1_ref.shape)
    d2_ref[...] = matmul(gt[...], hidden).astype(bf16).reshape(d2_ref.shape)

    @pl.when(j == pl.num_programs(0) - 1)
    def _():
        out_ref[...] = out_sum[...].astype(out_ref.dtype)
        back_ref[...] = back_sum[...].astype(back_ref.dtype)


def mlp(x, g, w1, w2, out_dtype, name):
    rows, width = x.shape
    if w1.ndim == 3:
        blocks, _, size = w1.shape
        w1_spec = pl.BlockSpec((1, width, size), lambda j: (j, 0, 0))
        w2_spec = pl.BlockSpec((1, size, width), lambda j: (j, 0, 0))
        d_shape = (blocks, width, size)
    else:
        size = BLOCK
        blocks = w1.shape[1] // size
        w1_spec = pl.BlockSpec((width, size), lambda j: (0, j))
        w2_spec = pl.BlockSpec((size, width), lambda j: (j, 0))
        d_shape = (width, blocks * size)
    whole = pl.BlockSpec((rows, width), lambda j: (0, 0))
    return pl.pallas_call(
        mlp_kernel,
        grid=(blocks,),
        out_shape=[jax.ShapeDtypeStruct((rows, width), out_dtype)] * 2
        + [jax.ShapeDtypeStruct(d_shape, bf16)] * 2,
        in_specs=[whole, whole, w1_spec, w2_spec],
        out_specs=[whole, whole, w1_spec, w1_spec],
        scratch_shapes=[
            pltpu.VMEM((width, rows), bf16),
            pltpu.VMEM((width, rows), bf16),
            pltpu.VMEM((rows, width), f32),
            pltpu.VMEM((rows, width), f32),
        ],
        cost_estimate=pl.CostEstimate(
            flops=12 * rows * width * blocks * size,
            bytes_accessed=8 * width * blocks * size,
            transcendentals=rows * blocks * size,
        ),
        compiler_params=pltpu.CompilerParams(vmem_limit_bytes=56 * MIB),
        name=name,
    )(x, g, w1, w2)


def neighbour(axis):
    return [(n, n ^ axis) for n in range(8)]


CORE, X, Y = 1, 2, 4


def hop(values, axis):
    return lax.ppermute(values, "node", neighbour(axis))


def add(*terms):
    return functools.reduce(jnp.add, [t.astype(f32) for t in terms])


def scatter_plane(parts):
    n = lax.axis_index("node")
    k, x, y = lax.rem(n, 2), lax.rem(n // 2, 2), n // 4
    pick = lambda a, i: lax.dynamic_index_in_dim(a, i, 0, keepdims=False)
    rest = parts.shape[1:]
    by_core = parts.reshape((4, 2) + rest)
    take = lambda i: lax.dynamic_index_in_dim(by_core, i, 1, keepdims=False)
    chip = add(take(k), hop(take(1 - k), CORE)).astype(bf16)
    place = y * 2 + x
    own, to_x, to_y, diag = (pick(chip, place ^ i) for i in (0, 1, 2, 3))
    from_x = hop(jnp.stack([diag[0], to_x[0]]), X)
    from_y = hop(jnp.stack([diag[1], to_y[1]]), Y)
    last_x = hop(add(to_x[1], from_y[0]).astype(bf16), X)
    last_y = hop(add(to_y[0], from_x[0]).astype(bf16), Y)
    return jnp.stack([add(own[0], from_x[1], last_y), add(own[1], last_x, from_y[1])])


def scatter_all(parts, experts):
    rest = parts.shape[1:]
    e = lax.axis_index("expert")
    plane = scatter_plane(parts.reshape((8, 2, experts // 2) + rest)).reshape((experts,) + rest)
    mine = lambda i: lax.dynamic_index_in_dim(plane, lax.rem(e + i, experts), 0, keepdims=False)
    terms = [mine(0)]
    for j in range(1, experts):
        shift = [(s, (s + j) % experts) for s in range(experts)]
        terms.append(lax.ppermute(mine(j).astype(bf16), "expert", shift))
    return add(*terms)


def shards(
    fast,
    tokens,
    gain_attn,
    w_qkv,
    w_out,
    gain_mix,
    w_fc,
    w_proj,
    w_router,
    w_coef,
    expert_in,
    expert_out,
    routes,
    dropped,
    cotangent,
):
    experts = lax.axis_size("expert")
    nodes = lax.axis_size("node")
    devices = nodes * experts
    width = tokens.shape[1]
    tok_rows = tokens.shape[0]
    ff = w_fc.shape[1]
    share = w_qkv.shape[0]
    small = jnp.concatenate([gain_attn[:, None], gain_mix[:, None], w_router, w_coef], axis=1)
    small = jnp.pad(small, ((0, 0), (0, 128 - small.shape[1])))
    win, wout = expert_in[0], expert_out[0]
    if fast:
        third = w_qkv.shape[1] // 3
        small_full, qkv_full, out_full = gather(
            [small, w_qkv, w_out],
            [True] * 3,
            [(0, 0, 128)] + [(1, i * third, third) for i in range(3)] + [(2, 0, width)],
            nodes,
            experts,
            1,
            "gather_first",
        )
        quarter = lambda a, d, m: [(a, i * (d // m), d // m) for i in range(m)]
        fc_full, proj_full, win_full, wout_full = gather(
            [w_fc, w_proj, win, wout],
            [True, True, False, False],
            quarter(0, ff, 4) + quarter(1, width, 4) + quarter(2, win.shape[1], 2) + quarter(3, width, 2),
            nodes,
            experts,
            2,
            "gather_rest",
        )
    else:
        small_full, qkv_full, out_full, fc_full, proj_full = (
            lax.all_gather(a, AXES, axis=0, tiled=False) for a in (small, w_qkv, w_out, w_fc, w_proj)
        )
        win_full, wout_full = (lax.all_gather(a, "node", axis=0, tiled=False) for a in (win, wout))
    small_full, qkv_full, out_full, fc_full, proj_full = (
        a.reshape((devices * a.shape[1],) + a.shape[2:])
        for a in (small_full, qkv_full, out_full, fc_full, proj_full)
    )

    def scatter(parts):
        if fast:
            return scatter_all(parts, experts)
        return lax.psum_scatter(parts, AXES, scatter_dimension=0, tiled=False).astype(f32)

    def scatter_experts(parts):
        if fast:
            halves = parts.reshape((nodes, 2, parts.shape[1] // 2) + parts.shape[2:])
            return scatter_plane(halves).reshape(parts.shape[1:])
        return lax.psum_scatter(parts, "node", scatter_dimension=0, tiled=False).astype(f32)

    gain_first = small_full[:, 0].astype(f32)
    gain_second = small_full[:, 1].astype(f32)
    heads = small_full[:, 2 : 4 + experts]

    residual = tokens.astype(f32)
    normed_one, scale_one = normalize(residual)
    attn_in = (normed_one * gain_first).astype(bf16)
    qkv_rows = matmul(attn_in, qkv_full).astype(bf16)
    attended, lse = attend_forward(qkv_rows, width)
    after_attn = residual + matmul(attended, out_full)
    normed_two, scale_two = normalize(after_attn)
    mixed_in = (normed_two * gain_second).astype(bf16)
    logits = matmul(mixed_in, small_full)
    router_probs = jax.nn.softmax(logits[:, 2 : 2 + experts], axis=-1)
    coef_tok = jax.nn.softmax(logits[:, 2 + experts : 4 + experts], axis=-1)

    route_tok = routes[:, 0]
    capacity = -(-(tok_rows * 10) // (8 * experts))
    chosen = (route_tok[:, None] == jnp.arange(experts, dtype=jnp.int32)[None, :]).astype(f32)
    earlier = (
        lax.broadcasted_iota(jnp.int32, (tok_rows, tok_rows), 0)
        > lax.broadcasted_iota(jnp.int32, (tok_rows, tok_rows), 1)
    ).astype(bf16)
    position = jnp.sum(chosen * matmul(earlier, chosen.astype(bf16)), axis=1).astype(jnp.int32)
    turn = lax.rem(route_tok - lax.axis_index("expert") + experts, experts)
    target = turn * capacity + position
    dispatch = (
        lax.broadcasted_iota(jnp.int32, (experts * capacity, tok_rows), 0) == target[None, :]
    ).astype(bf16)
    kept_tok = (1 - dropped).astype(f32)
    gate_prob = jnp.sum(router_probs * chosen, axis=1)
    gate_tok = gate_prob * kept_tok
    weight_tok = coef_tok[:, 1:] * gate_tok[:, None]
    grad_out = cotangent.astype(f32)
    grad_dense = (coef_tok[:, :1] * grad_out).astype(bf16)
    grad_expert = (weight_tok * grad_out).astype(bf16)

    def exchange(parts, sign):
        moved = [parts[0]]
        for j in range(1, experts):
            shift = [(s, (s + sign * j) % experts) for s in range(experts)]
            moved.append(lax.ppermute(parts[j], "expert", shift))
        return jnp.concatenate(moved, axis=0)

    leaving = matmul(dispatch, jnp.concatenate([mixed_in, grad_expert], axis=1)).astype(bf16)
    arrived = exchange(leaving.reshape(experts, capacity, 2 * width), 1)

    dense_out, grad_mixed, d_fc, d_proj = mlp(mixed_in, grad_dense, fc_full, proj_full, f32, "dense_mlp")
    returned, grad_rows, d_win, d_wout = mlp(
        arrived[:, :width], arrived[:, width:], win_full, wout_full, bf16, "expert_mlp"
    )
    leaving = jnp.concatenate([returned, grad_rows], axis=1)
    came_back = exchange(leaving.reshape(experts, capacity, 2 * width), -1)
    came_back = product_tn(dispatch, came_back)
    expert_tok, grad_back = came_back[:, :width], came_back[:, width:]

    grad_fc = scatter(d_fc.reshape(devices, share, ff))
    by_unit = d_proj.reshape(width, devices, ff // devices).transpose(1, 0, 2)
    grad_proj = scatter(by_unit).T
    grad_win = scatter_experts(d_win)[None]
    grad_wout = scatter_experts(d_wout).T[None]

    mixed = after_attn + coef_tok[:, :1] * dense_out + weight_tok * expert_tok
    shared = jnp.sum(grad_out * expert_tok, axis=1)
    grad_coef = jnp.stack([jnp.sum(grad_out * dense_out, axis=1), shared * gate_tok], axis=1)
    grad_coef_logit = coef_tok * (grad_coef - jnp.sum(coef_tok * grad_coef, axis=1, keepdims=True))
    grad_gate = shared * coef_tok[:, 1] * kept_tok
    grad_route_logit = (grad_gate * gate_prob)[:, None] * (chosen - router_probs)
    grad_logits = jnp.concatenate([grad_route_logit, grad_coef_logit], axis=1)
    grad_mixed = grad_mixed + grad_back
    grad_mixed = grad_mixed + jnp.dot(grad_logits, heads.astype(f32).T, precision=highest)
    grad_heads = jnp.dot(mixed_in.astype(f32).T, grad_logits, precision=highest)
    grad_gain_two = jnp.sum(grad_mixed * normed_two, axis=0)
    grad_after = grad_out + norm_back(grad_mixed * gain_second, normed_two, scale_two)
    grad_attn = grad_after.astype(bf16)
    grad_wo = scatter(product_tn(attended, grad_attn).astype(bf16).reshape(devices, share, width))
    grad_attended = outer_nt(grad_attn, out_full).astype(bf16)
    grad_qkv = attend_backward(qkv_rows, lse, grad_attended, width)
    d_qkv = jnp.concatenate([product_tn(attn_in, grad_qkv[i]).astype(bf16) for i in range(3)], axis=1)
    grad_attn_in = sum(outer_nt(grad_qkv[i], qkv_full[:, i * width : (i + 1) * width]) for i in range(3))
    grad_gain_one = jnp.sum(grad_attn_in * normed_one, axis=0)
    tokens_grad = grad_after + norm_back(grad_attn_in * gain_first, normed_one, scale_one)
    grad_wqkv = scatter(d_qkv.reshape(devices, share, 3 * width))
    d_small = jnp.concatenate([grad_gain_one[:, None], grad_gain_two[:, None], grad_heads], axis=1)
    d_small = jnp.pad(d_small, ((0, 0), (0, 128 - d_small.shape[1]))).astype(bf16)
    grad_small = scatter(d_small.reshape(devices, share, 128))
    return (
        mixed.astype(bf16),
        tokens_grad,
        grad_small[:, 0],
        grad_wqkv,
        grad_wo,
        grad_small[:, 1],
        grad_fc,
        grad_proj,
        grad_small[:, 2 : 2 + experts],
        grad_small[:, 2 + experts : 4 + experts],
        grad_win,
        grad_wout,
    )


def solution(mesh):
    rows = P(AXES, None)
    in_specs = (
        rows,
        P(AXES),
        rows,
        rows,
        P(AXES),
        rows,
        rows,
        rows,
        rows,
        P("expert", None, "node"),
        P("expert", "node", None),
        rows,
        P(AXES),
        rows,
    )
    out_specs = (
        rows,
        rows,
        P(AXES),
        rows,
        rows,
        P(AXES),
        rows,
        rows,
        rows,
        rows,
        P("expert", None, "node"),
        P("expert", "node", None),
    )
    fast = mesh.shape["node"] == 8 and mesh.shape["expert"] % 2 == 0
    return jax.shard_map(
        functools.partial(shards, fast), mesh=mesh, in_specs=in_specs, out_specs=out_specs, check_vma=False
    )
```

```python
import functools
import math

import jax
import jax.numpy as jnp
from jax import lax
from jax.experimental import pallas as pl
from jax.experimental.pallas import tpu as pltpu
from jax.sharding import PartitionSpec as P

HD = 64
PAIR = 2 * HD
SEQ = 512
QB = 256
BLOCK = 512
MIB = 1 << 20
AXES = ("node", "expert")
MESH = pl.DeviceIdType.MESH
highest = lax.Precision.HIGHEST
epsilon = 1e-05
f32 = jnp.float32
bf16 = jnp.bfloat16


def normalize(values):
    centered = values - jnp.mean(values, axis=-1, keepdims=True)
    inv_scale = lax.rsqrt(jnp.mean(centered * centered, axis=-1, keepdims=True) + epsilon)
    return (centered * inv_scale, inv_scale)


def norm_back(grad_norm, normed, inv_scale):
    mean_grad = jnp.mean(grad_norm, axis=-1, keepdims=True)
    mean_cross = jnp.mean(grad_norm * normed, axis=-1, keepdims=True)
    return inv_scale * (grad_norm - mean_grad - normed * mean_cross)


def contract(left_op, right_op, left_dim, right_dim):
    return lax.dot_general(
        left_op, right_op, (((left_dim,), (right_dim,)), ((), ())), preferred_element_type=f32
    )


def matmul(left_op, right_op):
    return contract(left_op, right_op, 1, 0)


def product_tn(left_op, right_op):
    return contract(left_op, right_op, 0, 0)


def outer_nt(left_op, right_op):
    return contract(left_op, right_op, 1, 1)


class Place:
    def __init__(self, experts):
        self.experts = experts
        self.n, self.e = lax.axis_index("node"), lax.axis_index("expert")
        n = self.n
        self.k, self.x, self.y = lax.rem(n, 2), lax.rem(n // 2, 2), n // 4
        k, x, y = self.k, self.x, self.y
        self.nx, self.ny = y * 4 + (1 - x) * 2 + k, (1 - y) * 4 + x * 2 + k
        self.nd, self.nc = (1 - y) * 4 + (1 - x) * 2 + k, y * 4 + x * 2 + 1 - k

    def z(self, j):
        return (self.n, lax.rem(self.e + j, self.experts))

    def greet(self, along_z):
        barrier = pltpu.get_barrier_semaphore()
        peers = [(self.nx, self.e), (self.ny, self.e), (self.nc, self.e)]
        if along_z:
            peers += [self.z(j) for j in range(1, self.experts)]
        for peer in peers:
            pl.semaphore_signal(barrier, inc=1, device_id=peer, device_id_type=MESH)
        pl.semaphore_wait(barrier, len(peers))


def when(condition):
    return pl.when(condition)


class Gather:
    late = 4

    def __init__(self, args, dense, items, nodes, experts):
        self.args, self.dense, self.items, self.experts = args, dense, items, experts
        self.outs = [
            jax.ShapeDtypeStruct(((nodes * experts if d else nodes),) + a.shape, a.dtype)
            for a, d in zip(args, dense)
        ]
        hbm = pl.BlockSpec(memory_space=pltpu.HBM)
        self.in_specs, self.out_specs = [hbm] * len(args), [hbm] * len(args)
        m = len(items)
        self.scratch = [
            pltpu.SemaphoreType.DMA((m, experts + 7)),
            pltpu.SemaphoreType.DMA((m, experts + 7)),
            pltpu.SemaphoreType.DMA((m,)),
        ]
        self.turns = m + self.late
        self.along_z = any(dense)

    def bind(self, ins, outs, scratch, place):
        experts = self.experts
        send, recv, loc = scratch
        p, e = place, place.e

        def remote(source, target, item, kind, device):
            return pltpu.make_async_remote_copy(
                src_ref=source,
                dst_ref=target,
                send_sem=send.at[item, kind],
                recv_sem=recv.at[item, kind],
                device_id=device,
                device_id_type=MESH,
            )

        self.bound = []
        for i, (arg, start, size) in enumerate(self.items):
            dense = self.dense[arg]
            cols = pl.ds(start, size)
            shard, whole = ins[arg], outs[arg]
            rows = shard.shape[0]
            per = experts if dense else 1
            own = p.n * per + (e if dense else 0)

            def bundle(m, whole=whole, per=per, cols=cols):
                return whole.at[pl.ds(m * per, per), :, cols]

            def half(m, h, whole=whole, per=per, cols=cols, dense=dense, rows=rows):
                if dense:
                    return whole.at[pl.ds(m * per + h * (per // 2), per // 2), :, cols]
                return whole.at[m, pl.ds(h * (rows // 2), rows // 2), cols]

            mine = shard.at[:, cols]
            local = pltpu.make_async_copy(mine, whole.at[own, :, cols], loc.at[i])
            z = []
            if dense:
                z = [remote(mine, whole.at[own, :, cols], i, j - 1, p.z(j)) for j in range(1, experts)]
                first, land = bundle(p.n), bundle(p.n)
            else:
                first, land = mine, whole.at[p.n, :, cols]
            b = experts - 1
            xy = [remote(first, land, i, b, (p.nx, e)), remote(first, land, i, b + 1, (p.ny, e))]
            diag = [
                remote(half(p.nx, 0), half(p.nx, 0), i, b + 2, (p.ny, e)),
                remote(half(p.ny, 1), half(p.ny, 1), i, b + 3, (p.nx, e)),
            ]
            core = [remote(first, land, i, b + 4, (p.nc, e))] + [
                remote(bundle(m), bundle(m), i, b + 5 + j, (p.nc, e)) for j, m in enumerate((p.nx, p.ny, p.nd))
            ]
            self.bound.append((local, z, xy, diag, core))

    def turn(self, now):
        steps = (self.along, self.across, self.corner, self.over, self.end)
        for t in range(self.turns):

            @when(now == t)
            def _(t=t):
                for late, step in enumerate(steps):
                    if 0 <= t - late < len(self.items):
                        step(*self.bound[t - late])

    def along(self, local, z, xy, diag, core):
        local.start()
        for copy in z:
            copy.start()

    def across(self, local, z, xy, diag, core):
        for copy in z:
            copy.wait()
        local.wait()
        xy[0].start()
        xy[1].start()
        core[0].start()

    def corner(self, local, z, xy, diag, core):
        for i in range(2):
            xy[i].wait()
            diag[i].start()
            core[1 + i].start()

    def over(self, local, z, xy, diag, core):
        diag[0].wait()
        diag[1].wait()
        core[3].start()

    def end(self, local, z, xy, diag, core):
        for copy in core:
            copy.wait()


class Scatter:
    def __init__(self, arrays, layout, experts):
        self.args, self.layout, self.experts = arrays, layout, experts
        dense = self.dense = layout != "plane"
        shape = arrays[0].shape
        if layout == "plane":
            counts, h = [a.shape[2] for a in arrays], shape[4:]
        elif layout == "rows":
            counts, h = [a.shape[4] for a in arrays], shape[3:4] + shape[5:]
        else:
            counts, h = [a.shape[5] // BLOCK for a in arrays], shape[3:5] + (BLOCK,)
        self.starts = [sum(counts[:a]) for a in range(len(arrays) + 1)]
        m = self.m = sum(counts)
        self.half = h
        unit = h[1:] if dense else (2,) + h
        self.outs = [jax.ShapeDtypeStruct((m,) + unit, f32)]
        self.in_specs = [pl.BlockSpec(memory_space=pltpu.HBM)] * len(arrays)
        self.out_specs = [pl.BlockSpec(memory_space=pltpu.VMEM)]
        kinds = 7 + experts
        self.scratch = [
            pltpu.VMEM((m, 4, 2) + h, bf16),
            pltpu.VMEM((m, 4, 2) + h, bf16),
            pltpu.VMEM((m, 2) + h, bf16),
            pltpu.VMEM((m, 2) + h, bf16),
            pltpu.VMEM((m,) + h, bf16),
            pltpu.VMEM((m,) + h, bf16),
            pltpu.SemaphoreType.DMA((m, kinds)),
            pltpu.SemaphoreType.DMA((m, kinds)),
            pltpu.SemaphoreType.DMA((m,)),
        ]
        if dense:
            self.scratch.append(pltpu.VMEM((m, experts - 1) + unit, bf16))
        self.late = 4 if dense else 3
        self.turns = m + self.late
        self.along_z = dense

    def bind(self, ins, outs, scratch, place):
        self.ins, self.out, self.place = ins, outs[0], place
        self.own, self.rc, self.rx, self.ry, self.lx, self.ly, self.send, self.recv, self.loc = scratch[:9]
        self.rz = scratch[9] if self.dense else None

    def remote(self, source, target, item, kind, device):
        return pltpu.make_async_remote_copy(
            src_ref=source,
            dst_ref=target,
            send_sem=self.send.at[item, kind],
            recv_sem=self.recv.at[item, kind],
            device_id=device,
            device_id_type=MESH,
        )

    def part(self, source, core, chunk):
        if self.layout == "plane":
            return source.at[:, core, chunk]
        if self.layout == "rows":
            return source.at[:, core, :, :, chunk]
        return source.at[:, core, :, :, :, pl.ds(pl.multiple_of(chunk * BLOCK, BLOCK), BLOCK)]

    def first(self, source, i, chunk):
        p = self.place
        local = pltpu.make_async_copy(self.part(source, p.k, chunk), self.own.at[i], self.loc.at[i])
        over = self.remote(self.part(source, 1 - p.k, chunk), self.rc.at[i], i, 0, (p.nc, p.e))
        return local, over

    def sites(self):
        p = self.place
        return p.y * 2 + p.x, p.y * 2 + 1 - p.x, (1 - p.y) * 2 + p.x, (1 - p.y) * 2 + 1 - p.x

    def round_one(self, i):
        p = self.place
        _, to_x, to_y, diag = self.sites()
        return [
            self.remote(self.own.at[i, diag, 0], self.rx.at[i, 0], i, 1, (p.nx, p.e)),
            self.remote(self.own.at[i, diag, 1], self.ry.at[i, 0], i, 2, (p.ny, p.e)),
            self.remote(self.own.at[i, to_x, 0], self.rx.at[i, 1], i, 3, (p.nx, p.e)),
            self.remote(self.own.at[i, to_y, 1], self.ry.at[i, 1], i, 4, (p.ny, p.e)),
        ]

    def round_two(self, i):
        p = self.place
        _, to_x, to_y, _ = self.sites()
        return [
            self.remote(self.own.at[i, to_x, 1], self.lx.at[i], i, 5, (p.nx, p.e)),
            self.remote(self.own.at[i, to_y, 0], self.ly.at[i], i, 6, (p.ny, p.e)),
        ]

    def round_z(self, i):
        p = self.place
        mine, _, _, _ = self.sites()
        s = self.experts // 2
        copies = []
        for j in range(1, self.experts):
            to = lax.rem(p.e + j, self.experts)
            source = self.own.at[i, mine, to // s, lax.rem(to, s)]
            copies.append(self.remote(source, self.rz.at[i, j - 1], i, 6 + j, p.z(j)))
        return copies

    def turn(self, now):
        steps = (self.load, self.chip, self.cross, self.plane, self.column)
        for late, step in enumerate(steps[: self.late + 1]):
            i = now - late

            @when(jnp.logical_and(i >= 0, i < self.m))
            def _(step=step, i=i):
                step(i)

    def load(self, i):
        for a, source in enumerate(self.ins):

            @when(jnp.logical_and(i >= self.starts[a], i < self.starts[a + 1]))
            def _(a=a, source=source):
                local, over = self.first(source, i, i - self.starts[a])
                over.start()
                local.start()

    def chip(self, i):
        local, over = self.first(self.ins[0], i, 0)
        local.wait()
        over.wait()

        def sum_one(q, _):
            self.own[i, q] = add(self.own[i, q], self.rc[i, q]).astype(bf16)
            return 0

        lax.fori_loop(0, 4, sum_one, 0)
        for copy in self.round_one(i):
            copy.start()

    def cross(self, i):
        one = self.round_one(i)
        two = self.round_two(i)
        _, to_x, to_y, _ = self.sites()
        for copy in one:
            copy.wait()
        self.own[i, to_x, 1] = add(self.own[i, to_x, 1], self.ry[i, 0]).astype(bf16)
        two[0].start()
        self.own[i, to_y, 0] = add(self.own[i, to_y, 0], self.rx[i, 0]).astype(bf16)
        two[1].start()

    def plane(self, i):
        for copy in self.round_two(i):
            copy.wait()
        mine, _, _, _ = self.sites()
        sums = (
            add(self.own[i, mine, 0], self.rx[i, 1], self.ly[i]),
            add(self.own[i, mine, 1], self.lx[i], self.ry[i, 1]),
        )
        if not self.dense:
            for h in range(2):
                self.out[i, h] = sums[h]
            return
        for h in range(2):
            self.own[i, mine, h] = sums[h].astype(bf16)
        for copy in self.round_z(i):
            copy.start()

    def column(self, i):
        for copy in self.round_z(i):
            copy.wait()
        p = self.place
        mine, _, _, _ = self.sites()
        s = self.experts // 2
        terms = [self.own[i, mine, p.e // s, lax.rem(p.e, s)]] + [self.rz[i, j] for j in range(self.experts - 1)]
        self.out[i] = add(*terms)


def add(*terms):
    return functools.reduce(jnp.add, [t.astype(f32) for t in terms])


def call(name, steps, body, args, in_specs, outs, out_specs, scratch, moves, collective_id, experts, flops):
    total = max(steps, moves.turns if moves else 0)

    def hold(spec):
        if spec.block_shape is None:
            return spec
        index = spec.index_map
        return pl.BlockSpec(spec.block_shape, lambda j: index(jnp.minimum(j, steps - 1)))

    n_in, n_out, n_scratch = len(args), len(outs), len(scratch)
    m_in, m_out = (len(moves.args), len(moves.outs)) if moves else (0, 0)

    def kernel(*refs):
        refs = list(refs)
        take = lambda count: [refs.pop(0) for _ in range(count)]
        ins, m_ins, os, m_os, own = take(n_in), take(m_in), take(n_out), take(m_out), take(n_scratch)
        now = pl.program_id(0)
        if moves:
            place = Place(experts)
            moves.bind(m_ins, m_os, refs, place)

            @when(now == 0)
            def _():
                place.greet(moves.along_z)

            moves.turn(now)
        if body is not None:

            @when(now < steps)
            def _():
                body(now, steps, *ins, *os, *own)

    return pl.pallas_call(
        kernel,
        grid=(total,),
        out_shape=list(outs) + (moves.outs if moves else []),
        in_specs=[hold(s) for s in in_specs] + (moves.in_specs if moves else []),
        out_specs=[hold(s) for s in out_specs] + (moves.out_specs if moves else []),
        scratch_shapes=list(scratch) + (moves.scratch if moves else []),
        cost_estimate=pl.CostEstimate(flops=flops, bytes_accessed=32 * MIB, transcendentals=0),
        compiler_params=pltpu.CompilerParams(
            vmem_limit_bytes=60 * MIB,
            **({"collective_id": collective_id, "has_side_effects": True} if moves else {}),
        ),
        name=name,
    )(*args, *(moves.args if moves else []))


def masks():
    lanes = lax.broadcasted_iota(jnp.int32, (1, PAIR), 1)
    return [(lanes // HD == h).astype(bf16) for h in range(2)]


def causal(scores_t, start):
    keys = lax.broadcasted_iota(jnp.int32, scores_t.shape, 0)
    queries = lax.broadcasted_iota(jnp.int32, scores_t.shape, 1) + start
    return jnp.where(keys <= queries, scores_t, -jnp.inf)


def attend_forward_kernel(q_ref, k_ref, v_ref, o_ref, lse_ref):
    q = q_ref[...] * (1.0 / math.sqrt(HD))
    k = k_ref[...]
    vt = v_ref[...].T
    length = q.shape[0]
    outs = []
    for h, mask in enumerate(masks()):
        kh = k * mask
        row = []
        for start in range(0, length, QB):
            end = start + QB
            scores = causal(outer_nt(kh[:end], q[start:end]), start)
            top = jnp.max(scores, axis=0, keepdims=True)
            expd = jnp.exp(scores - top)
            total = jnp.sum(expd, axis=0, keepdims=True)
            probs = (expd / total).astype(bf16)
            row.append(matmul(vt[h * HD : (h + 1) * HD, :end], probs))
            lse_ref[0, h : h + 1, start:end] = top + jnp.log(total)
        outs.append(jnp.concatenate(row, axis=1))
    o_ref[...] = jnp.concatenate(outs, axis=0).T.astype(bf16)


def attend_forward(qkv, width, moves, collective_id, experts):
    length = qkv.shape[0]
    pairs = width // PAIR
    part = lambda p: pl.BlockSpec((SEQ, PAIR), lambda j: (j // pairs, p * pairs + lax.rem(j, pairs)))
    steps = length // SEQ * pairs
    return call(
        "attend_forward",
        steps,
        lambda now, steps, *refs: attend_forward_kernel(*refs),
        [qkv] * 3,
        [part(0), part(1), part(2)],
        [
            jax.ShapeDtypeStruct((length, width), bf16),
            jax.ShapeDtypeStruct((steps, 2, SEQ), f32),
        ],
        [part(0), pl.BlockSpec((1, 2, SEQ), lambda j: (j, 0, 0))],
        [],
        moves,
        collective_id,
        experts,
        4 * length * SEQ * width,
    )


def attend_backward_kernel(q_ref, k_ref, v_ref, g_ref, lse_ref, d_ref):
    scaling = 1.0 / math.sqrt(HD)
    q, k, v, g = q_ref[...], k_ref[...], v_ref[...], g_ref[...]
    qs = q * scaling
    kt = k.T
    length = q.shape[0]
    grad_k = [0.0] * (length // QB)
    grad_v = [0.0] * (length // QB)
    grad_q = []
    for h, mask in enumerate(masks()):
        kh, vh, qh, gh = k * mask, v * mask, q * mask, g * mask
        row = []
        for c, start in enumerate(range(0, length, QB)):
            end = start + QB
            scores = causal(outer_nt(kh[:end], qs[start:end]), start)
            probs = jnp.exp(scores - lse_ref[0, h : h + 1, start:end])
            grad_probs = outer_nt(vh[:end], g[start:end])
            delta = jnp.sum(probs * grad_probs, axis=0, keepdims=True)
            grad_scores = (probs * (grad_probs - delta)).astype(bf16)
            more_v = matmul(probs.astype(bf16), gh[start:end])
            more_k = matmul(grad_scores, qh[start:end])
            for b in range(c + 1):
                rows = slice(b * QB, (b + 1) * QB)
                grad_v[b] = grad_v[b] + more_v[rows]
                grad_k[b] = grad_k[b] + more_k[rows]
            row.append(matmul(kt[h * HD : (h + 1) * HD, :end], grad_scores))
        grad_q.append(jnp.concatenate(row, axis=1))
    d_ref[0] = (jnp.concatenate(grad_q, axis=0).T * scaling).astype(bf16)
    for b in range(length // QB):
        d_ref[1, b * QB : (b + 1) * QB] = (grad_k[b] * scaling).astype(bf16)
        d_ref[2, b * QB : (b + 1) * QB] = grad_v[b].astype(bf16)


def attend_backward(qkv, lse, grad, width, moves, collective_id, experts):
    length = qkv.shape[0]
    pairs = width // PAIR
    part = lambda p: pl.BlockSpec((SEQ, PAIR), lambda j: (j // pairs, p * pairs + lax.rem(j, pairs)))
    return call(
        "attend_backward",
        length // SEQ * pairs,
        lambda now, steps, *refs: attend_backward_kernel(*refs),
        [qkv, qkv, qkv, grad, lse],
        [part(0), part(1), part(2), part(0), pl.BlockSpec((1, 2, SEQ), lambda j: (j, 0, 0))],
        [jax.ShapeDtypeStruct((3, length, width), bf16)],
        [pl.BlockSpec((3, SEQ, PAIR), lambda j: (0, j // pairs, lax.rem(j, pairs)))],
        [],
        moves,
        collective_id,
        experts,
        10 * length * SEQ * width,
    )


def gelu_both(v):
    c = math.sqrt(2.0 / math.pi)
    square = v * v
    t = jnp.tanh(c * (v + 0.044715 * (square * v)))
    half = 0.5 * (1.0 + t)
    slope = half + 0.5 * v * (1.0 - t * t) * (c * (1.0 + (3 * 0.044715) * square))
    return v * half, slope


def mlp_kernel(share, now, steps, x_ref, g_ref, w1_ref, w2_ref, out_ref, back_ref, d1_ref, d2_ref, xt, gt, out_sum, back_sum):
    @when(now == 0)
    def _():
        xt[...] = x_ref[...].T
        gt[...] = g_ref[...].T
        out_sum[...] = jnp.zeros_like(out_sum)
        back_sum[...] = jnp.zeros_like(back_sum)

    w1 = w1_ref[...].reshape(w1_ref.shape[-2:])
    w2 = w2_ref[...].reshape(w2_ref.shape[-2:])
    hidden, slope = gelu_both(matmul(x_ref[...], w1))
    hidden = hidden.astype(bf16)
    grad_pre = (slope * outer_nt(g_ref[...], w2)).astype(bf16)
    out_sum[...] += matmul(hidden, w2)
    back_sum[...] += outer_nt(grad_pre, w1)
    d1 = matmul(xt[...], grad_pre).astype(bf16)
    d2 = matmul(gt[...], hidden).astype(bf16)
    if share is None:
        d1_ref[...] = d1.reshape(d1_ref.shape)
        d2_ref[...] = d2.reshape(d2_ref.shape)
    else:
        for c in range(d1.shape[1] // 128):
            cols = slice(c * 128, (c + 1) * 128)
            for s in range(d1_ref.shape[0]):
                d1_ref[s, c * share : (c + 1) * share] = d1[s * share : (s + 1) * share, cols]
            d2_ref[c] = d2[:, cols]

    @when(now == steps - 1)
    def _():
        out_ref[...] = out_sum[...].astype(out_ref.dtype)
        back_ref[...] = back_sum[...].astype(back_ref.dtype)


def mlp(x, g, w1, w2, out_dtype, name, moves, collective_id, experts, devices=None):
    rows, width = x.shape
    share = None
    if w1.ndim == 3:
        blocks, _, size = w1.shape
        w1_spec = pl.BlockSpec((1, width, size), lambda j: (j, 0, 0))
        w2_spec = pl.BlockSpec((1, size, width), lambda j: (j, 0, 0))
        d_shape, d_specs = (blocks, width, size), [w1_spec] * 2
    else:
        size = BLOCK
        blocks = w1.shape[1] // size
        w1_spec = pl.BlockSpec((width, size), lambda j: (0, j))
        w2_spec = pl.BlockSpec((size, width), lambda j: (j, 0))
        d_shape, d_specs = (width, blocks * size), [w1_spec] * 2
        if devices:
            share = width // devices
            d_shape = (devices, width, 128)
            d_specs = [
                pl.BlockSpec((devices, size // 128 * share, 128), lambda j: (0, j, 0)),
                pl.BlockSpec((size // 128, width, 128), lambda j: (j, 0, 0)),
            ]
    whole = pl.BlockSpec(memory_space=pltpu.VMEM)
    return call(
        name,
        blocks,
        functools.partial(mlp_kernel, share),
        [x, g, w1, w2],
        [whole, whole, w1_spec, w2_spec],
        [jax.ShapeDtypeStruct((rows, width), out_dtype)] * 2 + [jax.ShapeDtypeStruct(d_shape, bf16)] * 2,
        [whole, whole] + d_specs,
        [
            pltpu.VMEM((width, rows), bf16),
            pltpu.VMEM((width, rows), bf16),
            pltpu.VMEM((rows, width), f32),
            pltpu.VMEM((rows, width), f32),
        ],
        moves,
        collective_id,
        experts,
        12 * rows * width * blocks * size,
    )


def move(name, moves, collective_id, experts):
    return call(name, 1, None, [], [], [], [], [], moves, collective_id, experts, 0)


def shards(
    fast,
    tokens,
    gain_attn,
    w_qkv,
    w_out,
    gain_mix,
    w_fc,
    w_proj,
    w_router,
    w_coef,
    expert_in,
    expert_out,
    routes,
    dropped,
    cotangent,
):
    experts = lax.axis_size("expert")
    nodes = lax.axis_size("node")
    devices = nodes * experts
    width = tokens.shape[1]
    tok_rows = tokens.shape[0]
    ff = w_fc.shape[1]
    share = w_qkv.shape[0]
    small = jnp.concatenate([gain_attn[:, None], gain_mix[:, None], w_router, w_coef], axis=1)
    small = jnp.pad(small, ((0, 0), (0, 128 - small.shape[1])))
    win, wout = expert_in[0], expert_out[0]
    together = lambda a: a.reshape((devices * a.shape[1],) + a.shape[2:])
    cut = lambda a, d, m: [(a, i * (d // m), d // m) for i in range(m)]
    gather_dense = gather_experts = None
    if fast:
        first = Gather(
            [small, w_qkv, w_out],
            [True] * 3,
            [(0, 0, 128)] + cut(1, 3 * width, 3) + [(2, 0, width)],
            nodes,
            experts,
        )
        small_full, qkv_full, out_full = move("gather_first", first, 1, experts)
        gather_dense = Gather([w_fc, w_proj], [True] * 2, cut(0, ff, 4) + cut(1, width, 4), nodes, experts)
        gather_experts = Gather(
            [win, wout], [False] * 2, cut(0, win.shape[1], 4) + cut(1, width, 4), nodes, experts
        )
    else:
        small_full, qkv_full, out_full, fc_full, proj_full = (
            lax.all_gather(a, AXES, axis=0, tiled=False) for a in (small, w_qkv, w_out, w_fc, w_proj)
        )
        win_full, wout_full = (lax.all_gather(a, "node", axis=0, tiled=False) for a in (win, wout))
    small_full, qkv_full, out_full = (together(a) for a in (small_full, qkv_full, out_full))

    def scatter_xla(parts, axes):
        return lax.psum_scatter(parts, axes, scatter_dimension=0, tiled=False).astype(f32)

    gain_first = small_full[:, 0].astype(f32)
    gain_second = small_full[:, 1].astype(f32)
    heads = small_full[:, 2 : 4 + experts]

    residual = tokens.astype(f32)
    normed_one, scale_one = normalize(residual)
    attn_in = (normed_one * gain_first).astype(bf16)
    qkv_rows = matmul(attn_in, qkv_full).astype(bf16)
    attended, lse, *gathered = attend_forward(qkv_rows, width, gather_dense, 2, experts)
    if fast:
        fc_full, proj_full = gathered
    fc_full, proj_full = together(fc_full), together(proj_full)
    after_attn = residual + matmul(attended, out_full)
    normed_two, scale_two = normalize(after_attn)
    mixed_in = (normed_two * gain_second).astype(bf16)
    logits = matmul(mixed_in, small_full)
    router_probs = jax.nn.softmax(logits[:, 2 : 2 + experts], axis=-1)
    coef_tok = jax.nn.softmax(logits[:, 2 + experts : 4 + experts], axis=-1)

    route_tok = routes[:, 0]
    capacity = -(-(tok_rows * 10) // (8 * experts))
    chosen = (route_tok[:, None] == jnp.arange(experts, dtype=jnp.int32)[None, :]).astype(f32)
    earlier = (
        lax.broadcasted_iota(jnp.int32, (tok_rows, tok_rows), 0)
        > lax.broadcasted_iota(jnp.int32, (tok_rows, tok_rows), 1)
    ).astype(bf16)
    position = jnp.sum(chosen * matmul(earlier, chosen.astype(bf16)), axis=1).astype(jnp.int32)
    turn = lax.rem(route_tok - lax.axis_index("expert") + experts, experts)
    target = turn * capacity + position
    dispatch = (
        lax.broadcasted_iota(jnp.int32, (experts * capacity, tok_rows), 0) == target[None, :]
    ).astype(bf16)
    kept_tok = (1 - dropped).astype(f32)
    gate_prob = jnp.sum(router_probs * chosen, axis=1)
    gate_tok = gate_prob * kept_tok
    weight_tok = coef_tok[:, 1:] * gate_tok[:, None]
    grad_out = cotangent.astype(f32)
    grad_dense = (coef_tok[:, :1] * grad_out).astype(bf16)
    grad_expert = (weight_tok * grad_out).astype(bf16)

    def exchange(parts, sign):
        moved = [parts[0]]
        for j in range(1, experts):
            shift = [(s, (s + sign * j) % experts) for s in range(experts)]
            moved.append(lax.ppermute(parts[j], "expert", shift))
        return jnp.concatenate(moved, axis=0)

    leaving = matmul(dispatch, jnp.concatenate([mixed_in, grad_expert], axis=1)).astype(bf16)
    arrived = exchange(leaving.reshape(experts, capacity, 2 * width), 1)

    dense_out, grad_mixed, d_fc, d_proj, *gathered = mlp(
        mixed_in, grad_dense, fc_full, proj_full, f32, "dense_mlp", gather_experts, 3, experts, devices if fast else None
    )
    scatter_dense = None
    if fast:
        win_full, wout_full = gathered
        by_chip = lambda a: a.reshape(4, 2, 2, experts // 2, 4, width // 4, 128)
        scatter_dense = Scatter([by_chip(d_fc), by_chip(d_proj)], "rows", experts)
    returned, grad_rows, d_win, d_wout, *scattered = mlp(
        arrived[:, :width], arrived[:, width:], win_full, wout_full, bf16, "expert_mlp", scatter_dense, 4, experts
    )
    leaving = jnp.concatenate([returned, grad_rows], axis=1)
    came_back = exchange(leaving.reshape(experts, capacity, 2 * width), -1)
    if fast:
        by_column = scattered[0].reshape(2, width, 128)
        grad_fc = by_column[0].reshape(ff // 128, share, 128).transpose(1, 0, 2).reshape(share, ff)
        grad_proj = by_column[1].T
        cut_rows = lambda a: a.reshape(4, 2, 8, 2, width // 16, a.shape[2])
        scatter_win = Scatter([cut_rows(d_win)], "plane", experts)
        scatter_wout = Scatter([cut_rows(d_wout)], "plane", experts)
        (grad_win,) = move("scatter_win", scatter_win, 5, experts)
        grad_win = grad_win.reshape(width, -1)
    else:
        grad_fc = scatter_xla(d_fc.reshape(devices, share, ff), AXES)
        by_unit = d_proj.reshape(width, devices, ff // devices).transpose(1, 0, 2)
        grad_proj = scatter_xla(by_unit, AXES).T
        grad_win = scatter_xla(d_win, "node")
        grad_wout = scatter_xla(d_wout, "node")
        scatter_wout = None
    came_back = product_tn(dispatch, came_back)
    expert_tok, grad_back = came_back[:, :width], came_back[:, width:]

    mixed = after_attn + coef_tok[:, :1] * dense_out + weight_tok * expert_tok
    shared = jnp.sum(grad_out * expert_tok, axis=1)
    grad_coef = jnp.stack([jnp.sum(grad_out * dense_out, axis=1), shared * gate_tok], axis=1)
    grad_coef_logit = coef_tok * (grad_coef - jnp.sum(coef_tok * grad_coef, axis=1, keepdims=True))
    grad_gate = shared * coef_tok[:, 1] * kept_tok
    grad_route_logit = (grad_gate * gate_prob)[:, None] * (chosen - router_probs)
    grad_logits = jnp.concatenate([grad_route_logit, grad_coef_logit], axis=1)
    grad_mixed = grad_mixed + grad_back
    grad_mixed = grad_mixed + jnp.dot(grad_logits, heads.astype(f32).T, precision=highest)
    grad_heads = jnp.dot(mixed_in.astype(f32).T, grad_logits, precision=highest)
    grad_gain_two = jnp.sum(grad_mixed * normed_two, axis=0)
    grad_after = grad_out + norm_back(grad_mixed * gain_second, normed_two, scale_two)
    grad_attn = grad_after.astype(bf16)
    d_out = product_tn(attended, grad_attn).astype(bf16)
    grad_attended = outer_nt(grad_attn, out_full).astype(bf16)
    grad_qkv, *scattered = attend_backward(qkv_rows, lse, grad_attended, width, scatter_wout, 6, experts)
    if fast:
        grad_wout = scattered[0].reshape(width, -1)
    d_qkv = [product_tn(attn_in, grad_qkv[i]).astype(bf16) for i in range(3)]
    grad_attn_in = sum(outer_nt(grad_qkv[i], qkv_full[:, i * width : (i + 1) * width]) for i in range(3))
    grad_gain_one = jnp.sum(grad_attn_in * normed_one, axis=0)
    tokens_grad = grad_after + norm_back(grad_attn_in * gain_first, normed_one, scale_one)
    d_small = jnp.concatenate([grad_gain_one[:, None], grad_gain_two[:, None], grad_heads], axis=1)
    d_small = jnp.pad(d_small, ((0, 0), (0, 128 - d_small.shape[1]))).astype(bf16)
    if fast:
        last = [d_out] + d_qkv + [jnp.pad(d_small, ((0, 0), (0, BLOCK - 128)))]
        last = [a.reshape(4, 2, 2, experts // 2, share, a.shape[1]) for a in last]
        (summed,) = move("scatter_last", Scatter(last, "columns", experts), 7, experts)
        per = width // BLOCK
        grad_wo = jnp.concatenate([summed[i] for i in range(per)], axis=1)
        grad_wqkv = jnp.concatenate([summed[i] for i in range(per, 4 * per)], axis=1)
        grad_small = summed[4 * per]
    else:
        grad_small = scatter_xla(d_small.reshape(devices, share, 128), AXES)
        grad_wqkv = scatter_xla(jnp.concatenate(d_qkv, axis=1).reshape(devices, share, 3 * width), AXES)
        grad_wo = scatter_xla(d_out.reshape(devices, share, width), AXES)
    return (
        mixed.astype(bf16),
        tokens_grad,
        grad_small[:, 0],
        grad_wqkv,
        grad_wo,
        grad_small[:, 1],
        grad_fc,
        grad_proj,
        grad_small[:, 2 : 2 + experts],
        grad_small[:, 2 + experts : 4 + experts],
        grad_win[None],
        grad_wout.T[None],
    )


def solution(mesh):
    rows = P(AXES, None)
    in_specs = (
        rows,
        P(AXES),
        rows,
        rows,
        P(AXES),
        rows,
        rows,
        rows,
        rows,
        P("expert", None, "node"),
        P("expert", "node", None),
        rows,
        P(AXES),
        rows,
    )
    out_specs = (
        rows,
        rows,
        P(AXES),
        rows,
        rows,
        P(AXES),
        rows,
        rows,
        rows,
        rows,
        P("expert", None, "node"),
        P("expert", "node", None),
    )
    fast = mesh.shape["node"] == 8 and mesh.shape["expert"] % 2 == 0
    return jax.shard_map(
        functools.partial(shards, fast), mesh=mesh, in_specs=in_specs, out_specs=out_specs, check_vma=False
    )
```

```python
import functools
import math

import jax
import jax.numpy as jnp
from jax import lax
from jax.experimental import pallas as pl
from jax.experimental.pallas import tpu as pltpu
from jax.sharding import PartitionSpec as P

HD = 64
PAIR = 2 * HD
SEQ = 512
QB = 256
BLOCK = 512
MIB = 1 << 20
AXES = ("node", "expert")
MESH = pl.DeviceIdType.MESH
highest = lax.Precision.HIGHEST
epsilon = 1e-05
f32 = jnp.float32
bf16 = jnp.bfloat16


def normalize(values):
    centered = values - jnp.mean(values, axis=-1, keepdims=True)
    inv_scale = lax.rsqrt(jnp.mean(centered * centered, axis=-1, keepdims=True) + epsilon)
    return (centered * inv_scale, inv_scale)


def norm_back(grad_norm, normed, inv_scale):
    mean_grad = jnp.mean(grad_norm, axis=-1, keepdims=True)
    mean_cross = jnp.mean(grad_norm * normed, axis=-1, keepdims=True)
    return inv_scale * (grad_norm - mean_grad - normed * mean_cross)


def contract(left_op, right_op, left_dim, right_dim):
    return lax.dot_general(
        left_op, right_op, (((left_dim,), (right_dim,)), ((), ())), preferred_element_type=f32
    )


def matmul(left_op, right_op):
    return contract(left_op, right_op, 1, 0)


def product_tn(left_op, right_op):
    return contract(left_op, right_op, 0, 0)


def outer_nt(left_op, right_op):
    return contract(left_op, right_op, 1, 1)


class Place:
    def __init__(self, experts):
        self.experts = experts
        self.n, self.e = lax.axis_index("node"), lax.axis_index("expert")
        n = self.n
        self.k, self.x, self.y = lax.rem(n, 2), lax.rem(n // 2, 2), n // 4
        k, x, y = self.k, self.x, self.y
        self.nx, self.ny = y * 4 + (1 - x) * 2 + k, (1 - y) * 4 + x * 2 + k
        self.nd, self.nc = (1 - y) * 4 + (1 - x) * 2 + k, y * 4 + x * 2 + 1 - k

    def z(self, j):
        return (self.n, lax.rem(self.e + j, self.experts))

    def greet(self, along_z):
        barrier = pltpu.get_barrier_semaphore()
        peers = [(self.nx, self.e), (self.ny, self.e), (self.nc, self.e)]
        if along_z:
            peers += [self.z(j) for j in range(1, self.experts)]
        for peer in peers:
            pl.semaphore_signal(barrier, inc=1, device_id=peer, device_id_type=MESH)
        pl.semaphore_wait(barrier, len(peers))


def when(condition):
    return pl.when(condition)


class Gather:
    late = 4

    def __init__(self, args, dense, items, nodes, experts):
        self.args, self.dense, self.items, self.experts = args, dense, items, experts
        self.outs = [
            jax.ShapeDtypeStruct(((nodes * experts if d else nodes),) + a.shape, a.dtype)
            for a, d in zip(args, dense)
        ]
        hbm = pl.BlockSpec(memory_space=pltpu.HBM)
        self.in_specs, self.out_specs = [hbm] * len(args), [hbm] * len(args)
        m = sum(len(item) for item in items)
        self.scratch = [
            pltpu.SemaphoreType.DMA((m, experts + 7)),
            pltpu.SemaphoreType.DMA((m, experts + 7)),
            pltpu.SemaphoreType.DMA((m,)),
        ]
        self.turns = len(items) + self.late
        self.along_z = any(dense)

    def bind(self, ins, outs, scratch, place):
        experts = self.experts
        send, recv, loc = scratch
        p, e = place, place.e

        def remote(source, target, item, kind, device):
            return pltpu.make_async_remote_copy(
                src_ref=source,
                dst_ref=target,
                send_sem=send.at[item, kind],
                recv_sem=recv.at[item, kind],
                device_id=device,
                device_id_type=MESH,
            )

        self.full = outs
        self.bound = [[] for _ in self.items]
        pieces = [(turn, piece) for turn, item in enumerate(self.items) for piece in item]
        for i, (turn, (arg, row, rows, col, columns)) in enumerate(pieces):
            dense = self.dense[arg]
            shard, whole = ins[arg], outs[arg]
            per = experts if dense else 1
            own = p.n * per + (e if dense else 0)

            def view(ref, lead, start=0, size=None, whole_rows=rows, row=row, col=col, columns=columns):
                return ref.at[lead, pl.ds(row + start, size or whole_rows), pl.ds(col, columns)]

            def bundle(m, view=view, whole=whole, per=per):
                return view(whole, pl.ds(m * per, per))

            def half(m, h, view=view, whole=whole, per=per, dense=dense, rows=rows):
                if dense:
                    return view(whole, pl.ds(m * per + h * (per // 2), per // 2))
                return view(whole, m, h * (rows // 2), rows // 2)

            mine = shard.at[pl.ds(row, rows), pl.ds(col, columns)]
            land = view(whole, own)
            local = pltpu.make_async_copy(mine, land, loc.at[i])
            z = []
            if dense:
                z = [remote(mine, land, i, j - 1, p.z(j)) for j in range(1, experts)]
            first, last = (bundle(p.n), bundle(p.n)) if dense else (mine, land)
            b = experts - 1
            xy = [remote(first, last, i, b, (p.nx, e)), remote(first, last, i, b + 1, (p.ny, e))]
            diag = [
                remote(half(p.nx, 0), half(p.nx, 0), i, b + 2, (p.ny, e)),
                remote(half(p.ny, 1), half(p.ny, 1), i, b + 3, (p.nx, e)),
            ]
            core = [remote(first, last, i, b + 4, (p.nc, e))] + [
                remote(bundle(m), bundle(m), i, b + 5 + j, (p.nc, e)) for j, m in enumerate((p.nx, p.ny, p.nd))
            ]
            self.bound[turn].append((local, z, xy, diag, core))

    def turn(self, now):
        steps = (self.along, self.across, self.corner, self.over, self.end)
        for t in range(self.turns):

            @when(now == t)
            def _(t=t):
                for late, step in enumerate(steps):
                    if 0 <= t - late < len(self.items):
                        for piece in self.bound[t - late]:
                            step(*piece)

    def along(self, local, z, xy, diag, core):
        local.start()
        for copy in z:
            copy.start()

    def across(self, local, z, xy, diag, core):
        for copy in z:
            copy.wait()
        local.wait()
        xy[0].start()
        xy[1].start()
        core[0].start()

    def corner(self, local, z, xy, diag, core):
        for i in range(2):
            xy[i].wait()
            diag[i].start()
            core[1 + i].start()

    def over(self, local, z, xy, diag, core):
        diag[0].wait()
        diag[1].wait()
        core[3].start()

    def end(self, local, z, xy, diag, core):
        for copy in core:
            copy.wait()


class Scatter:
    def __init__(self, arrays, layout, experts):
        self.args, self.layout, self.experts = arrays, layout, experts
        dense = self.dense = layout != "plane"
        shape = arrays[0].shape
        if layout == "plane":
            counts, h = [a.shape[2] for a in arrays], shape[4:]
        elif layout == "rows":
            counts, h = [a.shape[4] for a in arrays], shape[3:4] + shape[5:]
        else:
            counts, h = [a.shape[5] // BLOCK for a in arrays], shape[3:5] + (BLOCK,)
        self.starts = [sum(counts[:a]) for a in range(len(arrays) + 1)]
        m = self.m = sum(counts)
        self.half = h
        unit = h[1:] if dense else (2,) + h
        self.outs = [jax.ShapeDtypeStruct((m,) + unit, f32)]
        self.in_specs = [pl.BlockSpec(memory_space=pltpu.HBM)] * len(arrays)
        self.out_specs = [pl.BlockSpec(memory_space=pltpu.VMEM)]
        kinds = 7 + experts
        self.scratch = [
            pltpu.VMEM((m, 4, 2) + h, bf16),
            pltpu.VMEM((m, 4, 2) + h, bf16),
            pltpu.VMEM((m, 2) + h, bf16),
            pltpu.VMEM((m, 2) + h, bf16),
            pltpu.VMEM((m,) + h, bf16),
            pltpu.VMEM((m,) + h, bf16),
            pltpu.SemaphoreType.DMA((m, kinds)),
            pltpu.SemaphoreType.DMA((m, kinds)),
            pltpu.SemaphoreType.DMA((m,)),
        ]
        if dense:
            self.scratch.append(pltpu.VMEM((m, experts - 1) + unit, bf16))
        self.late = 4 if dense else 3
        self.turns = m + self.late
        self.along_z = dense

    def bind(self, ins, outs, scratch, place):
        self.ins, self.out, self.place = ins, outs[0], place
        self.own, self.rc, self.rx, self.ry, self.lx, self.ly, self.send, self.recv, self.loc = scratch[:9]
        self.rz = scratch[9] if self.dense else None

    def remote(self, source, target, item, kind, device):
        return pltpu.make_async_remote_copy(
            src_ref=source,
            dst_ref=target,
            send_sem=self.send.at[item, kind],
            recv_sem=self.recv.at[item, kind],
            device_id=device,
            device_id_type=MESH,
        )

    def part(self, source, core, chunk):
        if self.layout == "plane":
            return source.at[:, core, chunk]
        if self.layout == "rows":
            return source.at[:, core, :, :, chunk]
        return source.at[:, core, :, :, :, pl.ds(pl.multiple_of(chunk * BLOCK, BLOCK), BLOCK)]

    def first(self, source, i, chunk):
        p = self.place
        local = pltpu.make_async_copy(self.part(source, p.k, chunk), self.own.at[i], self.loc.at[i])
        over = self.remote(self.part(source, 1 - p.k, chunk), self.rc.at[i], i, 0, (p.nc, p.e))
        return local, over

    def sites(self):
        p = self.place
        return p.y * 2 + p.x, p.y * 2 + 1 - p.x, (1 - p.y) * 2 + p.x, (1 - p.y) * 2 + 1 - p.x

    def round_one(self, i):
        p = self.place
        _, to_x, to_y, diag = self.sites()
        return [
            self.remote(self.own.at[i, diag, 0], self.rx.at[i, 0], i, 1, (p.nx, p.e)),
            self.remote(self.own.at[i, diag, 1], self.ry.at[i, 0], i, 2, (p.ny, p.e)),
            self.remote(self.own.at[i, to_x, 0], self.rx.at[i, 1], i, 3, (p.nx, p.e)),
            self.remote(self.own.at[i, to_y, 1], self.ry.at[i, 1], i, 4, (p.ny, p.e)),
        ]

    def round_two(self, i):
        p = self.place
        _, to_x, to_y, _ = self.sites()
        return [
            self.remote(self.own.at[i, to_x, 1], self.lx.at[i], i, 5, (p.nx, p.e)),
            self.remote(self.own.at[i, to_y, 0], self.ly.at[i], i, 6, (p.ny, p.e)),
        ]

    def round_z(self, i):
        p = self.place
        mine, _, _, _ = self.sites()
        s = self.experts // 2
        copies = []
        for j in range(1, self.experts):
            to = lax.rem(p.e + j, self.experts)
            source = self.own.at[i, mine, to // s, lax.rem(to, s)]
            copies.append(self.remote(source, self.rz.at[i, j - 1], i, 6 + j, p.z(j)))
        return copies

    def turn(self, now):
        steps = (self.load, self.chip, self.cross, self.plane, self.column)
        for late, step in enumerate(steps[: self.late + 1]):
            i = now - late

            @when(jnp.logical_and(i >= 0, i < self.m))
            def _(step=step, i=i):
                step(i)

    def load(self, i):
        for a, source in enumerate(self.ins):

            @when(jnp.logical_and(i >= self.starts[a], i < self.starts[a + 1]))
            def _(a=a, source=source):
                local, over = self.first(source, i, i - self.starts[a])
                over.start()
                local.start()

    def chip(self, i):
        local, over = self.first(self.ins[0], i, 0)
        local.wait()
        over.wait()

        def sum_one(q, _):
            self.own[i, q] = add(self.own[i, q], self.rc[i, q]).astype(bf16)
            return 0

        lax.fori_loop(0, 4, sum_one, 0)
        for copy in self.round_one(i):
            copy.start()

    def cross(self, i):
        one = self.round_one(i)
        two = self.round_two(i)
        _, to_x, to_y, _ = self.sites()
        for copy in one:
            copy.wait()
        self.own[i, to_x, 1] = add(self.own[i, to_x, 1], self.ry[i, 0]).astype(bf16)
        two[0].start()
        self.own[i, to_y, 0] = add(self.own[i, to_y, 0], self.rx[i, 0]).astype(bf16)
        two[1].start()

    def plane(self, i):
        for copy in self.round_two(i):
            copy.wait()
        mine, _, _, _ = self.sites()
        sums = (
            add(self.own[i, mine, 0], self.rx[i, 1], self.ly[i]),
            add(self.own[i, mine, 1], self.lx[i], self.ry[i, 1]),
        )
        if not self.dense:
            for h in range(2):
                self.out[i, h] = sums[h]
            return
        for h in range(2):
            self.own[i, mine, h] = sums[h].astype(bf16)
        for copy in self.round_z(i):
            copy.start()

    def column(self, i):
        for copy in self.round_z(i):
            copy.wait()
        p = self.place
        mine, _, _, _ = self.sites()
        s = self.experts // 2
        terms = [self.own[i, mine, p.e // s, lax.rem(p.e, s)]] + [self.rz[i, j] for j in range(self.experts - 1)]
        self.out[i] = add(*terms)


def add(*terms):
    return functools.reduce(jnp.add, [t.astype(f32) for t in terms])


def call(name, steps, body, args, in_specs, outs, out_specs, scratch, moves, collective_id, experts, flops):
    total = max(steps, moves.turns if moves else 0)

    def hold(spec):
        if spec.block_shape is None:
            return spec
        index = spec.index_map
        return pl.BlockSpec(spec.block_shape, lambda j: index(jnp.minimum(j, steps - 1)))

    n_in, n_out, n_scratch = len(args), len(outs), len(scratch)
    m_in, m_out = (len(moves.args), len(moves.outs)) if moves else (0, 0)

    def kernel(*refs):
        refs = list(refs)
        take = lambda count: [refs.pop(0) for _ in range(count)]
        ins, m_ins, os, m_os, own = take(n_in), take(m_in), take(n_out), take(m_out), take(n_scratch)
        now = pl.program_id(0)
        if moves:
            place = Place(experts)
            moves.bind(m_ins, m_os, refs, place)

            @when(now == 0)
            def _():
                place.greet(moves.along_z)

            moves.turn(now)
        if body is not None:

            @when(now < steps)
            def _():
                body(now, steps, *ins, *os, *own)

    return pl.pallas_call(
        kernel,
        grid=(total,),
        out_shape=list(outs) + (moves.outs if moves else []),
        in_specs=[hold(s) for s in in_specs] + (moves.in_specs if moves else []),
        out_specs=[hold(s) for s in out_specs] + (moves.out_specs if moves else []),
        scratch_shapes=list(scratch) + (moves.scratch if moves else []),
        cost_estimate=pl.CostEstimate(flops=flops, bytes_accessed=32 * MIB, transcendentals=0),
        compiler_params=pltpu.CompilerParams(
            vmem_limit_bytes=60 * MIB,
            **({"collective_id": collective_id, "has_side_effects": True} if moves else {}),
        ),
        name=name,
    )(*args, *(moves.args if moves else []))


def masks():
    lanes = lax.broadcasted_iota(jnp.int32, (1, PAIR), 1)
    return [(lanes // HD == h).astype(bf16) for h in range(2)]


def causal(scores_t, start):
    keys = lax.broadcasted_iota(jnp.int32, scores_t.shape, 0)
    queries = lax.broadcasted_iota(jnp.int32, scores_t.shape, 1) + start
    return jnp.where(keys <= queries, scores_t, -jnp.inf)


def attend_pair(q, k, v):
    q = q * (1.0 / math.sqrt(HD))
    vt = v.T
    length = q.shape[0]
    outs, tops = [], []
    for h, mask in enumerate(masks()):
        kh = k * mask
        row, logs = [], []
        for start in range(0, length, QB):
            end = start + QB
            scores = causal(outer_nt(kh[:end], q[start:end]), start)
            top = jnp.max(scores, axis=0, keepdims=True)
            expd = jnp.exp(scores - top)
            total = jnp.sum(expd, axis=0, keepdims=True)
            probs = (expd / total).astype(bf16)
            row.append(matmul(vt[h * HD : (h + 1) * HD, :end], probs))
            logs.append(top + jnp.log(total))
        outs.append(jnp.concatenate(row, axis=1))
        tops.append(jnp.concatenate(logs, axis=1))
    return jnp.concatenate(outs, axis=0).T.astype(bf16), jnp.concatenate(tops, axis=0)


class Front:
    def __init__(self, length, width, experts, devices, capacity, moves):
        self.length, self.width, self.experts, self.capacity, self.moves = length, width, experts, capacity, moves
        pairs = width // PAIR
        share = width // devices
        self.at_norm, self.at_qkv = 4, 6
        self.at_heads = self.at_qkv + 1
        self.per_turn = 2
        self.at_out = self.at_heads + length // SEQ * pairs // self.per_turn
        self.steps = max(self.at_out + 1, moves.turns if moves else 0)
        slots = experts * capacity
        rows = lambda c, t: jax.ShapeDtypeStruct((length, c), t)
        self.outs = [
            rows(3 * width, bf16),
            jax.ShapeDtypeStruct((length // SEQ * pairs, 2, SEQ), f32),
            rows(width, bf16),
            rows(width, f32),
            rows(width, bf16),
            rows(width, bf16),
            jax.ShapeDtypeStruct((slots, 2 * width), bf16),
            rows(slots, bf16),
            rows(128, f32),
        ]
        self.scratch = [
            pltpu.VMEM((devices, share, 128), bf16),
            pltpu.VMEM((devices, share, 3 * width), bf16),
            pltpu.VMEM((devices, share, width), bf16),
            pltpu.VMEM((8, width), f32),
            pltpu.VMEM((length, width), bf16),
            pltpu.SemaphoreType.DMA((3,)),
        ]

    def __call__(self, now, steps, tok, cot, route, drop, *refs):
        full = self.moves.full[:3] if self.moves else refs[:3]
        refs = refs if self.moves else refs[3:]
        qkv, lse, att, after, mixed, gd, leave, disp, info, ws, wq, wo, gains, attn_in, sems = refs
        width, length = self.width, self.length
        loads = [pltpu.make_async_copy(a, b, sems.at[i]) for i, (a, b) in enumerate(zip(full, (ws, wq, wo)))]

        @when(now == self.at_norm)
        def _():
            loads[0].start()
            loads[0].wait()
            gains[...] = ws[...].reshape(width, 128).astype(f32).T[:8]
            normed, _ = normalize(tok[...].astype(f32))
            attn_in[...] = (normed * gains[0:1]).astype(bf16)

        @when(now == self.at_qkv)
        def _():
            loads[1].start()
            loads[1].wait()

            def columns(c, _):
                cols = pl.ds(pl.multiple_of(c * BLOCK, BLOCK), BLOCK)
                weights = wq[:, :, cols].reshape(width, BLOCK)
                qkv[:, cols] = matmul(attn_in[...], weights).astype(bf16)
                return 0

            lax.fori_loop(0, 3 * width // BLOCK, columns, 0)

        @when(jnp.logical_and(now >= self.at_heads, now < self.at_out))
        def _():
            pairs = width // PAIR

            def pair(i, _):
                at = (now - self.at_heads) * self.per_turn + i
                seq, at_pair = at // pairs, lax.rem(at, pairs)
                rows = pl.ds(pl.multiple_of(seq * SEQ, SEQ), SEQ)
                cols = lambda part: pl.ds(pl.multiple_of(part * width + at_pair * PAIR, PAIR), PAIR)
                out, tops = attend_pair(qkv[rows, cols(0)], qkv[rows, cols(1)], qkv[rows, cols(2)])
                att[rows, cols(0)] = out
                lse[at] = tops
                return 0

            lax.fori_loop(0, self.per_turn, pair, 0)

        @when(now == self.at_out)
        def _():
            loads[2].start()
            loads[2].wait()
            self.route(tok, cot, route, drop, att, wo, ws, gains, after, mixed, gd, leave, disp, info)

    def route(self, tok, cot, route, drop, att, wo, ws, gains, after, mixed, gd, leave, disp, info):
        width, length, experts = self.width, self.length, self.experts
        after[...] = tok[...].astype(f32) + matmul(att[...], wo[...].reshape(width, width))
        normed, _ = normalize(after[...])
        mixed[...] = (normed * gains[1:2]).astype(bf16)
        logits = matmul(mixed[...], ws[...].reshape(width, 128))
        lane = lax.broadcasted_iota(jnp.int32, (length, 128), 1)

        def softmax(first, last):
            inside = jnp.logical_and(lane >= first, lane < last)
            top = jnp.max(jnp.where(inside, logits, -jnp.inf), axis=1, keepdims=True)
            expd = jnp.where(inside, jnp.exp(jnp.where(inside, logits, top) - top), 0.0)
            return expd / jnp.sum(expd, axis=1, keepdims=True)

        probs, coef = softmax(2, 2 + experts), softmax(2 + experts, 4 + experts)
        info[...] = probs + coef
        chosen = jnp.where(lane - 2 == route[...], 1.0, 0.0)
        over_lanes = lambda a: jnp.sum(a, axis=1, keepdims=True)
        gate = over_lanes(probs * chosen) * (1 - drop[...]).astype(f32)
        coef_0 = over_lanes(jnp.where(lane == 2 + experts, coef, 0.0))
        coef_1 = over_lanes(jnp.where(lane == 3 + experts, coef, 0.0))
        grad = cot[...].astype(f32)
        gd[...] = (coef_0 * grad).astype(bf16)
        square = lambda d: lax.broadcasted_iota(jnp.int32, (length, length), d)
        earlier = jnp.where(square(0) > square(1), 1.0, 0.0).astype(bf16)
        position = over_lanes(chosen * matmul(earlier, chosen.astype(bf16))).astype(jnp.int32)
        turn = route[...] - lax.axis_index("expert")
        target = jnp.where(turn < 0, turn + experts, turn) * self.capacity + position
        slot = lax.broadcasted_iota(jnp.int32, (length, experts * self.capacity), 1)
        disp[...] = jnp.where(slot == target, 1.0, 0.0).astype(bf16)
        leave[:, :width] = product_tn(disp[...], mixed[...]).astype(bf16)
        leave[:, width:] = product_tn(disp[...], (coef_1 * gate * grad).astype(bf16)).astype(bf16)


def attend_backward_kernel(q_ref, k_ref, v_ref, g_ref, lse_ref, d_ref):
    scaling = 1.0 / math.sqrt(HD)
    q, k, v, g = q_ref[...], k_ref[...], v_ref[...], g_ref[...]
    qs = q * scaling
    kt = k.T
    length = q.shape[0]
    grad_k = [0.0] * (length // QB)
    grad_v = [0.0] * (length // QB)
    grad_q = []
    for h, mask in enumerate(masks()):
        kh, vh, qh, gh = k * mask, v * mask, q * mask, g * mask
        row = []
        for c, start in enumerate(range(0, length, QB)):
            end = start + QB
            scores = causal(outer_nt(kh[:end], qs[start:end]), start)
            probs = jnp.exp(scores - lse_ref[0, h : h + 1, start:end])
            grad_probs = outer_nt(vh[:end], g[start:end])
            delta = jnp.sum(probs * grad_probs, axis=0, keepdims=True)
            grad_scores = (probs * (grad_probs - delta)).astype(bf16)
            more_v = matmul(probs.astype(bf16), gh[start:end])
            more_k = matmul(grad_scores, qh[start:end])
            for b in range(c + 1):
                rows = slice(b * QB, (b + 1) * QB)
                grad_v[b] = grad_v[b] + more_v[rows]
                grad_k[b] = grad_k[b] + more_k[rows]
            row.append(matmul(kt[h * HD : (h + 1) * HD, :end], grad_scores))
        grad_q.append(jnp.concatenate(row, axis=1))
    d_ref[0] = (jnp.concatenate(grad_q, axis=0).T * scaling).astype(bf16)
    for b in range(length // QB):
        d_ref[1, b * QB : (b + 1) * QB] = (grad_k[b] * scaling).astype(bf16)
        d_ref[2, b * QB : (b + 1) * QB] = grad_v[b].astype(bf16)


def attend_backward(qkv, lse, grad, width, moves, collective_id, experts):
    length = qkv.shape[0]
    pairs = width // PAIR
    part = lambda p: pl.BlockSpec((SEQ, PAIR), lambda j: (j // pairs, p * pairs + lax.rem(j, pairs)))
    return call(
        "attend_backward",
        length // SEQ * pairs,
        lambda now, steps, *refs: attend_backward_kernel(*refs),
        [qkv, qkv, qkv, grad, lse],
        [part(0), part(1), part(2), part(0), pl.BlockSpec((1, 2, SEQ), lambda j: (j, 0, 0))],
        [jax.ShapeDtypeStruct((3, length, width), bf16)],
        [pl.BlockSpec((3, SEQ, PAIR), lambda j: (0, j // pairs, lax.rem(j, pairs)))],
        [],
        moves,
        collective_id,
        experts,
        10 * length * SEQ * width,
    )


def gelu_both(v):
    c = math.sqrt(2.0 / math.pi)
    square = v * v
    t = jnp.tanh(c * (v + 0.044715 * (square * v)))
    half = 0.5 * (1.0 + t)
    slope = half + 0.5 * v * (1.0 - t * t) * (c * (1.0 + (3 * 0.044715) * square))
    return v * half, slope


def mlp_kernel(share, now, steps, x_ref, g_ref, w1_ref, w2_ref, out_ref, back_ref, d1_ref, d2_ref, xt, gt, out_sum, back_sum):
    @when(now == 0)
    def _():
        xt[...] = x_ref[...].T
        gt[...] = g_ref[...].T
        out_sum[...] = jnp.zeros_like(out_sum)
        back_sum[...] = jnp.zeros_like(back_sum)

    w1 = w1_ref[...].reshape(w1_ref.shape[-2:])
    w2 = w2_ref[...].reshape(w2_ref.shape[-2:])
    hidden, slope = gelu_both(matmul(x_ref[...], w1))
    hidden = hidden.astype(bf16)
    grad_pre = (slope * outer_nt(g_ref[...], w2)).astype(bf16)
    out_sum[...] += matmul(hidden, w2)
    back_sum[...] += outer_nt(grad_pre, w1)
    d1 = matmul(xt[...], grad_pre).astype(bf16)
    d2 = matmul(gt[...], hidden).astype(bf16)
    if share is None:
        d1_ref[...] = d1.reshape(d1_ref.shape)
        d2_ref[...] = d2.reshape(d2_ref.shape)
    else:
        for c in range(d1.shape[1] // 128):
            cols = slice(c * 128, (c + 1) * 128)
            for s in range(d1_ref.shape[0]):
                d1_ref[s, c * share : (c + 1) * share] = d1[s * share : (s + 1) * share, cols]
            d2_ref[c] = d2[:, cols]

    @when(now == steps - 1)
    def _():
        out_ref[...] = out_sum[...].astype(out_ref.dtype)
        back_ref[...] = back_sum[...].astype(back_ref.dtype)


def mlp(x, g, w1, w2, out_dtype, name, moves, collective_id, experts, devices=None):
    rows, width = x.shape
    share = None
    if w1.ndim == 3:
        blocks, _, size = w1.shape
        w1_spec = pl.BlockSpec((1, width, size), lambda j: (j, 0, 0))
        w2_spec = pl.BlockSpec((1, size, width), lambda j: (j, 0, 0))
        d_shape, d_specs = (blocks, width, size), [w1_spec] * 2
    else:
        size = BLOCK
        blocks = w1.shape[1] // size
        w1_spec = pl.BlockSpec((width, size), lambda j: (0, j))
        w2_spec = pl.BlockSpec((size, width), lambda j: (j, 0))
        d_shape, d_specs = (width, blocks * size), [w1_spec] * 2
        if devices:
            share = width // devices
            d_shape = (devices, width, 128)
            d_specs = [
                pl.BlockSpec((devices, size // 128 * share, 128), lambda j: (0, j, 0)),
                pl.BlockSpec((size // 128, width, 128), lambda j: (j, 0, 0)),
            ]
    whole = pl.BlockSpec(memory_space=pltpu.VMEM)
    return call(
        name,
        blocks,
        functools.partial(mlp_kernel, share),
        [x, g, w1, w2],
        [whole, whole, w1_spec, w2_spec],
        [jax.ShapeDtypeStruct((rows, width), out_dtype)] * 2 + [jax.ShapeDtypeStruct(d_shape, bf16)] * 2,
        [whole, whole] + d_specs,
        [
            pltpu.VMEM((width, rows), bf16),
            pltpu.VMEM((width, rows), bf16),
            pltpu.VMEM((rows, width), f32),
            pltpu.VMEM((rows, width), f32),
        ],
        moves,
        collective_id,
        experts,
        12 * rows * width * blocks * size,
    )


def move(name, moves, collective_id, experts):
    return call(name, 1, None, [], [], [], [], [], moves, collective_id, experts, 0)


def shards(
    fast,
    tokens,
    gain_attn,
    w_qkv,
    w_out,
    gain_mix,
    w_fc,
    w_proj,
    w_router,
    w_coef,
    expert_in,
    expert_out,
    routes,
    dropped,
    cotangent,
):
    experts = lax.axis_size("expert")
    nodes = lax.axis_size("node")
    devices = nodes * experts
    width = tokens.shape[1]
    tok_rows = tokens.shape[0]
    ff = w_fc.shape[1]
    share = w_qkv.shape[0]
    small = jnp.concatenate([gain_attn[:, None], gain_mix[:, None], w_router, w_coef], axis=1)
    small = jnp.pad(small, ((0, 0), (0, 128 - small.shape[1])))
    win, wout = expert_in[0], expert_out[0]
    together = lambda a: a.reshape((devices * a.shape[1],) + a.shape[2:])
    cut = lambda a, rows, columns, m, n: [
        [(a, i * (rows // m), rows // m, j * (columns // n), columns // n)] for i in range(m) for j in range(n)
    ]
    moves = gather_experts = None
    weights = (small, w_qkv, w_out, w_fc, w_proj)
    capacity = -(-(tok_rows * 10) // (8 * experts))
    if fast:
        items = cut(1, share, 3 * width, 1, 3) + cut(2, share, width, 1, 1)
        items += cut(3, share, ff, 1, 4) + cut(4, ff // devices, width, 4, 1)
        items[0] = cut(0, share, 128, 1, 1)[0] + items[0]
        moves = Gather(list(weights), [True] * 5, items, nodes, experts)
        gather_experts = Gather(
            [win, wout], [False] * 2, cut(0, width, win.shape[1], 4, 1) + cut(1, wout.shape[0], width, 4, 1), nodes, experts
        )
        full = []
    else:
        full = [lax.all_gather(a, AXES, axis=0, tiled=False) for a in weights]
        win_full, wout_full = (lax.all_gather(a, "node", axis=0, tiled=False) for a in (win, wout))
    front = Front(tok_rows, width, experts, devices, capacity, moves)
    kept = full[:3]
    whole, hbm = pl.BlockSpec(memory_space=pltpu.VMEM), pl.BlockSpec(memory_space=pltpu.HBM)
    results = call(
        "front",
        front.steps,
        front,
        [tokens, cotangent, routes, dropped[:, None]] + kept,
        [whole] * 4 + [hbm] * len(kept),
        front.outs,
        [whole] * len(front.outs),
        front.scratch,
        moves,
        1,
        experts,
        12 * tok_rows * width * width,
    )
    qkv_rows, lse, attended, after_attn, mixed_in, grad_dense, leaving, dispatch, probs = results[:9]
    full = results[9:] if fast else full
    small_full, qkv_full, out_full, fc_full, proj_full = (together(a) for a in full)

    def scatter_xla(parts, axes):
        return lax.psum_scatter(parts, axes, scatter_dimension=0, tiled=False).astype(f32)

    gain_first = small_full[:, 0].astype(f32)
    gain_second = small_full[:, 1].astype(f32)
    heads = small_full[:, 2 : 4 + experts]
    residual = tokens.astype(f32)
    normed_one, scale_one = normalize(residual)
    attn_in = (normed_one * gain_first).astype(bf16)
    normed_two, scale_two = normalize(after_attn)
    router_probs, coef_tok = probs[:, 2 : 2 + experts], probs[:, 2 + experts : 4 + experts]
    chosen = (routes == jnp.arange(experts, dtype=jnp.int32)[None, :]).astype(f32)
    kept_tok = (1 - dropped).astype(f32)
    gate_prob = jnp.sum(router_probs * chosen, axis=1)
    gate_tok = gate_prob * kept_tok
    weight_tok = coef_tok[:, 1:] * gate_tok[:, None]
    grad_out = cotangent.astype(f32)

    def exchange(parts, sign):
        moved = [parts[0]]
        for j in range(1, experts):
            shift = [(s, (s + sign * j) % experts) for s in range(experts)]
            moved.append(lax.ppermute(parts[j], "expert", shift))
        return jnp.concatenate(moved, axis=0)

    arrived = exchange(leaving.reshape(experts, capacity, 2 * width), 1)

    dense_out, grad_mixed, d_fc, d_proj, *gathered = mlp(
        mixed_in, grad_dense, fc_full, proj_full, f32, "dense_mlp", gather_experts, 3, experts, devices if fast else None
    )
    scatter_dense = None
    if fast:
        win_full, wout_full = gathered
        by_chip = lambda a: a.reshape(4, 2, 2, experts // 2, 4, width // 4, 128)
        scatter_dense = Scatter([by_chip(d_fc), by_chip(d_proj)], "rows", experts)
    returned, grad_rows, d_win, d_wout, *scattered = mlp(
        arrived[:, :width], arrived[:, width:], win_full, wout_full, bf16, "expert_mlp", scatter_dense, 4, experts
    )
    leaving = jnp.concatenate([returned, grad_rows], axis=1)
    came_back = exchange(leaving.reshape(experts, capacity, 2 * width), -1)
    if fast:
        by_column = scattered[0].reshape(2, width, 128)
        grad_fc = by_column[0].reshape(ff // 128, share, 128).transpose(1, 0, 2).reshape(share, ff)
        grad_proj = by_column[1].T
        cut_rows = lambda a: a.reshape(4, 2, 8, 2, width // 16, a.shape[2])
        scatter_win = Scatter([cut_rows(d_win)], "plane", experts)
        scatter_wout = Scatter([cut_rows(d_wout)], "plane", experts)
        (grad_win,) = move("scatter_win", scatter_win, 5, experts)
        grad_win = grad_win.reshape(width, -1)
    else:
        grad_fc = scatter_xla(d_fc.reshape(devices, share, ff), AXES)
        by_unit = d_proj.reshape(width, devices, ff // devices).transpose(1, 0, 2)
        grad_proj = scatter_xla(by_unit, AXES).T
        grad_win = scatter_xla(d_win, "node")
        grad_wout = scatter_xla(d_wout, "node")
        scatter_wout = None
    came_back = matmul(dispatch, came_back)
    expert_tok, grad_back = came_back[:, :width], came_back[:, width:]

    mixed = after_attn + coef_tok[:, :1] * dense_out + weight_tok * expert_tok
    shared = jnp.sum(grad_out * expert_tok, axis=1)
    grad_coef = jnp.stack([jnp.sum(grad_out * dense_out, axis=1), shared * gate_tok], axis=1)
    grad_coef_logit = coef_tok * (grad_coef - jnp.sum(coef_tok * grad_coef, axis=1, keepdims=True))
    grad_gate = shared * coef_tok[:, 1] * kept_tok
    grad_route_logit = (grad_gate * gate_prob)[:, None] * (chosen - router_probs)
    grad_logits = jnp.concatenate([grad_route_logit, grad_coef_logit], axis=1)
    grad_mixed = grad_mixed + grad_back
    grad_mixed = grad_mixed + jnp.dot(grad_logits, heads.astype(f32).T, precision=highest)
    grad_heads = jnp.dot(mixed_in.astype(f32).T, grad_logits, precision=highest)
    grad_gain_two = jnp.sum(grad_mixed * normed_two, axis=0)
    grad_after = grad_out + norm_back(grad_mixed * gain_second, normed_two, scale_two)
    grad_attn = grad_after.astype(bf16)
    d_out = product_tn(attended, grad_attn).astype(bf16)
    grad_attended = outer_nt(grad_attn, out_full).astype(bf16)
    grad_qkv, *scattered = attend_backward(qkv_rows, lse, grad_attended, width, scatter_wout, 6, experts)
    if fast:
        grad_wout = scattered[0].reshape(width, -1)
    d_qkv = [product_tn(attn_in, grad_qkv[i]).astype(bf16) for i in range(3)]
    grad_attn_in = sum(outer_nt(grad_qkv[i], qkv_full[:, i * width : (i + 1) * width]) for i in range(3))
    grad_gain_one = jnp.sum(grad_attn_in * normed_one, axis=0)
    tokens_grad = grad_after + norm_back(grad_attn_in * gain_first, normed_one, scale_one)
    d_small = jnp.concatenate([grad_gain_one[:, None], grad_gain_two[:, None], grad_heads], axis=1)
    d_small = jnp.pad(d_small, ((0, 0), (0, 128 - d_small.shape[1]))).astype(bf16)
    if fast:
        last = [d_out] + d_qkv + [jnp.pad(d_small, ((0, 0), (0, BLOCK - 128)))]
        last = [a.reshape(4, 2, 2, experts // 2, share, a.shape[1]) for a in last]
        (summed,) = move("scatter_last", Scatter(last, "columns", experts), 7, experts)
        per = width // BLOCK
        grad_wo = jnp.concatenate([summed[i] for i in range(per)], axis=1)
        grad_wqkv = jnp.concatenate([summed[i] for i in range(per, 4 * per)], axis=1)
        grad_small = summed[4 * per]
    else:
        grad_small = scatter_xla(d_small.reshape(devices, share, 128), AXES)
        grad_wqkv = scatter_xla(jnp.concatenate(d_qkv, axis=1).reshape(devices, share, 3 * width), AXES)
        grad_wo = scatter_xla(d_out.reshape(devices, share, width), AXES)
    return (
        mixed.astype(bf16),
        tokens_grad,
        grad_small[:, 0],
        grad_wqkv,
        grad_wo,
        grad_small[:, 1],
        grad_fc,
        grad_proj,
        grad_small[:, 2 : 2 + experts],
        grad_small[:, 2 + experts : 4 + experts],
        grad_win[None],
        grad_wout.T[None],
    )


def solution(mesh):
    rows = P(AXES, None)
    in_specs = (
        rows,
        P(AXES),
        rows,
        rows,
        P(AXES),
        rows,
        rows,
        rows,
        rows,
        P("expert", None, "node"),
        P("expert", "node", None),
        rows,
        P(AXES),
        rows,
    )
    out_specs = (
        rows,
        rows,
        P(AXES),
        rows,
        rows,
        P(AXES),
        rows,
        rows,
        rows,
        rows,
        P("expert", None, "node"),
        P("expert", "node", None),
    )
    fast = mesh.shape["node"] == 8 and mesh.shape["expert"] % 2 == 0
    return jax.shard_map(
        functools.partial(shards, fast), mesh=mesh, in_specs=in_specs, out_specs=out_specs, check_vma=False
    )
```

```python
import functools
import math

import jax
import jax.numpy as jnp
from jax import lax
from jax.experimental import pallas as pl
from jax.experimental.pallas import tpu as pltpu
from jax.sharding import PartitionSpec as P

HD = 64
PAIR = 2 * HD
SEQ = 512
QB = 256
BLOCK = 512
MIB = 1 << 20
AXES = ("node", "expert")
MESH = pl.DeviceIdType.MESH
epsilon = 1e-05
f32 = jnp.float32
bf16 = jnp.bfloat16


def normalize(values):
    centered = values - jnp.mean(values, axis=-1, keepdims=True)
    inv_scale = lax.rsqrt(jnp.mean(centered * centered, axis=-1, keepdims=True) + epsilon)
    return (centered * inv_scale, inv_scale)


def norm_back(grad_norm, normed, inv_scale):
    mean_grad = jnp.mean(grad_norm, axis=-1, keepdims=True)
    mean_cross = jnp.mean(grad_norm * normed, axis=-1, keepdims=True)
    return inv_scale * (grad_norm - mean_grad - normed * mean_cross)


def contract(left_op, right_op, left_dim, right_dim):
    return lax.dot_general(
        left_op, right_op, (((left_dim,), (right_dim,)), ((), ())), preferred_element_type=f32
    )


def matmul(left_op, right_op):
    return contract(left_op, right_op, 1, 0)


def product_tn(left_op, right_op):
    return contract(left_op, right_op, 0, 0)


def outer_nt(left_op, right_op):
    return contract(left_op, right_op, 1, 1)


class Place:
    def __init__(self, experts):
        self.experts = experts
        self.n, self.e = lax.axis_index("node"), lax.axis_index("expert")
        n = self.n
        self.k, self.x, self.y = lax.rem(n, 2), lax.rem(n // 2, 2), n // 4
        k, x, y = self.k, self.x, self.y
        self.nx, self.ny = y * 4 + (1 - x) * 2 + k, (1 - y) * 4 + x * 2 + k
        self.nd, self.nc = (1 - y) * 4 + (1 - x) * 2 + k, y * 4 + x * 2 + 1 - k

    def z(self, j):
        return (self.n, lax.rem(self.e + j, self.experts))

    def greet(self, along_z):
        barrier = pltpu.get_barrier_semaphore()
        peers = [(self.nx, self.e), (self.ny, self.e), (self.nc, self.e)]
        if along_z:
            peers += [self.z(j) for j in range(1, self.experts)]
        for peer in peers:
            pl.semaphore_signal(barrier, inc=1, device_id=peer, device_id_type=MESH)
        pl.semaphore_wait(barrier, len(peers))


def when(condition):
    return pl.when(condition)


class Gather:
    late = 4

    def __init__(self, args, dense, items, nodes, experts):
        self.args, self.dense, self.items, self.experts = args, dense, items, experts
        self.outs = [
            jax.ShapeDtypeStruct(((nodes * experts if d else nodes),) + a.shape, a.dtype)
            for a, d in zip(args, dense)
        ]
        hbm = pl.BlockSpec(memory_space=pltpu.HBM)
        self.in_specs, self.out_specs = [hbm] * len(args), [hbm] * len(args)
        m = sum(len(item) for item in items)
        self.scratch = [
            pltpu.SemaphoreType.DMA((m, experts + 7)),
            pltpu.SemaphoreType.DMA((m, experts + 7)),
            pltpu.SemaphoreType.DMA((m,)),
        ]
        self.turns = len(items) + self.late
        self.along_z = any(dense)

    def bind(self, ins, outs, scratch, place):
        experts = self.experts
        send, recv, loc = scratch
        p, e = place, place.e

        def remote(source, target, item, kind, device):
            return pltpu.make_async_remote_copy(
                src_ref=source,
                dst_ref=target,
                send_sem=send.at[item, kind],
                recv_sem=recv.at[item, kind],
                device_id=device,
                device_id_type=MESH,
            )

        self.full = outs
        self.bound = [[] for _ in self.items]
        pieces = [(turn, piece) for turn, item in enumerate(self.items) for piece in item]
        for i, (turn, (arg, row, rows, col, columns)) in enumerate(pieces):
            dense = self.dense[arg]
            shard, whole = ins[arg], outs[arg]
            per = experts if dense else 1
            own = p.n * per + (e if dense else 0)

            def view(ref, lead, start=0, size=None, whole_rows=rows, row=row, col=col, columns=columns):
                return ref.at[lead, pl.ds(row + start, size or whole_rows), pl.ds(col, columns)]

            def bundle(m, view=view, whole=whole, per=per):
                return view(whole, pl.ds(m * per, per))

            def half(m, h, view=view, whole=whole, per=per, dense=dense, rows=rows):
                if dense:
                    return view(whole, pl.ds(m * per + h * (per // 2), per // 2))
                return view(whole, m, h * (rows // 2), rows // 2)

            mine = shard.at[pl.ds(row, rows), pl.ds(col, columns)]
            land = view(whole, own)
            local = pltpu.make_async_copy(mine, land, loc.at[i])
            z = []
            if dense:
                z = [remote(mine, land, i, j - 1, p.z(j)) for j in range(1, experts)]
            first, last = (bundle(p.n), bundle(p.n)) if dense else (mine, land)
            b = experts - 1
            xy = [remote(first, last, i, b, (p.nx, e)), remote(first, last, i, b + 1, (p.ny, e))]
            diag = [
                remote(half(p.nx, 0), half(p.nx, 0), i, b + 2, (p.ny, e)),
                remote(half(p.ny, 1), half(p.ny, 1), i, b + 3, (p.nx, e)),
            ]
            core = [remote(first, last, i, b + 4, (p.nc, e))] + [
                remote(bundle(m), bundle(m), i, b + 5 + j, (p.nc, e)) for j, m in enumerate((p.nx, p.ny, p.nd))
            ]
            self.bound[turn].append((local, z, xy, diag, core))

    def turn(self, now):
        steps = (self.along, self.across, self.corner, self.over, self.end)
        for t in range(self.turns):

            @when(now == t)
            def _(t=t):
                for late, step in enumerate(steps):
                    if 0 <= t - late < len(self.items):
                        for piece in self.bound[t - late]:
                            step(*piece)

    def along(self, local, z, xy, diag, core):
        local.start()
        for copy in z:
            copy.start()

    def across(self, local, z, xy, diag, core):
        for copy in z:
            copy.wait()
        local.wait()
        xy[0].start()
        xy[1].start()
        core[0].start()

    def corner(self, local, z, xy, diag, core):
        for i in range(2):
            xy[i].wait()
            diag[i].start()
            core[1 + i].start()

    def over(self, local, z, xy, diag, core):
        diag[0].wait()
        diag[1].wait()
        core[3].start()

    def end(self, local, z, xy, diag, core):
        for copy in core:
            copy.wait()


class Scatter:
    RING = 4

    def __init__(self, arrays, layout, experts, outs, store, start=0, stride=1, made=None):
        self.layout, self.experts, self.outs, self.store = layout, experts, outs, store
        self.start, self.stride = start, stride
        self.args = [] if layout == "made" else arrays
        dense = self.dense = layout != "plane"
        if layout == "plane":
            counts, h = [a.shape[2] for a in arrays], arrays[0].shape[4:]
        elif layout == "rows":
            counts, h = [a.shape[4] for a in arrays], arrays[0].shape[3:4] + arrays[0].shape[5:]
        else:
            counts, h = [made[0]], made[4:]
        self.starts = [sum(counts[:a]) for a in range(len(counts) + 1)]
        m = self.m = sum(counts)
        unit = h[1:] if dense else (2,) + h
        ring = self.ring = min(self.RING, m)
        self.in_specs = [pl.BlockSpec(memory_space=pltpu.HBM)] * len(self.args)
        self.out_specs = [pl.BlockSpec(memory_space=pltpu.VMEM)] * len(outs)
        kinds = 7 + experts
        self.scratch = [
            pltpu.VMEM(made or (m, 4, 2) + h, bf16),
            pltpu.VMEM((ring, 4, 2) + h, bf16),
            pltpu.VMEM((m, 2) + h, bf16),
            pltpu.VMEM((m, 2) + h, bf16),
            pltpu.VMEM((m,) + h, bf16),
            pltpu.VMEM((m,) + h, bf16),
            pltpu.SemaphoreType.DMA((m, kinds)),
            pltpu.SemaphoreType.DMA((m, kinds)),
            pltpu.SemaphoreType.DMA((m,)),
        ]
        if dense:
            self.scratch.append(pltpu.VMEM((m, experts - 1) + unit, bf16))
        self.late = 4 if dense else 3
        self.turns = start + (m - 1) * stride + 1 + self.late
        self.along_z = dense

    def bind(self, ins, outs, scratch, place):
        self.ins, self.out, self.place = ins, outs, place
        self.own, self.rc, self.rx, self.ry, self.lx, self.ly, self.send, self.recv, self.loc = scratch[:9]
        self.rz = scratch[9] if self.dense else None

    def remote(self, source, target, item, kind, device):
        return pltpu.make_async_remote_copy(
            src_ref=source,
            dst_ref=target,
            send_sem=self.send.at[item, kind],
            recv_sem=self.recv.at[item, kind],
            device_id=device,
            device_id_type=MESH,
        )

    def part(self, source, core, chunk):
        if self.layout == "plane":
            return source.at[:, core, chunk]
        return source.at[:, core, :, :, chunk]

    def at(self, i, site, *more):
        return (i, site, self.place.k) + more if self.layout == "made" else (i, site) + more

    def first(self, source, i, chunk):
        p = self.place
        land = self.rc.at[lax.rem(i, self.ring)]
        if self.layout == "made":
            return [self.remote(self.own.at[i, :, 1 - p.k], land, i, 0, (p.nc, p.e))]
        local = pltpu.make_async_copy(self.part(source, p.k, chunk), self.own.at[i], self.loc.at[i])
        return [self.remote(self.part(source, 1 - p.k, chunk), land, i, 0, (p.nc, p.e)), local]

    def sites(self):
        p = self.place
        return p.y * 2 + p.x, p.y * 2 + 1 - p.x, (1 - p.y) * 2 + p.x, (1 - p.y) * 2 + 1 - p.x

    def round_one(self, i):
        p = self.place
        _, to_x, to_y, diag = self.sites()
        own = lambda *at: self.own.at[self.at(i, *at)]
        return [
            self.remote(own(diag, 0), self.rx.at[i, 0], i, 1, (p.nx, p.e)),
            self.remote(own(diag, 1), self.ry.at[i, 0], i, 2, (p.ny, p.e)),
            self.remote(own(to_x, 0), self.rx.at[i, 1], i, 3, (p.nx, p.e)),
            self.remote(own(to_y, 1), self.ry.at[i, 1], i, 4, (p.ny, p.e)),
        ]

    def round_two(self, i):
        p = self.place
        _, to_x, to_y, _ = self.sites()
        return [
            self.remote(self.own.at[self.at(i, to_x, 1)], self.lx.at[i], i, 5, (p.nx, p.e)),
            self.remote(self.own.at[self.at(i, to_y, 0)], self.ly.at[i], i, 6, (p.ny, p.e)),
        ]

    def round_z(self, i):
        p = self.place
        mine, _, _, _ = self.sites()
        s = self.experts // 2
        copies = []
        for j in range(1, self.experts):
            to = lax.rem(p.e + j, self.experts)
            source = self.own.at[self.at(i, mine, to // s, lax.rem(to, s))]
            copies.append(self.remote(source, self.rz.at[i, j - 1], i, 6 + j, p.z(j)))
        return copies

    def turn(self, now):
        steps = (self.load, self.chip, self.cross, self.plane, self.column)
        for late, step in enumerate(steps[: self.late + 1]):
            since = now - self.start - late
            i = since // self.stride
            due = jnp.logical_and(since >= 0, i < self.m)
            if self.stride > 1:
                due = jnp.logical_and(due, lax.rem(since, self.stride) == 0)

            @when(due)
            def _(step=step, i=i):
                step(i)

    def load(self, i):
        if self.layout == "made":
            self.first(None, i, 0)[0].start()
            return
        for a, source in enumerate(self.ins):

            @when(jnp.logical_and(i >= self.starts[a], i < self.starts[a + 1]))
            def _(a=a, source=source):
                for copy in self.first(source, i, i - self.starts[a]):
                    copy.start()

    def chip(self, i):
        for copy in self.first(None if self.layout == "made" else self.ins[0], i, 0):
            copy.wait()

        def sum_one(q, _):
            at = self.at(i, q)
            self.own[at] = add(self.own[at], self.rc[lax.rem(i, self.ring), q]).astype(bf16)
            return 0

        lax.fori_loop(0, 4, sum_one, 0)
        for copy in self.round_one(i):
            copy.start()

    def cross(self, i):
        one = self.round_one(i)
        two = self.round_two(i)
        _, to_x, to_y, _ = self.sites()
        for copy in one:
            copy.wait()
        at_x, at_y = self.at(i, to_x, 1), self.at(i, to_y, 0)
        self.own[at_x] = add(self.own[at_x], self.ry[i, 0]).astype(bf16)
        two[0].start()
        self.own[at_y] = add(self.own[at_y], self.rx[i, 0]).astype(bf16)
        two[1].start()

    def plane(self, i):
        for copy in self.round_two(i):
            copy.wait()
        mine, _, _, _ = self.sites()
        sums = (
            add(self.own[self.at(i, mine, 0)], self.rx[i, 1], self.ly[i]),
            add(self.own[self.at(i, mine, 1)], self.lx[i], self.ry[i, 1]),
        )
        if not self.dense:
            self.store(self.out, i, jnp.concatenate(sums, axis=0))
            return
        for h in range(2):
            self.own[self.at(i, mine, h)] = sums[h].astype(bf16)
        for copy in self.round_z(i):
            copy.start()

    def column(self, i):
        for copy in self.round_z(i):
            copy.wait()
        p = self.place
        mine, _, _, _ = self.sites()
        s = self.experts // 2
        terms = [self.own[self.at(i, mine, p.e // s, lax.rem(p.e, s))]]
        self.store(self.out, i, add(*terms, *(self.rz[i, j] for j in range(self.experts - 1))))


def add(*terms):
    return functools.reduce(jnp.add, [t.astype(f32) for t in terms])


def call(name, steps, body, args, in_specs, outs, out_specs, scratch, moves, collective_id, experts, flops):
    total = max([steps] + [m.turns for m in moves])

    def hold(spec):
        if spec.block_shape is None:
            return spec
        index = spec.index_map
        return pl.BlockSpec(spec.block_shape, lambda j: index(jnp.minimum(j, steps - 1)))

    join = lambda what: [x for m in moves for x in getattr(m, what)]

    def kernel(*refs):
        refs = list(refs)
        take = lambda group: [refs.pop(0) for _ in group]
        ins, m_ins = take(args), [take(m.args) for m in moves]
        os, m_os = take(outs), [take(m.outs) for m in moves]
        own, m_own = take(scratch), [take(m.scratch) for m in moves]
        now = pl.program_id(0)
        if moves:
            place = Place(experts)
            for m, a, o, r in zip(moves, m_ins, m_os, m_own):
                m.bind(a, o, r, place)

            @when(now == 0)
            def _():
                place.greet(any(m.along_z for m in moves))

            for m in moves:
                m.turn(now)
        if body is not None:

            @when(now < steps)
            def _():
                body(now, steps, *ins, *os, *own)

    return pl.pallas_call(
        kernel,
        grid=(total,),
        out_shape=list(outs) + join("outs"),
        in_specs=[hold(s) for s in in_specs] + join("in_specs"),
        out_specs=[hold(s) for s in out_specs] + join("out_specs"),
        scratch_shapes=list(scratch) + join("scratch"),
        cost_estimate=pl.CostEstimate(flops=flops, bytes_accessed=32 * MIB, transcendentals=0),
        compiler_params=pltpu.CompilerParams(
            vmem_limit_bytes=60 * MIB,
            **({"collective_id": collective_id, "has_side_effects": True} if moves else {}),
        ),
        name=name,
    )(*args, *join("args"))


def masks():
    lanes = lax.broadcasted_iota(jnp.int32, (1, PAIR), 1)
    return [(lanes // HD == h).astype(bf16) for h in range(2)]


def causal(scores_t, start):
    keys = lax.broadcasted_iota(jnp.int32, scores_t.shape, 0)
    queries = lax.broadcasted_iota(jnp.int32, scores_t.shape, 1) + start
    return jnp.where(keys <= queries, scores_t, -jnp.inf)


def attend_pair(q, k, v):
    q = q * (1.0 / math.sqrt(HD))
    vt = v.T
    length = q.shape[0]
    outs, tops = [], []
    for h, mask in enumerate(masks()):
        kh = k * mask
        row, logs = [], []
        for start in range(0, length, QB):
            end = start + QB
            scores = causal(outer_nt(kh[:end], q[start:end]), start)
            top = jnp.max(scores, axis=0, keepdims=True)
            expd = jnp.exp(scores - top)
            total = jnp.sum(expd, axis=0, keepdims=True)
            probs = (expd / total).astype(bf16)
            row.append(matmul(vt[h * HD : (h + 1) * HD, :end], probs))
            logs.append(top + jnp.log(total))
        outs.append(jnp.concatenate(row, axis=1))
        tops.append(jnp.concatenate(logs, axis=1))
    return jnp.concatenate(outs, axis=0).T.astype(bf16), jnp.concatenate(tops, axis=0)


class Front:
    def __init__(self, length, width, experts, devices, capacity, moves):
        self.length, self.width, self.experts, self.capacity, self.moves = length, width, experts, capacity, moves
        pairs = width // PAIR
        share = width // devices
        self.at_norm, self.at_qkv = 4, 6
        self.at_heads = self.at_qkv + 1
        self.per_turn = 2
        self.at_out = self.at_heads + length // SEQ * pairs // self.per_turn
        self.steps = max(self.at_out + 1, moves.turns if moves else 0)
        slots = experts * capacity
        rows = lambda c, t: jax.ShapeDtypeStruct((length, c), t)
        self.outs = [
            rows(3 * width, bf16),
            jax.ShapeDtypeStruct((length // SEQ * pairs, 2, SEQ), f32),
            rows(width, bf16),
            rows(width, f32),
            rows(width, bf16),
            rows(width, bf16),
            rows(slots, bf16),
            rows(128, f32),
        ] + [jax.ShapeDtypeStruct((capacity, 2 * width), bf16)] * experts
        self.scratch = [
            pltpu.VMEM((devices, share, 128), bf16),
            pltpu.VMEM((devices, share, 3 * width), bf16),
            pltpu.VMEM((devices, share, width), bf16),
            pltpu.VMEM((8, width), f32),
            pltpu.VMEM((length, width), bf16),
            pltpu.SemaphoreType.DMA((3,)),
        ]

    def __call__(self, now, steps, tok, cot, route, drop, *refs):
        full = self.moves.full[:3] if self.moves else refs[:3]
        refs = refs if self.moves else refs[3:]
        qkv, lse, att, after, mixed, gd, disp, info = refs[:8]
        leave = refs[8 : 8 + self.experts]
        ws, wq, wo, gains, attn_in, sems = refs[8 + self.experts :]
        width, length = self.width, self.length
        loads = [pltpu.make_async_copy(a, b, sems.at[i]) for i, (a, b) in enumerate(zip(full, (ws, wq, wo)))]

        @when(now == self.at_norm)
        def _():
            loads[0].start()
            loads[0].wait()
            gains[...] = ws[...].reshape(width, 128).astype(f32).T[:8]
            normed, _ = normalize(tok[...].astype(f32))
            attn_in[...] = (normed * gains[0:1]).astype(bf16)

        @when(now == self.at_qkv)
        def _():
            loads[1].start()
            loads[1].wait()

            def columns(c, _):
                cols = pl.ds(pl.multiple_of(c * BLOCK, BLOCK), BLOCK)
                weights = wq[:, :, cols].reshape(width, BLOCK)
                qkv[:, cols] = matmul(attn_in[...], weights).astype(bf16)
                return 0

            lax.fori_loop(0, 3 * width // BLOCK, columns, 0)

        @when(jnp.logical_and(now >= self.at_heads, now < self.at_out))
        def _():
            pairs = width // PAIR

            def pair(i, _):
                at = (now - self.at_heads) * self.per_turn + i
                seq, at_pair = at // pairs, lax.rem(at, pairs)
                rows = pl.ds(pl.multiple_of(seq * SEQ, SEQ), SEQ)
                cols = lambda part: pl.ds(pl.multiple_of(part * width + at_pair * PAIR, PAIR), PAIR)
                out, tops = attend_pair(qkv[rows, cols(0)], qkv[rows, cols(1)], qkv[rows, cols(2)])
                att[rows, cols(0)] = out
                lse[at] = tops
                return 0

            lax.fori_loop(0, self.per_turn, pair, 0)

        @when(now == self.at_out)
        def _():
            loads[2].start()
            loads[2].wait()
            self.route(tok, cot, route, drop, att, wo, ws, gains, after, mixed, gd, disp, info, leave)

    def route(self, tok, cot, route, drop, att, wo, ws, gains, after, mixed, gd, disp, info, leave):
        width, length, experts = self.width, self.length, self.experts
        after[...] = tok[...].astype(f32) + matmul(att[...], wo[...].reshape(width, width))
        normed, _ = normalize(after[...])
        mixed[...] = (normed * gains[1:2]).astype(bf16)
        logits = matmul(mixed[...], ws[...].reshape(width, 128))
        lane = lax.broadcasted_iota(jnp.int32, (length, 128), 1)

        def softmax(first, last):
            inside = jnp.logical_and(lane >= first, lane < last)
            top = jnp.max(jnp.where(inside, logits, -jnp.inf), axis=1, keepdims=True)
            expd = jnp.where(inside, jnp.exp(jnp.where(inside, logits, top) - top), 0.0)
            return expd / jnp.sum(expd, axis=1, keepdims=True)

        probs, coef = softmax(2, 2 + experts), softmax(2 + experts, 4 + experts)
        info[...] = probs + coef
        chosen = jnp.where(lane - 2 == route[...], 1.0, 0.0)
        over_lanes = lambda a: jnp.sum(a, axis=1, keepdims=True)
        gate = over_lanes(probs * chosen) * (1 - drop[...]).astype(f32)
        coef_0 = over_lanes(jnp.where(lane == 2 + experts, coef, 0.0))
        coef_1 = over_lanes(jnp.where(lane == 3 + experts, coef, 0.0))
        grad = cot[...].astype(f32)
        gd[...] = (coef_0 * grad).astype(bf16)
        square = lambda d: lax.broadcasted_iota(jnp.int32, (length, length), d)
        earlier = jnp.where(square(0) > square(1), 1.0, 0.0).astype(bf16)
        position = over_lanes(chosen * matmul(earlier, chosen.astype(bf16))).astype(jnp.int32)
        turn = route[...] - lax.axis_index("expert")
        target = jnp.where(turn < 0, turn + experts, turn) * self.capacity + position
        slot = lax.broadcasted_iota(jnp.int32, (length, experts * self.capacity), 1)
        disp[...] = jnp.where(slot == target, 1.0, 0.0).astype(bf16)
        sent = (mixed[...], (coef_1 * gate * grad).astype(bf16))
        for h, values in enumerate(sent):
            placed = product_tn(disp[...], values).astype(bf16)
            for j in range(experts):
                leave[j][:, h * width : (h + 1) * width] = placed[j * self.capacity : (j + 1) * self.capacity]


def attend_pair_backward(q, k, v, g, lse):
    scaling = 1.0 / math.sqrt(HD)
    qs = q * scaling
    kt = k.T
    length = q.shape[0]
    grad_k = [0.0] * (length // QB)
    grad_v = [0.0] * (length // QB)
    grad_q = []
    for h, mask in enumerate(masks()):
        kh, vh, qh, gh = k * mask, v * mask, q * mask, g * mask
        row = []
        for c, start in enumerate(range(0, length, QB)):
            end = start + QB
            scores = causal(outer_nt(kh[:end], qs[start:end]), start)
            probs = jnp.exp(scores - lse[h : h + 1, start:end])
            grad_probs = outer_nt(vh[:end], g[start:end])
            delta = jnp.sum(probs * grad_probs, axis=0, keepdims=True)
            grad_scores = (probs * (grad_probs - delta)).astype(bf16)
            more_v = matmul(probs.astype(bf16), gh[start:end])
            more_k = matmul(grad_scores, qh[start:end])
            for b in range(c + 1):
                rows = slice(b * QB, (b + 1) * QB)
                grad_v[b] = grad_v[b] + more_v[rows]
                grad_k[b] = grad_k[b] + more_k[rows]
            row.append(matmul(kt[h * HD : (h + 1) * HD, :end], grad_scores))
        grad_q.append(jnp.concatenate(row, axis=1))
    return (
        (jnp.concatenate(grad_q, axis=0).T * scaling).astype(bf16),
        (jnp.concatenate(grad_k, axis=0) * scaling).astype(bf16),
        jnp.concatenate(grad_v, axis=0).astype(bf16),
    )


def thirds(values):
    parts = []
    for _ in range(3):
        parts.append(values.astype(bf16))
        values = values - parts[-1].astype(f32)
    return parts


class Back:
    GROUP = 2

    def __init__(self, length, width, experts, devices, capacity):
        self.length, self.width, self.experts, self.capacity = length, width, experts, capacity
        self.devices, self.share = devices, width // devices
        self.pairs = width // PAIR
        self.groups = self.pairs // self.GROUP
        self.part = self.GROUP * PAIR
        self.columns = 3 * self.part
        self.rest = width - self.columns
        self.items = self.groups + 2
        self.heads_at = 3
        self.last = self.heads_at + self.pairs
        self.steps = self.last + 1
        self.first_item = self.heads_at
        self.outs = [
            jax.ShapeDtypeStruct((length, width), bf16),
            jax.ShapeDtypeStruct((length, width), f32),
        ]
        slots = experts * capacity
        self.scratch = [
            pltpu.VMEM((slots, 2 * width), bf16),
            pltpu.VMEM((length, width), f32),
            pltpu.VMEM((length, width), f32),
            pltpu.VMEM((devices, self.share, 128), bf16),
            pltpu.VMEM((devices, self.share, width), bf16),
            pltpu.VMEM((2, devices, self.share, self.columns), bf16),
            pltpu.VMEM((8, width), f32),
            pltpu.VMEM((128, width), f32),
            pltpu.VMEM((width, length), bf16),
            pltpu.VMEM((length, width), bf16),
            pltpu.VMEM((length, self.columns), bf16),
            pltpu.SemaphoreType.DMA((5 + experts,)),
            pltpu.SemaphoreType.DMA((2, 3)),
        ]

    def made(self):
        chips = (4, 2, 2, self.experts // 2) if self.devices == 8 * self.experts else (self.devices,)
        return (self.items,) + chips + (self.share, self.columns)

    def final_outs(self):
        share, width = self.share, self.width
        return [jax.ShapeDtypeStruct((share, c), f32) for c in (3 * width, width, 128)]

    def store(self, outs, i, value):
        d_qkv, d_out, d_small = outs
        part = self.part

        @when(i == 0)
        def _():
            d_out[:, : self.columns] = value

        @when(jnp.logical_and(i > 0, i <= self.groups))
        def _():
            for p in range(3):
                at = pl.multiple_of(p * self.width + (i - 1) * part, part)
                d_qkv[:, pl.ds(at, part)] = value[:, p * part : (p + 1) * part]

        @when(i == self.groups + 1)
        def _():
            d_out[:, self.columns :] = value[:, : self.rest]
            d_small[...] = value[:, self.rest : self.rest + 128]

    def __call__(self, now, steps, *refs):
        experts, width, length = self.experts, self.width, self.length
        refs = list(refs)
        tok, cot, route, drop, qkv, lse, att, mixed_in, disp, info = refs[:10]
        small_hbm, qkv_hbm, out_hbm, dense_hbm, grad_hbm, after_hbm = refs[10:16]
        came_hbm = refs[16 : 16 + experts]
        mixed, tokens_grad, *rest = refs[16 + experts :]
        if self.moves:
            made = self.moves[-1].own
        else:
            made = rest.pop(0)
        came, dense, grads, ws, wo, wq, gains, d_heads, attn_in_t, grad_att, d_group, sems, wq_sems = rest
        fetch = lambda a, b, i: pltpu.make_async_copy(a, b, sems.at[i])
        capacity = self.capacity
        loads = [fetch(came_hbm[j], came.at[pl.ds(j * capacity, capacity)], j) for j in range(experts)]
        loads += [
            fetch(a, b, experts + i)
            for i, (a, b) in enumerate(
                ((dense_hbm, dense), (grad_hbm, grads), (after_hbm, tokens_grad), (small_hbm, ws), (out_hbm, wo))
            )
        ]

        def group_weights(group):
            slot = lax.rem(group, 2)
            return [
                pltpu.make_async_copy(
                    qkv_hbm.at[:, :, pl.ds(pl.multiple_of(p * width + group * self.part, self.part), self.part)],
                    wq.at[slot, :, :, pl.ds(p * self.part, self.part)],
                    wq_sems.at[slot, p],
                )
                for p in range(3)
            ]

        put = lambda i, columns, values: self.put(made, i, columns, values)
        lane = lax.broadcasted_iota(jnp.int32, (length, 128), 1)
        over_lanes = lambda a: jnp.sum(a, axis=1, keepdims=True)

        @when(now == 0)
        def _():
            for copy in loads:
                copy.start()
            for copy in group_weights(0):
                copy.start()
            for copy in loads:
                copy.wait()
            probs = jnp.where(jnp.logical_and(lane >= 2, lane < 2 + experts), info[...], 0.0)
            coef_0 = over_lanes(jnp.where(lane == 2 + experts, info[...], 0.0))
            coef_1 = over_lanes(jnp.where(lane == 3 + experts, info[...], 0.0))
            chosen = jnp.where(lane - 2 == route[...], 1.0, 0.0)
            kept = (1 - drop[...]).astype(f32)
            gate_prob = over_lanes(probs * chosen)
            gate = gate_prob * kept
            grad = cot[...].astype(f32)
            expert_tok = matmul(disp[...], came[:, :width])
            mixed[...] = (tokens_grad[...] + coef_0 * dense[...] + (coef_1 * gate) * expert_tok).astype(bf16)
            shared = over_lanes(grad * expert_tok)
            grad_0, grad_1 = over_lanes(grad * dense[...]), shared * gate
            both = coef_0 * grad_0 + coef_1 * grad_1
            grad_gate = shared * coef_1 * kept
            logits = jnp.where(
                jnp.logical_and(lane >= 2, lane < 2 + experts), (grad_gate * gate_prob) * (chosen - probs), 0.0
            )
            logits = jnp.where(lane == 2 + experts, coef_0 * (grad_0 - both), logits)
            logits = jnp.where(lane == 3 + experts, coef_1 * (grad_1 - both), logits)
            pieces = thirds(logits)
            d_heads[...] = add(*(product_tn(p, mixed_in[...]) for p in pieces))
            weights = ws[...].reshape(width, 128)
            grads[...] = (
                grads[...] + matmul(disp[...], came[:, width:]) + add(*(outer_nt(p, weights) for p in pieces))
            )
            gains[...] = weights.astype(f32).T[:8]

        @when(now == 1)
        def _():
            normed, scale = normalize(tokens_grad[...])
            d_heads[1:2] = jnp.sum(grads[...] * normed, axis=0, keepdims=True)
            grads[...] = cot[...].astype(f32) + norm_back(grads[...] * gains[1:2], normed, scale)
            normed, _ = normalize(tok[...].astype(f32))
            attn_in_t[...] = (normed * gains[0:1]).astype(bf16).T

        @when(now == 2)
        def _():
            grad_attn = grads[...].astype(bf16)
            grad_att[...] = outer_nt(grad_attn, wo[...].reshape(width, width)).astype(bf16)
            d_out = product_tn(att[...], grad_attn).astype(bf16)
            put(0, slice(0, self.columns), d_out[:, : self.columns])
            put(self.groups + 1, slice(0, self.rest), d_out[:, self.columns :])
            dense[...] = jnp.zeros_like(dense)

        @when(jnp.logical_and(now >= self.heads_at, now < self.last))
        def _():
            pair = now - self.heads_at
            group, of_group = pair // self.GROUP, lax.rem(pair, self.GROUP)
            cols = lambda part: pl.ds(pl.multiple_of(part * width + pair * PAIR, PAIR), PAIR)
            results = attend_pair_backward(
                qkv[:, cols(0)], qkv[:, cols(1)], qkv[:, cols(2)], grad_att[:, cols(0)], lse[pair]
            )
            for p, values in enumerate(results):
                d_group[:, pl.ds(pl.multiple_of(p * self.part + of_group * PAIR, PAIR), PAIR)] = values

            @when(of_group == self.GROUP - 1)
            def _():
                for copy in group_weights(group):
                    copy.wait()

                @when(group + 1 < self.groups)
                def _():
                    for copy in group_weights(group + 1):
                        copy.start()

                put(group + 1, slice(None), matmul(attn_in_t[...], d_group[...]).astype(bf16))
                weights = wq[lax.rem(group, 2)].reshape(width, self.columns)
                dense[...] += outer_nt(d_group[...], weights)

        @when(now == self.last)
        def _():
            normed, scale = normalize(tok[...].astype(f32))
            d_heads[0:1] = jnp.sum(dense[...] * normed, axis=0, keepdims=True)
            put(self.groups + 1, slice(self.rest, self.rest + 128), d_heads[...].T.astype(bf16))
            put(
                self.groups + 1,
                slice(self.rest + 128, self.columns),
                jnp.zeros((width, self.columns - self.rest - 128), bf16),
            )
            tokens_grad[...] = grads[...] + norm_back(dense[...] * gains[0:1], normed, scale)

    def put(self, made, i, columns, values):
        lead = made.shape[1:-1]
        at = (i,) + (slice(None),) * len(lead) + (columns,)
        made[at] = values.reshape(lead + values.shape[1:])


def gelu_both(v):
    c = math.sqrt(2.0 / math.pi)
    square = v * v
    t = jnp.tanh(c * (v + 0.044715 * (square * v)))
    half = 0.5 * (1.0 + t)
    slope = half + 0.5 * v * (1.0 - t * t) * (c * (1.0 + (3 * 0.044715) * square))
    return v * half, slope


def mlp_kernel(share, parts, now, steps, *refs):
    if parts:
        pieces, (w1_ref, w2_ref), refs = refs[:parts], refs[parts : parts + 2], refs[parts + 2 :]
        results, (d1_ref, d2_ref) = refs[:parts], refs[parts : parts + 2]
        x, g, xt, gt, out_sum, back_sum = refs[parts + 2 :]
    else:
        x, g, w1_ref, w2_ref, out_sum, back_sum, d1_ref, d2_ref, xt, gt = refs
    width = xt.shape[0]

    @when(now == 0)
    def _():
        if parts:
            size = pieces[0].shape[0]
            for j, piece in enumerate(pieces):
                x[j * size : (j + 1) * size] = piece[:, :width]
                g[j * size : (j + 1) * size] = piece[:, width:]
        xt[...] = x[...].T
        gt[...] = g[...].T
        out_sum[...] = jnp.zeros_like(out_sum)
        back_sum[...] = jnp.zeros_like(back_sum)

    w1 = w1_ref[...].reshape(w1_ref.shape[-2:])
    w2 = w2_ref[...].reshape(w2_ref.shape[-2:])
    hidden, slope = gelu_both(matmul(x[...], w1))
    hidden = hidden.astype(bf16)
    grad_pre = (slope * outer_nt(g[...], w2)).astype(bf16)
    out_sum[...] += matmul(hidden, w2)
    back_sum[...] += outer_nt(grad_pre, w1)
    d1 = matmul(xt[...], grad_pre).astype(bf16)
    d2 = matmul(gt[...], hidden).astype(bf16)
    if share is None:
        d1_ref[...] = d1.reshape(d1_ref.shape)
        d2_ref[...] = d2.reshape(d2_ref.shape)
    else:
        for c in range(d1.shape[1] // 128):
            cols = slice(c * 128, (c + 1) * 128)
            for s in range(d1_ref.shape[0]):
                d1_ref[s, c * share : (c + 1) * share] = d1[s * share : (s + 1) * share, cols]
            d2_ref[c] = d2[:, cols]

    if parts:

        @when(now == steps - 1)
        def _():
            for h, total in enumerate((out_sum, back_sum)):
                for j, result in enumerate(results):
                    rows = slice(j * result.shape[0], (j + 1) * result.shape[0])
                    result[:, h * width : (h + 1) * width] = total[rows].astype(bf16)


def mlp(rows_in, w1, w2, name, moves, collective_id, experts, devices=None):
    share = None
    if w1.ndim == 3:
        blocks, width, size = w1.shape
        w1_spec = pl.BlockSpec((1, width, size), lambda j: (j, 0, 0))
        w2_spec = pl.BlockSpec((1, size, width), lambda j: (j, 0, 0))
        d_shape, d_specs = (blocks, width, size), [w1_spec] * 2
    else:
        size = BLOCK
        width = w1.shape[0]
        blocks = w1.shape[1] // size
        w1_spec = pl.BlockSpec((width, size), lambda j: (0, j))
        w2_spec = pl.BlockSpec((size, width), lambda j: (j, 0))
        d_shape, d_specs = (width, blocks * size), [w1_spec] * 2
        if devices:
            share = width // devices
            d_shape = (devices, width, 128)
            d_specs = [
                pl.BlockSpec((devices, size // 128 * share, 128), lambda j: (0, j, 0)),
                pl.BlockSpec((size // 128, width, 128), lambda j: (j, 0, 0)),
            ]
    whole = pl.BlockSpec(memory_space=pltpu.VMEM)
    joined = rows_in[0].shape[1] == 2 * width
    parts = len(rows_in) if joined else 0
    rows = sum(a.shape[0] for a in rows_in) if joined else rows_in[0].shape[0]
    if joined:
        outs = [jax.ShapeDtypeStruct(a.shape, bf16) for a in rows_in]
    else:
        outs = [jax.ShapeDtypeStruct((rows, width), f32)] * 2
    flat, across = pltpu.VMEM((rows, width), bf16), pltpu.VMEM((width, rows), bf16)
    sums = [pltpu.VMEM((rows, width), f32)] * 2
    return call(
        name,
        blocks,
        functools.partial(mlp_kernel, share, parts),
        list(rows_in) + [w1, w2],
        [whole] * len(rows_in) + [w1_spec, w2_spec],
        outs + [jax.ShapeDtypeStruct(d_shape, bf16)] * 2,
        [whole] * len(outs) + d_specs,
        [flat, flat, across, across] + sums if joined else [across, across],
        moves,
        collective_id,
        experts,
        12 * rows * width * blocks * size,
    )


def move(name, moves, collective_id, experts):
    return call(name, 1, None, [], [], [], [], [], moves, collective_id, experts, 0)


def shards(
    fast,
    tokens,
    gain_attn,
    w_qkv,
    w_out,
    gain_mix,
    w_fc,
    w_proj,
    w_router,
    w_coef,
    expert_in,
    expert_out,
    routes,
    dropped,
    cotangent,
):
    experts = lax.axis_size("expert")
    nodes = lax.axis_size("node")
    devices = nodes * experts
    width = tokens.shape[1]
    tok_rows = tokens.shape[0]
    ff = w_fc.shape[1]
    share = w_qkv.shape[0]
    small = jnp.concatenate([gain_attn[:, None], gain_mix[:, None], w_router, w_coef], axis=1)
    small = jnp.pad(small, ((0, 0), (0, 128 - small.shape[1])))
    win, wout = expert_in[0], expert_out[0]
    together = lambda a: a.reshape((devices * a.shape[1],) + a.shape[2:])
    cut = lambda a, rows, columns, m, n: [
        [(a, i * (rows // m), rows // m, j * (columns // n), columns // n)] for i in range(m) for j in range(n)
    ]
    weights = (small, w_qkv, w_out, w_fc, w_proj)
    capacity = -(-(tok_rows * 10) // (8 * experts))
    gather_dense, gather_experts = [], []
    if fast:
        items = cut(1, share, 3 * width, 1, 3) + cut(2, share, width, 1, 1)
        items += cut(3, share, ff, 1, 4) + cut(4, ff // devices, width, 4, 1)
        items[0] = cut(0, share, 128, 1, 1)[0] + items[0]
        gather_dense = [Gather(list(weights), [True] * 5, items, nodes, experts)]
        items = cut(0, width, win.shape[1], 4, 1) + cut(1, wout.shape[0], width, 4, 1)
        gather_experts = [Gather([win, wout], [False] * 2, items, nodes, experts)]
        full = []
    else:
        full = [lax.all_gather(a, AXES, axis=0, tiled=False) for a in weights]
        win_full, wout_full = (lax.all_gather(a, "node", axis=0, tiled=False) for a in (win, wout))

    def scatter_xla(parts, axes):
        return lax.psum_scatter(parts, axes, scatter_dimension=0, tiled=False).astype(f32)

    def exchange(parts, sign):
        moved = [parts[0]]
        for j in range(1, experts):
            shift = [(s, (s + sign * j) % experts) for s in range(experts)]
            moved.append(lax.ppermute(parts[j], "expert", shift))
        return moved

    front = Front(tok_rows, width, experts, devices, capacity, gather_dense[0] if fast else None)
    kept = full[:3]
    whole, hbm = pl.BlockSpec(memory_space=pltpu.VMEM), pl.BlockSpec(memory_space=pltpu.HBM)
    dropped = dropped[:, None]
    results = call(
        "front",
        front.steps,
        front,
        [tokens, cotangent, routes, dropped] + kept,
        [whole] * 4 + [hbm] * len(kept),
        front.outs,
        [whole] * len(front.outs),
        front.scratch,
        gather_dense,
        1,
        experts,
        12 * tok_rows * width * width,
    )
    qkv_rows, lse, attended, after_attn, mixed_in, grad_dense, dispatch, probs = results[:8]
    arrived = exchange(results[8 : 8 + experts], 1)
    small_full, qkv_full, out_full, fc_full, proj_full = results[8 + experts :] if fast else full

    dense_out, grad_mixed, d_fc, d_proj, *gathered = mlp(
        [mixed_in, grad_dense],
        together(fc_full),
        together(proj_full),
        "dense_mlp",
        gather_experts,
        2,
        experts,
        devices if fast else None,
    )
    scatter_dense = []
    if fast:
        win_full, wout_full = gathered
        chunks = 4
        by_chip = lambda a: a.reshape(4, 2, 2, experts // 2, chunks, width // chunks, 128)

        def store_dense(outs, i, value):
            step = width // chunks

            @when(i < chunks)
            def _():
                for q in range(step // share):
                    at = pl.multiple_of(i * (step // share * 128) + q * 128, 128)
                    outs[0][:, pl.ds(at, 128)] = value[q * share : (q + 1) * share]

            @when(i >= chunks)
            def _():
                at = pl.multiple_of((i - chunks) * step, step)
                outs[1][:, pl.ds(at, step)] = value.T

        outs = [jax.ShapeDtypeStruct((share, ff), f32), jax.ShapeDtypeStruct((ff // devices, width), f32)]
        scatter_dense = [Scatter([by_chip(d_fc), by_chip(d_proj)], "rows", experts, outs, store_dense)]
    *returned, d_win, d_wout, grad_fc, grad_proj = (
        list(mlp(arrived, win_full, wout_full, "expert_mlp", scatter_dense, 3, experts)) + ([] if fast else [None] * 2)
    )
    came_back = exchange(returned, -1)
    back = Back(tok_rows, width, experts, devices, capacity)
    back.moves = []
    if fast:
        chunks_e = 8
        size = width // chunks_e
        cut_rows = lambda a: a.reshape(4, 2, chunks_e, 2, size // 2, a.shape[2])
        at = lambda i: pl.ds(pl.multiple_of(i * size, size), size)

        def store_win(outs, i, value):
            outs[0][0, at(i)] = value

        def store_wout(outs, i, value):
            outs[0][0, :, at(i)] = value.T

        like = lambda a: [jax.ShapeDtypeStruct(a.shape, f32)]
        scatter_win = Scatter([cut_rows(d_win)], "plane", experts, like(expert_in), store_win)
        scatter_wout = Scatter([cut_rows(d_wout)], "plane", experts, like(expert_out), store_wout)
        (grad_win,) = move("scatter_win", [scatter_win], 4, experts)
        scatter_rest = Scatter(
            [], "made", experts, back.final_outs(), back.store, back.first_item, back.GROUP, back.made()
        )
        back.moves = [scatter_wout, scatter_rest]
    outs = back.outs + ([] if fast else [jax.ShapeDtypeStruct((back.items, width, back.columns), bf16)])
    mixed, tokens_grad, *results = call(
        "back",
        back.steps,
        back,
        [tokens, cotangent, routes, dropped, qkv_rows, lse, attended, mixed_in, dispatch, probs]
        + [small_full, qkv_full, out_full, dense_out, grad_mixed, after_attn]
        + came_back,
        [whole] * 10 + [hbm] * (6 + experts),
        outs,
        [whole] * len(outs),
        back.scratch,
        back.moves,
        5,
        experts,
        32 * tok_rows * width * width,
    )
    if fast:
        grad_wout, grad_wqkv, grad_wo, grad_small = results
    else:
        summed = scatter_xla(results[0].reshape(back.items, devices, share, -1).swapaxes(0, 1), AXES)
        grad_wo = jnp.concatenate([summed[0], summed[-1][:, : back.rest]], axis=1)
        grad_small = summed[-1][:, back.rest : back.rest + 128]
        groups = summed[1:-1].reshape(back.groups, share, 3, back.part)
        grad_wqkv = groups.transpose(1, 2, 0, 3).reshape(share, 3 * width)
        grad_fc = scatter_xla(d_fc.reshape(devices, share, ff), AXES)
        by_unit = d_proj.reshape(width, devices, ff // devices).transpose(1, 0, 2)
        grad_proj = scatter_xla(by_unit, AXES).T
        grad_win = scatter_xla(d_win, "node")[None]
        grad_wout = scatter_xla(d_wout, "node").T[None]
    return (
        mixed,
        tokens_grad,
        grad_small[:, 0],
        grad_wqkv,
        grad_wo,
        grad_small[:, 1],
        grad_fc,
        grad_proj,
        grad_small[:, 2 : 2 + experts],
        grad_small[:, 2 + experts : 4 + experts],
        grad_win,
        grad_wout,
    )


def solution(mesh):
    rows = P(AXES, None)
    in_specs = (
        rows,
        P(AXES),
        rows,
        rows,
        P(AXES),
        rows,
        rows,
        rows,
        rows,
        P("expert", None, "node"),
        P("expert", "node", None),
        rows,
        P(AXES),
        rows,
    )
    out_specs = (
        rows,
        rows,
        P(AXES),
        rows,
        rows,
        P(AXES),
        rows,
        rows,
        rows,
        rows,
        P("expert", None, "node"),
        P("expert", "node", None),
    )
    fast = mesh.shape["node"] == 8 and mesh.shape["expert"] % 2 == 0
    return jax.shard_map(
        functools.partial(shards, fast), mesh=mesh, in_specs=in_specs, out_specs=out_specs, check_vma=False
    )
```

```python
import functools
import math

import jax
import jax.numpy as jnp
from jax import lax
from jax.experimental import pallas as pl
from jax.experimental.pallas import tpu as pltpu
from jax.sharding import PartitionSpec as P

HD = 64
PAIR = 2 * HD
SEQ = 512
QB = 256
BLOCK = 512
MIB = 1 << 20
AXES = ("node", "expert")
MESH = pl.DeviceIdType.MESH
epsilon = 1e-05
f32 = jnp.float32
bf16 = jnp.bfloat16


def normalize(values):
    centered = values - jnp.mean(values, axis=-1, keepdims=True)
    inv_scale = lax.rsqrt(jnp.mean(centered * centered, axis=-1, keepdims=True) + epsilon)
    return (centered * inv_scale, inv_scale)


def norm_back(grad_norm, normed, inv_scale):
    mean_grad = jnp.mean(grad_norm, axis=-1, keepdims=True)
    mean_cross = jnp.mean(grad_norm * normed, axis=-1, keepdims=True)
    return inv_scale * (grad_norm - mean_grad - normed * mean_cross)


def contract(left_op, right_op, left_dim, right_dim):
    return lax.dot_general(
        left_op, right_op, (((left_dim,), (right_dim,)), ((), ())), preferred_element_type=f32
    )


def matmul(left_op, right_op):
    return contract(left_op, right_op, 1, 0)


def product_tn(left_op, right_op):
    return contract(left_op, right_op, 0, 0)


def outer_nt(left_op, right_op):
    return contract(left_op, right_op, 1, 1)


class Place:
    def __init__(self, experts):
        self.experts = experts
        self.n, self.e = lax.axis_index("node"), lax.axis_index("expert")
        n = self.n
        self.k, self.x, self.y = lax.rem(n, 2), lax.rem(n // 2, 2), n // 4
        k, x, y = self.k, self.x, self.y
        self.nx, self.ny = y * 4 + (1 - x) * 2 + k, (1 - y) * 4 + x * 2 + k
        self.nd, self.nc = (1 - y) * 4 + (1 - x) * 2 + k, y * 4 + x * 2 + 1 - k

    def z(self, j):
        return (self.n, lax.rem(self.e + j, self.experts))

    def greet(self, along_z):
        barrier = pltpu.get_barrier_semaphore()
        peers = [(self.nx, self.e), (self.ny, self.e), (self.nc, self.e)]
        if along_z:
            peers += [self.z(j) for j in range(1, self.experts)]
        for peer in peers:
            pl.semaphore_signal(barrier, inc=1, device_id=peer, device_id_type=MESH)
        pl.semaphore_wait(barrier, len(peers))


def when(condition):
    return pl.when(condition)


class Gather:
    def __init__(self, args, dense, items, nodes, experts):
        self.args, self.dense, self.items, self.experts = args, dense, items, experts
        self.outs = [
            jax.ShapeDtypeStruct(((nodes * experts if d else nodes),) + a.shape, a.dtype)
            for a, d in zip(args, dense)
        ]
        hbm = pl.BlockSpec(memory_space=pltpu.HBM)
        self.in_specs, self.out_specs = [hbm] * len(args), [hbm] * len(args)
        m = sum(len(item) for item in items)
        self.scratch = [
            pltpu.SemaphoreType.DMA((m, experts + 7)),
            pltpu.SemaphoreType.DMA((m, experts + 7)),
            pltpu.SemaphoreType.DMA((m,)),
        ]
        self.along_z = any(dense)
        self.steps = [self.along, self.across, self.corner, self.over, self.end][0 if self.along_z else 1 :]
        self.turns = len(items) + len(self.steps) - 1

    def bind(self, ins, outs, scratch, place):
        experts = self.experts
        send, recv, loc = scratch
        p, e = place, place.e

        def remote(source, target, item, kind, device):
            return pltpu.make_async_remote_copy(
                src_ref=source,
                dst_ref=target,
                send_sem=send.at[item, kind],
                recv_sem=recv.at[item, kind],
                device_id=device,
                device_id_type=MESH,
            )

        self.full = outs
        self.bound = [[] for _ in self.items]
        pieces = [(turn, piece) for turn, item in enumerate(self.items) for piece in item]
        for i, (turn, (arg, row, rows, col, columns)) in enumerate(pieces):
            dense = self.dense[arg]
            shard, whole = ins[arg], outs[arg]
            per = experts if dense else 1
            own = p.n * per + (e if dense else 0)

            def view(ref, lead, start=0, size=None, whole_rows=rows, row=row, col=col, columns=columns):
                return ref.at[lead, pl.ds(row + start, size or whole_rows), pl.ds(col, columns)]

            def bundle(m, view=view, whole=whole, per=per):
                return view(whole, pl.ds(m * per, per))

            def half(m, h, view=view, whole=whole, per=per, dense=dense, rows=rows):
                if dense:
                    return view(whole, pl.ds(m * per + h * (per // 2), per // 2))
                return view(whole, m, h * (rows // 2), rows // 2)

            mine = shard.at[pl.ds(row, rows), pl.ds(col, columns)]
            land = view(whole, own)
            local = pltpu.make_async_copy(mine, land, loc.at[i])
            z = []
            if dense:
                z = [remote(mine, land, i, j - 1, p.z(j)) for j in range(1, experts)]
            first, last = (bundle(p.n), bundle(p.n)) if dense else (mine, land)
            b = experts - 1
            xy = [remote(first, last, i, b, (p.nx, e)), remote(first, last, i, b + 1, (p.ny, e))]
            diag = [
                remote(half(p.nx, 0), half(p.nx, 0), i, b + 2, (p.ny, e)),
                remote(half(p.ny, 1), half(p.ny, 1), i, b + 3, (p.nx, e)),
            ]
            core = [remote(first, last, i, b + 4, (p.nc, e))] + [
                remote(bundle(m), bundle(m), i, b + 5 + j, (p.nc, e)) for j, m in enumerate((p.nx, p.ny, p.nd))
            ]
            self.bound[turn].append((local, z, xy, diag, core))

    def turn(self, now):
        for t in range(self.turns):

            @when(now == t)
            def _(t=t):
                for late, step in enumerate(self.steps):
                    if 0 <= t - late < len(self.items):
                        for piece in self.bound[t - late]:
                            step(*piece)

    def finish(self, now):
        pass

    def along(self, local, z, xy, diag, core):
        local.start()
        for copy in z:
            copy.start()

    def across(self, local, z, xy, diag, core):
        if not self.along_z:
            local.start()
        for copy in z:
            copy.wait()
        if self.along_z:
            local.wait()
        xy[0].start()
        xy[1].start()
        core[0].start()

    def corner(self, local, z, xy, diag, core):
        for i in range(2):
            xy[i].wait()
            diag[i].start()
            core[1 + i].start()

    def over(self, local, z, xy, diag, core):
        diag[0].wait()
        diag[1].wait()
        core[3].start()

    def end(self, local, z, xy, diag, core):
        if not self.along_z:
            local.wait()
        for copy in core:
            copy.wait()


class Exchange:
    along_z = True

    def __init__(self, pieces, sign, experts, start, turns, shape):
        self.args, self.sign, self.experts, self.start, self.turns = list(pieces), sign, experts, start, turns
        self.given = None
        self.outs = [jax.ShapeDtypeStruct(shape, bf16)] * (experts - 1)
        hbm = pl.BlockSpec(memory_space=pltpu.HBM)
        self.in_specs, self.out_specs = [hbm] * len(self.args), [hbm] * (experts - 1)
        self.scratch = [pltpu.SemaphoreType.DMA((experts,)), pltpu.SemaphoreType.DMA((experts,))]

    def bind(self, ins, outs, scratch, place):
        self.out, self.sems, self.place = outs, scratch, place
        if ins:
            self.sources = ins

    def copies(self):
        return [
            pltpu.make_async_remote_copy(
                src_ref=source,
                dst_ref=self.out[j],
                send_sem=self.sems[0].at[j],
                recv_sem=self.sems[1].at[j],
                device_id=self.place.z((self.sign * (j + 1)) % self.experts),
                device_id_type=MESH,
            )
            for j, source in enumerate(self.sources)
        ]

    def send(self):
        for copy in self.copies():
            copy.start()

    def turn(self, now):
        if self.start is not None:

            @when(now == self.start)
            def _():
                self.send()

    def finish(self, now):
        @when(now == self.turns - 1)
        def _():
            for copy in self.copies():
                copy.wait()


class Scatter:
    RING = 6
    CORE_RING = 4

    def __init__(self, parts, half, experts, outs, store, start=0, made=None, z_late=4):
        self.experts, self.outs, self.store, self.start, self.made = experts, outs, store, start, made
        self.parts = parts
        self.given = []
        self.args = [p[0] for p in parts if p[0] is not None]
        h = half
        self.starts = [sum(p[3] for p in parts[:a]) for a in range(len(parts) + 1)]
        m = self.m = self.starts[-1]
        self.m_z = sum(p[3] for p in parts if p[1])
        unit = h[1:]
        ring = self.ring = min(self.RING, m)
        self.core_ring = min(self.CORE_RING, m)
        self.in_specs = [pl.BlockSpec(memory_space=pltpu.HBM)] * len(self.args)
        self.out_specs = [pl.BlockSpec(memory_space=pltpu.VMEM)] * len(outs)
        kinds = 7 + experts
        self.scratch = [
            pltpu.VMEM(made or (ring, 4, 2) + h, bf16),
            pltpu.VMEM((self.core_ring, 4, 2) + h, bf16),
            pltpu.VMEM((ring, 2) + h, bf16),
            pltpu.VMEM((ring, 2) + h, bf16),
            pltpu.VMEM((ring,) + h, bf16),
            pltpu.VMEM((ring,) + h, bf16),
            pltpu.SemaphoreType.DMA((m, kinds)),
            pltpu.SemaphoreType.DMA((m, kinds)),
            pltpu.SemaphoreType.DMA((m,)),
        ]
        if self.m_z:
            self.scratch.append(pltpu.VMEM((self.m_z, experts - 1) + unit, bf16))
            self.scratch.append(pltpu.VMEM((self.m_z, experts) + unit, bf16))
        self.z_late = z_late
        self.turns = start + max(m + 3, self.m_z + z_late)
        self.along_z = self.m_z > 0

    def bind(self, ins, outs, scratch, place):
        ins = list(ins)
        given = list(self.given)
        self.sources = [given.pop(0) if p[0] is None else ins.pop(0) for p in self.parts] if not self.made else []
        self.out, self.place = outs, place
        self.own, self.rc, self.rx, self.ry, self.lx, self.ly, self.sent, self.recv, self.loc = scratch[:9]
        self.rz, self.zs = scratch[9:] if self.m_z else (None, None)

    def slot(self, i):
        return lax.rem(i, self.ring)

    def remote(self, source, target, item, kind, device):
        return pltpu.make_async_remote_copy(
            src_ref=source,
            dst_ref=target,
            send_sem=self.sent.at[item, kind],
            recv_sem=self.recv.at[item, kind],
            device_id=device,
            device_id_type=MESH,
        )

    def at(self, i, site, *more):
        return (i, site, self.place.k) + more if self.made else (self.slot(i), site) + more

    def first(self, source, i, chunk):
        p = self.place
        land = self.rc.at[lax.rem(i, self.core_ring)]
        if self.made:
            return [self.remote(self.own.at[i, :, 1 - p.k], land, i, 0, (p.nc, p.e))]
        part = lambda core: source.at[:, core, :, :, chunk]
        local = pltpu.make_async_copy(part(p.k), self.own.at[self.slot(i)], self.loc.at[i])
        return [self.remote(part(1 - p.k), land, i, 0, (p.nc, p.e)), local]

    def sites(self):
        p = self.place
        return p.y * 2 + p.x, p.y * 2 + 1 - p.x, (1 - p.y) * 2 + p.x, (1 - p.y) * 2 + 1 - p.x

    def round_one(self, i):
        p = self.place
        b = self.slot(i)
        _, to_x, to_y, diag = self.sites()
        own = lambda *at: self.own.at[self.at(i, *at)]
        return [
            self.remote(own(diag, 0), self.rx.at[b, 0], i, 1, (p.nx, p.e)),
            self.remote(own(diag, 1), self.ry.at[b, 0], i, 2, (p.ny, p.e)),
            self.remote(own(to_x, 0), self.rx.at[b, 1], i, 3, (p.nx, p.e)),
            self.remote(own(to_y, 1), self.ry.at[b, 1], i, 4, (p.ny, p.e)),
        ]

    def round_two(self, i):
        p = self.place
        b = self.slot(i)
        _, to_x, to_y, _ = self.sites()
        return [
            self.remote(self.own.at[self.at(i, to_x, 1)], self.lx.at[b], i, 5, (p.nx, p.e)),
            self.remote(self.own.at[self.at(i, to_y, 0)], self.ly.at[b], i, 6, (p.ny, p.e)),
        ]

    def round_z(self, i):
        p = self.place
        return [
            self.remote(self.zs.at[i, lax.rem(p.e + j, self.experts)], self.rz.at[i, j - 1], i, 6 + j, p.z(j))
            for j in range(1, self.experts)
        ]

    def turn(self, now):
        limits = (self.m, self.m, self.m, self.m, self.m_z)
        steps = (self.load, self.chip, self.cross, self.plane, self.column)
        for limit, late, step in zip(limits, (0, 1, 2, 3, self.z_late), steps):
            i = now - self.start - late
            if limit:

                @when(jnp.logical_and(i >= 0, i < limit))
                def _(step=step, i=i):
                    step(i)

    def finish(self, now):
        pass

    def load(self, i):
        if self.made:
            self.first(None, i, 0)[0].start()
            return
        for a, source in enumerate(self.sources):

            @when(jnp.logical_and(i >= self.starts[a], i < self.starts[a + 1]))
            def _(a=a, source=source):
                for copy in self.first(source, i, i - self.starts[a] + self.parts[a][2]):
                    copy.start()

    def chip(self, i):
        for copy in self.first(None if self.made else self.sources[0], i, 0):
            copy.wait()

        def sum_one(q, _):
            at = self.at(i, q)
            self.own[at] = add(self.own[at], self.rc[lax.rem(i, self.core_ring), q]).astype(bf16)
            return 0

        lax.fori_loop(0, 4, sum_one, 0)
        for copy in self.round_one(i):
            copy.start()

    def cross(self, i):
        one = self.round_one(i)
        two = self.round_two(i)
        b = self.slot(i)
        _, to_x, to_y, _ = self.sites()
        for copy in one:
            copy.wait()
        at_x, at_y = self.at(i, to_x, 1), self.at(i, to_y, 0)
        self.own[at_x] = add(self.own[at_x], self.ry[b, 0]).astype(bf16)
        two[0].start()
        self.own[at_y] = add(self.own[at_y], self.rx[b, 0]).astype(bf16)
        two[1].start()

    def plane(self, i):
        for copy in self.round_two(i):
            copy.wait()
        mine, _, _, _ = self.sites()
        b = self.slot(i)
        sums = lambda: (
            add(self.own[self.at(i, mine, 0)], self.rx[b, 1], self.ly[b]),
            add(self.own[self.at(i, mine, 1)], self.lx[b], self.ry[b, 1]),
        )
        if self.m_z:

            @when(i < self.m_z)
            def _():
                s = self.experts // 2
                for h, total in enumerate(sums()):
                    self.zs[i, h * s : (h + 1) * s] = total.astype(bf16)
                for copy in self.round_z(i):
                    copy.start()

        if self.m_z < self.m:

            @when(i >= self.m_z)
            def _():
                self.store(self.out, i, sums())

    def column(self, i):
        for copy in self.round_z(i):
            copy.wait()
        terms = [self.zs[i, self.place.e]] + [self.rz[i, j] for j in range(self.experts - 1)]
        self.store(self.out, i, add(*terms))


def add(*terms):
    return functools.reduce(jnp.add, [t.astype(f32) for t in terms])


def call(
    name, steps, body, args, in_specs, outs, out_specs, scratch, moves, collective_id, experts, flops, given=None
):
    total = max([steps] + [m.turns for m in moves])

    def hold(spec):
        if spec.block_shape is None:
            return spec
        index = spec.index_map
        return pl.BlockSpec(spec.block_shape, lambda j: index(jnp.minimum(j, steps - 1)))

    join = lambda what: [x for m in moves for x in getattr(m, what)]

    def kernel(*refs):
        refs = list(refs)
        take = lambda group: [refs.pop(0) for _ in group]
        ins, m_ins = take(args), [take(m.args) for m in moves]
        os, m_os = take(outs), [take(m.outs) for m in moves]
        own, m_own = take(scratch), [take(m.scratch) for m in moves]
        now = pl.program_id(0)
        if moves:
            place = Place(experts)
            if given is not None:
                given(ins, os, own)
            for m, a, o, r in zip(moves, m_ins, m_os, m_own):
                m.bind(a, o, r, place)

            @when(now == 0)
            def _():
                place.greet(any(m.along_z for m in moves))

            for m in moves:
                m.turn(now)
        if body is not None:

            @when(now < steps)
            def _():
                body(now, steps, *ins, *os, *own)

        for m in moves:
            m.finish(now)

    results = pl.pallas_call(
        kernel,
        grid=(total,),
        out_shape=list(outs) + join("outs"),
        in_specs=[hold(s) for s in in_specs] + join("in_specs"),
        out_specs=[hold(s) for s in out_specs] + join("out_specs"),
        scratch_shapes=list(scratch) + join("scratch"),
        cost_estimate=pl.CostEstimate(flops=flops, bytes_accessed=32 * MIB, transcendentals=0),
        compiler_params=pltpu.CompilerParams(
            vmem_limit_bytes=60 * MIB,
            **({"collective_id": collective_id, "has_side_effects": True} if moves else {}),
        ),
        name=name,
    )(*args, *join("args"))
    return list(results)


def masks():
    lanes = lax.broadcasted_iota(jnp.int32, (1, PAIR), 1)
    return [(lanes // HD == h).astype(bf16) for h in range(2)]


def causal(scores_t, start):
    keys = lax.broadcasted_iota(jnp.int32, scores_t.shape, 0)
    queries = lax.broadcasted_iota(jnp.int32, scores_t.shape, 1) + start
    return jnp.where(keys <= queries, scores_t, -jnp.inf)


def attend_pair(q, k, v):
    q = q * (1.0 / math.sqrt(HD))
    vt = v.T
    length = q.shape[0]
    outs, tops = [], []
    for h, mask in enumerate(masks()):
        kh = k * mask
        row, logs = [], []
        for start in range(0, length, QB):
            end = start + QB
            scores = causal(outer_nt(kh[:end], q[start:end]), start)
            top = jnp.max(scores, axis=0, keepdims=True)
            expd = jnp.exp(scores - top)
            total = jnp.sum(expd, axis=0, keepdims=True)
            probs = (expd / total).astype(bf16)
            row.append(matmul(vt[h * HD : (h + 1) * HD, :end], probs))
            logs.append(top + jnp.log(total))
        outs.append(jnp.concatenate(row, axis=1))
        tops.append(jnp.concatenate(logs, axis=1))
    return jnp.concatenate(outs, axis=0).T.astype(bf16), jnp.concatenate(tops, axis=0)


def columns_of(code):
    length = code.shape[1]
    return [jnp.broadcast_to(code[i : i + 1], (128, length)).T.astype(jnp.int32) for i in range(2)]


class Front:
    def __init__(self, length, width, experts, devices, capacity, moves):
        self.length, self.width, self.experts, self.capacity, self.moves = length, width, experts, capacity, moves
        pairs = width // PAIR
        share = width // devices
        self.at_norm, self.at_qkv = 4, 6
        self.at_heads = self.at_qkv + 1
        self.per_turn = 2
        self.at_out = self.at_heads + length // SEQ * pairs // self.per_turn
        self.steps = max(self.at_out + 1, moves.turns if moves else 0)
        slots = experts * capacity
        rows = lambda c, t: jax.ShapeDtypeStruct((length, c), t)
        self.outs = [
            rows(3 * width, bf16),
            jax.ShapeDtypeStruct((length // SEQ * pairs, 2, SEQ), f32),
            rows(width, bf16),
            rows(width, f32),
            rows(width, bf16),
            rows(width, bf16),
            rows(slots, bf16),
            rows(128, f32),
        ] + [jax.ShapeDtypeStruct((capacity, 2 * width), bf16)] * experts
        self.scratch = [
            pltpu.VMEM((devices, share, 128), bf16),
            pltpu.VMEM((devices, share, 3 * width), bf16),
            pltpu.VMEM((devices, share, width), bf16),
            pltpu.VMEM((8, width), f32),
            pltpu.VMEM((length, width), bf16),
            pltpu.SemaphoreType.DMA((3,)),
        ]

    def __call__(self, now, steps, tok, cot, code, *refs):
        full = self.moves.full[:3] if self.moves else refs[:3]
        refs = refs if self.moves else refs[3:]
        qkv, lse, att, after, mixed, gd, disp, info = refs[:8]
        leave = refs[8 : 8 + self.experts]
        ws, wq, wo, gains, attn_in, sems = refs[8 + self.experts :]
        width, length = self.width, self.length
        loads = [pltpu.make_async_copy(a, b, sems.at[i]) for i, (a, b) in enumerate(zip(full, (ws, wq, wo)))]

        @when(now == self.at_norm)
        def _():
            loads[0].start()
            loads[0].wait()
            gains[...] = ws[...].reshape(width, 128).astype(f32).T[:8]
            normed, _ = normalize(tok[...].astype(f32))
            attn_in[...] = (normed * gains[0:1]).astype(bf16)

        @when(now == self.at_qkv)
        def _():
            loads[1].start()
            loads[1].wait()

            def columns(c, _):
                cols = pl.ds(pl.multiple_of(c * BLOCK, BLOCK), BLOCK)
                weights = wq[:, :, cols].reshape(width, BLOCK)
                qkv[:, cols] = matmul(attn_in[...], weights).astype(bf16)
                return 0

            lax.fori_loop(0, 3 * width // BLOCK, columns, 0)

        @when(jnp.logical_and(now >= self.at_heads, now < self.at_out))
        def _():
            pairs = width // PAIR

            def pair(i, _):
                at = (now - self.at_heads) * self.per_turn + i
                seq, at_pair = at // pairs, lax.rem(at, pairs)
                rows = pl.ds(pl.multiple_of(seq * SEQ, SEQ), SEQ)
                cols = lambda part: pl.ds(pl.multiple_of(part * width + at_pair * PAIR, PAIR), PAIR)
                out, tops = attend_pair(qkv[rows, cols(0)], qkv[rows, cols(1)], qkv[rows, cols(2)])
                att[rows, cols(0)] = out
                lse[at] = tops
                return 0

            lax.fori_loop(0, self.per_turn, pair, 0)

        @when(now == self.at_out)
        def _():
            loads[2].start()
            loads[2].wait()
            self.route(tok, cot, code, att, wo, ws, gains, after, mixed, gd, disp, info, leave)

    def route(self, tok, cot, code, att, wo, ws, gains, after, mixed, gd, disp, info, leave):
        width, length, experts = self.width, self.length, self.experts
        route, drop = columns_of(code)
        after[...] = tok[...].astype(f32) + matmul(att[...], wo[...].reshape(width, width))
        normed, _ = normalize(after[...])
        mixed[...] = (normed * gains[1:2]).astype(bf16)
        logits = matmul(mixed[...], ws[...].reshape(width, 128))
        lane = lax.broadcasted_iota(jnp.int32, (length, 128), 1)

        def softmax(first, last):
            inside = jnp.logical_and(lane >= first, lane < last)
            top = jnp.max(jnp.where(inside, logits, -jnp.inf), axis=1, keepdims=True)
            expd = jnp.where(inside, jnp.exp(jnp.where(inside, logits, top) - top), 0.0)
            return expd / jnp.sum(expd, axis=1, keepdims=True)

        probs, coef = softmax(2, 2 + experts), softmax(2 + experts, 4 + experts)
        info[...] = probs + coef
        chosen = jnp.where(lane - 2 == route, 1.0, 0.0)
        over_lanes = lambda a: jnp.sum(a, axis=1, keepdims=True)
        gate = over_lanes(probs * chosen) * (1 - drop[:, :1]).astype(f32)
        coef_0 = over_lanes(jnp.where(lane == 2 + experts, coef, 0.0))
        coef_1 = over_lanes(jnp.where(lane == 3 + experts, coef, 0.0))
        grad = cot[...].astype(f32)
        gd[...] = (coef_0 * grad).astype(bf16)
        square = lambda d: lax.broadcasted_iota(jnp.int32, (length, length), d)
        earlier = jnp.where(square(0) > square(1), 1.0, 0.0).astype(bf16)
        position = over_lanes(chosen * matmul(earlier, chosen.astype(bf16))).astype(jnp.int32)
        turn = route[:, :1] - lax.axis_index("expert")
        target = jnp.where(turn < 0, turn + experts, turn) * self.capacity + position
        slot = lax.broadcasted_iota(jnp.int32, (length, experts * self.capacity), 1)
        disp[...] = jnp.where(slot == target, 1.0, 0.0).astype(bf16)
        sent = (mixed[...], (coef_1 * gate * grad).astype(bf16))
        for h, values in enumerate(sent):
            placed = product_tn(disp[...], values).astype(bf16)
            for j in range(experts):
                leave[j][:, h * width : (h + 1) * width] = placed[j * self.capacity : (j + 1) * self.capacity]


def attend_pair_backward(q, k, v, g, lse):
    scaling = 1.0 / math.sqrt(HD)
    qs = q * scaling
    kt = k.T
    length = q.shape[0]
    grad_k = [0.0] * (length // QB)
    grad_v = [0.0] * (length // QB)
    grad_q = []
    for h, mask in enumerate(masks()):
        kh, vh, qh, gh = k * mask, v * mask, q * mask, g * mask
        row = []
        for c, start in enumerate(range(0, length, QB)):
            end = start + QB
            scores = causal(outer_nt(kh[:end], qs[start:end]), start)
            probs = jnp.exp(scores - lse[h : h + 1, start:end])
            grad_probs = outer_nt(vh[:end], g[start:end])
            delta = jnp.sum(probs * grad_probs, axis=0, keepdims=True)
            grad_scores = (probs * (grad_probs - delta)).astype(bf16)
            more_v = matmul(probs.astype(bf16), gh[start:end])
            more_k = matmul(grad_scores, qh[start:end])
            for b in range(c + 1):
                rows = slice(b * QB, (b + 1) * QB)
                grad_v[b] = grad_v[b] + more_v[rows]
                grad_k[b] = grad_k[b] + more_k[rows]
            row.append(matmul(kt[h * HD : (h + 1) * HD, :end], grad_scores))
        grad_q.append(jnp.concatenate(row, axis=1))
    return (
        (jnp.concatenate(grad_q, axis=0).T * scaling).astype(bf16),
        (jnp.concatenate(grad_k, axis=0) * scaling).astype(bf16),
        jnp.concatenate(grad_v, axis=0).astype(bf16),
    )


def thirds(values):
    parts = []
    for _ in range(3):
        parts.append(values.astype(bf16))
        values = values - parts[-1].astype(f32)
    return parts


class Back:
    def __init__(self, length, width, experts, devices, capacity):
        self.length, self.width, self.experts, self.capacity = length, width, experts, capacity
        self.devices, self.share = devices, width // devices
        self.pairs = width // PAIR
        self.columns = 3 * PAIR
        self.firsts = width // self.columns
        self.rest = width - self.firsts * self.columns
        self.items = self.firsts + self.pairs + 1
        self.heads_at = 4
        self.last = self.heads_at + self.pairs
        self.steps = self.last + 1
        self.first_item = self.heads_at
        self.outs = [
            jax.ShapeDtypeStruct((length, width), bf16),
            jax.ShapeDtypeStruct((length, width), f32),
        ]
        slots = experts * capacity
        self.scratch = [
            pltpu.VMEM((slots, 2 * width), bf16),
            pltpu.VMEM((length, width), f32),
            pltpu.VMEM((length, width), f32),
            pltpu.VMEM((devices, self.share, 128), bf16),
            pltpu.VMEM((devices, self.share, width), bf16),
            pltpu.VMEM((2, devices, self.share, self.columns), bf16),
            pltpu.VMEM((8, width), f32),
            pltpu.VMEM((128, width), f32),
            pltpu.VMEM((width, length), bf16),
            pltpu.VMEM((length, width), bf16),
            pltpu.SemaphoreType.DMA((5 + experts,)),
            pltpu.SemaphoreType.DMA((2, 3)),
        ]

    def made(self):
        chips = (4, 2, 2, self.experts // 2) if self.devices == 8 * self.experts else (self.devices,)
        return (self.items,) + chips + (self.share, self.columns)

    def final_outs(self):
        share, width = self.share, self.width
        return [jax.ShapeDtypeStruct((share, c), f32) for c in (3 * width, width, 128)]

    def store(self, outs, i, value):
        d_qkv, d_out, d_small = outs
        final = self.items - 1

        for f in range(self.firsts):

            @when(i == f)
            def _(f=f):
                d_out[:, f * self.columns : (f + 1) * self.columns] = value

        @when(jnp.logical_and(i >= self.firsts, i < final))
        def _():
            for p in range(3):
                at = pl.multiple_of(p * self.width + (i - self.firsts) * PAIR, PAIR)
                d_qkv[:, pl.ds(at, PAIR)] = value[:, p * PAIR : (p + 1) * PAIR]

        @when(i == final)
        def _():
            d_out[:, self.firsts * self.columns :] = value[:, : self.rest]
            d_small[...] = value[:, self.rest : self.rest + 128]

    def __call__(self, now, steps, *refs):
        experts, width, length = self.experts, self.width, self.length
        refs = list(refs)
        tok, cot, code, qkv, lse, att, mixed_in, disp, info = refs[:9]
        small_hbm, qkv_hbm, out_hbm, dense_hbm, grad_hbm, after_hbm = refs[9:15]
        came_hbm = refs[15 : 15 + experts]
        mixed, tokens_grad, *rest = refs[15 + experts :]
        if self.moves:
            made = self.moves[-1].own
        else:
            made = rest.pop(0)
        came, dense, grads, ws, wo, wq, gains, d_heads, attn_in_t, grad_att, sems, wq_sems = rest
        fetch = lambda a, b, i: pltpu.make_async_copy(a, b, sems.at[i])
        capacity = self.capacity
        loads = [fetch(came_hbm[j], came.at[pl.ds(j * capacity, capacity)], j) for j in range(experts)]
        loads += [
            fetch(a, b, experts + i)
            for i, (a, b) in enumerate(
                ((dense_hbm, dense), (grad_hbm, grads), (after_hbm, tokens_grad), (small_hbm, ws), (out_hbm, wo))
            )
        ]

        def pair_weights(pair):
            slot = lax.rem(pair, 2)
            return [
                pltpu.make_async_copy(
                    qkv_hbm.at[:, :, pl.ds(pl.multiple_of(p * width + pair * PAIR, PAIR), PAIR)],
                    wq.at[slot, :, :, pl.ds(p * PAIR, PAIR)],
                    wq_sems.at[slot, p],
                )
                for p in range(3)
            ]

        put = lambda i, columns, values: self.put(made, i, columns, values)
        lane = lax.broadcasted_iota(jnp.int32, (length, 128), 1)
        over_lanes = lambda a: jnp.sum(a, axis=1, keepdims=True)

        @when(now == 0)
        def _():
            for copy in loads + pair_weights(0):
                copy.start()

        @when(now == 1)
        def _():
            for copy in loads:
                copy.wait()
            probs = jnp.where(jnp.logical_and(lane >= 2, lane < 2 + experts), info[...], 0.0)
            coef_0 = over_lanes(jnp.where(lane == 2 + experts, info[...], 0.0))
            coef_1 = over_lanes(jnp.where(lane == 3 + experts, info[...], 0.0))
            route, drop = columns_of(code)
            chosen = jnp.where(lane - 2 == route, 1.0, 0.0)
            kept = (1 - drop[:, :1]).astype(f32)
            gate_prob = over_lanes(probs * chosen)
            gate = gate_prob * kept
            grad = cot[...].astype(f32)
            expert_tok = matmul(disp[...], came[:, :width])
            mixed[...] = (tokens_grad[...] + coef_0 * dense[...] + (coef_1 * gate) * expert_tok).astype(bf16)
            shared = over_lanes(grad * expert_tok)
            grad_0, grad_1 = over_lanes(grad * dense[...]), shared * gate
            both = coef_0 * grad_0 + coef_1 * grad_1
            grad_gate = shared * coef_1 * kept
            logits = jnp.where(
                jnp.logical_and(lane >= 2, lane < 2 + experts), (grad_gate * gate_prob) * (chosen - probs), 0.0
            )
            logits = jnp.where(lane == 2 + experts, coef_0 * (grad_0 - both), logits)
            logits = jnp.where(lane == 3 + experts, coef_1 * (grad_1 - both), logits)
            pieces = thirds(logits)
            d_heads[...] = add(*(product_tn(p, mixed_in[...]) for p in pieces))
            weights = ws[...].reshape(width, 128)
            grads[...] = (
                grads[...] + matmul(disp[...], came[:, width:]) + add(*(outer_nt(p, weights) for p in pieces))
            )
            gains[...] = weights.astype(f32).T[:8]

        @when(now == 2)
        def _():
            normed, scale = normalize(tokens_grad[...])
            d_heads[1:2] = jnp.sum(grads[...] * normed, axis=0, keepdims=True)
            grads[...] = cot[...].astype(f32) + norm_back(grads[...] * gains[1:2], normed, scale)
            normed, _ = normalize(tok[...].astype(f32))
            attn_in_t[...] = (normed * gains[0:1]).astype(bf16).T

        @when(now == 3)
        def _():
            grad_attn = grads[...].astype(bf16)
            grad_att[...] = outer_nt(grad_attn, wo[...].reshape(width, width)).astype(bf16)
            d_out = product_tn(att[...], grad_attn).astype(bf16)
            for f in range(self.firsts):
                put(f, slice(None), d_out[:, f * self.columns : (f + 1) * self.columns])
            put(self.items - 1, slice(0, self.rest), d_out[:, self.firsts * self.columns :])
            dense[...] = jnp.zeros_like(dense)

        @when(jnp.logical_and(now >= self.heads_at, now < self.last))
        def _():
            pair = now - self.heads_at
            cols = lambda part: pl.ds(pl.multiple_of(part * width + pair * PAIR, PAIR), PAIR)
            d_pair = attend_pair_backward(
                qkv[:, cols(0)], qkv[:, cols(1)], qkv[:, cols(2)], grad_att[:, cols(0)], lse[pair]
            )
            d_pair = jnp.concatenate(d_pair, axis=1)
            for copy in pair_weights(pair):
                copy.wait()

            @when(pair + 1 < self.pairs)
            def _():
                for copy in pair_weights(pair + 1):
                    copy.start()

            put(pair + self.firsts, slice(None), matmul(attn_in_t[...], d_pair).astype(bf16))
            dense[...] += outer_nt(d_pair, wq[lax.rem(pair, 2)].reshape(width, self.columns))

        @when(now == self.last)
        def _():
            normed, scale = normalize(tok[...].astype(f32))
            d_heads[0:1] = jnp.sum(dense[...] * normed, axis=0, keepdims=True)
            put(self.items - 1, slice(self.rest, self.rest + 128), d_heads[...].T.astype(bf16))
            if self.rest + 128 < self.columns:
                spare = self.columns - self.rest - 128
                put(self.items - 1, slice(self.rest + 128, None), jnp.zeros((width, spare), bf16))
            tokens_grad[...] = grads[...] + norm_back(dense[...] * gains[0:1], normed, scale)

    def put(self, made, i, columns, values):
        lead = made.shape[1:-1]
        at = (i,) + (slice(None),) * len(lead) + (columns,)
        made[at] = values.reshape(lead + values.shape[1:])


def gelu_both(v):
    c = math.sqrt(2.0 / math.pi)
    square = v * v
    t = jnp.tanh(c * (v + 0.044715 * (square * v)))
    half = 0.5 * (1.0 + t)
    slope = half + 0.5 * v * (1.0 - t * t) * (c * (1.0 + (3 * 0.044715) * square))
    return v * half, slope


def mlp_block(x, g, xt, gt, w1, w2, out_sum, back_sum):
    hidden, slope = gelu_both(matmul(x[...], w1))
    hidden = hidden.astype(bf16)
    grad_pre = (slope * outer_nt(g[...], w2)).astype(bf16)
    out_sum[...] += matmul(hidden, w2)
    back_sum[...] += outer_nt(grad_pre, w1)
    return matmul(xt[...], grad_pre).astype(bf16), matmul(gt[...], hidden).astype(bf16)


def mlp_kernel(share, now, steps, x, g, w1, w2, out_sum, back_sum, d1_ref, d2_ref, xt, gt):
    @when(now == 0)
    def _():
        xt[...] = x[...].T
        gt[...] = g[...].T
        out_sum[...] = jnp.zeros_like(out_sum)
        back_sum[...] = jnp.zeros_like(back_sum)

    d1, d2 = mlp_block(x, g, xt, gt, w1[...], w2[...], out_sum, back_sum)
    if share is None:
        d1_ref[...] = d1
        d2_ref[...] = d2
    else:
        for c in range(d1.shape[1] // 128):
            cols = slice(c * 128, (c + 1) * 128)
            for s in range(d1_ref.shape[0]):
                d1_ref[s, c * share : (c + 1) * share] = d1[s * share : (s + 1) * share, cols]
            d2_ref[c] = d2[:, cols]


def mlp(x, g, w1, w2, name, moves, collective_id, experts, devices=None):
    share = None
    size = BLOCK
    rows, width = x.shape
    blocks = w1.shape[1] // size
    w1_spec = pl.BlockSpec((width, size), lambda j: (0, j))
    w2_spec = pl.BlockSpec((size, width), lambda j: (j, 0))
    d_shape, d_specs = (width, blocks * size), [w1_spec] * 2
    if devices:
        share = width // devices
        d_shape = (devices, width, 128)
        d_specs = [
            pl.BlockSpec((devices, size // 128 * share, 128), lambda j: (0, j, 0)),
            pl.BlockSpec((size // 128, width, 128), lambda j: (j, 0, 0)),
        ]
    whole = pl.BlockSpec(memory_space=pltpu.VMEM)
    return call(
        name,
        blocks,
        functools.partial(mlp_kernel, share),
        [x, g, w1, w2],
        [whole] * 2 + [w1_spec, w2_spec],
        [jax.ShapeDtypeStruct((rows, width), f32)] * 2 + [jax.ShapeDtypeStruct(d_shape, bf16)] * 2,
        [whole] * 2 + d_specs,
        [pltpu.VMEM((width, rows), bf16)] * 2,
        moves,
        collective_id,
        experts,
        12 * rows * width * blocks * size,
    )


class Experts:
    PER_STEP = 1

    def __init__(self, pieces, blocks, width, size, chunks, back):
        self.parts, self.piece = len(pieces), pieces[0].shape
        self.blocks, self.width, self.size, self.back = blocks, width, size, back
        rows = self.parts * self.piece[0]
        if chunks:
            self.block = (2, size // 256, chunks, width // chunks, 128)
            whole = (blocks // 2, 2) + self.block
        else:
            self.block = (width, size)
            whole = (blocks,) + self.block
        piece = jax.ShapeDtypeStruct(self.piece, bf16)
        self.outs = [piece] * self.parts + [jax.ShapeDtypeStruct(whole, bf16)] * 2
        self.scratch = (
            [pltpu.VMEM(self.piece, bf16)] * self.parts
            + [pltpu.VMEM((rows, width), bf16)] * 2
            + [pltpu.VMEM((width, rows), bf16)] * 2
            + [pltpu.VMEM((rows, width), f32)] * 2
            + [pltpu.VMEM((2,) + self.block, bf16)] * 2
            + [pltpu.SemaphoreType.DMA((2, 2)), pltpu.SemaphoreType.DMA((self.parts,))]
        )

    def __call__(self, now, steps, *refs):
        refs = list(refs)
        take = lambda count: [refs.pop(0) for _ in range(count)]
        pieces, (w1, w2) = take(self.parts), take(2)
        kept, targets, results = take(self.parts), take(2), take(self.parts)
        x, g, xt, gt, out_sum, back_sum, stage_1, stage_2, sems, kept_sems = refs
        width, size = self.width, self.piece[0]

        def flush(step):
            at = lax.rem(step, 2)
            where = (step // 2, at) if len(self.block) > 2 else (step,)
            return [
                pltpu.make_async_copy(stage.at[at], target.at[where], sems.at[at, i])
                for i, (stage, target) in enumerate(zip((stage_1, stage_2), targets))
            ]

        @when(now == 0)
        def _():
            for j, piece in enumerate(pieces):
                x[j * size : (j + 1) * size] = piece[:, :width]
                g[j * size : (j + 1) * size] = piece[:, width:]
            xt[...] = x[...].T
            gt[...] = g[...].T
            out_sum[...] = jnp.zeros_like(out_sum)
            back_sum[...] = jnp.zeros_like(back_sum)

        def block(b, _):
            step = now * self.PER_STEP + b

            @when(step >= 2)
            def _():
                for copy in flush(step - 2):
                    copy.wait()

            slot = lax.rem(step, 2)
            for stage, d in zip((stage_1, stage_2), mlp_block(x, g, xt, gt, w1[b], w2[b], out_sum, back_sum)):
                if len(self.block) == 2:
                    stage[slot] = d
                else:
                    for c in range(d.shape[1] // 128):
                        share = d[:, c * 128 : (c + 1) * 128].reshape(self.block[2:])
                        stage[slot, c // self.block[1], c % self.block[1]] = share
            for copy in flush(step):
                copy.start()
            return 0

        lax.fori_loop(0, self.PER_STEP, block, 0)

        @when(now == steps - 1)
        def _():
            for h, total in enumerate((out_sum, back_sum)):
                for j, result in enumerate(results):
                    result[:, h * width : (h + 1) * width] = total[j * size : (j + 1) * size].astype(bf16)
            keep = [pltpu.make_async_copy(a, b, kept_sems.at[j]) for j, (a, b) in enumerate(zip(results, kept))]
            for copy in keep:
                copy.start()
            for copy in keep:
                copy.wait()
            if self.back:
                self.back.send()
            for step in (self.blocks - 2, self.blocks - 1):
                for copy in flush(step):
                    copy.wait()


def move(name, moves, collective_id, experts):
    return call(name, 1, None, [], [], [], [], [], moves, collective_id, experts, 0)


def shards(
    fast,
    tokens,
    gain_attn,
    w_qkv,
    w_out,
    gain_mix,
    w_fc,
    w_proj,
    w_router,
    w_coef,
    expert_in,
    expert_out,
    routes,
    dropped,
    cotangent,
):
    experts = lax.axis_size("expert")
    nodes = lax.axis_size("node")
    devices = nodes * experts
    width = tokens.shape[1]
    tok_rows = tokens.shape[0]
    ff = w_fc.shape[1]
    share = w_qkv.shape[0]
    small = jnp.concatenate([gain_attn[:, None], gain_mix[:, None], w_router, w_coef], axis=1)
    small = jnp.pad(small, ((0, 0), (0, 128 - small.shape[1])))
    win, wout = expert_in[0], expert_out[0]
    together = lambda a: a.reshape((devices * a.shape[1],) + a.shape[2:])
    cut = lambda a, rows, columns, m, n: [
        [(a, i * (rows // m), rows // m, j * (columns // n), columns // n)] for i in range(m) for j in range(n)
    ]
    weights = (small, w_qkv, w_out, w_fc, w_proj)
    capacity = -(-(tok_rows * 10) // (8 * experts))
    gather_dense, gather_experts = [], []
    if fast:
        items = cut(1, share, 3 * width, 1, 3) + cut(2, share, width, 1, 1)
        items += cut(3, share, ff, 1, 4) + cut(4, ff // devices, width, 4, 1)
        items[0] = cut(0, share, 128, 1, 1)[0] + items[0]
        gather_dense = [Gather(list(weights), [True] * 5, items, nodes, experts)]
        items = cut(0, width, win.shape[1], 4, 1) + cut(1, wout.shape[0], width, 4, 1)
        gather_experts = [Gather([win, wout], [False] * 2, items, nodes, experts)]
        full = []
    else:
        full = [lax.all_gather(a, AXES, axis=0, tiled=False) for a in weights]
        win_full, wout_full = (lax.all_gather(a, "node", axis=0, tiled=False) for a in (win, wout))

    def scatter_xla(parts, axes):
        return lax.psum_scatter(parts, axes, scatter_dimension=0, tiled=False).astype(f32)

    def exchange(parts, sign):
        moved = [parts[0]]
        for j in range(1, experts):
            shift = [(s, (s + sign * j) % experts) for s in range(experts)]
            moved.append(lax.ppermute(parts[j], "expert", shift))
        return moved

    front = Front(tok_rows, width, experts, devices, capacity, gather_dense[0] if fast else None)
    kept = full[:3]
    whole, hbm = pl.BlockSpec(memory_space=pltpu.VMEM), pl.BlockSpec(memory_space=pltpu.HBM)
    code = jnp.stack([routes[:, 0], dropped]).astype(f32)
    results = call(
        "front",
        front.steps,
        front,
        [tokens, cotangent, code] + kept,
        [whole] * 3 + [hbm] * len(kept),
        front.outs,
        [whole] * len(front.outs),
        front.scratch,
        gather_dense,
        1,
        experts,
        12 * tok_rows * width * width,
    )
    qkv_rows, lse, attended, after_attn, mixed_in, grad_dense, dispatch, probs = results[:8]
    leaving = results[8 : 8 + experts]
    small_full, qkv_full, out_full, fc_full, proj_full = results[8 + experts :] if fast else full

    if fast:
        out_to = Exchange(leaving[1:], 1, experts, 0, gather_experts[0].turns, leaving[0].shape)
        gather_experts = [out_to] + gather_experts
    dense_out, grad_mixed, d_fc, d_proj, *moved = mlp(
        mixed_in,
        grad_dense,
        together(fc_full),
        together(proj_full),
        "dense_mlp",
        gather_experts,
        2,
        experts,
        devices if fast else None,
    )
    scatters, return_to, given = [], None, None
    chunks = 4
    step = width // chunks
    half = (experts // 2, step, 128)
    win_out = [jax.ShapeDtypeStruct(expert_in.shape, f32)]
    wout_out = [jax.ShapeDtypeStruct(expert_out.shape[:2] + (width // 2,), f32)]

    def store_wout(out, chunk, sums):
        at = pl.ds(pl.multiple_of(chunk * step, step), step)
        for h, total in enumerate(sums):
            for c in range(half[0]):
                out[0, (h * half[0] + c) * 128 : (h * half[0] + c + 1) * 128, at] = total[c].T

    if fast:
        arrived = leaving[:1] + moved[: experts - 1]
        win_full, wout_full = moved[experts - 1 :]
        by_chip = lambda a: a.reshape(4, 2, 2, experts // 2, chunks, step, 128)

        def store(outs, i, value):
            @when(i < chunks)
            def _():
                for q in range(step // share):
                    at = pl.multiple_of(i * (step // share * 128) + q * 128, 128)
                    outs[0][:, pl.ds(at, 128)] = value[q * share : (q + 1) * share]

            @when(i >= chunks)
            def _():
                outs[1][:, pl.ds(pl.multiple_of((i - chunks) * step, step), step)] = value.T

        def store_experts(outs, i, sums):
            first = 2 * chunks

            @when(i < first + chunks)
            def _():
                at = pl.ds(pl.multiple_of((i - first) * step, step), step)
                for h, total in enumerate(sums):
                    for c in range(half[0]):
                        outs[2][0, at, (h * half[0] + c) * 128 : (h * half[0] + c + 1) * 128] = total[c]

            @when(i >= first + chunks)
            def _():
                store_wout(outs[3], i - first - chunks, sums)

        def store_any(outs, i, value):
            (store_experts if isinstance(value, tuple) else store)(outs, i, value)

        outs = [jax.ShapeDtypeStruct((share, ff), f32), jax.ShapeDtypeStruct((ff // devices, width), f32)]
        parts = [(by_chip(d_fc), True, 0, chunks), (by_chip(d_proj), True, 0, chunks)]
        parts += [(None, False, 0, chunks), (None, False, 0, chunks // 2)]
        summing = Scatter(parts, half, experts, outs + win_out + wout_out, store_any, z_late=10)
        return_to = Exchange([], -1, experts, None, summing.turns, leaving[0].shape)
        scatters = [return_to, summing]
    else:
        arrived = exchange(leaving, 1)
    blocks, size = win_full.shape[0], win_full.shape[2]
    experts_kernel = Experts(arrived, blocks, width, size, chunks if fast else None, return_to)
    if fast:

        def given(ins, os, own):
            summing.given = os[experts : experts + 2]
            return_to.sources = os[1:experts]

    per = experts_kernel.PER_STEP
    results = call(
        "expert_mlp",
        blocks // per,
        experts_kernel,
        arrived + [win_full, wout_full],
        [whole] * experts
        + [pl.BlockSpec((per, width, size), lambda j: (j, 0, 0)), pl.BlockSpec((per, size, width), lambda j: (j, 0, 0))],
        experts_kernel.outs,
        [hbm] * len(experts_kernel.outs),
        experts_kernel.scratch,
        scatters,
        3,
        experts,
        12 * experts * capacity * width * blocks * size,
        given,
    )
    returned, (d_win, d_wout) = results[:experts], results[experts : experts + 2]
    if fast:
        results = results[experts + 2 :]
        came_back = returned[:1] + results[: experts - 1]
        grad_fc, grad_proj, grad_win, grad_wout = results[experts - 1 :]
    else:
        came_back = exchange(returned, -1)
    back = Back(tok_rows, width, experts, devices, capacity)
    back.moves = []
    if fast:
        parts = [(d_wout, False, chunks // 2, chunks // 2)]
        scatter_wout = Scatter(
            parts, half, experts, wout_out, lambda outs, i, sums: store_wout(outs[0], i, sums)
        )
        parts = [(None, True, 0, back.items)]
        made = back.made()
        scatter_rest = Scatter(
            parts, made[4:], experts, back.final_outs(), back.store, back.first_item, made
        )
        back.moves = [scatter_wout, scatter_rest]
    outs = back.outs + ([] if fast else [jax.ShapeDtypeStruct((back.items, width, back.columns), bf16)])
    mixed, tokens_grad, *results = call(
        "back",
        back.steps,
        back,
        [tokens, cotangent, code, qkv_rows, lse, attended, mixed_in, dispatch, probs]
        + [small_full, qkv_full, out_full, dense_out, grad_mixed, after_attn]
        + came_back,
        [whole] * 9 + [hbm] * (6 + experts),
        outs,
        [whole] * len(outs),
        back.scratch,
        back.moves,
        5,
        experts,
        32 * tok_rows * width * width,
    )
    if fast:
        more_wout, grad_wqkv, grad_wo, grad_small = results
        grad_wout = jnp.concatenate([grad_wout, more_wout], axis=2)
    else:
        summed = scatter_xla(results[0].reshape(back.items, devices, share, -1).swapaxes(0, 1), AXES)
        last = summed[-1]
        grad_wo = jnp.concatenate([*summed[: back.firsts], last[:, : back.rest]], axis=1)
        grad_small = last[:, back.rest : back.rest + 128]
        pairs = summed[back.firsts : -1].reshape(back.pairs, share, 3, PAIR)
        grad_wqkv = pairs.transpose(1, 2, 0, 3).reshape(share, 3 * width)
        grad_fc = scatter_xla(d_fc.reshape(devices, share, ff), AXES)
        by_unit = d_proj.reshape(width, devices, ff // devices).transpose(1, 0, 2)
        grad_proj = scatter_xla(by_unit, AXES).T
        grad_win = scatter_xla(d_win, "node")[None]
        grad_wout = scatter_xla(d_wout, "node").T[None]
    return (
        mixed,
        tokens_grad,
        grad_small[:, 0],
        grad_wqkv,
        grad_wo,
        grad_small[:, 1],
        grad_fc,
        grad_proj,
        grad_small[:, 2 : 2 + experts],
        grad_small[:, 2 + experts : 4 + experts],
        grad_win,
        grad_wout,
    )


def solution(mesh):
    rows = P(AXES, None)
    in_specs = (
        rows,
        P(AXES),
        rows,
        rows,
        P(AXES),
        rows,
        rows,
        rows,
        rows,
        P("expert", None, "node"),
        P("expert", "node", None),
        rows,
        P(AXES),
        rows,
    )
    out_specs = (
        rows,
        rows,
        P(AXES),
        rows,
        rows,
        P(AXES),
        rows,
        rows,
        rows,
        rows,
        P("expert", None, "node"),
        P("expert", "node", None),
    )
    fast = mesh.shape["node"] == 8 and mesh.shape["expert"] == 4
    return jax.shard_map(
        functools.partial(shards, fast), mesh=mesh, in_specs=in_specs, out_specs=out_specs, check_vma=False
    )
```

```python
import functools
import math

import jax
import jax.numpy as jnp
from jax import lax
from jax.experimental import pallas as pl
from jax.experimental.pallas import tpu as pltpu
from jax.sharding import PartitionSpec as P

HD = 64
PAIR = 2 * HD
SEQ = 512
QB = 256
BLOCK = 512
MIB = 1 << 20
AXES = ("node", "expert")
MESH = pl.DeviceIdType.MESH
epsilon = 1e-05
f32 = jnp.float32
bf16 = jnp.bfloat16


def normalize(values):
    centered = values - jnp.mean(values, axis=-1, keepdims=True)
    inv_scale = lax.rsqrt(jnp.mean(centered * centered, axis=-1, keepdims=True) + epsilon)
    return (centered * inv_scale, inv_scale)


def norm_back(grad_norm, normed, inv_scale):
    mean_grad = jnp.mean(grad_norm, axis=-1, keepdims=True)
    mean_cross = jnp.mean(grad_norm * normed, axis=-1, keepdims=True)
    return inv_scale * (grad_norm - mean_grad - normed * mean_cross)


def contract(left_op, right_op, left_dim, right_dim):
    return lax.dot_general(
        left_op, right_op, (((left_dim,), (right_dim,)), ((), ())), preferred_element_type=f32
    )


def matmul(left_op, right_op):
    return contract(left_op, right_op, 1, 0)


def product_tn(left_op, right_op):
    return contract(left_op, right_op, 0, 0)


def outer_nt(left_op, right_op):
    return contract(left_op, right_op, 1, 1)


class Place:
    def __init__(self, experts):
        self.experts = experts
        self.n, self.e = lax.axis_index("node"), lax.axis_index("expert")
        n = self.n
        self.k, self.x, self.y = lax.rem(n, 2), lax.rem(n // 2, 2), n // 4
        k, x, y = self.k, self.x, self.y
        self.nx, self.ny = y * 4 + (1 - x) * 2 + k, (1 - y) * 4 + x * 2 + k
        self.nd, self.nc = (1 - y) * 4 + (1 - x) * 2 + k, y * 4 + x * 2 + 1 - k

    def z(self, j):
        return (self.n, lax.rem(self.e + j, self.experts))

    def greet(self, along_z):
        barrier = pltpu.get_barrier_semaphore()
        peers = [(self.nx, self.e), (self.ny, self.e), (self.nc, self.e)]
        if along_z:
            peers += [self.z(j) for j in range(1, self.experts)]
        for peer in peers:
            pl.semaphore_signal(barrier, inc=1, device_id=peer, device_id_type=MESH)
        pl.semaphore_wait(barrier, len(peers))


def when(condition):
    return pl.when(condition)


class Gather:
    def __init__(self, args, dense, items, nodes, experts):
        self.args, self.dense, self.items, self.experts = args, dense, items, experts
        self.outs = [
            jax.ShapeDtypeStruct(((nodes * experts if d else nodes),) + a.shape, a.dtype)
            for a, d in zip(args, dense)
        ]
        hbm = pl.BlockSpec(memory_space=pltpu.HBM)
        self.in_specs, self.out_specs = [hbm] * len(args), [hbm] * len(args)
        m = sum(len(item) for item in items)
        self.scratch = [
            pltpu.SemaphoreType.DMA((m, experts + 7)),
            pltpu.SemaphoreType.DMA((m, experts + 7)),
            pltpu.SemaphoreType.DMA((m,)),
        ]
        self.along_z = any(dense)
        self.steps = [self.along, self.across, self.corner, self.over, self.end]
        self.turns = len(items) + len(self.steps) - 1

    def bind(self, ins, outs, scratch, place):
        experts = self.experts
        send, recv, loc = scratch
        p, e = place, place.e

        def remote(source, target, item, kind, device):
            return pltpu.make_async_remote_copy(
                src_ref=source,
                dst_ref=target,
                send_sem=send.at[item, kind],
                recv_sem=recv.at[item, kind],
                device_id=device,
                device_id_type=MESH,
            )

        self.full = outs
        self.bound = [[] for _ in self.items]
        pieces = [(turn, piece) for turn, item in enumerate(self.items) for piece in item]
        for i, (turn, (arg, row, rows, col, columns)) in enumerate(pieces):
            dense = self.dense[arg]
            shard, whole = ins[arg], outs[arg]
            per = experts if dense else 1
            own = p.n * per + (e if dense else 0)

            def view(ref, lead, start=0, size=None, whole_rows=rows, row=row, col=col, columns=columns):
                return ref.at[lead, pl.ds(row + start, size or whole_rows), pl.ds(col, columns)]

            def bundle(m, view=view, whole=whole, per=per):
                return view(whole, pl.ds(m * per, per))

            def half(m, h, view=view, whole=whole, per=per, dense=dense, rows=rows):
                if dense:
                    return view(whole, pl.ds(m * per + h * (per // 2), per // 2))
                return view(whole, m, h * (rows // 2), rows // 2)

            mine = shard.at[pl.ds(row, rows), pl.ds(col, columns)]
            land = view(whole, own)
            local = pltpu.make_async_copy(mine, land, loc.at[i])
            z = []
            if dense:
                z = [remote(mine, land, i, j - 1, p.z(j)) for j in range(1, experts)]
            first, last = (bundle(p.n), bundle(p.n)) if dense else (mine, land)
            b = experts - 1
            xy = [remote(first, last, i, b, (p.nx, e)), remote(first, last, i, b + 1, (p.ny, e))]
            diag = [
                remote(half(p.nx, 0), half(p.nx, 0), i, b + 2, (p.ny, e)),
                remote(half(p.ny, 1), half(p.ny, 1), i, b + 3, (p.nx, e)),
            ]
            core = [remote(first, last, i, b + 4, (p.nc, e))] + [
                remote(bundle(m), bundle(m), i, b + 5 + j, (p.nc, e)) for j, m in enumerate((p.nx, p.ny, p.nd))
            ]
            self.bound[turn].append((local, z, xy, diag, core))

    def turn(self, now):
        for t in range(self.turns):

            @when(now == t)
            def _(t=t):
                for late, step in enumerate(self.steps):
                    if 0 <= t - late < len(self.items):
                        for piece in self.bound[t - late]:
                            step(*piece)

    def finish(self, now):
        pass

    def along(self, local, z, xy, diag, core):
        local.start()
        for copy in z:
            copy.start()

    def across(self, local, z, xy, diag, core):
        for copy in z:
            copy.wait()
        local.wait()
        xy[0].start()
        xy[1].start()
        core[0].start()

    def corner(self, local, z, xy, diag, core):
        for i in range(2):
            xy[i].wait()
            diag[i].start()
            core[1 + i].start()

    def over(self, local, z, xy, diag, core):
        diag[0].wait()
        diag[1].wait()
        core[3].start()

    def end(self, local, z, xy, diag, core):
        for copy in core:
            copy.wait()


class Exchange:
    along_z = True

    def __init__(self, pieces, sign, experts, start, turns, shape):
        self.args, self.sign, self.experts, self.start, self.turns = list(pieces), sign, experts, start, turns
        self.given = None
        self.outs = [jax.ShapeDtypeStruct(shape, bf16)] * (experts - 1)
        hbm = pl.BlockSpec(memory_space=pltpu.HBM)
        self.in_specs, self.out_specs = [hbm] * len(self.args), [hbm] * (experts - 1)
        self.scratch = [pltpu.SemaphoreType.DMA((experts,)), pltpu.SemaphoreType.DMA((experts,))]

    def bind(self, ins, outs, scratch, place):
        self.out, self.sems, self.place = outs, scratch, place
        if ins:
            self.sources = ins

    def copies(self):
        return [
            pltpu.make_async_remote_copy(
                src_ref=source,
                dst_ref=self.out[j],
                send_sem=self.sems[0].at[j],
                recv_sem=self.sems[1].at[j],
                device_id=self.place.z((self.sign * (j + 1)) % self.experts),
                device_id_type=MESH,
            )
            for j, source in enumerate(self.sources)
        ]

    def send(self):
        for copy in self.copies():
            copy.start()

    def turn(self, now):
        if self.start is not None:

            @when(now == self.start)
            def _():
                self.send()

    def finish(self, now):
        @when(now == self.turns - 1)
        def _():
            for copy in self.copies():
                copy.wait()


class Scatter:
    RING = 6
    CORE_RING = 4

    def __init__(self, parts, half, experts, outs, store, start=0, made=None, z_late=4):
        self.experts, self.outs, self.store, self.start, self.made = experts, outs, store, start, made
        self.parts = parts
        self.given = []
        self.args = [p[0] for p in parts if p[0] is not None]
        h = half
        self.starts = [sum(p[3] for p in parts[:a]) for a in range(len(parts) + 1)]
        m = self.m = self.starts[-1]
        self.m_z = sum(p[3] for p in parts if p[1])
        unit = h[1:]
        ring = self.ring = min(self.RING, m)
        self.core_ring = min(self.CORE_RING, m)
        self.in_specs = [pl.BlockSpec(memory_space=pltpu.HBM)] * len(self.args)
        self.out_specs = [pl.BlockSpec(memory_space=pltpu.VMEM)] * len(outs)
        kinds = 7 + experts
        self.scratch = [
            pltpu.VMEM(made or (ring, 4, 2) + h, bf16),
            pltpu.VMEM((self.core_ring, 4, 2) + h, bf16),
            pltpu.VMEM((ring, 2) + h, bf16),
            pltpu.VMEM((ring, 2) + h, bf16),
            pltpu.VMEM((ring,) + h, bf16),
            pltpu.VMEM((ring,) + h, bf16),
            pltpu.SemaphoreType.DMA((m, kinds)),
            pltpu.SemaphoreType.DMA((m, kinds)),
            pltpu.SemaphoreType.DMA((m,)),
        ]
        if self.m_z:
            self.scratch.append(pltpu.VMEM((self.m_z, experts - 1) + unit, bf16))
            self.scratch.append(pltpu.VMEM((self.m_z, experts) + unit, bf16))
        self.z_late = z_late
        self.turns = start + max(m + 3, self.m_z + z_late)
        self.along_z = self.m_z > 0

    def bind(self, ins, outs, scratch, place):
        ins = list(ins)
        given = list(self.given)
        self.sources = [given.pop(0) if p[0] is None else ins.pop(0) for p in self.parts] if not self.made else []
        self.out, self.place = outs, place
        self.own, self.rc, self.rx, self.ry, self.lx, self.ly, self.sent, self.recv, self.loc = scratch[:9]
        self.rz, self.zs = scratch[9:] if self.m_z else (None, None)

    def slot(self, i):
        return lax.rem(i, self.ring)

    def remote(self, source, target, item, kind, device):
        return pltpu.make_async_remote_copy(
            src_ref=source,
            dst_ref=target,
            send_sem=self.sent.at[item, kind],
            recv_sem=self.recv.at[item, kind],
            device_id=device,
            device_id_type=MESH,
        )

    def at(self, i, site, *more):
        return (i, site, self.place.k) + more if self.made else (self.slot(i), site) + more

    def first(self, source, i, chunk):
        p = self.place
        land = self.rc.at[lax.rem(i, self.core_ring)]
        if self.made:
            return [self.remote(self.own.at[i, :, 1 - p.k], land, i, 0, (p.nc, p.e))]
        part = lambda core: source.at[:, core, :, :, chunk]
        local = pltpu.make_async_copy(part(p.k), self.own.at[self.slot(i)], self.loc.at[i])
        return [self.remote(part(1 - p.k), land, i, 0, (p.nc, p.e)), local]

    def sites(self):
        p = self.place
        return p.y * 2 + p.x, p.y * 2 + 1 - p.x, (1 - p.y) * 2 + p.x, (1 - p.y) * 2 + 1 - p.x

    def round_one(self, i):
        p = self.place
        b = self.slot(i)
        _, to_x, to_y, diag = self.sites()
        own = lambda *at: self.own.at[self.at(i, *at)]
        return [
            self.remote(own(diag, 0), self.rx.at[b, 0], i, 1, (p.nx, p.e)),
            self.remote(own(diag, 1), self.ry.at[b, 0], i, 2, (p.ny, p.e)),
            self.remote(own(to_x, 0), self.rx.at[b, 1], i, 3, (p.nx, p.e)),
            self.remote(own(to_y, 1), self.ry.at[b, 1], i, 4, (p.ny, p.e)),
        ]

    def round_two(self, i):
        p = self.place
        b = self.slot(i)
        _, to_x, to_y, _ = self.sites()
        return [
            self.remote(self.own.at[self.at(i, to_x, 1)], self.lx.at[b], i, 5, (p.nx, p.e)),
            self.remote(self.own.at[self.at(i, to_y, 0)], self.ly.at[b], i, 6, (p.ny, p.e)),
        ]

    def round_z(self, i):
        p = self.place
        return [
            self.remote(self.zs.at[i, lax.rem(p.e + j, self.experts)], self.rz.at[i, j - 1], i, 6 + j, p.z(j))
            for j in range(1, self.experts)
        ]

    def turn(self, now):
        limits = (self.m, self.m, self.m, self.m, self.m_z)
        steps = (self.load, self.chip, self.cross, self.plane, self.column)
        for limit, late, step in zip(limits, (0, 1, 2, 3, self.z_late), steps):
            i = now - self.start - late
            if limit:

                @when(jnp.logical_and(i >= 0, i < limit))
                def _(step=step, i=i):
                    step(i)

    def finish(self, now):
        pass

    def load(self, i):
        if self.made:
            self.first(None, i, 0)[0].start()
            return
        for a, source in enumerate(self.sources):

            @when(jnp.logical_and(i >= self.starts[a], i < self.starts[a + 1]))
            def _(a=a, source=source):
                for copy in self.first(source, i, i - self.starts[a] + self.parts[a][2]):
                    copy.start()

    def chip(self, i):
        for copy in self.first(None if self.made else self.sources[0], i, 0):
            copy.wait()

        def sum_one(q, _):
            at = self.at(i, q)
            self.own[at] = add(self.own[at], self.rc[lax.rem(i, self.core_ring), q]).astype(bf16)
            return 0

        lax.fori_loop(0, 4, sum_one, 0)
        for copy in self.round_one(i):
            copy.start()

    def cross(self, i):
        one = self.round_one(i)
        two = self.round_two(i)
        b = self.slot(i)
        _, to_x, to_y, _ = self.sites()
        for copy in one:
            copy.wait()
        at_x, at_y = self.at(i, to_x, 1), self.at(i, to_y, 0)
        self.own[at_x] = add(self.own[at_x], self.ry[b, 0]).astype(bf16)
        two[0].start()
        self.own[at_y] = add(self.own[at_y], self.rx[b, 0]).astype(bf16)
        two[1].start()

    def plane(self, i):
        for copy in self.round_two(i):
            copy.wait()
        mine, _, _, _ = self.sites()
        b = self.slot(i)
        sums = lambda: (
            add(self.own[self.at(i, mine, 0)], self.rx[b, 1], self.ly[b]),
            add(self.own[self.at(i, mine, 1)], self.lx[b], self.ry[b, 1]),
        )
        if self.m_z:

            @when(i < self.m_z)
            def _():
                s = self.experts // 2
                for h, total in enumerate(sums()):
                    self.zs[i, h * s : (h + 1) * s] = total.astype(bf16)
                for copy in self.round_z(i):
                    copy.start()

        if self.m_z < self.m:

            @when(i >= self.m_z)
            def _():
                self.store(self.out, i, sums())

    def column(self, i):
        for copy in self.round_z(i):
            copy.wait()
        terms = [self.zs[i, self.place.e]] + [self.rz[i, j] for j in range(self.experts - 1)]
        self.store(self.out, i, add(*terms))


def add(*terms):
    return functools.reduce(jnp.add, [t.astype(f32) for t in terms])


def call(
    name, steps, body, args, in_specs, outs, out_specs, scratch, moves, collective_id, experts, flops, given=None
):
    total = max([steps] + [m.turns for m in moves])

    def hold(spec):
        if spec.block_shape is None:
            return spec
        index = spec.index_map
        return pl.BlockSpec(spec.block_shape, lambda j: index(jnp.minimum(j, steps - 1)))

    join = lambda what: [x for m in moves for x in getattr(m, what)]

    def kernel(*refs):
        refs = list(refs)
        take = lambda group: [refs.pop(0) for _ in group]
        ins, m_ins = take(args), [take(m.args) for m in moves]
        os, m_os = take(outs), [take(m.outs) for m in moves]
        own, m_own = take(scratch), [take(m.scratch) for m in moves]
        now = pl.program_id(0)
        if moves:
            place = Place(experts)
            if given is not None:
                given(ins, os, own)
            for m, a, o, r in zip(moves, m_ins, m_os, m_own):
                m.bind(a, o, r, place)

            @when(now == 0)
            def _():
                place.greet(any(m.along_z for m in moves))

            for m in moves:
                m.turn(now)
        if body is not None:

            @when(now < steps)
            def _():
                body(now, steps, *ins, *os, *own)

        for m in moves:
            m.finish(now)

    results = pl.pallas_call(
        kernel,
        grid=(total,),
        out_shape=list(outs) + join("outs"),
        in_specs=[hold(s) for s in in_specs] + join("in_specs"),
        out_specs=[hold(s) for s in out_specs] + join("out_specs"),
        scratch_shapes=list(scratch) + join("scratch"),
        cost_estimate=pl.CostEstimate(flops=flops, bytes_accessed=32 * MIB, transcendentals=0),
        compiler_params=pltpu.CompilerParams(
            vmem_limit_bytes=60 * MIB,
            **({"collective_id": collective_id, "has_side_effects": True} if moves else {}),
        ),
        name=name,
    )(*args, *join("args"))
    return list(results)


def masks():
    lanes = lax.broadcasted_iota(jnp.int32, (1, PAIR), 1)
    return [(lanes // HD == h).astype(bf16) for h in range(2)]


def causal(scores_t, start):
    keys = lax.broadcasted_iota(jnp.int32, scores_t.shape, 0)
    queries = lax.broadcasted_iota(jnp.int32, scores_t.shape, 1) + start
    return jnp.where(keys <= queries, scores_t, -jnp.inf)


def attend_pair(q, k, v):
    q = q * (1.0 / math.sqrt(HD))
    vt = v.T
    length = q.shape[0]
    outs, tops = [], []
    for h, mask in enumerate(masks()):
        kh = k * mask
        row, logs = [], []
        for start in range(0, length, QB):
            end = start + QB
            scores = causal(outer_nt(kh[:end], q[start:end]), start)
            top = jnp.max(scores, axis=0, keepdims=True)
            expd = jnp.exp(scores - top)
            total = jnp.sum(expd, axis=0, keepdims=True)
            probs = (expd / total).astype(bf16)
            row.append(matmul(vt[h * HD : (h + 1) * HD, :end], probs))
            logs.append(top + jnp.log(total))
        outs.append(jnp.concatenate(row, axis=1))
        tops.append(jnp.concatenate(logs, axis=1))
    return jnp.concatenate(outs, axis=0).T.astype(bf16), jnp.concatenate(tops, axis=0)


def columns_of(code):
    length = code.shape[1]
    return [jnp.broadcast_to(code[i : i + 1], (128, length)).T.astype(jnp.int32) for i in range(2)]


class Forward:
    def __init__(self, length, width, experts, devices, capacity, ff, gather, leave):
        self.length, self.width, self.experts, self.capacity = length, width, experts, capacity
        self.gather, self.leave = gather, leave
        pairs = width // PAIR
        share = self.share = width // devices
        self.blocks = ff // BLOCK
        self.per_block = BLOCK * devices // ff
        self.at_norm, self.at_qkv = 4, 6
        self.at_heads = self.at_qkv + 1
        self.per_turn = 2
        self.at_out = self.at_heads + length // SEQ * pairs // self.per_turn
        self.at_leave = self.at_out + 1
        self.at_mlp = max(self.at_leave + 2, self.DENSE_ITEMS + 3)
        self.steps = self.at_mlp + self.blocks
        slots = experts * capacity
        rows = lambda c, t: jax.ShapeDtypeStruct((length, c), t)
        piece = (capacity, 2 * width)
        self.kept = 1 if leave else experts
        self.outs = [
            rows(3 * width, bf16),
            jax.ShapeDtypeStruct((length // SEQ * pairs, 2, SEQ), f32),
            rows(width, bf16),
            rows(width, f32),
            rows(width, bf16),
            rows(slots, bf16),
            rows(128, f32),
            rows(width, f32),
            rows(width, f32),
        ] + [jax.ShapeDtypeStruct(piece, bf16)] * self.kept
        if gather:
            stages = [(devices, self.per_block * share * devices // ff * (ff // devices // 128), 128)]
            stages = [(devices, BLOCK // 128 * share, 128), (self.per_block, width, 128)]
            targets = [(devices, width, 128)] * 2
        else:
            stages, targets = [(width, BLOCK)] * 2, [(width, ff)] * 2
        self.targets = [jax.ShapeDtypeStruct(t, bf16) for t in targets]
        self.scratch = [pltpu.VMEM(piece, bf16)] * (experts - self.kept) + [
            pltpu.VMEM((devices, share, 128), bf16),
            pltpu.VMEM((devices, share, 3 * width), bf16),
            pltpu.VMEM((devices, share, width), bf16),
            pltpu.VMEM((8, width), f32),
            pltpu.VMEM((length, width), bf16),
            pltpu.SemaphoreType.DMA((3,)),
            pltpu.VMEM((length, width), bf16),
            pltpu.VMEM((length, width), bf16),
            pltpu.VMEM((width, length), bf16),
            pltpu.VMEM((width, length), bf16),
            pltpu.VMEM((2, devices, share, BLOCK), bf16),
            pltpu.VMEM((2, self.per_block, ff // devices, width), bf16),
            pltpu.VMEM((2,) + stages[0], bf16),
            pltpu.VMEM((2,) + stages[1], bf16),
            pltpu.SemaphoreType.DMA((2, 2)),
            pltpu.SemaphoreType.DMA((2, 2)),
        ]

    DENSE_ITEMS = 12

    def __call__(self, now, steps, tok, cot, code, *refs):
        refs = list(refs)
        take = lambda count: [refs.pop(0) for _ in range(count)]
        full = self.gather.full[:5] if self.gather else take(5)
        qkv, lse, att, after, mixed, disp, info, dense_out, grad_mixed = take(9)
        leave = take(self.kept)
        targets = take(2)
        leave += take(self.experts - self.kept)
        ws, wq, wo, gains, attn_in, sems, gd, ge, xt, gt, w1, w2, stage_1, stage_2, w_sems, d_sems = refs
        width, length = self.width, self.length
        loads = [pltpu.make_async_copy(a, b, sems.at[i]) for i, (a, b) in enumerate(zip(full, (ws, wq, wo)))]

        def weights(block):
            at = lax.rem(block, 2)
            cols = pl.ds(pl.multiple_of(block * BLOCK, BLOCK), BLOCK)
            return [
                pltpu.make_async_copy(full[3].at[:, :, cols], w1.at[at], w_sems.at[at, 0]),
                pltpu.make_async_copy(full[4].at[pl.ds(block * self.per_block, self.per_block)], w2.at[at], w_sems.at[at, 1]),
            ]

        def flush(block):
            at = lax.rem(block, 2)
            if self.gather:
                size = BLOCK // 128 * self.share
                first = targets[0].at[:, pl.ds(pl.multiple_of(block * size, size), size)]
                second = targets[1].at[pl.ds(block * self.per_block, self.per_block)]
            else:
                cols = pl.ds(pl.multiple_of(block * BLOCK, BLOCK), BLOCK)
                first, second = targets[0].at[:, cols], targets[1].at[:, cols]
            return [
                pltpu.make_async_copy(stage_1.at[at], first, d_sems.at[at, 0]),
                pltpu.make_async_copy(stage_2.at[at], second, d_sems.at[at, 1]),
            ]

        @when(now == self.at_norm)
        def _():
            loads[0].start()
            loads[0].wait()
            gains[...] = ws[...].reshape(width, 128).astype(f32).T[:8]
            normed, _ = normalize(tok[...].astype(f32))
            attn_in[...] = (normed * gains[0:1]).astype(bf16)

        @when(now == self.at_qkv)
        def _():
            loads[1].start()
            loads[1].wait()

            def columns(c, _):
                cols = pl.ds(pl.multiple_of(c * BLOCK, BLOCK), BLOCK)
                weights = wq[:, :, cols].reshape(width, BLOCK)
                qkv[:, cols] = matmul(attn_in[...], weights).astype(bf16)
                return 0

            lax.fori_loop(0, 3 * width // BLOCK, columns, 0)

        @when(jnp.logical_and(now >= self.at_heads, now < self.at_out))
        def _():
            pairs = width // PAIR

            def pair(i, _):
                at = (now - self.at_heads) * self.per_turn + i
                seq, at_pair = at // pairs, lax.rem(at, pairs)
                rows = pl.ds(pl.multiple_of(seq * SEQ, SEQ), SEQ)
                cols = lambda part: pl.ds(pl.multiple_of(part * width + at_pair * PAIR, PAIR), PAIR)
                out, tops = attend_pair(qkv[rows, cols(0)], qkv[rows, cols(1)], qkv[rows, cols(2)])
                att[rows, cols(0)] = out
                lse[at] = tops
                return 0

            lax.fori_loop(0, self.per_turn, pair, 0)

        @when(now == self.at_out)
        def _():
            loads[2].start()
            loads[2].wait()
            self.route(tok, cot, code, att, wo, ws, gains, after, mixed, gd, ge, disp, info)

        @when(now == self.at_leave)
        def _():
            for h, values in enumerate((mixed, ge)):
                placed = product_tn(disp[...], values[...]).astype(bf16)
                for j in range(self.experts):
                    leave[j][:, h * width : (h + 1) * width] = placed[j * self.capacity : (j + 1) * self.capacity]
            if self.leave:
                self.leave.send()

        @when(now == self.at_mlp - 1)
        def _():
            xt[...] = mixed[...].T
            gt[...] = gd[...].T
            dense_out[...] = jnp.zeros_like(dense_out)
            grad_mixed[...] = jnp.zeros_like(grad_mixed)

        @when(jnp.logical_and(now >= self.at_mlp, now < self.at_mlp + self.blocks))
        def _():
            block = now - self.at_mlp
            at = lax.rem(block, 2)

            @when(block == 0)
            def _():
                for copy in weights(0):
                    copy.start()

            @when(block + 1 < self.blocks)
            def _():
                for copy in weights(block + 1):
                    copy.start()

            for copy in weights(block):
                copy.wait()

            @when(block >= 2)
            def _():
                for copy in flush(block - 2):
                    copy.wait()

            d1, d2 = mlp_block(
                mixed,
                gd,
                xt,
                gt,
                w1[at].reshape(width, BLOCK),
                w2[at].reshape(BLOCK, width),
                dense_out,
                grad_mixed,
            )
            if self.gather:
                share = self.share
                for c in range(BLOCK // 128):
                    cols = slice(c * 128, (c + 1) * 128)
                    for s in range(width // share):
                        stage_1[at, s, c * share : (c + 1) * share] = d1[s * share : (s + 1) * share, cols]
                    stage_2[at, c] = d2[:, cols]
            else:
                stage_1[at] = d1
                stage_2[at] = d2
            for copy in flush(block):
                copy.start()

            @when(block == self.blocks - 1)
            def _():
                for last in (self.blocks - 2, self.blocks - 1):
                    for copy in flush(last):
                        copy.wait()

    def route(self, tok, cot, code, att, wo, ws, gains, after, mixed, gd, ge, disp, info):
        width, length, experts = self.width, self.length, self.experts
        route, drop = columns_of(code)
        after[...] = tok[...].astype(f32) + matmul(att[...], wo[...].reshape(width, width))
        normed, _ = normalize(after[...])
        mixed[...] = (normed * gains[1:2]).astype(bf16)
        logits = matmul(mixed[...], ws[...].reshape(width, 128))
        lane = lax.broadcasted_iota(jnp.int32, (length, 128), 1)

        def softmax(first, last):
            inside = jnp.logical_and(lane >= first, lane < last)
            top = jnp.max(jnp.where(inside, logits, -jnp.inf), axis=1, keepdims=True)
            expd = jnp.where(inside, jnp.exp(jnp.where(inside, logits, top) - top), 0.0)
            return expd / jnp.sum(expd, axis=1, keepdims=True)

        probs, coef = softmax(2, 2 + experts), softmax(2 + experts, 4 + experts)
        info[...] = probs + coef
        chosen = jnp.where(lane - 2 == route, 1.0, 0.0)
        over_lanes = lambda a: jnp.sum(a, axis=1, keepdims=True)
        gate = over_lanes(probs * chosen) * (1 - drop[:, :1]).astype(f32)
        coef_0 = over_lanes(jnp.where(lane == 2 + experts, coef, 0.0))
        coef_1 = over_lanes(jnp.where(lane == 3 + experts, coef, 0.0))
        grad = cot[...].astype(f32)
        gd[...] = (coef_0 * grad).astype(bf16)
        ge[...] = (coef_1 * gate * grad).astype(bf16)
        square = lambda d: lax.broadcasted_iota(jnp.int32, (length, length), d)
        earlier = jnp.where(square(0) > square(1), 1.0, 0.0).astype(bf16)
        position = over_lanes(chosen * matmul(earlier, chosen.astype(bf16))).astype(jnp.int32)
        turn = route[:, :1] - lax.axis_index("expert")
        target = jnp.where(turn < 0, turn + experts, turn) * self.capacity + position
        slot = lax.broadcasted_iota(jnp.int32, (length, experts * self.capacity), 1)
        disp[...] = jnp.where(slot == target, 1.0, 0.0).astype(bf16)


def attend_pair_backward(q, k, v, g, lse):
    scaling = 1.0 / math.sqrt(HD)
    qs = q * scaling
    kt = k.T
    length = q.shape[0]
    grad_k = [0.0] * (length // QB)
    grad_v = [0.0] * (length // QB)
    grad_q = []
    for h, mask in enumerate(masks()):
        kh, vh, qh, gh = k * mask, v * mask, q * mask, g * mask
        row = []
        for c, start in enumerate(range(0, length, QB)):
            end = start + QB
            scores = causal(outer_nt(kh[:end], qs[start:end]), start)
            probs = jnp.exp(scores - lse[h : h + 1, start:end])
            grad_probs = outer_nt(vh[:end], g[start:end])
            delta = jnp.sum(probs * grad_probs, axis=0, keepdims=True)
            grad_scores = (probs * (grad_probs - delta)).astype(bf16)
            more_v = matmul(probs.astype(bf16), gh[start:end])
            more_k = matmul(grad_scores, qh[start:end])
            for b in range(c + 1):
                rows = slice(b * QB, (b + 1) * QB)
                grad_v[b] = grad_v[b] + more_v[rows]
                grad_k[b] = grad_k[b] + more_k[rows]
            row.append(matmul(kt[h * HD : (h + 1) * HD, :end], grad_scores))
        grad_q.append(jnp.concatenate(row, axis=1))
    return (
        (jnp.concatenate(grad_q, axis=0).T * scaling).astype(bf16),
        (jnp.concatenate(grad_k, axis=0) * scaling).astype(bf16),
        jnp.concatenate(grad_v, axis=0).astype(bf16),
    )


def thirds(values):
    parts = []
    for _ in range(3):
        parts.append(values.astype(bf16))
        values = values - parts[-1].astype(f32)
    return parts


class Back:
    def __init__(self, length, width, experts, devices, capacity):
        self.length, self.width, self.experts, self.capacity = length, width, experts, capacity
        self.devices, self.share = devices, width // devices
        self.pairs = width // PAIR
        self.columns = 3 * PAIR
        self.firsts = width // self.columns
        self.rest = width - self.firsts * self.columns
        self.items = self.firsts + self.pairs + 1
        self.heads_at = 3
        self.last = self.heads_at + self.pairs
        self.steps = self.last + 1
        self.first_item = self.heads_at
        self.outs = [
            jax.ShapeDtypeStruct((length, width), bf16),
            jax.ShapeDtypeStruct((length, width), f32),
        ]
        slots = experts * capacity
        self.scratch = [
            pltpu.VMEM((slots, 2 * width), bf16),
            pltpu.VMEM((length, width), f32),
            pltpu.VMEM((length, width), f32),
            pltpu.VMEM((devices, self.share, 128), bf16),
            pltpu.VMEM((devices, self.share, width), bf16),
            pltpu.VMEM((2, devices, self.share, self.columns), bf16),
            pltpu.VMEM((8, width), f32),
            pltpu.VMEM((128, width), f32),
            pltpu.VMEM((width, length), bf16),
            pltpu.VMEM((length, width), bf16),
            pltpu.SemaphoreType.DMA((5 + experts,)),
            pltpu.SemaphoreType.DMA((2, 3)),
        ]

    def made(self):
        chips = (4, 2, 2, self.experts // 2) if self.devices == 8 * self.experts else (self.devices,)
        return (self.items,) + chips + (self.share, self.columns)

    def final_outs(self):
        share, width = self.share, self.width
        return [jax.ShapeDtypeStruct((share, c), f32) for c in (3 * width, width, 128)]

    def store(self, outs, i, value):
        d_qkv, d_out, d_small = outs
        final = self.items - 1

        for f in range(self.firsts):

            @when(i == f)
            def _(f=f):
                d_out[:, f * self.columns : (f + 1) * self.columns] = value

        @when(jnp.logical_and(i >= self.firsts, i < final))
        def _():
            for p in range(3):
                at = pl.multiple_of(p * self.width + (i - self.firsts) * PAIR, PAIR)
                d_qkv[:, pl.ds(at, PAIR)] = value[:, p * PAIR : (p + 1) * PAIR]

        @when(i == final)
        def _():
            d_out[:, self.firsts * self.columns :] = value[:, : self.rest]
            d_small[...] = value[:, self.rest : self.rest + 128]

    def __call__(self, now, steps, *refs):
        experts, width, length = self.experts, self.width, self.length
        refs = list(refs)
        tok, cot, code, qkv, lse, att, mixed_in, disp, info = refs[:9]
        small_hbm, qkv_hbm, out_hbm, dense_hbm, grad_hbm, after_hbm = refs[9:15]
        came_hbm = refs[15 : 15 + experts]
        mixed, tokens_grad, *rest = refs[15 + experts :]
        if self.moves:
            made = self.moves[-1].own
        else:
            made = rest.pop(0)
        came, dense, grads, ws, wo, wq, gains, d_heads, attn_in_t, grad_att, sems, wq_sems = rest
        fetch = lambda a, b, i: pltpu.make_async_copy(a, b, sems.at[i])
        capacity = self.capacity
        loads = [fetch(came_hbm[j], came.at[pl.ds(j * capacity, capacity)], j) for j in range(experts)]
        loads += [
            fetch(a, b, experts + i)
            for i, (a, b) in enumerate(
                ((dense_hbm, dense), (grad_hbm, grads), (after_hbm, tokens_grad), (small_hbm, ws), (out_hbm, wo))
            )
        ]

        def pair_weights(pair):
            slot = lax.rem(pair, 2)
            return [
                pltpu.make_async_copy(
                    qkv_hbm.at[:, :, pl.ds(pl.multiple_of(p * width + pair * PAIR, PAIR), PAIR)],
                    wq.at[slot, :, :, pl.ds(p * PAIR, PAIR)],
                    wq_sems.at[slot, p],
                )
                for p in range(3)
            ]

        put = lambda i, columns, values: self.put(made, i, columns, values)
        lane = lax.broadcasted_iota(jnp.int32, (length, 128), 1)
        over_lanes = lambda a: jnp.sum(a, axis=1, keepdims=True)

        @when(now == 0)
        def _():
            for copy in loads + pair_weights(0):
                copy.start()

            for copy in loads:
                copy.wait()
            probs = jnp.where(jnp.logical_and(lane >= 2, lane < 2 + experts), info[...], 0.0)
            coef_0 = over_lanes(jnp.where(lane == 2 + experts, info[...], 0.0))
            coef_1 = over_lanes(jnp.where(lane == 3 + experts, info[...], 0.0))
            route, drop = columns_of(code)
            chosen = jnp.where(lane - 2 == route, 1.0, 0.0)
            kept = (1 - drop[:, :1]).astype(f32)
            gate_prob = over_lanes(probs * chosen)
            gate = gate_prob * kept
            grad = cot[...].astype(f32)
            expert_tok = matmul(disp[...], came[:, :width])
            mixed[...] = (tokens_grad[...] + coef_0 * dense[...] + (coef_1 * gate) * expert_tok).astype(bf16)
            shared = over_lanes(grad * expert_tok)
            grad_0, grad_1 = over_lanes(grad * dense[...]), shared * gate
            both = coef_0 * grad_0 + coef_1 * grad_1
            grad_gate = shared * coef_1 * kept
            logits = jnp.where(
                jnp.logical_and(lane >= 2, lane < 2 + experts), (grad_gate * gate_prob) * (chosen - probs), 0.0
            )
            logits = jnp.where(lane == 2 + experts, coef_0 * (grad_0 - both), logits)
            logits = jnp.where(lane == 3 + experts, coef_1 * (grad_1 - both), logits)
            pieces = thirds(logits)
            d_heads[...] = add(*(product_tn(p, mixed_in[...]) for p in pieces))
            weights = ws[...].reshape(width, 128)
            grads[...] = (
                grads[...] + matmul(disp[...], came[:, width:]) + add(*(outer_nt(p, weights) for p in pieces))
            )
            gains[...] = weights.astype(f32).T[:8]

        @when(now == 1)
        def _():
            normed, scale = normalize(tokens_grad[...])
            d_heads[1:2] = jnp.sum(grads[...] * normed, axis=0, keepdims=True)
            grads[...] = cot[...].astype(f32) + norm_back(grads[...] * gains[1:2], normed, scale)
            normed, _ = normalize(tok[...].astype(f32))
            attn_in_t[...] = (normed * gains[0:1]).astype(bf16).T

        @when(now == 2)
        def _():
            grad_attn = grads[...].astype(bf16)
            grad_att[...] = outer_nt(grad_attn, wo[...].reshape(width, width)).astype(bf16)
            d_out = product_tn(att[...], grad_attn).astype(bf16)
            for f in range(self.firsts):
                put(f, slice(None), d_out[:, f * self.columns : (f + 1) * self.columns])
            put(self.items - 1, slice(0, self.rest), d_out[:, self.firsts * self.columns :])
            dense[...] = jnp.zeros_like(dense)

        @when(jnp.logical_and(now >= self.heads_at, now < self.last))
        def _():
            pair = now - self.heads_at
            cols = lambda part: pl.ds(pl.multiple_of(part * width + pair * PAIR, PAIR), PAIR)
            d_pair = attend_pair_backward(
                qkv[:, cols(0)], qkv[:, cols(1)], qkv[:, cols(2)], grad_att[:, cols(0)], lse[pair]
            )
            d_pair = jnp.concatenate(d_pair, axis=1)
            for copy in pair_weights(pair):
                copy.wait()

            @when(pair + 1 < self.pairs)
            def _():
                for copy in pair_weights(pair + 1):
                    copy.start()

            put(pair + self.firsts, slice(None), matmul(attn_in_t[...], d_pair).astype(bf16))
            dense[...] += outer_nt(d_pair, wq[lax.rem(pair, 2)].reshape(width, self.columns))

        @when(now == self.last)
        def _():
            normed, scale = normalize(tok[...].astype(f32))
            d_heads[0:1] = jnp.sum(dense[...] * normed, axis=0, keepdims=True)
            put(self.items - 1, slice(self.rest, self.rest + 128), d_heads[...].T.astype(bf16))
            if self.rest + 128 < self.columns:
                spare = self.columns - self.rest - 128
                put(self.items - 1, slice(self.rest + 128, None), jnp.zeros((width, spare), bf16))
            tokens_grad[...] = grads[...] + norm_back(dense[...] * gains[0:1], normed, scale)

    def put(self, made, i, columns, values):
        lead = made.shape[1:-1]
        at = (i,) + (slice(None),) * len(lead) + (columns,)
        made[at] = values.reshape(lead + values.shape[1:])


def gelu_both(v):
    c = math.sqrt(2.0 / math.pi)
    square = v * v
    t = jnp.tanh(c * (v + 0.044715 * (square * v)))
    half = 0.5 * (1.0 + t)
    slope = half + 0.5 * v * (1.0 - t * t) * (c * (1.0 + (3 * 0.044715) * square))
    return v * half, slope


def mlp_block(x, g, xt, gt, w1, w2, out_sum, back_sum):
    hidden, slope = gelu_both(matmul(x[...], w1))
    hidden = hidden.astype(bf16)
    grad_pre = (slope * outer_nt(g[...], w2)).astype(bf16)
    out_sum[...] += matmul(hidden, w2)
    back_sum[...] += outer_nt(grad_pre, w1)
    return matmul(xt[...], grad_pre).astype(bf16), matmul(gt[...], hidden).astype(bf16)


class Experts:
    PER_STEP = 1

    def __init__(self, pieces, blocks, width, size, chunks, back):
        self.parts, self.piece = len(pieces), pieces[0].shape
        self.blocks, self.width, self.size, self.back = blocks, width, size, back
        rows = self.parts * self.piece[0]
        if chunks:
            self.block = (2, size // 256, chunks, width // chunks, 128)
            whole = (blocks // 2, 2) + self.block
        else:
            self.block = (width, size)
            whole = (blocks,) + self.block
        piece = jax.ShapeDtypeStruct(self.piece, bf16)
        self.outs = [piece] * self.parts + [jax.ShapeDtypeStruct(whole, bf16)] * 2
        self.scratch = (
            [pltpu.VMEM(self.piece, bf16)] * self.parts
            + [pltpu.VMEM((rows, width), bf16)] * 2
            + [pltpu.VMEM((width, rows), bf16)] * 2
            + [pltpu.VMEM((rows, width), f32)] * 2
            + [pltpu.VMEM((2,) + self.block, bf16)] * 2
            + [pltpu.SemaphoreType.DMA((2, 2)), pltpu.SemaphoreType.DMA((self.parts,))]
        )

    def __call__(self, now, steps, *refs):
        refs = list(refs)
        take = lambda count: [refs.pop(0) for _ in range(count)]
        pieces, (w1, w2) = take(self.parts), take(2)
        kept, targets, results = take(self.parts), take(2), take(self.parts)
        x, g, xt, gt, out_sum, back_sum, stage_1, stage_2, sems, kept_sems = refs
        width, size = self.width, self.piece[0]

        def flush(step):
            at = lax.rem(step, 2)
            where = (step // 2, at) if len(self.block) > 2 else (step,)
            return [
                pltpu.make_async_copy(stage.at[at], target.at[where], sems.at[at, i])
                for i, (stage, target) in enumerate(zip((stage_1, stage_2), targets))
            ]

        @when(now == 0)
        def _():
            for j, piece in enumerate(pieces):
                x[j * size : (j + 1) * size] = piece[:, :width]
                g[j * size : (j + 1) * size] = piece[:, width:]
            xt[...] = x[...].T
            gt[...] = g[...].T
            out_sum[...] = jnp.zeros_like(out_sum)
            back_sum[...] = jnp.zeros_like(back_sum)

        def block(b, _):
            step = now * self.PER_STEP + b

            @when(step >= 2)
            def _():
                for copy in flush(step - 2):
                    copy.wait()

            slot = lax.rem(step, 2)
            for stage, d in zip((stage_1, stage_2), mlp_block(x, g, xt, gt, w1[b], w2[b], out_sum, back_sum)):
                if len(self.block) == 2:
                    stage[slot] = d
                else:
                    for c in range(d.shape[1] // 128):
                        share = d[:, c * 128 : (c + 1) * 128].reshape(self.block[2:])
                        stage[slot, c // self.block[1], c % self.block[1]] = share
            for copy in flush(step):
                copy.start()
            return 0

        lax.fori_loop(0, self.PER_STEP, block, 0)

        @when(now == steps - 1)
        def _():
            for h, total in enumerate((out_sum, back_sum)):
                for j, result in enumerate(results):
                    result[:, h * width : (h + 1) * width] = total[j * size : (j + 1) * size].astype(bf16)
            keep = [pltpu.make_async_copy(a, b, kept_sems.at[j]) for j, (a, b) in enumerate(zip(results, kept))]
            for copy in keep:
                copy.start()
            for copy in keep:
                copy.wait()
            if self.back:
                self.back.send()
            for step in (self.blocks - 2, self.blocks - 1):
                for copy in flush(step):
                    copy.wait()


def move(name, moves, collective_id, experts):
    return call(name, 1, None, [], [], [], [], [], moves, collective_id, experts, 0)


def shards(
    fast,
    tokens,
    gain_attn,
    w_qkv,
    w_out,
    gain_mix,
    w_fc,
    w_proj,
    w_router,
    w_coef,
    expert_in,
    expert_out,
    routes,
    dropped,
    cotangent,
):
    experts = lax.axis_size("expert")
    nodes = lax.axis_size("node")
    devices = nodes * experts
    width = tokens.shape[1]
    tok_rows = tokens.shape[0]
    ff = w_fc.shape[1]
    share = w_qkv.shape[0]
    small = jnp.concatenate([gain_attn[:, None], gain_mix[:, None], w_router, w_coef], axis=1)
    small = jnp.pad(small, ((0, 0), (0, 128 - small.shape[1])))
    win, wout = expert_in[0], expert_out[0]
    cut = lambda a, rows, columns, m, n: [
        [(a, i * (rows // m), rows // m, j * (columns // n), columns // n)] for i in range(m) for j in range(n)
    ]
    weights = (small, w_qkv, w_out, w_fc, w_proj)
    capacity = -(-(tok_rows * 10) // (8 * experts))
    moves, given = [], None
    if fast:
        items = cut(1, share, 3 * width, 1, 3) + cut(2, share, width, 1, 1)
        items += cut(3, share, ff, 1, 4) + cut(4, ff // devices, width, 4, 1)
        items[0] = cut(0, share, 128, 1, 1)[0] + items[0]
        assert len(items) == Forward.DENSE_ITEMS
        items += cut(5, width, win.shape[1], 4, 1) + cut(6, wout.shape[0], width, 4, 1)
        moves = [Gather(list(weights) + [win, wout], [True] * 5 + [False] * 2, items, nodes, experts)]
        moves.append(Exchange([], 1, experts, None, moves[0].turns, (capacity, 2 * width)))
        full = []
    else:
        full = [lax.all_gather(a, AXES, axis=0, tiled=False) for a in weights]
        win_full, wout_full = (lax.all_gather(a, "node", axis=0, tiled=False) for a in (win, wout))

    def scatter_xla(parts, axes):
        return lax.psum_scatter(parts, axes, scatter_dimension=0, tiled=False).astype(f32)

    def exchange(parts, sign):
        moved = [parts[0]]
        for j in range(1, experts):
            shift = [(s, (s + sign * j) % experts) for s in range(experts)]
            moved.append(lax.ppermute(parts[j], "expert", shift))
        return moved

    forward = Forward(tok_rows, width, experts, devices, capacity, ff, *(moves or (None, None)))
    whole, hbm = pl.BlockSpec(memory_space=pltpu.VMEM), pl.BlockSpec(memory_space=pltpu.HBM)
    code = jnp.stack([routes[:, 0], dropped]).astype(f32)
    if fast:

        def given(ins, os, own):
            moves[1].sources = own[: experts - 1]

    results = call(
        "forward",
        forward.steps,
        forward,
        [tokens, cotangent, code] + full,
        [whole] * 3 + [hbm] * len(full),
        forward.outs + forward.targets,
        [whole] * len(forward.outs) + [hbm] * 2,
        forward.scratch,
        moves,
        1,
        experts,
        12 * tok_rows * width * (width + ff),
        given,
    )
    qkv_rows, lse, attended, after_attn, mixed_in, dispatch, probs, dense_out, grad_mixed = results[:9]
    results = results[9:]
    leaving, (d_fc, d_proj), moved = (
        results[: forward.kept],
        results[forward.kept : forward.kept + 2],
        results[forward.kept + 2 :],
    )
    small_full, qkv_full, out_full = (moved if fast else full)[:3]
    scatters, return_to, given = [], None, None
    chunks = 4
    step = width // chunks
    half = (experts // 2, step, 128)
    win_out = [jax.ShapeDtypeStruct(expert_in.shape, f32)]
    wout_out = [jax.ShapeDtypeStruct(expert_out.shape, f32)]

    def store_wout(out, chunk, sums):
        at = pl.ds(pl.multiple_of(chunk * step, step), step)
        for h, total in enumerate(sums):
            for c in range(half[0]):
                out[0, (h * half[0] + c) * 128 : (h * half[0] + c + 1) * 128, at] = total[c].T

    if fast:
        win_full, wout_full = moved[5:7]
        arrived = leaving + moved[7:]
        by_chip = lambda a: a.reshape(4, 2, 2, experts // 2, chunks, step, 128)

        def store(outs, i, value):
            @when(i < chunks)
            def _():
                for q in range(step // share):
                    at = pl.multiple_of(i * (step // share * 128) + q * 128, 128)
                    outs[0][:, pl.ds(at, 128)] = value[q * share : (q + 1) * share]

            @when(i >= chunks)
            def _():
                outs[1][:, pl.ds(pl.multiple_of((i - chunks) * step, step), step)] = value.T

        def store_experts(outs, i, sums):
            first = 2 * chunks

            @when(i < first + chunks)
            def _():
                at = pl.ds(pl.multiple_of((i - first) * step, step), step)
                for h, total in enumerate(sums):
                    for c in range(half[0]):
                        outs[2][0, at, (h * half[0] + c) * 128 : (h * half[0] + c + 1) * 128] = total[c]

            @when(i >= first + chunks)
            def _():
                store_wout(outs[3], i - first - chunks, sums)

        def store_any(outs, i, value):
            (store_experts if isinstance(value, tuple) else store)(outs, i, value)

        outs = [jax.ShapeDtypeStruct((share, ff), f32), jax.ShapeDtypeStruct((ff // devices, width), f32)]
        parts = [(by_chip(d_fc), True, 0, chunks), (by_chip(d_proj), True, 0, chunks)]
        parts += [(None, False, 0, chunks)] * 2
        summing = Scatter(parts, half, experts, outs + win_out + wout_out, store_any, z_late=12)
        return_to = Exchange([], -1, experts, None, summing.turns, leaving[0].shape)
        scatters = [return_to, summing]
    else:
        arrived = exchange(leaving, 1)
    blocks, size = win_full.shape[0], win_full.shape[2]
    experts_kernel = Experts(arrived, blocks, width, size, chunks if fast else None, return_to)
    if fast:

        def given(ins, os, own):
            summing.given = os[experts : experts + 2]
            return_to.sources = os[1:experts]

    per = experts_kernel.PER_STEP
    results = call(
        "expert_mlp",
        blocks // per,
        experts_kernel,
        arrived + [win_full, wout_full],
        [whole] * experts
        + [pl.BlockSpec((per, width, size), lambda j: (j, 0, 0)), pl.BlockSpec((per, size, width), lambda j: (j, 0, 0))],
        experts_kernel.outs,
        [hbm] * len(experts_kernel.outs),
        experts_kernel.scratch,
        scatters,
        3,
        experts,
        12 * experts * capacity * width * blocks * size,
        given,
    )
    returned, (d_win, d_wout) = results[:experts], results[experts : experts + 2]
    if fast:
        results = results[experts + 2 :]
        came_back = returned[:1] + results[: experts - 1]
        grad_fc, grad_proj, grad_win, grad_wout = results[experts - 1 :]
    else:
        came_back = exchange(returned, -1)
    back = Back(tok_rows, width, experts, devices, capacity)
    back.moves = []
    if fast:
        parts = [(None, True, 0, back.items)]
        made = back.made()
        scatter_rest = Scatter(
            parts, made[4:], experts, back.final_outs(), back.store, back.first_item, made
        )
        back.moves = [scatter_rest]
    outs = back.outs + ([] if fast else [jax.ShapeDtypeStruct((back.items, width, back.columns), bf16)])
    mixed, tokens_grad, *results = call(
        "back",
        back.steps,
        back,
        [tokens, cotangent, code, qkv_rows, lse, attended, mixed_in, dispatch, probs]
        + [small_full, qkv_full, out_full, dense_out, grad_mixed, after_attn]
        + came_back,
        [whole] * 9 + [hbm] * (6 + experts),
        outs,
        [whole] * len(outs),
        back.scratch,
        back.moves,
        5,
        experts,
        32 * tok_rows * width * width,
    )
    if fast:
        grad_wqkv, grad_wo, grad_small = results
    else:
        summed = scatter_xla(results[0].reshape(back.items, devices, share, -1).swapaxes(0, 1), AXES)
        last = summed[-1]
        grad_wo = jnp.concatenate([*summed[: back.firsts], last[:, : back.rest]], axis=1)
        grad_small = last[:, back.rest : back.rest + 128]
        pairs = summed[back.firsts : -1].reshape(back.pairs, share, 3, PAIR)
        grad_wqkv = pairs.transpose(1, 2, 0, 3).reshape(share, 3 * width)
        grad_fc = scatter_xla(d_fc.reshape(devices, share, ff), AXES)
        by_unit = d_proj.reshape(width, devices, ff // devices).transpose(1, 0, 2)
        grad_proj = scatter_xla(by_unit, AXES).T
        grad_win = scatter_xla(d_win, "node")[None]
        grad_wout = scatter_xla(d_wout, "node").T[None]
    return (
        mixed,
        tokens_grad,
        grad_small[:, 0],
        grad_wqkv,
        grad_wo,
        grad_small[:, 1],
        grad_fc,
        grad_proj,
        grad_small[:, 2 : 2 + experts],
        grad_small[:, 2 + experts : 4 + experts],
        grad_win,
        grad_wout,
    )


def solution(mesh):
    rows = P(AXES, None)
    in_specs = (
        rows,
        P(AXES),
        rows,
        rows,
        P(AXES),
        rows,
        rows,
        rows,
        rows,
        P("expert", None, "node"),
        P("expert", "node", None),
        rows,
        P(AXES),
        rows,
    )
    out_specs = (
        rows,
        rows,
        P(AXES),
        rows,
        rows,
        P(AXES),
        rows,
        rows,
        rows,
        rows,
        P("expert", None, "node"),
        P("expert", "node", None),
    )
    fast = mesh.shape["node"] == 8 and mesh.shape["expert"] == 4
    return jax.shard_map(
        functools.partial(shards, fast), mesh=mesh, in_specs=in_specs, out_specs=out_specs, check_vma=False
    )
```

```python
import functools
import math

import jax
import jax.numpy as jnp
from jax import lax
from jax.experimental import pallas as pl
from jax.experimental.pallas import tpu as pltpu
from jax.sharding import PartitionSpec as P

HD = 64
PAIR = 2 * HD
SEQ = 512
QB = 256
BLOCK = 512
MIB = 1 << 20
AXES = ("node", "expert")
MESH = pl.DeviceIdType.MESH
epsilon = 1e-05
f32 = jnp.float32
bf16 = jnp.bfloat16


def normalize(values):
    centered = values - jnp.mean(values, axis=-1, keepdims=True)
    inv_scale = lax.rsqrt(jnp.mean(centered * centered, axis=-1, keepdims=True) + epsilon)
    return (centered * inv_scale, inv_scale)


def norm_back(grad_norm, normed, inv_scale):
    mean_grad = jnp.mean(grad_norm, axis=-1, keepdims=True)
    mean_cross = jnp.mean(grad_norm * normed, axis=-1, keepdims=True)
    return inv_scale * (grad_norm - mean_grad - normed * mean_cross)


def contract(left_op, right_op, left_dim, right_dim):
    return lax.dot_general(
        left_op, right_op, (((left_dim,), (right_dim,)), ((), ())), preferred_element_type=f32
    )


def matmul(left_op, right_op):
    return contract(left_op, right_op, 1, 0)


def product_tn(left_op, right_op):
    return contract(left_op, right_op, 0, 0)


def outer_nt(left_op, right_op):
    return contract(left_op, right_op, 1, 1)


class Place:
    def __init__(self, experts):
        self.experts = experts
        self.n, self.e = lax.axis_index("node"), lax.axis_index("expert")
        n = self.n
        self.k, self.x, self.y = lax.rem(n, 2), lax.rem(n // 2, 2), n // 4
        k, x, y = self.k, self.x, self.y
        self.nx, self.ny = y * 4 + (1 - x) * 2 + k, (1 - y) * 4 + x * 2 + k
        self.nd, self.nc = (1 - y) * 4 + (1 - x) * 2 + k, y * 4 + x * 2 + 1 - k

    def z(self, j):
        return (self.n, lax.rem(self.e + j, self.experts))

    def greet(self, along_z):
        barrier = pltpu.get_barrier_semaphore()
        peers = [(self.nx, self.e), (self.ny, self.e), (self.nc, self.e)]
        if along_z:
            peers += [self.z(j) for j in range(1, self.experts)]
        for peer in peers:
            pl.semaphore_signal(barrier, inc=1, device_id=peer, device_id_type=MESH)
        pl.semaphore_wait(barrier, len(peers))


def when(condition):
    return pl.when(condition)


class Gather:
    def __init__(self, args, dense, items, nodes, experts):
        self.args, self.dense, self.items, self.experts = args, dense, items, experts
        self.outs = [
            jax.ShapeDtypeStruct(((nodes * experts if d else nodes),) + a.shape, a.dtype)
            for a, d in zip(args, dense)
        ]
        hbm = pl.BlockSpec(memory_space=pltpu.HBM)
        self.in_specs, self.out_specs = [hbm] * len(args), [hbm] * len(args)
        m = sum(len(item) for item in items)
        self.scratch = [
            pltpu.SemaphoreType.DMA((m, experts + 7)),
            pltpu.SemaphoreType.DMA((m, experts + 7)),
            pltpu.SemaphoreType.DMA((m,)),
        ]
        self.along_z = any(dense)
        self.steps = [self.along, self.across, self.corner, self.over, self.end]
        self.turns = len(items) + len(self.steps) - 1

    def bind(self, ins, outs, scratch, place):
        experts = self.experts
        send, recv, loc = scratch
        p, e = place, place.e

        def remote(source, target, item, kind, device):
            return pltpu.make_async_remote_copy(
                src_ref=source,
                dst_ref=target,
                send_sem=send.at[item, kind],
                recv_sem=recv.at[item, kind],
                device_id=device,
                device_id_type=MESH,
            )

        self.full = outs
        self.bound = [[] for _ in self.items]
        pieces = [(turn, piece) for turn, item in enumerate(self.items) for piece in item]
        for i, (turn, (arg, row, rows, col, columns)) in enumerate(pieces):
            dense = self.dense[arg]
            shard, whole = ins[arg], outs[arg]
            per = experts if dense else 1
            own = p.n * per + (e if dense else 0)

            def view(ref, lead, start=0, size=None, whole_rows=rows, row=row, col=col, columns=columns):
                return ref.at[lead, pl.ds(row + start, size or whole_rows), pl.ds(col, columns)]

            def bundle(m, view=view, whole=whole, per=per):
                return view(whole, pl.ds(m * per, per))

            def half(m, h, view=view, whole=whole, per=per, dense=dense, rows=rows):
                if dense:
                    return view(whole, pl.ds(m * per + h * (per // 2), per // 2))
                return view(whole, m, h * (rows // 2), rows // 2)

            mine = shard.at[pl.ds(row, rows), pl.ds(col, columns)]
            land = view(whole, own)
            local = pltpu.make_async_copy(mine, land, loc.at[i])
            z = []
            if dense:
                z = [remote(mine, land, i, j - 1, p.z(j)) for j in range(1, experts)]
            first, last = (bundle(p.n), bundle(p.n)) if dense else (mine, land)
            b = experts - 1
            xy = [remote(first, last, i, b, (p.nx, e)), remote(first, last, i, b + 1, (p.ny, e))]
            diag = [
                remote(half(p.nx, 0), half(p.nx, 0), i, b + 2, (p.ny, e)),
                remote(half(p.ny, 1), half(p.ny, 1), i, b + 3, (p.nx, e)),
            ]
            core = [remote(first, last, i, b + 4, (p.nc, e))] + [
                remote(bundle(m), bundle(m), i, b + 5 + j, (p.nc, e)) for j, m in enumerate((p.nx, p.ny, p.nd))
            ]
            self.bound[turn].append((local, z, xy, diag, core))

    def turn(self, now):
        for t in range(self.turns):

            @when(now == t)
            def _(t=t):
                for late, step in enumerate(self.steps):
                    if 0 <= t - late < len(self.items):
                        for piece in self.bound[t - late]:
                            step(*piece)

    def finish(self, now):
        pass

    def along(self, local, z, xy, diag, core):
        local.start()
        for copy in z:
            copy.start()

    def across(self, local, z, xy, diag, core):
        for copy in z:
            copy.wait()
        local.wait()
        xy[0].start()
        xy[1].start()
        core[0].start()

    def corner(self, local, z, xy, diag, core):
        for i in range(2):
            xy[i].wait()
            diag[i].start()
            core[1 + i].start()

    def over(self, local, z, xy, diag, core):
        diag[0].wait()
        diag[1].wait()
        core[3].start()

    def end(self, local, z, xy, diag, core):
        for copy in core:
            copy.wait()


class Exchange:
    along_z = True

    def __init__(self, pieces, sign, experts, start, turns, shape):
        self.args, self.sign, self.experts, self.start, self.turns = list(pieces), sign, experts, start, turns
        self.given = None
        self.outs = [jax.ShapeDtypeStruct(shape, bf16)] * (experts - 1)
        hbm = pl.BlockSpec(memory_space=pltpu.HBM)
        self.in_specs, self.out_specs = [hbm] * len(self.args), [hbm] * (experts - 1)
        self.scratch = [pltpu.SemaphoreType.DMA((experts,)), pltpu.SemaphoreType.DMA((experts,))]

    def bind(self, ins, outs, scratch, place):
        self.out, self.sems, self.place = outs, scratch, place
        if ins:
            self.sources = ins

    def copies(self):
        return [
            pltpu.make_async_remote_copy(
                src_ref=source,
                dst_ref=self.out[j],
                send_sem=self.sems[0].at[j],
                recv_sem=self.sems[1].at[j],
                device_id=self.place.z((self.sign * (j + 1)) % self.experts),
                device_id_type=MESH,
            )
            for j, source in enumerate(self.sources)
        ]

    def send(self):
        for copy in self.copies():
            copy.start()

    def turn(self, now):
        if self.start is not None:

            @when(now == self.start)
            def _():
                self.send()

    def finish(self, now):
        @when(now == self.turns - 1)
        def _():
            for copy in self.copies():
                copy.wait()


class Scatter:
    RING, SPREAD_RING, CORE_RING = 6, 8, 4

    def __init__(self, parts, half, experts, outs, store, start=0, made=None, spread=False):
        self.experts, self.outs, self.store, self.start, self.made = experts, outs, store, start, made
        self.parts = parts
        self.given = []
        self.args = [p[0] for p in parts if p[0] is not None]
        h = half
        self.starts = [sum(p[3] for p in parts[:a]) for a in range(len(parts) + 1)]
        m = self.m = self.starts[-1]
        self.m_z = sum(p[3] for p in parts if p[1])
        unit = h[1:]
        ring = self.ring = min(self.SPREAD_RING if spread else self.RING, m)
        self.core_ring = min(self.CORE_RING, m)
        self.in_specs = [pl.BlockSpec(memory_space=pltpu.HBM)] * len(self.args)
        self.out_specs = [pl.BlockSpec(memory_space=pltpu.VMEM)] * len(outs)
        kinds = 7 + experts
        self.scratch = [
            pltpu.VMEM(made or (ring, 4, 2) + h, bf16),
            pltpu.VMEM((self.core_ring, 4, 2) + h, bf16),
            pltpu.VMEM((ring, 2) + h, bf16),
            pltpu.VMEM((ring, 2) + h, bf16),
            pltpu.VMEM((ring,) + h, bf16),
            pltpu.VMEM((ring,) + h, bf16),
            pltpu.SemaphoreType.DMA((m, kinds)),
            pltpu.SemaphoreType.DMA((m, kinds)),
            pltpu.SemaphoreType.DMA((m,)),
        ]
        if self.m_z:
            self.scratch.append(pltpu.VMEM((self.m_z, experts - 1) + unit, bf16))
            self.scratch.append(pltpu.VMEM((self.m_z, experts) + unit, bf16))
        self.stages = (0, 1, 3, 5, 7) if spread else (0, 1, 2, 3, 4)
        self.turns = start + m + self.stages[4 if self.m_z else 3]
        self.along_z = self.m_z > 0

    def bind(self, ins, outs, scratch, place):
        ins = list(ins)
        given = list(self.given)
        self.sources = [given.pop(0) if p[0] is None else ins.pop(0) for p in self.parts] if not self.made else []
        self.out, self.place = outs, place
        self.own, self.rc, self.rx, self.ry, self.lx, self.ly, self.sent, self.recv, self.loc = scratch[:9]
        self.rz, self.zs = scratch[9:] if self.m_z else (None, None)

    def slot(self, i):
        return lax.rem(i, self.ring)

    def remote(self, source, target, item, kind, device):
        return pltpu.make_async_remote_copy(
            src_ref=source,
            dst_ref=target,
            send_sem=self.sent.at[item, kind],
            recv_sem=self.recv.at[item, kind],
            device_id=device,
            device_id_type=MESH,
        )

    def at(self, i, site, *more):
        return (i, site, self.place.k) + more if self.made else (self.slot(i), site) + more

    def first(self, source, i, chunk):
        p = self.place
        land = self.rc.at[lax.rem(i, self.core_ring)]
        if self.made:
            return [self.remote(self.own.at[i, :, 1 - p.k], land, i, 0, (p.nc, p.e))]
        part = lambda core: source.at[:, core, :, :, chunk]
        local = pltpu.make_async_copy(part(p.k), self.own.at[self.slot(i)], self.loc.at[i])
        return [self.remote(part(1 - p.k), land, i, 0, (p.nc, p.e)), local]

    def sites(self):
        p = self.place
        return p.y * 2 + p.x, p.y * 2 + 1 - p.x, (1 - p.y) * 2 + p.x, (1 - p.y) * 2 + 1 - p.x

    def round_one(self, i):
        p = self.place
        b = self.slot(i)
        _, to_x, to_y, diag = self.sites()
        own = lambda *at: self.own.at[self.at(i, *at)]
        return [
            self.remote(own(diag, 0), self.rx.at[b, 0], i, 1, (p.nx, p.e)),
            self.remote(own(diag, 1), self.ry.at[b, 0], i, 2, (p.ny, p.e)),
            self.remote(own(to_x, 0), self.rx.at[b, 1], i, 3, (p.nx, p.e)),
            self.remote(own(to_y, 1), self.ry.at[b, 1], i, 4, (p.ny, p.e)),
        ]

    def round_two(self, i):
        p = self.place
        b = self.slot(i)
        _, to_x, to_y, _ = self.sites()
        return [
            self.remote(self.own.at[self.at(i, to_x, 1)], self.lx.at[b], i, 5, (p.nx, p.e)),
            self.remote(self.own.at[self.at(i, to_y, 0)], self.ly.at[b], i, 6, (p.ny, p.e)),
        ]

    def round_z(self, i):
        p = self.place
        return [
            self.remote(self.zs.at[i, lax.rem(p.e + j, self.experts)], self.rz.at[i, j - 1], i, 6 + j, p.z(j))
            for j in range(1, self.experts)
        ]

    def turn(self, now):
        limits = (self.m, self.m, self.m, self.m, self.m_z)
        steps = (self.load, self.chip, self.cross, self.plane, self.column)
        for limit, late, step in zip(limits, self.stages, steps):
            i = now - self.start - late
            if limit:

                @when(jnp.logical_and(i >= 0, i < limit))
                def _(step=step, i=i):
                    step(i)

    def finish(self, now):
        pass

    def load(self, i):
        if self.made:
            self.first(None, i, 0)[0].start()
            return
        for a, source in enumerate(self.sources):

            @when(jnp.logical_and(i >= self.starts[a], i < self.starts[a + 1]))
            def _(a=a, source=source):
                for copy in self.first(source, i, i - self.starts[a] + self.parts[a][2]):
                    copy.start()

    def chip(self, i):
        for copy in self.first(None if self.made else self.sources[0], i, 0):
            copy.wait()

        def sum_one(q, _):
            at = self.at(i, q)
            self.own[at] = add(self.own[at], self.rc[lax.rem(i, self.core_ring), q]).astype(bf16)
            return 0

        lax.fori_loop(0, 4, sum_one, 0)
        for copy in self.round_one(i):
            copy.start()

    def cross(self, i):
        one = self.round_one(i)
        two = self.round_two(i)
        b = self.slot(i)
        _, to_x, to_y, _ = self.sites()
        for copy in one:
            copy.wait()
        at_x, at_y = self.at(i, to_x, 1), self.at(i, to_y, 0)
        self.own[at_x] = add(self.own[at_x], self.ry[b, 0]).astype(bf16)
        two[0].start()
        self.own[at_y] = add(self.own[at_y], self.rx[b, 0]).astype(bf16)
        two[1].start()

    def plane(self, i):
        for copy in self.round_two(i):
            copy.wait()
        mine, _, _, _ = self.sites()
        b = self.slot(i)
        sums = lambda: (
            add(self.own[self.at(i, mine, 0)], self.rx[b, 1], self.ly[b]),
            add(self.own[self.at(i, mine, 1)], self.lx[b], self.ry[b, 1]),
        )
        if self.m_z:

            @when(i < self.m_z)
            def _():
                s = self.experts // 2
                for h, total in enumerate(sums()):
                    self.zs[i, h * s : (h + 1) * s] = total.astype(bf16)
                for copy in self.round_z(i):
                    copy.start()

        if self.m_z < self.m:

            @when(i >= self.m_z)
            def _():
                self.store(self.out, i, sums())

    def column(self, i):
        for copy in self.round_z(i):
            copy.wait()
        terms = [self.zs[i, self.place.e]] + [self.rz[i, j] for j in range(self.experts - 1)]
        self.store(self.out, i, add(*terms))


class Along:
    along_z = True

    def __init__(self, shares, experts, outs, store, turns):
        self.args, self.experts, self.outs, self.store, self.turns = [shares], experts, outs, store, turns
        self.in_specs = [pl.BlockSpec(memory_space=pltpu.HBM)]
        self.out_specs = [pl.BlockSpec(memory_space=pltpu.VMEM)] * len(outs)
        self.items = shares.shape[1]
        self.scratch = [
            pltpu.VMEM(shares.shape, bf16),
            pltpu.SemaphoreType.DMA((experts,)),
            pltpu.SemaphoreType.DMA((experts,)),
        ]

    def bind(self, ins, outs, scratch, place):
        self.source, self.out, self.place = ins[0], outs, place
        self.land, self.sent, self.recv = scratch

    def copies(self):
        p = self.place
        copies = [pltpu.make_async_copy(self.source.at[p.e], self.land.at[0], self.recv.at[0])]
        return copies + [
            pltpu.make_async_remote_copy(
                src_ref=self.source.at[lax.rem(p.e + j, self.experts)],
                dst_ref=self.land.at[j],
                send_sem=self.sent.at[j],
                recv_sem=self.recv.at[j],
                device_id=p.z(j),
                device_id_type=MESH,
            )
            for j in range(1, self.experts)
        ]

    def turn(self, now):
        @when(now == 0)
        def _():
            for copy in self.copies():
                copy.start()

    def finish(self, now):
        @when(now == self.turns - 1)
        def _():
            for copy in self.copies():
                copy.wait()
            for i in range(self.items):
                self.store(self.out, i, add(*(self.land[j, i] for j in range(self.experts))))


def add(*terms):
    return functools.reduce(jnp.add, [t.astype(f32) for t in terms])


def call(
    name, steps, body, args, in_specs, outs, out_specs, scratch, moves, collective_id, experts, flops, given=None
):
    total = max([steps] + [m.turns for m in moves])

    def hold(spec):
        if spec.block_shape is None:
            return spec
        index = spec.index_map
        return pl.BlockSpec(spec.block_shape, lambda j: index(jnp.minimum(j, steps - 1)))

    join = lambda what: [x for m in moves for x in getattr(m, what)]

    def kernel(*refs):
        refs = list(refs)
        take = lambda group: [refs.pop(0) for _ in group]
        ins, m_ins = take(args), [take(m.args) for m in moves]
        os, m_os = take(outs), [take(m.outs) for m in moves]
        own, m_own = take(scratch), [take(m.scratch) for m in moves]
        now = pl.program_id(0)
        if moves:
            place = Place(experts)
            if given is not None:
                given(ins, os, own)
            for m, a, o, r in zip(moves, m_ins, m_os, m_own):
                m.bind(a, o, r, place)

            @when(now == 0)
            def _():
                place.greet(any(m.along_z for m in moves))

            for m in moves:
                m.turn(now)
        if body is not None:

            @when(now < steps)
            def _():
                body(now, steps, *ins, *os, *own)

        for m in moves:
            m.finish(now)

    results = pl.pallas_call(
        kernel,
        grid=(total,),
        out_shape=list(outs) + join("outs"),
        in_specs=[hold(s) for s in in_specs] + join("in_specs"),
        out_specs=[hold(s) for s in out_specs] + join("out_specs"),
        scratch_shapes=list(scratch) + join("scratch"),
        cost_estimate=pl.CostEstimate(flops=flops, bytes_accessed=32 * MIB, transcendentals=0),
        compiler_params=pltpu.CompilerParams(
            vmem_limit_bytes=60 * MIB,
            **({"collective_id": collective_id, "has_side_effects": True} if moves else {}),
        ),
        name=name,
    )(*args, *join("args"))
    return list(results)


def masks():
    lanes = lax.broadcasted_iota(jnp.int32, (1, PAIR), 1)
    return [(lanes // HD == h).astype(bf16) for h in range(2)]


def causal(scores_t, start):
    keys = lax.broadcasted_iota(jnp.int32, scores_t.shape, 0)
    queries = lax.broadcasted_iota(jnp.int32, scores_t.shape, 1) + start
    return jnp.where(keys <= queries, scores_t, -jnp.inf)


def attend_pair(q, k, v):
    q = q * (1.0 / math.sqrt(HD))
    vt = v.T
    length = q.shape[0]
    outs, tops = [], []
    for h, mask in enumerate(masks()):
        kh = k * mask
        row, logs = [], []
        for start in range(0, length, QB):
            end = start + QB
            scores = causal(outer_nt(kh[:end], q[start:end]), start)
            top = jnp.max(scores, axis=0, keepdims=True)
            expd = jnp.exp(scores - top)
            total = jnp.sum(expd, axis=0, keepdims=True)
            probs = (expd / total).astype(bf16)
            row.append(matmul(vt[h * HD : (h + 1) * HD, :end], probs))
            logs.append(top + jnp.log(total))
        outs.append(jnp.concatenate(row, axis=1))
        tops.append(jnp.concatenate(logs, axis=1))
    return jnp.concatenate(outs, axis=0).T.astype(bf16), jnp.concatenate(tops, axis=0)


def columns_of(code):
    length = code.shape[1]
    return [jnp.broadcast_to(code[i : i + 1], (128, length)).T.astype(jnp.int32) for i in range(2)]


class Forward:
    def __init__(self, length, width, experts, devices, capacity, ff, gather, leave):
        self.length, self.width, self.experts, self.capacity = length, width, experts, capacity
        self.gather, self.leave = gather, leave
        pairs = width // PAIR
        share = self.share = width // devices
        self.blocks = ff // BLOCK
        self.per_block = BLOCK * devices // ff
        self.at_norm, self.at_qkv = 4, 6
        self.at_heads = self.at_qkv + 1
        self.per_turn = 2
        self.at_out = self.at_heads + length // SEQ * pairs // self.per_turn
        self.at_leave = self.at_out + 1
        self.at_mlp = max(self.at_leave + 2, self.DENSE_ITEMS + 3)
        self.steps = self.at_mlp + self.blocks
        slots = experts * capacity
        rows = lambda c, t: jax.ShapeDtypeStruct((length, c), t)
        piece = (capacity, 2 * width)
        self.kept = 1 if leave else experts
        self.outs = [
            rows(3 * width, bf16),
            jax.ShapeDtypeStruct((length // SEQ * pairs, 2, SEQ), f32),
            rows(width, bf16),
            rows(width, f32),
            rows(width, bf16),
            rows(slots, bf16),
            rows(128, f32),
            rows(width, f32),
            rows(width, f32),
        ] + [jax.ShapeDtypeStruct(piece, bf16)] * self.kept
        if gather:
            stages = [(devices, self.per_block * share * devices // ff * (ff // devices // 128), 128)]
            stages = [(devices, BLOCK // 128 * share, 128), (self.per_block, width, 128)]
            targets = [(devices, width, 128)] * 2
        else:
            stages, targets = [(width, BLOCK)] * 2, [(width, ff)] * 2
        self.targets = [jax.ShapeDtypeStruct(t, bf16) for t in targets]
        self.scratch = [pltpu.VMEM(piece, bf16)] * (experts - self.kept) + [
            pltpu.VMEM((devices, share, 128), bf16),
            pltpu.VMEM((devices, share, 3 * width), bf16),
            pltpu.VMEM((devices, share, width), bf16),
            pltpu.VMEM((8, width), f32),
            pltpu.VMEM((length, width), bf16),
            pltpu.SemaphoreType.DMA((3,)),
            pltpu.VMEM((length, width), bf16),
            pltpu.VMEM((length, width), bf16),
            pltpu.VMEM((width, length), bf16),
            pltpu.VMEM((width, length), bf16),
            pltpu.VMEM((2, devices, share, BLOCK), bf16),
            pltpu.VMEM((2, self.per_block, ff // devices, width), bf16),
            pltpu.VMEM((2,) + stages[0], bf16),
            pltpu.VMEM((2,) + stages[1], bf16),
            pltpu.SemaphoreType.DMA((2, 2)),
            pltpu.SemaphoreType.DMA((2, 2)),
        ]

    DENSE_ITEMS = 12

    def __call__(self, now, steps, tok, cot, code, *refs):
        refs = list(refs)
        take = lambda count: [refs.pop(0) for _ in range(count)]
        full = self.gather.full[:5] if self.gather else take(5)
        qkv, lse, att, after, mixed, disp, info, dense_out, grad_mixed = take(9)
        leave = take(self.kept)
        targets = take(2)
        leave += take(self.experts - self.kept)
        ws, wq, wo, gains, attn_in, sems, gd, ge, xt, gt, w1, w2, stage_1, stage_2, w_sems, d_sems = refs
        width, length = self.width, self.length
        loads = [pltpu.make_async_copy(a, b, sems.at[i]) for i, (a, b) in enumerate(zip(full, (ws, wq, wo)))]

        def weights(block):
            at = lax.rem(block, 2)
            cols = pl.ds(pl.multiple_of(block * BLOCK, BLOCK), BLOCK)
            return [
                pltpu.make_async_copy(full[3].at[:, :, cols], w1.at[at], w_sems.at[at, 0]),
                pltpu.make_async_copy(full[4].at[pl.ds(block * self.per_block, self.per_block)], w2.at[at], w_sems.at[at, 1]),
            ]

        def flush(block):
            at = lax.rem(block, 2)
            if self.gather:
                size = BLOCK // 128 * self.share
                first = targets[0].at[:, pl.ds(pl.multiple_of(block * size, size), size)]
                second = targets[1].at[pl.ds(block * self.per_block, self.per_block)]
            else:
                cols = pl.ds(pl.multiple_of(block * BLOCK, BLOCK), BLOCK)
                first, second = targets[0].at[:, cols], targets[1].at[:, cols]
            return [
                pltpu.make_async_copy(stage_1.at[at], first, d_sems.at[at, 0]),
                pltpu.make_async_copy(stage_2.at[at], second, d_sems.at[at, 1]),
            ]

        @when(now == self.at_norm)
        def _():
            loads[0].start()
            loads[0].wait()
            gains[...] = ws[...].reshape(width, 128).astype(f32).T[:8]
            normed, _ = normalize(tok[...].astype(f32))
            attn_in[...] = (normed * gains[0:1]).astype(bf16)

        @when(now == self.at_qkv)
        def _():
            loads[1].start()
            loads[1].wait()

            def columns(c, _):
                cols = pl.ds(pl.multiple_of(c * BLOCK, BLOCK), BLOCK)
                weights = wq[:, :, cols].reshape(width, BLOCK)
                qkv[:, cols] = matmul(attn_in[...], weights).astype(bf16)
                return 0

            lax.fori_loop(0, 3 * width // BLOCK, columns, 0)

        @when(jnp.logical_and(now >= self.at_heads, now < self.at_out))
        def _():
            pairs = width // PAIR

            def pair(i, _):
                at = (now - self.at_heads) * self.per_turn + i
                seq, at_pair = at // pairs, lax.rem(at, pairs)
                rows = pl.ds(pl.multiple_of(seq * SEQ, SEQ), SEQ)
                cols = lambda part: pl.ds(pl.multiple_of(part * width + at_pair * PAIR, PAIR), PAIR)
                out, tops = attend_pair(qkv[rows, cols(0)], qkv[rows, cols(1)], qkv[rows, cols(2)])
                att[rows, cols(0)] = out
                lse[at] = tops
                return 0

            lax.fori_loop(0, self.per_turn, pair, 0)

        @when(now == self.at_out)
        def _():
            loads[2].start()
            loads[2].wait()
            self.route(tok, cot, code, att, wo, ws, gains, after, mixed, gd, ge, disp, info)

        @when(now == self.at_leave)
        def _():
            for h, values in enumerate((mixed, ge)):
                placed = product_tn(disp[...], values[...]).astype(bf16)
                for j in range(self.experts):
                    leave[j][:, h * width : (h + 1) * width] = placed[j * self.capacity : (j + 1) * self.capacity]
            if self.leave:
                self.leave.send()

        @when(now == self.at_mlp - 1)
        def _():
            xt[...] = mixed[...].T
            gt[...] = gd[...].T
            dense_out[...] = jnp.zeros_like(dense_out)
            grad_mixed[...] = jnp.zeros_like(grad_mixed)

        @when(jnp.logical_and(now >= self.at_mlp, now < self.at_mlp + self.blocks))
        def _():
            block = now - self.at_mlp
            at = lax.rem(block, 2)

            @when(block == 0)
            def _():
                for copy in weights(0):
                    copy.start()

            @when(block + 1 < self.blocks)
            def _():
                for copy in weights(block + 1):
                    copy.start()

            for copy in weights(block):
                copy.wait()

            @when(block >= 2)
            def _():
                for copy in flush(block - 2):
                    copy.wait()

            d1, d2 = mlp_block(
                mixed,
                gd,
                xt,
                gt,
                w1[at].reshape(width, BLOCK),
                w2[at].reshape(BLOCK, width),
                dense_out,
                grad_mixed,
            )
            if self.gather:
                share = self.share
                for c in range(BLOCK // 128):
                    cols = slice(c * 128, (c + 1) * 128)
                    for s in range(width // share):
                        stage_1[at, s, c * share : (c + 1) * share] = d1[s * share : (s + 1) * share, cols]
                    stage_2[at, c] = d2[:, cols]
            else:
                stage_1[at] = d1
                stage_2[at] = d2
            for copy in flush(block):
                copy.start()

            @when(block == self.blocks - 1)
            def _():
                for last in (self.blocks - 2, self.blocks - 1):
                    for copy in flush(last):
                        copy.wait()

    def route(self, tok, cot, code, att, wo, ws, gains, after, mixed, gd, ge, disp, info):
        width, length, experts = self.width, self.length, self.experts
        route, drop = columns_of(code)
        after[...] = tok[...].astype(f32) + matmul(att[...], wo[...].reshape(width, width))
        normed, _ = normalize(after[...])
        mixed[...] = (normed * gains[1:2]).astype(bf16)
        logits = matmul(mixed[...], ws[...].reshape(width, 128))
        lane = lax.broadcasted_iota(jnp.int32, (length, 128), 1)

        def softmax(first, last):
            inside = jnp.logical_and(lane >= first, lane < last)
            top = jnp.max(jnp.where(inside, logits, -jnp.inf), axis=1, keepdims=True)
            expd = jnp.where(inside, jnp.exp(jnp.where(inside, logits, top) - top), 0.0)
            return expd / jnp.sum(expd, axis=1, keepdims=True)

        probs, coef = softmax(2, 2 + experts), softmax(2 + experts, 4 + experts)
        info[...] = probs + coef
        chosen = jnp.where(lane - 2 == route, 1.0, 0.0)
        over_lanes = lambda a: jnp.sum(a, axis=1, keepdims=True)
        gate = over_lanes(probs * chosen) * (1 - drop[:, :1]).astype(f32)
        coef_0 = over_lanes(jnp.where(lane == 2 + experts, coef, 0.0))
        coef_1 = over_lanes(jnp.where(lane == 3 + experts, coef, 0.0))
        grad = cot[...].astype(f32)
        gd[...] = (coef_0 * grad).astype(bf16)
        ge[...] = (coef_1 * gate * grad).astype(bf16)
        square = lambda d: lax.broadcasted_iota(jnp.int32, (length, length), d)
        earlier = jnp.where(square(0) > square(1), 1.0, 0.0).astype(bf16)
        position = over_lanes(chosen * matmul(earlier, chosen.astype(bf16))).astype(jnp.int32)
        turn = route[:, :1] - lax.axis_index("expert")
        target = jnp.where(turn < 0, turn + experts, turn) * self.capacity + position
        slot = lax.broadcasted_iota(jnp.int32, (length, experts * self.capacity), 1)
        disp[...] = jnp.where(slot == target, 1.0, 0.0).astype(bf16)


def attend_pair_backward(q, k, v, g, lse):
    scaling = 1.0 / math.sqrt(HD)
    qs = q * scaling
    kt = k.T
    length = q.shape[0]
    grad_k = [0.0] * (length // QB)
    grad_v = [0.0] * (length // QB)
    grad_q = []
    for h, mask in enumerate(masks()):
        kh, vh, qh, gh = k * mask, v * mask, q * mask, g * mask
        row = []
        for c, start in enumerate(range(0, length, QB)):
            end = start + QB
            scores = causal(outer_nt(kh[:end], qs[start:end]), start)
            probs = jnp.exp(scores - lse[h : h + 1, start:end])
            grad_probs = outer_nt(vh[:end], g[start:end])
            delta = jnp.sum(probs * grad_probs, axis=0, keepdims=True)
            grad_scores = (probs * (grad_probs - delta)).astype(bf16)
            more_v = matmul(probs.astype(bf16), gh[start:end])
            more_k = matmul(grad_scores, qh[start:end])
            for b in range(c + 1):
                rows = slice(b * QB, (b + 1) * QB)
                grad_v[b] = grad_v[b] + more_v[rows]
                grad_k[b] = grad_k[b] + more_k[rows]
            row.append(matmul(kt[h * HD : (h + 1) * HD, :end], grad_scores))
        grad_q.append(jnp.concatenate(row, axis=1))
    return (
        (jnp.concatenate(grad_q, axis=0).T * scaling).astype(bf16),
        (jnp.concatenate(grad_k, axis=0) * scaling).astype(bf16),
        jnp.concatenate(grad_v, axis=0).astype(bf16),
    )


def thirds(values):
    parts = []
    for _ in range(3):
        parts.append(values.astype(bf16))
        values = values - parts[-1].astype(f32)
    return parts


class Back:
    def __init__(self, length, width, experts, devices, capacity):
        self.length, self.width, self.experts, self.capacity = length, width, experts, capacity
        self.devices, self.share = devices, width // devices
        self.pairs = width // PAIR
        self.columns = 3 * PAIR
        self.firsts = width // self.columns
        self.rest = width - self.firsts * self.columns
        self.items = self.firsts + self.pairs + 1
        self.heads_at = 4
        self.last = self.heads_at + self.pairs
        self.steps = self.last + 1
        self.first_item = self.heads_at
        self.outs = [
            jax.ShapeDtypeStruct((length, width), bf16),
            jax.ShapeDtypeStruct((length, width), f32),
        ]
        slots = experts * capacity
        self.scratch = [
            pltpu.VMEM((slots, 2 * width), bf16),
            pltpu.VMEM((length, width), f32),
            pltpu.VMEM((length, width), f32),
            pltpu.VMEM((devices, self.share, 128), bf16),
            pltpu.VMEM((devices, self.share, width), bf16),
            pltpu.VMEM((2, devices, self.share, self.columns), bf16),
            pltpu.VMEM((8, width), f32),
            pltpu.VMEM((128, width), f32),
            pltpu.VMEM((width, length), bf16),
            pltpu.VMEM((length, width), bf16),
            pltpu.SemaphoreType.DMA((5 + experts,)),
            pltpu.SemaphoreType.DMA((2, 3)),
        ]

    def made(self):
        chips = (4, 2, 2, self.experts // 2) if self.devices == 8 * self.experts else (self.devices,)
        return (self.items,) + chips + (self.share, self.columns)

    def final_outs(self):
        share, width = self.share, self.width
        return [jax.ShapeDtypeStruct((share, c), f32) for c in (3 * width, width, 128)]

    def store(self, outs, i, value):
        d_qkv, d_out, d_small = outs
        final = self.items - 1

        for f in range(self.firsts):

            @when(i == f)
            def _(f=f):
                d_out[:, f * self.columns : (f + 1) * self.columns] = value

        @when(jnp.logical_and(i >= self.firsts, i < final))
        def _():
            for p in range(3):
                at = pl.multiple_of(p * self.width + (i - self.firsts) * PAIR, PAIR)
                d_qkv[:, pl.ds(at, PAIR)] = value[:, p * PAIR : (p + 1) * PAIR]

        @when(i == final)
        def _():
            d_out[:, self.firsts * self.columns :] = value[:, : self.rest]
            d_small[...] = value[:, self.rest : self.rest + 128]

    def __call__(self, now, steps, *refs):
        experts, width, length = self.experts, self.width, self.length
        refs = list(refs)
        tok, cot, code, qkv, lse, att, mixed_in, disp, info = refs[:9]
        small_hbm, qkv_hbm, out_hbm, dense_hbm, grad_hbm, after_hbm = refs[9:15]
        came_hbm = refs[15 : 15 + experts]
        mixed, tokens_grad, *rest = refs[15 + experts :]
        if self.moves:
            made = self.moves[-1].own
        else:
            made = rest.pop(0)
        came, dense, grads, ws, wo, wq, gains, d_heads, attn_in_t, grad_att, sems, wq_sems = rest
        fetch = lambda a, b, i: pltpu.make_async_copy(a, b, sems.at[i])
        capacity = self.capacity
        loads = [fetch(came_hbm[j], came.at[pl.ds(j * capacity, capacity)], j) for j in range(experts)]
        loads += [
            fetch(a, b, experts + i)
            for i, (a, b) in enumerate(
                ((dense_hbm, dense), (grad_hbm, grads), (after_hbm, tokens_grad), (small_hbm, ws), (out_hbm, wo))
            )
        ]

        def pair_weights(pair):
            slot = lax.rem(pair, 2)
            return [
                pltpu.make_async_copy(
                    qkv_hbm.at[:, :, pl.ds(pl.multiple_of(p * width + pair * PAIR, PAIR), PAIR)],
                    wq.at[slot, :, :, pl.ds(p * PAIR, PAIR)],
                    wq_sems.at[slot, p],
                )
                for p in range(3)
            ]

        put = lambda i, columns, values: self.put(made, i, columns, values)
        lane = lax.broadcasted_iota(jnp.int32, (length, 128), 1)
        over_lanes = lambda a: jnp.sum(a, axis=1, keepdims=True)

        @when(now == 0)
        def _():
            for copy in loads + pair_weights(0):
                copy.start()

        @when(now == 1)
        def _():
            for copy in loads:
                copy.wait()
            probs = jnp.where(jnp.logical_and(lane >= 2, lane < 2 + experts), info[...], 0.0)
            coef_0 = over_lanes(jnp.where(lane == 2 + experts, info[...], 0.0))
            coef_1 = over_lanes(jnp.where(lane == 3 + experts, info[...], 0.0))
            route, drop = columns_of(code)
            chosen = jnp.where(lane - 2 == route, 1.0, 0.0)
            kept = (1 - drop[:, :1]).astype(f32)
            gate_prob = over_lanes(probs * chosen)
            gate = gate_prob * kept
            grad = cot[...].astype(f32)
            expert_tok = matmul(disp[...], came[:, :width])
            mixed[...] = (tokens_grad[...] + coef_0 * dense[...] + (coef_1 * gate) * expert_tok).astype(bf16)
            shared = over_lanes(grad * expert_tok)
            grad_0, grad_1 = over_lanes(grad * dense[...]), shared * gate
            both = coef_0 * grad_0 + coef_1 * grad_1
            grad_gate = shared * coef_1 * kept
            logits = jnp.where(
                jnp.logical_and(lane >= 2, lane < 2 + experts), (grad_gate * gate_prob) * (chosen - probs), 0.0
            )
            logits = jnp.where(lane == 2 + experts, coef_0 * (grad_0 - both), logits)
            logits = jnp.where(lane == 3 + experts, coef_1 * (grad_1 - both), logits)
            pieces = thirds(logits)
            d_heads[...] = add(*(product_tn(p, mixed_in[...]) for p in pieces))
            weights = ws[...].reshape(width, 128)
            grads[...] = (
                grads[...] + matmul(disp[...], came[:, width:]) + add(*(outer_nt(p, weights) for p in pieces))
            )
            gains[...] = weights.astype(f32).T[:8]

        @when(now == 2)
        def _():
            normed, scale = normalize(tokens_grad[...])
            d_heads[1:2] = jnp.sum(grads[...] * normed, axis=0, keepdims=True)
            grads[...] = cot[...].astype(f32) + norm_back(grads[...] * gains[1:2], normed, scale)
            normed, _ = normalize(tok[...].astype(f32))
            attn_in_t[...] = (normed * gains[0:1]).astype(bf16).T

        @when(now == 3)
        def _():
            grad_attn = grads[...].astype(bf16)
            grad_att[...] = outer_nt(grad_attn, wo[...].reshape(width, width)).astype(bf16)
            d_out = product_tn(att[...], grad_attn).astype(bf16)
            for f in range(self.firsts):
                put(f, slice(None), d_out[:, f * self.columns : (f + 1) * self.columns])
            put(self.items - 1, slice(0, self.rest), d_out[:, self.firsts * self.columns :])
            dense[...] = jnp.zeros_like(dense)

        @when(jnp.logical_and(now >= self.heads_at, now < self.last))
        def _():
            pair = now - self.heads_at
            cols = lambda part: pl.ds(pl.multiple_of(part * width + pair * PAIR, PAIR), PAIR)
            d_pair = attend_pair_backward(
                qkv[:, cols(0)], qkv[:, cols(1)], qkv[:, cols(2)], grad_att[:, cols(0)], lse[pair]
            )
            d_pair = jnp.concatenate(d_pair, axis=1)
            for copy in pair_weights(pair):
                copy.wait()

            @when(pair + 1 < self.pairs)
            def _():
                for copy in pair_weights(pair + 1):
                    copy.start()

            put(pair + self.firsts, slice(None), matmul(attn_in_t[...], d_pair).astype(bf16))
            dense[...] += outer_nt(d_pair, wq[lax.rem(pair, 2)].reshape(width, self.columns))

        @when(now == self.last)
        def _():
            normed, scale = normalize(tok[...].astype(f32))
            d_heads[0:1] = jnp.sum(dense[...] * normed, axis=0, keepdims=True)
            put(self.items - 1, slice(self.rest, self.rest + 128), d_heads[...].T.astype(bf16))
            if self.rest + 128 < self.columns:
                spare = self.columns - self.rest - 128
                put(self.items - 1, slice(self.rest + 128, None), jnp.zeros((width, spare), bf16))
            tokens_grad[...] = grads[...] + norm_back(dense[...] * gains[0:1], normed, scale)

    def put(self, made, i, columns, values):
        lead = made.shape[1:-1]
        at = (i,) + (slice(None),) * len(lead) + (columns,)
        made[at] = values.reshape(lead + values.shape[1:])


def gelu_both(v):
    c = math.sqrt(2.0 / math.pi)
    square = v * v
    t = jnp.tanh(c * (v + 0.044715 * (square * v)))
    half = 0.5 * (1.0 + t)
    slope = half + 0.5 * v * (1.0 - t * t) * (c * (1.0 + (3 * 0.044715) * square))
    return v * half, slope


def mlp_block(x, g, xt, gt, w1, w2, out_sum, back_sum):
    hidden, slope = gelu_both(matmul(x[...], w1))
    hidden = hidden.astype(bf16)
    grad_pre = (slope * outer_nt(g[...], w2)).astype(bf16)
    out_sum[...] += matmul(hidden, w2)
    back_sum[...] += outer_nt(grad_pre, w1)
    return matmul(xt[...], grad_pre).astype(bf16), matmul(gt[...], hidden).astype(bf16)


class Experts:
    TURNS = 6

    def __init__(self, pieces, blocks, width, size, chunks, back):
        self.parts, self.piece = len(pieces), pieces[0].shape
        self.blocks, self.width, self.size, self.back = blocks, width, size, back
        rows = self.parts * self.piece[0]
        if chunks:
            self.block = (2, size // 256, chunks, width // chunks, 128)
            whole = (blocks // 2, 2) + self.block
        else:
            self.block = (width, size)
            whole = (blocks,) + self.block
        piece = jax.ShapeDtypeStruct(self.piece, bf16)
        self.outs = [piece] * self.parts + [jax.ShapeDtypeStruct(whole, bf16)] * 2
        self.scratch = (
            [pltpu.VMEM(self.piece, bf16)] * self.parts
            + [pltpu.VMEM((rows, width), bf16)] * 2
            + [pltpu.VMEM((width, rows), bf16)] * 2
            + [pltpu.VMEM((rows, width), f32)] * 2
            + [pltpu.VMEM((2,) + self.block, bf16)] * 2
            + [pltpu.SemaphoreType.DMA((2, 2)), pltpu.SemaphoreType.DMA((self.parts,))]
            + [pltpu.VMEM((2, width, size), bf16), pltpu.VMEM((2, size, width), bf16)]
            + [pltpu.SemaphoreType.DMA((2, 2))]
        )

    def __call__(self, now, steps, *refs):
        refs = list(refs)
        take = lambda count: [refs.pop(0) for _ in range(count)]
        pieces, full = take(self.parts), take(2)
        kept, targets, results = take(self.parts), take(2), take(self.parts)
        x, g, xt, gt, out_sum, back_sum, stage_1, stage_2, sems, kept_sems, w1, w2, w_sems = refs
        width, size = self.width, self.piece[0]

        def flush(step):
            at = lax.rem(step, 2)
            where = (step // 2, at) if len(self.block) > 2 else (step,)
            return [
                pltpu.make_async_copy(stage.at[at], target.at[where], sems.at[at, i])
                for i, (stage, target) in enumerate(zip((stage_1, stage_2), targets))
            ]

        def weights(step):
            at = lax.rem(step, 2)
            return [
                pltpu.make_async_copy(a.at[step], b.at[at], w_sems.at[at, i])
                for i, (a, b) in enumerate(zip(full, (w1, w2)))
            ]

        @when(now == 0)
        def _():
            for copy in weights(0):
                copy.start()
            for j, piece in enumerate(pieces):
                x[j * size : (j + 1) * size] = piece[:, :width]
                g[j * size : (j + 1) * size] = piece[:, width:]
            xt[...] = x[...].T
            gt[...] = g[...].T
            out_sum[...] = jnp.zeros_like(out_sum)
            back_sum[...] = jnp.zeros_like(back_sum)

        def block(step, _):
            for copy in weights(step):
                copy.wait()

            @when(step + 1 < self.blocks)
            def _():
                for copy in weights(step + 1):
                    copy.start()

            @when(step >= 2)
            def _():
                for copy in flush(step - 2):
                    copy.wait()

            slot = lax.rem(step, 2)
            for stage, d in zip((stage_1, stage_2), mlp_block(x, g, xt, gt, w1[slot], w2[slot], out_sum, back_sum)):
                if len(self.block) == 2:
                    stage[slot] = d
                else:
                    for c in range(d.shape[1] // 128):
                        share = d[:, c * 128 : (c + 1) * 128].reshape(self.block[2:])
                        stage[slot, c // self.block[1], c % self.block[1]] = share
            for copy in flush(step):
                copy.start()
            return 0

        lax.fori_loop(now * self.blocks // steps, (now + 1) * self.blocks // steps, block, 0)

        @when(now == steps - 1)
        def _():
            for h, total in enumerate((out_sum, back_sum)):
                for j, result in enumerate(results):
                    result[:, h * width : (h + 1) * width] = total[j * size : (j + 1) * size].astype(bf16)
            keep = [pltpu.make_async_copy(a, b, kept_sems.at[j]) for j, (a, b) in enumerate(zip(results, kept))]
            for copy in keep:
                copy.start()
            for copy in keep:
                copy.wait()
            if self.back:
                self.back.send()
            for step in (self.blocks - 2, self.blocks - 1):
                for copy in flush(step):
                    copy.wait()


def move(name, moves, collective_id, experts):
    return call(name, 1, None, [], [], [], [], [], moves, collective_id, experts, 0)


def shards(
    fast,
    tokens,
    gain_attn,
    w_qkv,
    w_out,
    gain_mix,
    w_fc,
    w_proj,
    w_router,
    w_coef,
    expert_in,
    expert_out,
    routes,
    dropped,
    cotangent,
):
    experts = lax.axis_size("expert")
    nodes = lax.axis_size("node")
    devices = nodes * experts
    width = tokens.shape[1]
    tok_rows = tokens.shape[0]
    ff = w_fc.shape[1]
    share = w_qkv.shape[0]
    small = jnp.concatenate([gain_attn[:, None], gain_mix[:, None], w_router, w_coef], axis=1)
    small = jnp.pad(small, ((0, 0), (0, 128 - small.shape[1])))
    win, wout = expert_in[0], expert_out[0]
    cut = lambda a, rows, columns, m, n: [
        [(a, i * (rows // m), rows // m, j * (columns // n), columns // n)] for i in range(m) for j in range(n)
    ]
    weights = (small, w_qkv, w_out, w_fc, w_proj)
    capacity = -(-(tok_rows * 10) // (8 * experts))
    moves, given = [], None
    if fast:
        items = cut(1, share, 3 * width, 1, 3) + cut(2, share, width, 1, 1)
        items += cut(3, share, ff, 1, 4) + cut(4, ff // devices, width, 4, 1)
        items[0] = cut(0, share, 128, 1, 1)[0] + items[0]
        assert len(items) == Forward.DENSE_ITEMS
        items += cut(5, width, win.shape[1], 4, 1) + cut(6, wout.shape[0], width, 4, 1)
        moves = [Gather(list(weights) + [win, wout], [True] * 5 + [False] * 2, items, nodes, experts)]
        moves.append(Exchange([], 1, experts, None, moves[0].turns, (capacity, 2 * width)))
        full = []
    else:
        full = [lax.all_gather(a, AXES, axis=0, tiled=False) for a in weights]
        win_full, wout_full = (lax.all_gather(a, "node", axis=0, tiled=False) for a in (win, wout))

    def scatter_xla(parts, axes):
        return lax.psum_scatter(parts, axes, scatter_dimension=0, tiled=False).astype(f32)

    def exchange(parts, sign):
        moved = [parts[0]]
        for j in range(1, experts):
            shift = [(s, (s + sign * j) % experts) for s in range(experts)]
            moved.append(lax.ppermute(parts[j], "expert", shift))
        return moved

    forward = Forward(tok_rows, width, experts, devices, capacity, ff, *(moves or (None, None)))
    whole, hbm = pl.BlockSpec(memory_space=pltpu.VMEM), pl.BlockSpec(memory_space=pltpu.HBM)
    code = jnp.stack([routes[:, 0], dropped]).astype(f32)
    if fast:

        def given(ins, os, own):
            moves[1].sources = own[: experts - 1]

    results = call(
        "forward",
        forward.steps,
        forward,
        [tokens, cotangent, code] + full,
        [whole] * 3 + [hbm] * len(full),
        forward.outs + forward.targets,
        [whole] * len(forward.outs) + [hbm] * 2,
        forward.scratch,
        moves,
        1,
        experts,
        12 * tok_rows * width * (width + ff),
        given,
    )
    qkv_rows, lse, attended, after_attn, mixed_in, dispatch, probs, dense_out, grad_mixed = results[:9]
    results = results[9:]
    leaving, (d_fc, d_proj), moved = (
        results[: forward.kept],
        results[forward.kept : forward.kept + 2],
        results[forward.kept + 2 :],
    )
    small_full, qkv_full, out_full = (moved if fast else full)[:3]
    scatters, return_to, given = [], None, None
    chunks = 4
    step = width // chunks
    half = (experts // 2, step, 128)
    win_out = [jax.ShapeDtypeStruct(expert_in.shape, f32)]
    wout_out = [jax.ShapeDtypeStruct(expert_out.shape, f32)]

    def store_wout(out, chunk, sums):
        at = pl.ds(pl.multiple_of(chunk * step, step), step)
        for h, total in enumerate(sums):
            for c in range(half[0]):
                out[0, (h * half[0] + c) * 128 : (h * half[0] + c + 1) * 128, at] = total[c].T

    if fast:
        win_full, wout_full = moved[5:7]
        arrived = leaving + moved[7:]
        by_chip = lambda a: a.reshape(4, 2, 2, experts // 2, chunks, step, 128)

        def store(outs, i, value):
            if i < chunks:
                for q in range(step // share):
                    at = (i * (step // share) + q) * 128
                    outs[0][:, at : at + 128] = value[q * share : (q + 1) * share]
            else:
                outs[1][:, (i - chunks) * step : (i - chunks + 1) * step] = value.T

        def store_plane(outs, i, sums):
            @when(i < 2 * chunks)
            def _():
                for h, total in enumerate(sums):
                    outs[0][h * half[0] : (h + 1) * half[0], i] = total.astype(bf16)

            @when(i >= 2 * chunks)
            def _():
                at = pl.ds(pl.multiple_of((i - 2 * chunks) * step, step), step)
                for h, total in enumerate(sums):
                    for c in range(half[0]):
                        outs[1][0, at, (h * half[0] + c) * 128 : (h * half[0] + c + 1) * 128] = total[c]

        outs = [jax.ShapeDtypeStruct((experts, 2 * chunks) + half[1:], bf16)]
        parts = [(by_chip(d_fc), False, 0, chunks), (by_chip(d_proj), False, 0, chunks), (None, False, 0, chunks)]
        summing = Scatter(parts, half, experts, outs + win_out, store_plane, spread=True)
        return_to = Exchange([], -1, experts, None, summing.turns, leaving[0].shape)
        scatters = [return_to, summing]
    else:
        arrived = exchange(leaving, 1)
    blocks, size = win_full.shape[0], win_full.shape[2]
    experts_kernel = Experts(arrived, blocks, width, size, chunks if fast else None, return_to)
    if fast:

        def given(ins, os, own):
            summing.given = [os[experts]]
            return_to.sources = os[1:experts]

    results = call(
        "expert_mlp",
        experts_kernel.TURNS,
        experts_kernel,
        arrived + [win_full, wout_full],
        [whole] * experts + [hbm] * 2,
        experts_kernel.outs,
        [hbm] * len(experts_kernel.outs),
        experts_kernel.scratch,
        scatters,
        3,
        experts,
        12 * experts * capacity * width * blocks * size,
        given,
    )
    returned, (d_win, d_wout) = results[:experts], results[experts : experts + 2]
    if fast:
        results = results[experts + 2 :]
        came_back = returned[:1] + results[: experts - 1]
        plane_sums, grad_win = results[experts - 1 :]
    else:
        came_back = exchange(returned, -1)
    back = Back(tok_rows, width, experts, devices, capacity)
    back.moves = []
    if fast:
        parts = [(None, True, 0, back.items)]
        made = back.made()
        scatter_rest = Scatter(
            parts, made[4:], experts, back.final_outs(), back.store, back.first_item, made, spread=True
        )
        parts = [(d_wout, False, 0, chunks)]
        scatter_wout = Scatter(
            parts, half, experts, wout_out, lambda outs, i, sums: store_wout(outs[0], i, sums), spread=True
        )
        outs = [jax.ShapeDtypeStruct((share, ff), f32), jax.ShapeDtypeStruct((ff // devices, width), f32)]
        along = Along(plane_sums, experts, outs, store, max(scatter_rest.turns, scatter_wout.turns))
        back.moves = [along, scatter_wout, scatter_rest]
    outs = back.outs + ([] if fast else [jax.ShapeDtypeStruct((back.items, width, back.columns), bf16)])
    mixed, tokens_grad, *results = call(
        "back",
        back.steps,
        back,
        [tokens, cotangent, code, qkv_rows, lse, attended, mixed_in, dispatch, probs]
        + [small_full, qkv_full, out_full, dense_out, grad_mixed, after_attn]
        + came_back,
        [whole] * 9 + [hbm] * (6 + experts),
        outs,
        [whole] * len(outs),
        back.scratch,
        back.moves,
        5,
        experts,
        32 * tok_rows * width * width,
    )
    if fast:
        grad_fc, grad_proj, grad_wout, grad_wqkv, grad_wo, grad_small = results
    else:
        summed = scatter_xla(results[0].reshape(back.items, devices, share, -1).swapaxes(0, 1), AXES)
        last = summed[-1]
        grad_wo = jnp.concatenate([*summed[: back.firsts], last[:, : back.rest]], axis=1)
        grad_small = last[:, back.rest : back.rest + 128]
        pairs = summed[back.firsts : -1].reshape(back.pairs, share, 3, PAIR)
        grad_wqkv = pairs.transpose(1, 2, 0, 3).reshape(share, 3 * width)
        grad_fc = scatter_xla(d_fc.reshape(devices, share, ff), AXES)
        by_unit = d_proj.reshape(width, devices, ff // devices).transpose(1, 0, 2)
        grad_proj = scatter_xla(by_unit, AXES).T
        grad_win = scatter_xla(d_win, "node")[None]
        grad_wout = scatter_xla(d_wout, "node").T[None]
    return (
        mixed,
        tokens_grad,
        grad_small[:, 0],
        grad_wqkv,
        grad_wo,
        grad_small[:, 1],
        grad_fc,
        grad_proj,
        grad_small[:, 2 : 2 + experts],
        grad_small[:, 2 + experts : 4 + experts],
        grad_win,
        grad_wout,
    )


def solution(mesh):
    rows = P(AXES, None)
    in_specs = (
        rows,
        P(AXES),
        rows,
        rows,
        P(AXES),
        rows,
        rows,
        rows,
        rows,
        P("expert", None, "node"),
        P("expert", "node", None),
        rows,
        P(AXES),
        rows,
    )
    out_specs = (
        rows,
        rows,
        P(AXES),
        rows,
        rows,
        P(AXES),
        rows,
        rows,
        rows,
        rows,
        P("expert", None, "node"),
        P("expert", "node", None),
    )
    fast = mesh.shape["node"] == 8 and mesh.shape["expert"] == 4
    return jax.shard_map(
        functools.partial(shards, fast), mesh=mesh, in_specs=in_specs, out_specs=out_specs, check_vma=False
    )
```

```python
import functools
import math

import jax
import jax.numpy as jnp
from jax import lax
from jax.experimental import pallas as pl
from jax.experimental.pallas import tpu as pltpu
from jax.sharding import PartitionSpec as P

HD = 64
PAIR = 2 * HD
SEQ = 512
QB = 256
BLOCK = 512
MIB = 1 << 20
AXES = ("node", "expert")
MESH = pl.DeviceIdType.MESH
epsilon = 1e-05
f32 = jnp.float32
bf16 = jnp.bfloat16


def normalize(values):
    centered = values - jnp.mean(values, axis=-1, keepdims=True)
    inv_scale = lax.rsqrt(jnp.mean(centered * centered, axis=-1, keepdims=True) + epsilon)
    return (centered * inv_scale, inv_scale)


def norm_back(grad_norm, normed, inv_scale):
    mean_grad = jnp.mean(grad_norm, axis=-1, keepdims=True)
    mean_cross = jnp.mean(grad_norm * normed, axis=-1, keepdims=True)
    return inv_scale * (grad_norm - mean_grad - normed * mean_cross)


def contract(left_op, right_op, left_dim, right_dim):
    return lax.dot_general(
        left_op, right_op, (((left_dim,), (right_dim,)), ((), ())), preferred_element_type=f32
    )


def matmul(left_op, right_op):
    return contract(left_op, right_op, 1, 0)


def product_tn(left_op, right_op):
    return contract(left_op, right_op, 0, 0)


def outer_nt(left_op, right_op):
    return contract(left_op, right_op, 1, 1)


class Place:
    def __init__(self, experts):
        self.experts = experts
        self.n, self.e = lax.axis_index("node"), lax.axis_index("expert")
        n = self.n
        self.k, self.x, self.y = lax.rem(n, 2), lax.rem(n // 2, 2), n // 4
        k, x, y = self.k, self.x, self.y
        self.nx, self.ny = y * 4 + (1 - x) * 2 + k, (1 - y) * 4 + x * 2 + k
        self.nd, self.nc = (1 - y) * 4 + (1 - x) * 2 + k, y * 4 + x * 2 + 1 - k

    def z(self, j):
        return (self.n, lax.rem(self.e + j, self.experts))

    def greet(self, along_z):
        barrier = pltpu.get_barrier_semaphore()
        peers = [(self.nx, self.e), (self.ny, self.e), (self.nc, self.e)]
        if along_z:
            peers += [self.z(j) for j in range(1, self.experts)]
        for peer in peers:
            pl.semaphore_signal(barrier, inc=1, device_id=peer, device_id_type=MESH)
        pl.semaphore_wait(barrier, len(peers))


def when(condition):
    return pl.when(condition)


class Gather:
    def __init__(self, args, dense, items, nodes, experts):
        self.args, self.dense, self.items, self.experts = args, dense, items, experts
        self.outs = [
            jax.ShapeDtypeStruct(((nodes * experts if d else nodes),) + a.shape, a.dtype)
            for a, d in zip(args, dense)
        ]
        hbm = pl.BlockSpec(memory_space=pltpu.HBM)
        self.in_specs, self.out_specs = [hbm] * len(args), [hbm] * len(args)
        m = sum(len(item) for item in items)
        self.scratch = [
            pltpu.SemaphoreType.DMA((m, experts + 7)),
            pltpu.SemaphoreType.DMA((m, experts + 7)),
            pltpu.SemaphoreType.DMA((m,)),
        ]
        self.along_z = any(dense)
        self.steps = [self.along, self.across, self.corner, self.over, self.end]
        self.turns = len(items) + len(self.steps) - 1

    def bind(self, ins, outs, scratch, place):
        experts = self.experts
        send, recv, loc = scratch
        p, e = place, place.e

        def remote(source, target, item, kind, device):
            return pltpu.make_async_remote_copy(
                src_ref=source,
                dst_ref=target,
                send_sem=send.at[item, kind],
                recv_sem=recv.at[item, kind],
                device_id=device,
                device_id_type=MESH,
            )

        self.full = outs
        self.bound = [[] for _ in self.items]
        pieces = [(turn, piece) for turn, item in enumerate(self.items) for piece in item]
        for i, (turn, (arg, row, rows, col, columns)) in enumerate(pieces):
            dense = self.dense[arg]
            shard, whole = ins[arg], outs[arg]
            per = experts if dense else 1
            own = p.n * per + (e if dense else 0)

            def view(ref, lead, start=0, size=None, whole_rows=rows, row=row, col=col, columns=columns):
                return ref.at[lead, pl.ds(row + start, size or whole_rows), pl.ds(col, columns)]

            def bundle(m, view=view, whole=whole, per=per):
                return view(whole, pl.ds(m * per, per))

            def half(m, h, view=view, whole=whole, per=per, dense=dense, rows=rows):
                if dense:
                    return view(whole, pl.ds(m * per + h * (per // 2), per // 2))
                return view(whole, m, h * (rows // 2), rows // 2)

            mine = shard.at[pl.ds(row, rows), pl.ds(col, columns)]
            land = view(whole, own)
            local = pltpu.make_async_copy(mine, land, loc.at[i])
            z = []
            if dense:
                z = [remote(mine, land, i, j - 1, p.z(j)) for j in range(1, experts)]
            first, last = (bundle(p.n), bundle(p.n)) if dense else (mine, land)
            b = experts - 1
            xy = [remote(first, last, i, b, (p.nx, e)), remote(first, last, i, b + 1, (p.ny, e))]
            diag = [
                remote(half(p.nx, 0), half(p.nx, 0), i, b + 2, (p.ny, e)),
                remote(half(p.ny, 1), half(p.ny, 1), i, b + 3, (p.nx, e)),
            ]
            core = [remote(first, last, i, b + 4, (p.nc, e))] + [
                remote(bundle(m), bundle(m), i, b + 5 + j, (p.nc, e)) for j, m in enumerate((p.nx, p.ny, p.nd))
            ]
            self.bound[turn].append((local, z, xy, diag, core))

    def turn(self, now):
        for t in range(self.turns):

            @when(now == t)
            def _(t=t):
                for late, step in enumerate(self.steps):
                    if 0 <= t - late < len(self.items):
                        for piece in self.bound[t - late]:
                            step(*piece)

    def finish(self, now):
        pass

    def along(self, local, z, xy, diag, core):
        local.start()
        for copy in z:
            copy.start()

    def across(self, local, z, xy, diag, core):
        for copy in z:
            copy.wait()
        local.wait()
        xy[0].start()
        xy[1].start()
        core[0].start()

    def corner(self, local, z, xy, diag, core):
        for i in range(2):
            xy[i].wait()
            diag[i].start()
            core[1 + i].start()

    def over(self, local, z, xy, diag, core):
        diag[0].wait()
        diag[1].wait()
        core[3].start()

    def end(self, local, z, xy, diag, core):
        for copy in core:
            copy.wait()


class Exchange:
    along_z = True

    def __init__(self, pieces, sign, experts, start, turns, shape):
        self.args, self.sign, self.experts, self.start, self.turns = list(pieces), sign, experts, start, turns
        self.given = None
        self.outs = [jax.ShapeDtypeStruct(shape, bf16)] * (experts - 1)
        hbm = pl.BlockSpec(memory_space=pltpu.HBM)
        self.in_specs, self.out_specs = [hbm] * len(self.args), [hbm] * (experts - 1)
        self.scratch = [pltpu.SemaphoreType.DMA((experts,)), pltpu.SemaphoreType.DMA((experts,))]

    def bind(self, ins, outs, scratch, place):
        self.out, self.sems, self.place = outs, scratch, place
        if ins:
            self.sources = ins

    def copies(self):
        return [
            pltpu.make_async_remote_copy(
                src_ref=source,
                dst_ref=self.out[j],
                send_sem=self.sems[0].at[j],
                recv_sem=self.sems[1].at[j],
                device_id=self.place.z((self.sign * (j + 1)) % self.experts),
                device_id_type=MESH,
            )
            for j, source in enumerate(self.sources)
        ]

    def send(self):
        for copy in self.copies():
            copy.start()

    def turn(self, now):
        if self.start is not None:

            @when(now == self.start)
            def _():
                self.send()

    def finish(self, now):
        @when(now == self.turns - 1)
        def _():
            for copy in self.copies():
                copy.wait()


class Scatter:
    RING, SPREAD_RING, CORE_RING = 6, 8, 4

    def __init__(self, parts, half, experts, outs, store, start=0, made=None, spread=False):
        self.experts, self.outs, self.store, self.start, self.made = experts, outs, store, start, made
        self.parts = parts
        self.given = []
        self.args = [p[0] for p in parts if p[0] is not None]
        h = half
        self.starts = [sum(p[3] for p in parts[:a]) for a in range(len(parts) + 1)]
        m = self.m = self.starts[-1]
        self.m_z = sum(p[3] for p in parts if p[1])
        unit = h[1:]
        ring = self.ring = min(self.SPREAD_RING if spread else self.RING, m)
        self.core_ring = min(self.CORE_RING, m)
        self.in_specs = [pl.BlockSpec(memory_space=pltpu.HBM)] * len(self.args)
        self.out_specs = [pl.BlockSpec(memory_space=pltpu.VMEM)] * len(outs)
        kinds = 7 + experts
        self.scratch = [
            pltpu.VMEM(made or (ring, 4, 2) + h, bf16),
            pltpu.VMEM((self.core_ring, 4, 2) + h, bf16),
            pltpu.VMEM((ring, 2) + h, bf16),
            pltpu.VMEM((ring, 2) + h, bf16),
            pltpu.VMEM((ring,) + h, bf16),
            pltpu.VMEM((ring,) + h, bf16),
            pltpu.SemaphoreType.DMA((m, kinds)),
            pltpu.SemaphoreType.DMA((m, kinds)),
            pltpu.SemaphoreType.DMA((m,)),
        ]
        if self.m_z:
            self.scratch.append(pltpu.VMEM((self.m_z, experts - 1) + unit, bf16))
            self.scratch.append(pltpu.VMEM((self.m_z, experts) + unit, bf16))
        self.stages = (0, 1, 3, 5, 7) if spread else (0, 1, 2, 3, 4)
        self.turns = start + m + self.stages[4 if self.m_z else 3]
        self.along_z = self.m_z > 0

    def bind(self, ins, outs, scratch, place):
        ins = list(ins)
        given = list(self.given)
        self.sources = [given.pop(0) if p[0] is None else ins.pop(0) for p in self.parts] if not self.made else []
        self.out, self.place = outs, place
        self.own, self.rc, self.rx, self.ry, self.lx, self.ly, self.sent, self.recv, self.loc = scratch[:9]
        self.rz, self.zs = scratch[9:] if self.m_z else (None, None)

    def slot(self, i):
        return lax.rem(i, self.ring)

    def remote(self, source, target, item, kind, device):
        return pltpu.make_async_remote_copy(
            src_ref=source,
            dst_ref=target,
            send_sem=self.sent.at[item, kind],
            recv_sem=self.recv.at[item, kind],
            device_id=device,
            device_id_type=MESH,
        )

    def at(self, i, site, *more):
        return (i, site, self.place.k) + more if self.made else (self.slot(i), site) + more

    def first(self, source, i, chunk):
        p = self.place
        land = self.rc.at[lax.rem(i, self.core_ring)]
        if self.made:
            return [self.remote(self.own.at[i, :, 1 - p.k], land, i, 0, (p.nc, p.e))]
        part = lambda core: source.at[:, core, :, :, chunk]
        local = pltpu.make_async_copy(part(p.k), self.own.at[self.slot(i)], self.loc.at[i])
        return [self.remote(part(1 - p.k), land, i, 0, (p.nc, p.e)), local]

    def sites(self):
        p = self.place
        return p.y * 2 + p.x, p.y * 2 + 1 - p.x, (1 - p.y) * 2 + p.x, (1 - p.y) * 2 + 1 - p.x

    def round_one(self, i):
        p = self.place
        b = self.slot(i)
        _, to_x, to_y, diag = self.sites()
        own = lambda *at: self.own.at[self.at(i, *at)]
        return [
            self.remote(own(diag, 0), self.rx.at[b, 0], i, 1, (p.nx, p.e)),
            self.remote(own(diag, 1), self.ry.at[b, 0], i, 2, (p.ny, p.e)),
            self.remote(own(to_x, 0), self.rx.at[b, 1], i, 3, (p.nx, p.e)),
            self.remote(own(to_y, 1), self.ry.at[b, 1], i, 4, (p.ny, p.e)),
        ]

    def round_two(self, i):
        p = self.place
        b = self.slot(i)
        _, to_x, to_y, _ = self.sites()
        return [
            self.remote(self.own.at[self.at(i, to_x, 1)], self.lx.at[b], i, 5, (p.nx, p.e)),
            self.remote(self.own.at[self.at(i, to_y, 0)], self.ly.at[b], i, 6, (p.ny, p.e)),
        ]

    def round_z(self, i):
        p = self.place
        return [
            self.remote(self.zs.at[i, lax.rem(p.e + j, self.experts)], self.rz.at[i, j - 1], i, 6 + j, p.z(j))
            for j in range(1, self.experts)
        ]

    def turn(self, now):
        limits = (self.m, self.m, self.m, self.m, self.m_z)
        steps = (self.load, self.chip, self.cross, self.plane, self.column)
        for limit, late, step in zip(limits, self.stages, steps):
            i = now - self.start - late
            if limit:

                @when(jnp.logical_and(i >= 0, i < limit))
                def _(step=step, i=i):
                    step(i)

    def finish(self, now):
        pass

    def load(self, i):
        if self.made:
            self.first(None, i, 0)[0].start()
            return
        for a, source in enumerate(self.sources):

            @when(jnp.logical_and(i >= self.starts[a], i < self.starts[a + 1]))
            def _(a=a, source=source):
                for copy in self.first(source, i, i - self.starts[a] + self.parts[a][2]):
                    copy.start()

    def chip(self, i):
        for copy in self.first(None if self.made else self.sources[0], i, 0):
            copy.wait()

        def sum_one(q, _):
            at = self.at(i, q)
            self.own[at] = add(self.own[at], self.rc[lax.rem(i, self.core_ring), q]).astype(bf16)
            return 0

        lax.fori_loop(0, 4, sum_one, 0)
        for copy in self.round_one(i):
            copy.start()

    def cross(self, i):
        one = self.round_one(i)
        two = self.round_two(i)
        b = self.slot(i)
        _, to_x, to_y, _ = self.sites()
        for copy in one:
            copy.wait()
        at_x, at_y = self.at(i, to_x, 1), self.at(i, to_y, 0)
        self.own[at_x] = add(self.own[at_x], self.ry[b, 0]).astype(bf16)
        two[0].start()
        self.own[at_y] = add(self.own[at_y], self.rx[b, 0]).astype(bf16)
        two[1].start()

    def plane(self, i):
        for copy in self.round_two(i):
            copy.wait()
        mine, _, _, _ = self.sites()
        b = self.slot(i)
        sums = lambda: (
            add(self.own[self.at(i, mine, 0)], self.rx[b, 1], self.ly[b]),
            add(self.own[self.at(i, mine, 1)], self.lx[b], self.ry[b, 1]),
        )
        if self.m_z:

            @when(i < self.m_z)
            def _():
                s = self.experts // 2
                for h, total in enumerate(sums()):
                    self.zs[i, h * s : (h + 1) * s] = total.astype(bf16)
                for copy in self.round_z(i):
                    copy.start()

        if self.m_z < self.m:

            @when(i >= self.m_z)
            def _():
                self.store(self.out, i, sums())

    def column(self, i):
        for copy in self.round_z(i):
            copy.wait()
        terms = [self.zs[i, self.place.e]] + [self.rz[i, j] for j in range(self.experts - 1)]
        self.store(self.out, i, add(*terms))


class Along:
    along_z = True

    def __init__(self, shares, experts, outs, store, turns):
        self.args, self.experts, self.outs, self.store, self.turns = [shares], experts, outs, store, turns
        self.in_specs = [pl.BlockSpec(memory_space=pltpu.HBM)]
        self.out_specs = [pl.BlockSpec(memory_space=pltpu.VMEM)] * len(outs)
        self.items = shares.shape[1]
        self.scratch = [
            pltpu.VMEM(shares.shape, bf16),
            pltpu.SemaphoreType.DMA((experts,)),
            pltpu.SemaphoreType.DMA((experts,)),
        ]

    def bind(self, ins, outs, scratch, place):
        self.source, self.out, self.place = ins[0], outs, place
        self.land, self.sent, self.recv = scratch

    def copies(self):
        p = self.place
        copies = [pltpu.make_async_copy(self.source.at[p.e], self.land.at[0], self.recv.at[0])]
        return copies + [
            pltpu.make_async_remote_copy(
                src_ref=self.source.at[lax.rem(p.e + j, self.experts)],
                dst_ref=self.land.at[j],
                send_sem=self.sent.at[j],
                recv_sem=self.recv.at[j],
                device_id=p.z(j),
                device_id_type=MESH,
            )
            for j in range(1, self.experts)
        ]

    def turn(self, now):
        @when(now == 0)
        def _():
            for copy in self.copies():
                copy.start()

    def finish(self, now):
        @when(now == self.turns - 1)
        def _():
            for copy in self.copies():
                copy.wait()
            for i in range(self.items):
                self.store(self.out, i, add(*(self.land[j, i] for j in range(self.experts))))


def add(*terms):
    return functools.reduce(jnp.add, [t.astype(f32) for t in terms])


def call(
    name, steps, body, args, in_specs, outs, out_specs, scratch, moves, collective_id, experts, flops, given=None
):
    total = max([steps] + [m.turns for m in moves])

    def hold(spec):
        if spec.block_shape is None:
            return spec
        index = spec.index_map
        return pl.BlockSpec(spec.block_shape, lambda j: index(jnp.minimum(j, steps - 1)))

    join = lambda what: [x for m in moves for x in getattr(m, what)]

    def kernel(*refs):
        refs = list(refs)
        take = lambda group: [refs.pop(0) for _ in group]
        ins, m_ins = take(args), [take(m.args) for m in moves]
        os, m_os = take(outs), [take(m.outs) for m in moves]
        own, m_own = take(scratch), [take(m.scratch) for m in moves]
        now = pl.program_id(0)
        if moves:
            place = Place(experts)
            if given is not None:
                given(ins, os, own)
            for m, a, o, r in zip(moves, m_ins, m_os, m_own):
                m.bind(a, o, r, place)

            @when(now == 0)
            def _():
                place.greet(any(m.along_z for m in moves))

            for m in moves:
                m.turn(now)
        if body is not None:

            @when(now < steps)
            def _():
                body(now, steps, *ins, *os, *own)

        for m in moves:
            m.finish(now)

    results = pl.pallas_call(
        kernel,
        grid=(total,),
        out_shape=list(outs) + join("outs"),
        in_specs=[hold(s) for s in in_specs] + join("in_specs"),
        out_specs=[hold(s) for s in out_specs] + join("out_specs"),
        scratch_shapes=list(scratch) + join("scratch"),
        cost_estimate=pl.CostEstimate(flops=flops, bytes_accessed=32 * MIB, transcendentals=0),
        compiler_params=pltpu.CompilerParams(
            vmem_limit_bytes=60 * MIB,
            **({"collective_id": collective_id, "has_side_effects": True} if moves else {}),
        ),
        name=name,
    )(*args, *join("args"))
    return list(results)


def masks():
    lanes = lax.broadcasted_iota(jnp.int32, (1, PAIR), 1)
    return [(lanes // HD == h).astype(bf16) for h in range(2)]


def causal(scores_t, start):
    keys = lax.broadcasted_iota(jnp.int32, scores_t.shape, 0)
    queries = lax.broadcasted_iota(jnp.int32, scores_t.shape, 1) + start
    return jnp.where(keys <= queries, scores_t, -jnp.inf)


def attend_pair(q, k, v):
    q = q * (1.0 / math.sqrt(HD))
    vt = v.T
    length = q.shape[0]
    outs, tops = [], []
    for h, mask in enumerate(masks()):
        kh = k * mask
        row, logs = [], []
        for start in range(0, length, QB):
            end = start + QB
            scores = causal(outer_nt(kh[:end], q[start:end]), start)
            top = jnp.max(scores, axis=0, keepdims=True)
            expd = jnp.exp(scores - top)
            total = jnp.sum(expd, axis=0, keepdims=True)
            probs = (expd / total).astype(bf16)
            row.append(matmul(vt[h * HD : (h + 1) * HD, :end], probs))
            logs.append(top + jnp.log(total))
        outs.append(jnp.concatenate(row, axis=1))
        tops.append(jnp.concatenate(logs, axis=1))
    return jnp.concatenate(outs, axis=0).T.astype(bf16), jnp.concatenate(tops, axis=0)


def columns_of(*rows):
    return [jnp.broadcast_to(r[...].astype(f32), (128, r.shape[1])).T.astype(jnp.int32) for r in rows]


class Forward:
    def __init__(self, length, width, experts, devices, capacity, ff, gather, leave):
        self.length, self.width, self.experts, self.capacity = length, width, experts, capacity
        self.gather, self.leave = gather, leave
        pairs = width // PAIR
        share = self.share = width // devices
        self.blocks = ff // BLOCK
        self.per_block = BLOCK * devices // ff
        self.at_norm, self.at_qkv = 4, 6
        self.at_heads = self.at_qkv + 1
        self.per_turn = 2
        self.at_out = self.at_heads + length // SEQ * pairs // self.per_turn
        self.at_leave = self.at_out + 1
        self.at_mlp = max(self.at_leave + 2, self.DENSE_ITEMS + 3)
        self.steps = self.at_mlp + self.blocks
        slots = experts * capacity
        rows = lambda c, t: jax.ShapeDtypeStruct((length, c), t)
        piece = (capacity, 2 * width)
        self.kept = 1 if leave else experts
        self.outs = [
            rows(3 * width, bf16),
            jax.ShapeDtypeStruct((length // SEQ * pairs, 2, SEQ), f32),
            rows(width, bf16),
            rows(width, f32),
            rows(width, bf16),
            rows(slots, bf16),
            rows(128, f32),
            rows(width, f32),
            rows(width, f32),
        ] + [jax.ShapeDtypeStruct(piece, bf16)] * self.kept
        if gather:
            stages = [(devices, self.per_block * share * devices // ff * (ff // devices // 128), 128)]
            stages = [(devices, BLOCK // 128 * share, 128), (self.per_block, width, 128)]
            targets = [(devices, width, 128)] * 2
        else:
            stages, targets = [(width, BLOCK)] * 2, [(width, ff)] * 2
        self.targets = [jax.ShapeDtypeStruct(t, bf16) for t in targets]
        self.scratch = [pltpu.VMEM(piece, bf16)] * (experts - self.kept) + [
            pltpu.VMEM((devices, share, 128), bf16),
            pltpu.VMEM((devices, share, 3 * width), bf16),
            pltpu.VMEM((devices, share, width), bf16),
            pltpu.VMEM((8, width), f32),
            pltpu.VMEM((length, width), bf16),
            pltpu.SemaphoreType.DMA((3,)),
            pltpu.VMEM((length, width), bf16),
            pltpu.VMEM((length, width), bf16),
            pltpu.VMEM((width, length), bf16),
            pltpu.VMEM((width, length), bf16),
            pltpu.VMEM((2, devices, share, BLOCK), bf16),
            pltpu.VMEM((2, self.per_block, ff // devices, width), bf16),
            pltpu.VMEM((2,) + stages[0], bf16),
            pltpu.VMEM((2,) + stages[1], bf16),
            pltpu.SemaphoreType.DMA((2, 2)),
            pltpu.SemaphoreType.DMA((2, 2)),
        ]

    DENSE_ITEMS = 12

    def __call__(self, now, steps, tok, cot, routes, dropped, *refs):
        refs = list(refs)
        take = lambda count: [refs.pop(0) for _ in range(count)]
        full = self.gather.full[:5] if self.gather else take(5)
        qkv, lse, att, after, mixed, disp, info, dense_out, grad_mixed = take(9)
        leave = take(self.kept)
        targets = take(2)
        leave += take(self.experts - self.kept)
        ws, wq, wo, gains, attn_in, sems, gd, ge, xt, gt, w1, w2, stage_1, stage_2, w_sems, d_sems = refs
        width, length = self.width, self.length
        loads = [pltpu.make_async_copy(a, b, sems.at[i]) for i, (a, b) in enumerate(zip(full, (ws, wq, wo)))]

        def weights(block):
            at = lax.rem(block, 2)
            cols = pl.ds(pl.multiple_of(block * BLOCK, BLOCK), BLOCK)
            return [
                pltpu.make_async_copy(full[3].at[:, :, cols], w1.at[at], w_sems.at[at, 0]),
                pltpu.make_async_copy(full[4].at[pl.ds(block * self.per_block, self.per_block)], w2.at[at], w_sems.at[at, 1]),
            ]

        def flush(block):
            at = lax.rem(block, 2)
            if self.gather:
                size = BLOCK // 128 * self.share
                first = targets[0].at[:, pl.ds(pl.multiple_of(block * size, size), size)]
                second = targets[1].at[pl.ds(block * self.per_block, self.per_block)]
            else:
                cols = pl.ds(pl.multiple_of(block * BLOCK, BLOCK), BLOCK)
                first, second = targets[0].at[:, cols], targets[1].at[:, cols]
            return [
                pltpu.make_async_copy(stage_1.at[at], first, d_sems.at[at, 0]),
                pltpu.make_async_copy(stage_2.at[at], second, d_sems.at[at, 1]),
            ]

        @when(now == self.at_norm)
        def _():
            loads[0].start()
            loads[0].wait()
            gains[...] = ws[...].reshape(width, 128).astype(f32).T[:8]
            normed, _ = normalize(tok[...].astype(f32))
            attn_in[...] = (normed * gains[0:1]).astype(bf16)

        @when(now == self.at_qkv)
        def _():
            loads[1].start()
            loads[1].wait()

            def columns(c, _):
                cols = pl.ds(pl.multiple_of(c * BLOCK, BLOCK), BLOCK)
                weights = wq[:, :, cols].reshape(width, BLOCK)
                qkv[:, cols] = matmul(attn_in[...], weights).astype(bf16)
                return 0

            lax.fori_loop(0, 3 * width // BLOCK, columns, 0)

        @when(jnp.logical_and(now >= self.at_heads, now < self.at_out))
        def _():
            pairs = width // PAIR

            def pair(i, _):
                at = (now - self.at_heads) * self.per_turn + i
                seq, at_pair = at // pairs, lax.rem(at, pairs)
                rows = pl.ds(pl.multiple_of(seq * SEQ, SEQ), SEQ)
                cols = lambda part: pl.ds(pl.multiple_of(part * width + at_pair * PAIR, PAIR), PAIR)
                out, tops = attend_pair(qkv[rows, cols(0)], qkv[rows, cols(1)], qkv[rows, cols(2)])
                att[rows, cols(0)] = out
                lse[at] = tops
                return 0

            lax.fori_loop(0, self.per_turn, pair, 0)

        @when(now == self.at_out)
        def _():
            loads[2].start()
            loads[2].wait()
            self.route(tok, cot, routes, dropped, att, wo, ws, gains, after, mixed, gd, ge, disp, info)

        @when(now == self.at_leave)
        def _():
            for h, values in enumerate((mixed, ge)):
                placed = product_tn(disp[...], values[...]).astype(bf16)
                for j in range(self.experts):
                    leave[j][:, h * width : (h + 1) * width] = placed[j * self.capacity : (j + 1) * self.capacity]
            if self.leave:
                self.leave.send()

        @when(now == self.at_mlp - 1)
        def _():
            xt[...] = mixed[...].T
            gt[...] = gd[...].T
            dense_out[...] = jnp.zeros_like(dense_out)
            grad_mixed[...] = jnp.zeros_like(grad_mixed)

        @when(jnp.logical_and(now >= self.at_mlp, now < self.at_mlp + self.blocks))
        def _():
            block = now - self.at_mlp
            at = lax.rem(block, 2)

            @when(block == 0)
            def _():
                for copy in weights(0):
                    copy.start()

            @when(block + 1 < self.blocks)
            def _():
                for copy in weights(block + 1):
                    copy.start()

            for copy in weights(block):
                copy.wait()

            @when(block >= 2)
            def _():
                for copy in flush(block - 2):
                    copy.wait()

            d1, d2 = mlp_block(
                mixed,
                gd,
                xt,
                gt,
                w1[at].reshape(width, BLOCK),
                w2[at].reshape(BLOCK, width),
                dense_out,
                grad_mixed,
            )
            if self.gather:
                share = self.share
                for c in range(BLOCK // 128):
                    cols = slice(c * 128, (c + 1) * 128)
                    for s in range(width // share):
                        stage_1[at, s, c * share : (c + 1) * share] = d1[s * share : (s + 1) * share, cols]
                    stage_2[at, c] = d2[:, cols]
            else:
                stage_1[at] = d1
                stage_2[at] = d2
            for copy in flush(block):
                copy.start()

            @when(block == self.blocks - 1)
            def _():
                for last in (self.blocks - 2, self.blocks - 1):
                    for copy in flush(last):
                        copy.wait()

    def route(self, tok, cot, routes, dropped, att, wo, ws, gains, after, mixed, gd, ge, disp, info):
        width, length, experts = self.width, self.length, self.experts
        route, drop = columns_of(routes, dropped)
        after[...] = tok[...].astype(f32) + matmul(att[...], wo[...].reshape(width, width))
        normed, _ = normalize(after[...])
        mixed[...] = (normed * gains[1:2]).astype(bf16)
        logits = matmul(mixed[...], ws[...].reshape(width, 128))
        lane = lax.broadcasted_iota(jnp.int32, (length, 128), 1)

        def softmax(first, last):
            inside = jnp.logical_and(lane >= first, lane < last)
            top = jnp.max(jnp.where(inside, logits, -jnp.inf), axis=1, keepdims=True)
            expd = jnp.where(inside, jnp.exp(jnp.where(inside, logits, top) - top), 0.0)
            return expd / jnp.sum(expd, axis=1, keepdims=True)

        probs, coef = softmax(2, 2 + experts), softmax(2 + experts, 4 + experts)
        info[...] = probs + coef
        chosen = jnp.where(lane - 2 == route, 1.0, 0.0)
        over_lanes = lambda a: jnp.sum(a, axis=1, keepdims=True)
        gate = over_lanes(probs * chosen) * (1 - drop[:, :1]).astype(f32)
        coef_0 = over_lanes(jnp.where(lane == 2 + experts, coef, 0.0))
        coef_1 = over_lanes(jnp.where(lane == 3 + experts, coef, 0.0))
        grad = cot[...].astype(f32)
        gd[...] = (coef_0 * grad).astype(bf16)
        ge[...] = (coef_1 * gate * grad).astype(bf16)
        square = lambda d: lax.broadcasted_iota(jnp.int32, (length, length), d)
        earlier = jnp.where(square(0) > square(1), 1.0, 0.0).astype(bf16)
        position = over_lanes(chosen * matmul(earlier, chosen.astype(bf16))).astype(jnp.int32)
        turn = route[:, :1] - lax.axis_index("expert")
        target = jnp.where(turn < 0, turn + experts, turn) * self.capacity + position
        slot = lax.broadcasted_iota(jnp.int32, (length, experts * self.capacity), 1)
        disp[...] = jnp.where(slot == target, 1.0, 0.0).astype(bf16)


def attend_pair_backward(q, k, v, g, lse):
    scaling = 1.0 / math.sqrt(HD)
    qs = q * scaling
    kt = k.T
    length = q.shape[0]
    grad_k = [0.0] * (length // QB)
    grad_v = [0.0] * (length // QB)
    grad_q = []
    for h, mask in enumerate(masks()):
        kh, vh, qh, gh = k * mask, v * mask, q * mask, g * mask
        row = []
        for c, start in enumerate(range(0, length, QB)):
            end = start + QB
            scores = causal(outer_nt(kh[:end], qs[start:end]), start)
            probs = jnp.exp(scores - lse[h : h + 1, start:end])
            grad_probs = outer_nt(vh[:end], g[start:end])
            delta = jnp.sum(probs * grad_probs, axis=0, keepdims=True)
            grad_scores = (probs * (grad_probs - delta)).astype(bf16)
            more_v = matmul(probs.astype(bf16), gh[start:end])
            more_k = matmul(grad_scores, qh[start:end])
            for b in range(c + 1):
                rows = slice(b * QB, (b + 1) * QB)
                grad_v[b] = grad_v[b] + more_v[rows]
                grad_k[b] = grad_k[b] + more_k[rows]
            row.append(matmul(kt[h * HD : (h + 1) * HD, :end], grad_scores))
        grad_q.append(jnp.concatenate(row, axis=1))
    return (
        (jnp.concatenate(grad_q, axis=0).T * scaling).astype(bf16),
        (jnp.concatenate(grad_k, axis=0) * scaling).astype(bf16),
        jnp.concatenate(grad_v, axis=0).astype(bf16),
    )


def thirds(values):
    parts = []
    for _ in range(3):
        parts.append(values.astype(bf16))
        values = values - parts[-1].astype(f32)
    return parts


class Back:
    def __init__(self, length, width, experts, devices, capacity):
        self.length, self.width, self.experts, self.capacity = length, width, experts, capacity
        self.devices, self.share = devices, width // devices
        self.pairs = width // PAIR
        self.columns = 3 * PAIR
        self.firsts = width // self.columns
        self.rest = width - self.firsts * self.columns
        self.items = self.firsts + self.pairs + 1
        self.heads_at = 4
        self.last = self.heads_at + self.pairs
        self.steps = self.last + 1
        self.first_item = self.heads_at
        self.outs = [
            jax.ShapeDtypeStruct((length, width), bf16),
            jax.ShapeDtypeStruct((length, width), f32),
        ]
        slots = experts * capacity
        self.scratch = [
            pltpu.VMEM((slots, 2 * width), bf16),
            pltpu.VMEM((length, width), f32),
            pltpu.VMEM((length, width), f32),
            pltpu.VMEM((devices, self.share, 128), bf16),
            pltpu.VMEM((devices, self.share, width), bf16),
            pltpu.VMEM((2, devices, self.share, self.columns), bf16),
            pltpu.VMEM((8, width), f32),
            pltpu.VMEM((128, width), f32),
            pltpu.VMEM((width, length), bf16),
            pltpu.VMEM((length, width), bf16),
            pltpu.SemaphoreType.DMA((5 + experts,)),
            pltpu.SemaphoreType.DMA((2, 3)),
        ]

    def made(self):
        chips = (4, 2, 2, self.experts // 2) if self.devices == 8 * self.experts else (self.devices,)
        return (self.items,) + chips + (self.share, self.columns)

    def final_outs(self):
        share, width = self.share, self.width
        return [jax.ShapeDtypeStruct((share, c), f32) for c in (3 * width, width, 128)]

    def store(self, outs, i, value):
        d_qkv, d_out, d_small = outs
        final = self.items - 1

        for f in range(self.firsts):

            @when(i == f)
            def _(f=f):
                d_out[:, f * self.columns : (f + 1) * self.columns] = value

        @when(jnp.logical_and(i >= self.firsts, i < final))
        def _():
            for p in range(3):
                at = pl.multiple_of(p * self.width + (i - self.firsts) * PAIR, PAIR)
                d_qkv[:, pl.ds(at, PAIR)] = value[:, p * PAIR : (p + 1) * PAIR]

        @when(i == final)
        def _():
            d_out[:, self.firsts * self.columns :] = value[:, : self.rest]
            d_small[...] = value[:, self.rest : self.rest + 128]

    def __call__(self, now, steps, *refs):
        experts, width, length = self.experts, self.width, self.length
        refs = list(refs)
        tok, cot, routes, dropped, qkv, lse, att, mixed_in, disp, info = refs[:10]
        small_hbm, qkv_hbm, out_hbm, dense_hbm, grad_hbm, after_hbm = refs[10:16]
        came_hbm = refs[16 : 16 + experts]
        mixed, tokens_grad, *rest = refs[16 + experts :]
        if self.moves:
            made = self.moves[-1].own
        else:
            made = rest.pop(0)
        came, dense, grads, ws, wo, wq, gains, d_heads, attn_in_t, grad_att, sems, wq_sems = rest
        fetch = lambda a, b, i: pltpu.make_async_copy(a, b, sems.at[i])
        capacity = self.capacity
        loads = [fetch(came_hbm[j], came.at[pl.ds(j * capacity, capacity)], j) for j in range(experts)]
        loads += [
            fetch(a, b, experts + i)
            for i, (a, b) in enumerate(
                ((dense_hbm, dense), (grad_hbm, grads), (after_hbm, tokens_grad), (small_hbm, ws), (out_hbm, wo))
            )
        ]

        def pair_weights(pair):
            slot = lax.rem(pair, 2)
            return [
                pltpu.make_async_copy(
                    qkv_hbm.at[:, :, pl.ds(pl.multiple_of(p * width + pair * PAIR, PAIR), PAIR)],
                    wq.at[slot, :, :, pl.ds(p * PAIR, PAIR)],
                    wq_sems.at[slot, p],
                )
                for p in range(3)
            ]

        put = lambda i, columns, values: self.put(made, i, columns, values)
        lane = lax.broadcasted_iota(jnp.int32, (length, 128), 1)
        over_lanes = lambda a: jnp.sum(a, axis=1, keepdims=True)

        @when(now == 0)
        def _():
            for copy in loads + pair_weights(0):
                copy.start()

        @when(now == 1)
        def _():
            for copy in loads:
                copy.wait()
            probs = jnp.where(jnp.logical_and(lane >= 2, lane < 2 + experts), info[...], 0.0)
            coef_0 = over_lanes(jnp.where(lane == 2 + experts, info[...], 0.0))
            coef_1 = over_lanes(jnp.where(lane == 3 + experts, info[...], 0.0))
            route, drop = columns_of(routes, dropped)
            chosen = jnp.where(lane - 2 == route, 1.0, 0.0)
            kept = (1 - drop[:, :1]).astype(f32)
            gate_prob = over_lanes(probs * chosen)
            gate = gate_prob * kept
            grad = cot[...].astype(f32)
            expert_tok = matmul(disp[...], came[:, :width])
            mixed[...] = (tokens_grad[...] + coef_0 * dense[...] + (coef_1 * gate) * expert_tok).astype(bf16)
            shared = over_lanes(grad * expert_tok)
            grad_0, grad_1 = over_lanes(grad * dense[...]), shared * gate
            both = coef_0 * grad_0 + coef_1 * grad_1
            grad_gate = shared * coef_1 * kept
            logits = jnp.where(
                jnp.logical_and(lane >= 2, lane < 2 + experts), (grad_gate * gate_prob) * (chosen - probs), 0.0
            )
            logits = jnp.where(lane == 2 + experts, coef_0 * (grad_0 - both), logits)
            logits = jnp.where(lane == 3 + experts, coef_1 * (grad_1 - both), logits)
            pieces = thirds(logits)
            d_heads[...] = add(*(product_tn(p, mixed_in[...]) for p in pieces))
            weights = ws[...].reshape(width, 128)
            grads[...] = (
                grads[...] + matmul(disp[...], came[:, width:]) + add(*(outer_nt(p, weights) for p in pieces))
            )
            gains[...] = weights.astype(f32).T[:8]

        @when(now == 2)
        def _():
            normed, scale = normalize(tokens_grad[...])
            d_heads[1:2] = jnp.sum(grads[...] * normed, axis=0, keepdims=True)
            grads[...] = cot[...].astype(f32) + norm_back(grads[...] * gains[1:2], normed, scale)
            normed, _ = normalize(tok[...].astype(f32))
            attn_in_t[...] = (normed * gains[0:1]).astype(bf16).T

        @when(now == 3)
        def _():
            grad_attn = grads[...].astype(bf16)
            grad_att[...] = outer_nt(grad_attn, wo[...].reshape(width, width)).astype(bf16)
            d_out = product_tn(att[...], grad_attn).astype(bf16)
            for f in range(self.firsts):
                put(f, slice(None), d_out[:, f * self.columns : (f + 1) * self.columns])
            put(self.items - 1, slice(0, self.rest), d_out[:, self.firsts * self.columns :])
            dense[...] = jnp.zeros_like(dense)

        @when(jnp.logical_and(now >= self.heads_at, now < self.last))
        def _():
            pair = now - self.heads_at
            cols = lambda part: pl.ds(pl.multiple_of(part * width + pair * PAIR, PAIR), PAIR)
            d_pair = attend_pair_backward(
                qkv[:, cols(0)], qkv[:, cols(1)], qkv[:, cols(2)], grad_att[:, cols(0)], lse[pair]
            )
            d_pair = jnp.concatenate(d_pair, axis=1)
            for copy in pair_weights(pair):
                copy.wait()

            @when(pair + 1 < self.pairs)
            def _():
                for copy in pair_weights(pair + 1):
                    copy.start()

            put(pair + self.firsts, slice(None), matmul(attn_in_t[...], d_pair).astype(bf16))
            dense[...] += outer_nt(d_pair, wq[lax.rem(pair, 2)].reshape(width, self.columns))

        @when(now == self.last)
        def _():
            normed, scale = normalize(tok[...].astype(f32))
            d_heads[0:1] = jnp.sum(dense[...] * normed, axis=0, keepdims=True)
            put(self.items - 1, slice(self.rest, self.rest + 128), d_heads[...].T.astype(bf16))
            if self.rest + 128 < self.columns:
                spare = self.columns - self.rest - 128
                put(self.items - 1, slice(self.rest + 128, None), jnp.zeros((width, spare), bf16))
            tokens_grad[...] = grads[...] + norm_back(dense[...] * gains[0:1], normed, scale)

    def put(self, made, i, columns, values):
        lead = made.shape[1:-1]
        at = (i,) + (slice(None),) * len(lead) + (columns,)
        made[at] = values.reshape(lead + values.shape[1:])


def gelu_both(v):
    c = math.sqrt(2.0 / math.pi)
    square = v * v
    t = jnp.tanh(c * (v + 0.044715 * (square * v)))
    half = 0.5 * (1.0 + t)
    slope = half + 0.5 * v * (1.0 - t * t) * (c * (1.0 + (3 * 0.044715) * square))
    return v * half, slope


def mlp_block(x, g, xt, gt, w1, w2, out_sum, back_sum):
    hidden, slope = gelu_both(matmul(x[...], w1))
    hidden = hidden.astype(bf16)
    grad_pre = (slope * outer_nt(g[...], w2)).astype(bf16)
    out_sum[...] += matmul(hidden, w2)
    back_sum[...] += outer_nt(grad_pre, w1)
    return matmul(xt[...], grad_pre).astype(bf16), matmul(gt[...], hidden).astype(bf16)


class Experts:
    TURNS = 6

    def __init__(self, pieces, blocks, width, size, chunks, back):
        self.parts, self.piece = len(pieces), pieces[0].shape
        self.blocks, self.width, self.size, self.back = blocks, width, size, back
        rows = self.parts * self.piece[0]
        if chunks:
            self.block = (2, size // 256, chunks, width // chunks, 128)
            whole = (blocks // 2, 2) + self.block
        else:
            self.block = (width, size)
            whole = (blocks,) + self.block
        piece = jax.ShapeDtypeStruct(self.piece, bf16)
        self.outs = [piece] * self.parts + [jax.ShapeDtypeStruct(whole, bf16)] * 2
        self.scratch = (
            [pltpu.VMEM(self.piece, bf16)] * self.parts
            + [pltpu.VMEM((rows, width), bf16)] * 2
            + [pltpu.VMEM((width, rows), bf16)] * 2
            + [pltpu.VMEM((rows, width), f32)] * 2
            + [pltpu.VMEM((2,) + self.block, bf16)] * 2
            + [pltpu.SemaphoreType.DMA((2, 2)), pltpu.SemaphoreType.DMA((self.parts,))]
            + [pltpu.VMEM((2, width, size), bf16), pltpu.VMEM((2, size, width), bf16)]
            + [pltpu.SemaphoreType.DMA((2, 2))]
        )

    def __call__(self, now, steps, *refs):
        refs = list(refs)
        take = lambda count: [refs.pop(0) for _ in range(count)]
        pieces, full = take(self.parts), take(2)
        kept, targets, results = take(self.parts), take(2), take(self.parts)
        x, g, xt, gt, out_sum, back_sum, stage_1, stage_2, sems, kept_sems, w1, w2, w_sems = refs
        width, size = self.width, self.piece[0]

        def flush(step):
            at = lax.rem(step, 2)
            where = (step // 2, at) if len(self.block) > 2 else (step,)
            return [
                pltpu.make_async_copy(stage.at[at], target.at[where], sems.at[at, i])
                for i, (stage, target) in enumerate(zip((stage_1, stage_2), targets))
            ]

        def weights(step):
            at = lax.rem(step, 2)
            return [
                pltpu.make_async_copy(a.at[step], b.at[at], w_sems.at[at, i])
                for i, (a, b) in enumerate(zip(full, (w1, w2)))
            ]

        @when(now == 0)
        def _():
            for copy in weights(0):
                copy.start()
            for j, piece in enumerate(pieces):
                x[j * size : (j + 1) * size] = piece[:, :width]
                g[j * size : (j + 1) * size] = piece[:, width:]
            xt[...] = x[...].T
            gt[...] = g[...].T
            out_sum[...] = jnp.zeros_like(out_sum)
            back_sum[...] = jnp.zeros_like(back_sum)

        def block(step, _):
            for copy in weights(step):
                copy.wait()

            @when(step + 1 < self.blocks)
            def _():
                for copy in weights(step + 1):
                    copy.start()

            @when(step >= 2)
            def _():
                for copy in flush(step - 2):
                    copy.wait()

            slot = lax.rem(step, 2)
            for stage, d in zip((stage_1, stage_2), mlp_block(x, g, xt, gt, w1[slot], w2[slot], out_sum, back_sum)):
                if len(self.block) == 2:
                    stage[slot] = d
                else:
                    for c in range(d.shape[1] // 128):
                        share = d[:, c * 128 : (c + 1) * 128].reshape(self.block[2:])
                        stage[slot, c // self.block[1], c % self.block[1]] = share
            for copy in flush(step):
                copy.start()
            return 0

        lax.fori_loop(now * self.blocks // steps, (now + 1) * self.blocks // steps, block, 0)

        @when(now == steps - 1)
        def _():
            for h, total in enumerate((out_sum, back_sum)):
                for j, result in enumerate(results):
                    result[:, h * width : (h + 1) * width] = total[j * size : (j + 1) * size].astype(bf16)
            keep = [pltpu.make_async_copy(a, b, kept_sems.at[j]) for j, (a, b) in enumerate(zip(results, kept))]
            for copy in keep:
                copy.start()
            for copy in keep:
                copy.wait()
            if self.back:
                self.back.send()
            for step in (self.blocks - 2, self.blocks - 1):
                for copy in flush(step):
                    copy.wait()


def finish(arrays, small, cuts):
    pieces = []
    for i, a in enumerate(arrays):
        axis = 1 if a.shape[0] == 1 else 0
        parts = 4 if a.size * a.dtype.itemsize >= MIB else 1
        size = a.shape[axis] // parts
        pieces += [(i, (0,) * axis + (pl.ds(p * size, size),)) for p in range(parts)]
    n = len(arrays)

    def kernel(*refs):
        ins, columns, outs, rows = refs[:n], refs[n], refs[n + 1 : 2 * n + 1], refs[2 * n + 1 : -n - 1]
        held, sems = refs[-n - 1 : -1], refs[-1]
        move = lambda a, b, way: [
            pltpu.make_async_copy(a[i].at[at], b[i].at[at], sems.at[way, c]) for c, (i, at) in enumerate(pieces)
        ]
        loads, copies = move(ins, held, 0), move(held, outs, 1)
        for load in loads:
            load.start()
        for load, copy in zip(loads, copies):
            load.wait()
            copy.start()
        turned = columns[...].T
        for ref, first, last in zip(rows, cuts, cuts[1:]):
            ref[...] = turned[first:last]
        for copy in copies:
            copy.wait()

    whole, hbm = pl.BlockSpec(memory_space=pltpu.VMEM), pl.BlockSpec(memory_space=pltpu.HBM)
    shapes = [jax.ShapeDtypeStruct(a.shape, a.dtype) for a in arrays]
    shapes += [jax.ShapeDtypeStruct((b - a, small.shape[0]), f32) for a, b in zip(cuts, cuts[1:])]
    results = pl.pallas_call(
        kernel,
        out_shape=shapes,
        in_specs=[hbm] * n + [whole],
        out_specs=[hbm] * n + [whole] * (len(cuts) - 1),
        scratch_shapes=[pltpu.VMEM(a.shape, a.dtype) for a in arrays] + [pltpu.SemaphoreType.DMA((2, len(pieces)))],
        compiler_params=pltpu.CompilerParams(vmem_limit_bytes=60 * MIB),
        name="finish",
    )(*arrays, small)
    return results[:n], results[n:]


def move(name, moves, collective_id, experts):
    return call(name, 1, None, [], [], [], [], [], moves, collective_id, experts, 0)


def shards(
    fast,
    tokens,
    gain_attn,
    w_qkv,
    w_out,
    gain_mix,
    w_fc,
    w_proj,
    w_router,
    w_coef,
    expert_in,
    expert_out,
    routes,
    dropped,
    cotangent,
):
    experts = lax.axis_size("expert")
    nodes = lax.axis_size("node")
    devices = nodes * experts
    width = tokens.shape[1]
    tok_rows = tokens.shape[0]
    ff = w_fc.shape[1]
    share = w_qkv.shape[0]
    small = jnp.concatenate([gain_attn[:, None], gain_mix[:, None], w_router, w_coef], axis=1)
    small = jnp.pad(small, ((0, 0), (0, 128 - small.shape[1])))
    win, wout = expert_in[0], expert_out[0]
    cut = lambda a, rows, columns, m, n: [
        [(a, i * (rows // m), rows // m, j * (columns // n), columns // n)] for i in range(m) for j in range(n)
    ]
    weights = (small, w_qkv, w_out, w_fc, w_proj)
    capacity = -(-(tok_rows * 10) // (8 * experts))
    moves, given = [], None
    if fast:
        items = cut(1, share, 3 * width, 1, 3) + cut(2, share, width, 1, 1)
        items += cut(3, share, ff, 1, 4) + cut(4, ff // devices, width, 4, 1)
        items[0] = cut(0, share, 128, 1, 1)[0] + items[0]
        assert len(items) == Forward.DENSE_ITEMS
        items += cut(5, width, win.shape[1], 4, 1) + cut(6, wout.shape[0], width, 4, 1)
        moves = [Gather(list(weights) + [win, wout], [True] * 5 + [False] * 2, items, nodes, experts)]
        moves.append(Exchange([], 1, experts, None, moves[0].turns, (capacity, 2 * width)))
        full = []
    else:
        full = [lax.all_gather(a, AXES, axis=0, tiled=False) for a in weights]
        win_full, wout_full = (lax.all_gather(a, "node", axis=0, tiled=False) for a in (win, wout))

    def scatter_xla(parts, axes):
        return lax.psum_scatter(parts, axes, scatter_dimension=0, tiled=False).astype(f32)

    def exchange(parts, sign):
        moved = [parts[0]]
        for j in range(1, experts):
            shift = [(s, (s + sign * j) % experts) for s in range(experts)]
            moved.append(lax.ppermute(parts[j], "expert", shift))
        return moved

    forward = Forward(tok_rows, width, experts, devices, capacity, ff, *(moves or (None, None)))
    whole, hbm = pl.BlockSpec(memory_space=pltpu.VMEM), pl.BlockSpec(memory_space=pltpu.HBM)
    routes, dropped = routes.reshape(1, tok_rows), dropped.reshape(1, tok_rows)
    if fast:

        def given(ins, os, own):
            moves[1].sources = own[: experts - 1]

    results = call(
        "forward",
        forward.steps,
        forward,
        [tokens, cotangent, routes, dropped] + full,
        [whole] * 4 + [hbm] * len(full),
        forward.outs + forward.targets,
        [whole] * len(forward.outs) + [hbm] * 2,
        forward.scratch,
        moves,
        1,
        experts,
        12 * tok_rows * width * (width + ff),
        given,
    )
    qkv_rows, lse, attended, after_attn, mixed_in, dispatch, probs, dense_out, grad_mixed = results[:9]
    results = results[9:]
    leaving, (d_fc, d_proj), moved = (
        results[: forward.kept],
        results[forward.kept : forward.kept + 2],
        results[forward.kept + 2 :],
    )
    small_full, qkv_full, out_full = (moved if fast else full)[:3]
    scatters, return_to, given = [], None, None
    chunks = 4
    step = width // chunks
    half = (experts // 2, step, 128)
    win_out = [jax.ShapeDtypeStruct(expert_in.shape, f32)]
    wout_out = [jax.ShapeDtypeStruct(expert_out.shape, f32)]

    def store_wout(out, chunk, sums):
        at = pl.ds(pl.multiple_of(chunk * step, step), step)
        for h, total in enumerate(sums):
            for c in range(half[0]):
                out[0, (h * half[0] + c) * 128 : (h * half[0] + c + 1) * 128, at] = total[c].T

    if fast:
        win_full, wout_full = moved[5:7]
        arrived = leaving + moved[7:]
        by_chip = lambda a: a.reshape(4, 2, 2, experts // 2, chunks, step, 128)

        def store(outs, i, value):
            if i < chunks:
                for q in range(step // share):
                    at = (i * (step // share) + q) * 128
                    outs[0][:, at : at + 128] = value[q * share : (q + 1) * share]
            else:
                outs[1][:, (i - chunks) * step : (i - chunks + 1) * step] = value.T

        def store_plane(outs, i, sums):
            @when(i < 2 * chunks)
            def _():
                for h, total in enumerate(sums):
                    outs[0][h * half[0] : (h + 1) * half[0], i] = total.astype(bf16)

            @when(i >= 2 * chunks)
            def _():
                at = pl.ds(pl.multiple_of((i - 2 * chunks) * step, step), step)
                for h, total in enumerate(sums):
                    for c in range(half[0]):
                        outs[1][0, at, (h * half[0] + c) * 128 : (h * half[0] + c + 1) * 128] = total[c]

        outs = [jax.ShapeDtypeStruct((experts, 2 * chunks) + half[1:], bf16)]
        parts = [(by_chip(d_fc), False, 0, chunks), (by_chip(d_proj), False, 0, chunks), (None, False, 0, chunks)]
        summing = Scatter(parts, half, experts, outs + win_out, store_plane, spread=True)
        return_to = Exchange([], -1, experts, None, summing.turns, leaving[0].shape)
        scatters = [return_to, summing]
    else:
        arrived = exchange(leaving, 1)
    blocks, size = win_full.shape[0], win_full.shape[2]
    experts_kernel = Experts(arrived, blocks, width, size, chunks if fast else None, return_to)
    if fast:

        def given(ins, os, own):
            summing.given = [os[experts]]
            return_to.sources = os[1:experts]

    results = call(
        "expert_mlp",
        experts_kernel.TURNS,
        experts_kernel,
        arrived + [win_full, wout_full],
        [whole] * experts + [hbm] * 2,
        experts_kernel.outs,
        [hbm] * len(experts_kernel.outs),
        experts_kernel.scratch,
        scatters,
        3,
        experts,
        12 * experts * capacity * width * blocks * size,
        given,
    )
    returned, (d_win, d_wout) = results[:experts], results[experts : experts + 2]
    if fast:
        results = results[experts + 2 :]
        came_back = returned[:1] + results[: experts - 1]
        plane_sums, grad_win = results[experts - 1 :]
    else:
        came_back = exchange(returned, -1)
    back = Back(tok_rows, width, experts, devices, capacity)
    back.moves = []
    if fast:
        parts = [(None, True, 0, back.items)]
        made = back.made()
        scatter_rest = Scatter(
            parts, made[4:], experts, back.final_outs(), back.store, back.first_item, made, spread=True
        )
        parts = [(d_wout, False, 0, chunks)]
        scatter_wout = Scatter(
            parts, half, experts, wout_out, lambda outs, i, sums: store_wout(outs[0], i, sums), spread=True
        )
        outs = [jax.ShapeDtypeStruct((share, ff), f32), jax.ShapeDtypeStruct((ff // devices, width), f32)]
        along = Along(plane_sums, experts, outs, store, max(scatter_rest.turns, scatter_wout.turns))
        back.moves = [along, scatter_wout, scatter_rest]
    outs = back.outs + ([] if fast else [jax.ShapeDtypeStruct((back.items, width, back.columns), bf16)])
    mixed, tokens_grad, *results = call(
        "back",
        back.steps,
        back,
        [tokens, cotangent, routes, dropped, qkv_rows, lse, attended, mixed_in, dispatch, probs]
        + [small_full, qkv_full, out_full, dense_out, grad_mixed, after_attn]
        + came_back,
        [whole] * 10 + [hbm] * (6 + experts),
        outs,
        [whole] * len(outs),
        back.scratch,
        back.moves,
        5,
        experts,
        32 * tok_rows * width * width,
    )
    if fast:
        done, (gain_1, gain_2, router, coef) = finish(
            [mixed, tokens_grad, grad_win] + results[:5], results[5], (0, 1, 2, 2 + experts, 4 + experts)
        )
        mixed, tokens_grad, grad_win, grad_fc, grad_proj, grad_wout, grad_wqkv, grad_wo = done
        small_grads = (gain_1[0], gain_2[0], router.T, coef.T)
    else:
        summed = scatter_xla(results[0].reshape(back.items, devices, share, -1).swapaxes(0, 1), AXES)
        last = summed[-1]
        grad_wo = jnp.concatenate([*summed[: back.firsts], last[:, : back.rest]], axis=1)
        grad_small = last[:, back.rest : back.rest + 128]
        small_grads = (
            grad_small[:, 0],
            grad_small[:, 1],
            grad_small[:, 2 : 2 + experts],
            grad_small[:, 2 + experts : 4 + experts],
        )
        pairs = summed[back.firsts : -1].reshape(back.pairs, share, 3, PAIR)
        grad_wqkv = pairs.transpose(1, 2, 0, 3).reshape(share, 3 * width)
        grad_fc = scatter_xla(d_fc.reshape(devices, share, ff), AXES)
        by_unit = d_proj.reshape(width, devices, ff // devices).transpose(1, 0, 2)
        grad_proj = scatter_xla(by_unit, AXES).T
        grad_win = scatter_xla(d_win, "node")[None]
        grad_wout = scatter_xla(d_wout, "node").T[None]
    return (
        mixed,
        tokens_grad,
        small_grads[0],
        grad_wqkv,
        grad_wo,
        small_grads[1],
        grad_fc,
        grad_proj,
        small_grads[2],
        small_grads[3],
        grad_win,
        grad_wout,
    )


def solution(mesh):
    rows = P(AXES, None)
    in_specs = (
        rows,
        P(AXES),
        rows,
        rows,
        P(AXES),
        rows,
        rows,
        rows,
        rows,
        P("expert", None, "node"),
        P("expert", "node", None),
        rows,
        P(AXES),
        rows,
    )
    out_specs = (
        rows,
        rows,
        P(AXES),
        rows,
        rows,
        P(AXES),
        rows,
        rows,
        rows,
        rows,
        P("expert", None, "node"),
        P("expert", "node", None),
    )
    fast = mesh.shape["node"] == 8 and mesh.shape["expert"] == 4
    return jax.shard_map(
        functools.partial(shards, fast), mesh=mesh, in_specs=in_specs, out_specs=out_specs, check_vma=False
    )
```

```python
import functools
import math

import jax
import jax.numpy as jnp
from jax import lax
from jax.experimental import pallas as pl
from jax.experimental.pallas import tpu as pltpu
from jax.sharding import PartitionSpec as P

HD = 64
PAIR = 2 * HD
SEQ = 512
QB = 256
BLOCK = 512
MIB = 1 << 20
AXES = ("node", "expert")
MESH = pl.DeviceIdType.MESH
epsilon = 1e-05
f32 = jnp.float32
bf16 = jnp.bfloat16


def normalize(values):
    centered = values - jnp.mean(values, axis=-1, keepdims=True)
    inv_scale = lax.rsqrt(jnp.mean(centered * centered, axis=-1, keepdims=True) + epsilon)
    return (centered * inv_scale, inv_scale)


def norm_back(grad_norm, normed, inv_scale):
    mean_grad = jnp.mean(grad_norm, axis=-1, keepdims=True)
    mean_cross = jnp.mean(grad_norm * normed, axis=-1, keepdims=True)
    return inv_scale * (grad_norm - mean_grad - normed * mean_cross)


def contract(left_op, right_op, left_dim, right_dim):
    return lax.dot_general(
        left_op, right_op, (((left_dim,), (right_dim,)), ((), ())), preferred_element_type=f32
    )


def matmul(left_op, right_op):
    return contract(left_op, right_op, 1, 0)


def product_tn(left_op, right_op):
    return contract(left_op, right_op, 0, 0)


def outer_nt(left_op, right_op):
    return contract(left_op, right_op, 1, 1)


class Place:
    def __init__(self, experts):
        self.experts = experts
        self.n, self.e = lax.axis_index("node"), lax.axis_index("expert")
        n = self.n
        self.k, self.x, self.y = lax.rem(n, 2), lax.rem(n // 2, 2), n // 4
        k, x, y = self.k, self.x, self.y
        self.nx, self.ny = y * 4 + (1 - x) * 2 + k, (1 - y) * 4 + x * 2 + k
        self.nd, self.nc = (1 - y) * 4 + (1 - x) * 2 + k, y * 4 + x * 2 + 1 - k

    def z(self, j):
        return (self.n, lax.rem(self.e + j, self.experts))

    def greet(self, along_z):
        barrier = pltpu.get_barrier_semaphore()
        peers = [(self.nx, self.e), (self.ny, self.e), (self.nc, self.e)]
        if along_z:
            peers += [self.z(j) for j in range(1, self.experts)]
        for peer in peers:
            pl.semaphore_signal(barrier, inc=1, device_id=peer, device_id_type=MESH)
        pl.semaphore_wait(barrier, len(peers))


def when(condition):
    return pl.when(condition)


class Gather:
    def __init__(self, args, dense, items, nodes, experts):
        self.args, self.dense, self.items, self.experts = args, dense, items, experts
        self.outs = [
            jax.ShapeDtypeStruct(((nodes * experts if d else nodes),) + a.shape, a.dtype)
            for a, d in zip(args, dense)
        ]
        hbm = pl.BlockSpec(memory_space=pltpu.HBM)
        self.in_specs, self.out_specs = [hbm] * len(args), [hbm] * len(args)
        m = sum(len(item) for item in items)
        self.scratch = [
            pltpu.SemaphoreType.DMA((m, experts + 7)),
            pltpu.SemaphoreType.DMA((m, experts + 7)),
            pltpu.SemaphoreType.DMA((m,)),
        ]
        self.along_z = any(dense)
        self.steps = [self.along, self.across, self.corner, self.over, self.end]
        self.turns = len(items) + len(self.steps) - 1

    def bind(self, ins, outs, scratch, place):
        experts = self.experts
        send, recv, loc = scratch
        p, e = place, place.e

        def remote(source, target, item, kind, device):
            return pltpu.make_async_remote_copy(
                src_ref=source,
                dst_ref=target,
                send_sem=send.at[item, kind],
                recv_sem=recv.at[item, kind],
                device_id=device,
                device_id_type=MESH,
            )

        self.full = outs
        self.bound = [[] for _ in self.items]
        pieces = [(turn, piece) for turn, item in enumerate(self.items) for piece in item]
        for i, (turn, (arg, row, rows, col, columns)) in enumerate(pieces):
            dense = self.dense[arg]
            shard, whole = ins[arg], outs[arg]
            per = experts if dense else 1
            own = p.n * per + (e if dense else 0)

            def view(ref, lead, start=0, size=None, whole_rows=rows, row=row, col=col, columns=columns):
                return ref.at[lead, pl.ds(row + start, size or whole_rows), pl.ds(col, columns)]

            def bundle(m, view=view, whole=whole, per=per):
                return view(whole, pl.ds(m * per, per))

            def half(m, h, view=view, whole=whole, per=per, dense=dense, rows=rows):
                if dense:
                    return view(whole, pl.ds(m * per + h * (per // 2), per // 2))
                return view(whole, m, h * (rows // 2), rows // 2)

            mine = shard.at[pl.ds(row, rows), pl.ds(col, columns)]
            land = view(whole, own)
            local = pltpu.make_async_copy(mine, land, loc.at[i])
            z = []
            if dense:
                z = [remote(mine, land, i, j - 1, p.z(j)) for j in range(1, experts)]
            first, last = (bundle(p.n), bundle(p.n)) if dense else (mine, land)
            b = experts - 1
            xy = [remote(first, last, i, b, (p.nx, e)), remote(first, last, i, b + 1, (p.ny, e))]
            diag = [
                remote(half(p.nx, 0), half(p.nx, 0), i, b + 2, (p.ny, e)),
                remote(half(p.ny, 1), half(p.ny, 1), i, b + 3, (p.nx, e)),
            ]
            core = [remote(first, last, i, b + 4, (p.nc, e))] + [
                remote(bundle(m), bundle(m), i, b + 5 + j, (p.nc, e)) for j, m in enumerate((p.nx, p.ny, p.nd))
            ]
            self.bound[turn].append((local, z, xy, diag, core))

    def turn(self, now):
        for t in range(self.turns):

            @when(now == t)
            def _(t=t):
                for late, step in enumerate(self.steps):
                    if 0 <= t - late < len(self.items):
                        for piece in self.bound[t - late]:
                            step(*piece)

    def finish(self, now):
        pass

    def along(self, local, z, xy, diag, core):
        local.start()
        for copy in z:
            copy.start()

    def across(self, local, z, xy, diag, core):
        for copy in z:
            copy.wait()
        local.wait()
        xy[0].start()
        xy[1].start()
        core[0].start()

    def corner(self, local, z, xy, diag, core):
        for i in range(2):
            xy[i].wait()
            diag[i].start()
            core[1 + i].start()

    def over(self, local, z, xy, diag, core):
        diag[0].wait()
        diag[1].wait()
        core[3].start()

    def end(self, local, z, xy, diag, core):
        for copy in core:
            copy.wait()


class Exchange:
    along_z = True

    def __init__(self, pieces, sign, experts, start, turns, shape):
        self.args, self.sign, self.experts, self.start, self.turns = list(pieces), sign, experts, start, turns
        self.given = None
        self.outs = [jax.ShapeDtypeStruct(shape, bf16)] * (experts - 1)
        hbm = pl.BlockSpec(memory_space=pltpu.HBM)
        self.in_specs, self.out_specs = [hbm] * len(self.args), [hbm] * (experts - 1)
        self.scratch = [pltpu.SemaphoreType.DMA((experts,)), pltpu.SemaphoreType.DMA((experts,))]

    def bind(self, ins, outs, scratch, place):
        self.out, self.sems, self.place = outs, scratch, place
        if ins:
            self.sources = ins

    def copies(self):
        return [
            pltpu.make_async_remote_copy(
                src_ref=source,
                dst_ref=self.out[j],
                send_sem=self.sems[0].at[j],
                recv_sem=self.sems[1].at[j],
                device_id=self.place.z((self.sign * (j + 1)) % self.experts),
                device_id_type=MESH,
            )
            for j, source in enumerate(self.sources)
        ]

    def send(self):
        for copy in self.copies():
            copy.start()

    def turn(self, now):
        if self.start is not None:

            @when(now == self.start)
            def _():
                self.send()

    def finish(self, now):
        @when(now == self.turns - 1)
        def _():
            for copy in self.copies():
                copy.wait()


class Scatter:
    RING, SPREAD_RING, CORE_RING = 6, 8, 4

    def __init__(self, parts, half, experts, outs, store, start=0, made=None, spread=False):
        self.experts, self.outs, self.store, self.start, self.made = experts, outs, store, start, made
        self.parts = parts
        self.given = []
        self.args = [p[0] for p in parts if p[0] is not None]
        h = half
        self.starts = [sum(p[3] for p in parts[:a]) for a in range(len(parts) + 1)]
        m = self.m = self.starts[-1]
        self.m_z = sum(p[3] for p in parts if p[1])
        unit = h[1:]
        ring = self.ring = min(self.SPREAD_RING if spread else self.RING, m)
        self.core_ring = min(self.CORE_RING, m)
        self.in_specs = [pl.BlockSpec(memory_space=pltpu.HBM)] * len(self.args)
        self.out_specs = [pl.BlockSpec(memory_space=pltpu.VMEM)] * len(outs)
        kinds = 7 + experts
        self.scratch = [
            pltpu.VMEM(made or (ring, 4, 2) + h, bf16),
            pltpu.VMEM((self.core_ring, 4, 2) + h, bf16),
            pltpu.VMEM((ring, 2) + h, bf16),
            pltpu.VMEM((ring, 2) + h, bf16),
            pltpu.VMEM((ring,) + h, bf16),
            pltpu.VMEM((ring,) + h, bf16),
            pltpu.SemaphoreType.DMA((m, kinds)),
            pltpu.SemaphoreType.DMA((m, kinds)),
            pltpu.SemaphoreType.DMA((m,)),
        ]
        if self.m_z:
            self.scratch.append(pltpu.VMEM((self.m_z, experts - 1) + unit, bf16))
            self.scratch.append(pltpu.VMEM((self.m_z, experts) + unit, bf16))
        self.stages = (0, 1, 3, 5, 7) if spread else (0, 1, 2, 3, 4)
        self.turns = start + m + self.stages[4 if self.m_z else 3]
        self.along_z = self.m_z > 0

    def bind(self, ins, outs, scratch, place):
        ins = list(ins)
        given = list(self.given)
        self.sources = [given.pop(0) if p[0] is None else ins.pop(0) for p in self.parts] if not self.made else []
        self.out, self.place = outs, place
        self.own, self.rc, self.rx, self.ry, self.lx, self.ly, self.sent, self.recv, self.loc = scratch[:9]
        self.rz, self.zs = scratch[9:] if self.m_z else (None, None)

    def slot(self, i):
        return lax.rem(i, self.ring)

    def remote(self, source, target, item, kind, device):
        return pltpu.make_async_remote_copy(
            src_ref=source,
            dst_ref=target,
            send_sem=self.sent.at[item, kind],
            recv_sem=self.recv.at[item, kind],
            device_id=device,
            device_id_type=MESH,
        )

    def at(self, i, site, *more):
        return (i, site, self.place.k) + more if self.made else (self.slot(i), site) + more

    def first(self, source, i, chunk):
        p = self.place
        land = self.rc.at[lax.rem(i, self.core_ring)]
        if self.made:
            return [self.remote(self.own.at[i, :, 1 - p.k], land, i, 0, (p.nc, p.e))]
        part = lambda core: source.at[:, core, :, :, chunk]
        local = pltpu.make_async_copy(part(p.k), self.own.at[self.slot(i)], self.loc.at[i])
        return [self.remote(part(1 - p.k), land, i, 0, (p.nc, p.e)), local]

    def sites(self):
        p = self.place
        return p.y * 2 + p.x, p.y * 2 + 1 - p.x, (1 - p.y) * 2 + p.x, (1 - p.y) * 2 + 1 - p.x

    def round_one(self, i):
        p = self.place
        b = self.slot(i)
        _, to_x, to_y, diag = self.sites()
        own = lambda *at: self.own.at[self.at(i, *at)]
        return [
            self.remote(own(diag, 0), self.rx.at[b, 0], i, 1, (p.nx, p.e)),
            self.remote(own(diag, 1), self.ry.at[b, 0], i, 2, (p.ny, p.e)),
            self.remote(own(to_x, 0), self.rx.at[b, 1], i, 3, (p.nx, p.e)),
            self.remote(own(to_y, 1), self.ry.at[b, 1], i, 4, (p.ny, p.e)),
        ]

    def round_two(self, i):
        p = self.place
        b = self.slot(i)
        _, to_x, to_y, _ = self.sites()
        return [
            self.remote(self.own.at[self.at(i, to_x, 1)], self.lx.at[b], i, 5, (p.nx, p.e)),
            self.remote(self.own.at[self.at(i, to_y, 0)], self.ly.at[b], i, 6, (p.ny, p.e)),
        ]

    def round_z(self, i):
        p = self.place
        return [
            self.remote(self.zs.at[i, lax.rem(p.e + j, self.experts)], self.rz.at[i, j - 1], i, 6 + j, p.z(j))
            for j in range(1, self.experts)
        ]

    def turn(self, now):
        limits = (self.m, self.m, self.m, self.m, self.m_z)
        steps = (self.load, self.chip, self.cross, self.plane, self.column)
        for limit, late, step in zip(limits, self.stages, steps):
            i = now - self.start - late
            if limit:

                @when(jnp.logical_and(i >= 0, i < limit))
                def _(step=step, i=i):
                    step(i)

    def finish(self, now):
        pass

    def load(self, i):
        if self.made:
            self.first(None, i, 0)[0].start()
            return
        for a, source in enumerate(self.sources):

            @when(jnp.logical_and(i >= self.starts[a], i < self.starts[a + 1]))
            def _(a=a, source=source):
                for copy in self.first(source, i, i - self.starts[a] + self.parts[a][2]):
                    copy.start()

    def chip(self, i):
        for copy in self.first(None if self.made else self.sources[0], i, 0):
            copy.wait()

        def sum_one(q, _):
            at = self.at(i, q)
            self.own[at] = add(self.own[at], self.rc[lax.rem(i, self.core_ring), q]).astype(bf16)
            return 0

        lax.fori_loop(0, 4, sum_one, 0)
        for copy in self.round_one(i):
            copy.start()

    def cross(self, i):
        one = self.round_one(i)
        two = self.round_two(i)
        b = self.slot(i)
        _, to_x, to_y, _ = self.sites()
        for copy in one:
            copy.wait()
        at_x, at_y = self.at(i, to_x, 1), self.at(i, to_y, 0)
        self.own[at_x] = add(self.own[at_x], self.ry[b, 0]).astype(bf16)
        two[0].start()
        self.own[at_y] = add(self.own[at_y], self.rx[b, 0]).astype(bf16)
        two[1].start()

    def plane(self, i):
        for copy in self.round_two(i):
            copy.wait()
        mine, _, _, _ = self.sites()
        b = self.slot(i)
        sums = lambda: (
            add(self.own[self.at(i, mine, 0)], self.rx[b, 1], self.ly[b]),
            add(self.own[self.at(i, mine, 1)], self.lx[b], self.ry[b, 1]),
        )
        if self.m_z:

            @when(i < self.m_z)
            def _():
                s = self.experts // 2
                for h, total in enumerate(sums()):
                    self.zs[i, h * s : (h + 1) * s] = total.astype(bf16)
                for copy in self.round_z(i):
                    copy.start()

        if self.m_z < self.m:

            @when(i >= self.m_z)
            def _():
                self.store(self.out, i, sums())

    def column(self, i):
        for copy in self.round_z(i):
            copy.wait()
        terms = [self.zs[i, self.place.e]] + [self.rz[i, j] for j in range(self.experts - 1)]
        self.store(self.out, i, add(*terms))


class Along:
    along_z = True

    def __init__(self, shares, experts, outs, store, turns):
        self.args, self.experts, self.outs, self.store, self.turns = [shares], experts, outs, store, turns
        self.in_specs = [pl.BlockSpec(memory_space=pltpu.HBM)]
        self.out_specs = [pl.BlockSpec(memory_space=pltpu.VMEM)] * len(outs)
        self.items = shares.shape[1]
        self.scratch = [
            pltpu.VMEM(shares.shape, bf16),
            pltpu.SemaphoreType.DMA((experts,)),
            pltpu.SemaphoreType.DMA((experts,)),
        ]

    def bind(self, ins, outs, scratch, place):
        self.source, self.out, self.place = ins[0], outs, place
        self.land, self.sent, self.recv = scratch

    def copies(self):
        p = self.place
        copies = [pltpu.make_async_copy(self.source.at[p.e], self.land.at[0], self.recv.at[0])]
        return copies + [
            pltpu.make_async_remote_copy(
                src_ref=self.source.at[lax.rem(p.e + j, self.experts)],
                dst_ref=self.land.at[j],
                send_sem=self.sent.at[j],
                recv_sem=self.recv.at[j],
                device_id=p.z(j),
                device_id_type=MESH,
            )
            for j in range(1, self.experts)
        ]

    def turn(self, now):
        @when(now == 0)
        def _():
            for copy in self.copies():
                copy.start()

    def finish(self, now):
        @when(now == self.turns - 1)
        def _():
            for copy in self.copies():
                copy.wait()
            for i in range(self.items):
                self.store(self.out, i, add(*(self.land[j, i] for j in range(self.experts))))


def add(*terms):
    return functools.reduce(jnp.add, [t.astype(f32) for t in terms])


def call(
    name, steps, body, args, in_specs, outs, out_specs, scratch, moves, collective_id, experts, flops, given=None
):
    total = max([steps] + [m.turns for m in moves])

    def hold(spec):
        if spec.block_shape is None:
            return spec
        index = spec.index_map
        return pl.BlockSpec(spec.block_shape, lambda j: index(jnp.minimum(j, steps - 1)))

    join = lambda what: [x for m in moves for x in getattr(m, what)]

    def kernel(*refs):
        refs = list(refs)
        take = lambda group: [refs.pop(0) for _ in group]
        ins, m_ins = take(args), [take(m.args) for m in moves]
        os, m_os = take(outs), [take(m.outs) for m in moves]
        own, m_own = take(scratch), [take(m.scratch) for m in moves]
        now = pl.program_id(0)
        if moves:
            place = Place(experts)
            if given is not None:
                given(ins, os, own)
            for m, a, o, r in zip(moves, m_ins, m_os, m_own):
                m.bind(a, o, r, place)

            @when(now == 0)
            def _():
                place.greet(any(m.along_z for m in moves))

            for m in moves:
                m.turn(now)
        if body is not None:

            @when(now < steps)
            def _():
                body(now, steps, *ins, *os, *own)

        for m in moves:
            m.finish(now)

    results = pl.pallas_call(
        kernel,
        grid=(total,),
        out_shape=list(outs) + join("outs"),
        in_specs=[hold(s) for s in in_specs] + join("in_specs"),
        out_specs=[hold(s) for s in out_specs] + join("out_specs"),
        scratch_shapes=list(scratch) + join("scratch"),
        cost_estimate=pl.CostEstimate(flops=flops, bytes_accessed=32 * MIB, transcendentals=0),
        compiler_params=pltpu.CompilerParams(
            vmem_limit_bytes=60 * MIB,
            **({"collective_id": collective_id, "has_side_effects": True} if moves else {}),
        ),
        name=name,
    )(*args, *join("args"))
    return list(results)


def masks():
    lanes = lax.broadcasted_iota(jnp.int32, (1, PAIR), 1)
    return [(lanes // HD == h).astype(bf16) for h in range(2)]


def causal(scores_t, start):
    keys = lax.broadcasted_iota(jnp.int32, scores_t.shape, 0)
    queries = lax.broadcasted_iota(jnp.int32, scores_t.shape, 1) + start
    return jnp.where(keys <= queries, scores_t, -jnp.inf)


def attend_pair(q, k, v):
    q = q * (1.0 / math.sqrt(HD))
    vt = v.T
    length = q.shape[0]
    outs, tops = [], []
    for h, mask in enumerate(masks()):
        kh = k * mask
        row, logs = [], []
        for start in range(0, length, QB):
            end = start + QB
            scores = causal(outer_nt(kh[:end], q[start:end]), start)
            top = jnp.max(scores, axis=0, keepdims=True)
            expd = jnp.exp(scores - top)
            total = jnp.sum(expd, axis=0, keepdims=True)
            probs = (expd / total).astype(bf16)
            row.append(matmul(vt[h * HD : (h + 1) * HD, :end], probs))
            logs.append(top + jnp.log(total))
        outs.append(jnp.concatenate(row, axis=1))
        tops.append(jnp.concatenate(logs, axis=1))
    return jnp.concatenate(outs, axis=0).T.astype(bf16), jnp.concatenate(tops, axis=0)


def columns_of(*rows):
    return [jnp.broadcast_to(r[...].astype(f32), (128, r.shape[1])).T.astype(jnp.int32) for r in rows]


class Forward:
    def __init__(self, length, width, experts, devices, capacity, ff, gather, leave):
        self.length, self.width, self.experts, self.capacity = length, width, experts, capacity
        self.gather, self.leave = gather, leave
        pairs = width // PAIR
        share = self.share = width // devices
        self.blocks = ff // BLOCK
        self.per_block = BLOCK * devices // ff
        self.at_norm, self.at_qkv = 4, 7
        self.at_heads = self.at_qkv + 1
        self.per_turn = 2
        self.at_out = self.at_heads + length // SEQ * pairs // self.per_turn
        self.at_leave = self.at_out + 1
        self.at_mlp = max(self.at_leave + 2, self.DENSE_ITEMS + 3)
        self.steps = self.at_mlp + self.blocks
        slots = experts * capacity
        rows = lambda c, t: jax.ShapeDtypeStruct((length, c), t)
        piece = (capacity, 2 * width)
        self.kept = 1 if leave else experts
        self.outs = [
            rows(3 * width, bf16),
            jax.ShapeDtypeStruct((length // SEQ * pairs, 2, SEQ), f32),
            rows(width, bf16),
            rows(width, f32),
            rows(width, bf16),
            rows(slots, bf16),
            rows(128, f32),
            rows(width, f32),
            rows(width, f32),
        ] + [jax.ShapeDtypeStruct(piece, bf16)] * self.kept
        if gather:
            stages = [(devices, self.per_block * share * devices // ff * (ff // devices // 128), 128)]
            stages = [(devices, BLOCK // 128 * share, 128), (self.per_block, width, 128)]
            targets = [(devices, width, 128)] * 2
        else:
            stages, targets = [(width, BLOCK)] * 2, [(width, ff)] * 2
        self.targets = [jax.ShapeDtypeStruct(t, bf16) for t in targets]
        self.scratch = [pltpu.VMEM(piece, bf16)] * (experts - self.kept) + [
            pltpu.VMEM((devices, share, 128), bf16),
            pltpu.VMEM((devices, share, 3 * width), bf16),
            pltpu.VMEM((devices, share, width), bf16),
            pltpu.VMEM((8, width), f32),
            pltpu.VMEM((length, width), bf16),
            pltpu.SemaphoreType.DMA((3,)),
            pltpu.VMEM((length, width), bf16),
            pltpu.VMEM((length, width), bf16),
            pltpu.VMEM((width, length), bf16),
            pltpu.VMEM((width, length), bf16),
            pltpu.VMEM((2, devices, share, BLOCK), bf16),
            pltpu.VMEM((2, self.per_block, ff // devices, width), bf16),
            pltpu.VMEM((2,) + stages[0], bf16),
            pltpu.VMEM((2,) + stages[1], bf16),
            pltpu.SemaphoreType.DMA((2, 2)),
            pltpu.SemaphoreType.DMA((2, 2)),
        ]

    DENSE_ITEMS = 13

    def __call__(self, now, steps, tok, cot, routes, dropped, *refs):
        refs = list(refs)
        take = lambda count: [refs.pop(0) for _ in range(count)]
        full = self.gather.full[:5] if self.gather else take(5)
        qkv, lse, att, after, mixed, disp, info, dense_out, grad_mixed = take(9)
        leave = take(self.kept)
        targets = take(2)
        leave += take(self.experts - self.kept)
        ws, wq, wo, gains, attn_in, sems, gd, ge, xt, gt, w1, w2, stage_1, stage_2, w_sems, d_sems = refs
        width, length = self.width, self.length
        loads = [pltpu.make_async_copy(a, b, sems.at[i]) for i, (a, b) in enumerate(zip(full, (ws, wq, wo)))]

        def weights(block):
            at = lax.rem(block, 2)
            cols = pl.ds(pl.multiple_of(block * BLOCK, BLOCK), BLOCK)
            return [
                pltpu.make_async_copy(full[3].at[:, :, cols], w1.at[at], w_sems.at[at, 0]),
                pltpu.make_async_copy(full[4].at[pl.ds(block * self.per_block, self.per_block)], w2.at[at], w_sems.at[at, 1]),
            ]

        def flush(block):
            at = lax.rem(block, 2)
            if self.gather:
                size = BLOCK // 128 * self.share
                first = targets[0].at[:, pl.ds(pl.multiple_of(block * size, size), size)]
                second = targets[1].at[pl.ds(block * self.per_block, self.per_block)]
            else:
                cols = pl.ds(pl.multiple_of(block * BLOCK, BLOCK), BLOCK)
                first, second = targets[0].at[:, cols], targets[1].at[:, cols]
            return [
                pltpu.make_async_copy(stage_1.at[at], first, d_sems.at[at, 0]),
                pltpu.make_async_copy(stage_2.at[at], second, d_sems.at[at, 1]),
            ]

        @when(now == self.at_norm)
        def _():
            loads[0].start()
            loads[0].wait()
            gains[...] = ws[...].reshape(width, 128).astype(f32).T[:8]
            normed, _ = normalize(tok[...].astype(f32))
            attn_in[...] = (normed * gains[0:1]).astype(bf16)

        @when(now == self.at_qkv)
        def _():
            loads[1].start()
            loads[1].wait()

            def columns(c, _):
                cols = pl.ds(pl.multiple_of(c * BLOCK, BLOCK), BLOCK)
                weights = wq[:, :, cols].reshape(width, BLOCK)
                qkv[:, cols] = matmul(attn_in[...], weights).astype(bf16)
                return 0

            lax.fori_loop(0, 3 * width // BLOCK, columns, 0)

        @when(jnp.logical_and(now >= self.at_heads, now < self.at_out))
        def _():
            pairs = width // PAIR

            def pair(i, _):
                at = (now - self.at_heads) * self.per_turn + i
                seq, at_pair = at // pairs, lax.rem(at, pairs)
                rows = pl.ds(pl.multiple_of(seq * SEQ, SEQ), SEQ)
                cols = lambda part: pl.ds(pl.multiple_of(part * width + at_pair * PAIR, PAIR), PAIR)
                out, tops = attend_pair(qkv[rows, cols(0)], qkv[rows, cols(1)], qkv[rows, cols(2)])
                att[rows, cols(0)] = out
                lse[at] = tops
                return 0

            lax.fori_loop(0, self.per_turn, pair, 0)

        @when(now == self.at_out)
        def _():
            loads[2].start()
            loads[2].wait()
            self.route(tok, cot, routes, dropped, att, wo, ws, gains, after, mixed, gd, ge, disp, info)

        @when(now == self.at_leave)
        def _():
            for h, values in enumerate((mixed, ge)):
                placed = product_tn(disp[...], values[...]).astype(bf16)
                for j in range(self.experts):
                    leave[j][:, h * width : (h + 1) * width] = placed[j * self.capacity : (j + 1) * self.capacity]
            if self.leave:
                self.leave.send()

        @when(now == self.at_mlp - 1)
        def _():
            xt[...] = mixed[...].T
            gt[...] = gd[...].T
            dense_out[...] = jnp.zeros_like(dense_out)
            grad_mixed[...] = jnp.zeros_like(grad_mixed)

        @when(jnp.logical_and(now >= self.at_mlp, now < self.at_mlp + self.blocks))
        def _():
            block = now - self.at_mlp
            at = lax.rem(block, 2)

            @when(block == 0)
            def _():
                for copy in weights(0):
                    copy.start()

            @when(block + 1 < self.blocks)
            def _():
                for copy in weights(block + 1):
                    copy.start()

            for copy in weights(block):
                copy.wait()

            @when(block >= 2)
            def _():
                for copy in flush(block - 2):
                    copy.wait()

            d1, d2 = mlp_block(
                mixed,
                gd,
                xt,
                gt,
                w1[at].reshape(width, BLOCK),
                w2[at].reshape(BLOCK, width),
                dense_out,
                grad_mixed,
            )
            if self.gather:
                share = self.share
                for c in range(BLOCK // 128):
                    cols = slice(c * 128, (c + 1) * 128)
                    for s in range(width // share):
                        stage_1[at, s, c * share : (c + 1) * share] = d1[s * share : (s + 1) * share, cols]
                    stage_2[at, c] = d2[:, cols]
            else:
                stage_1[at] = d1
                stage_2[at] = d2
            for copy in flush(block):
                copy.start()

            @when(block == self.blocks - 1)
            def _():
                for last in (self.blocks - 2, self.blocks - 1):
                    for copy in flush(last):
                        copy.wait()

    def route(self, tok, cot, routes, dropped, att, wo, ws, gains, after, mixed, gd, ge, disp, info):
        width, length, experts = self.width, self.length, self.experts
        route, drop = columns_of(routes, dropped)
        after[...] = tok[...].astype(f32) + matmul(att[...], wo[...].reshape(width, width))
        normed, _ = normalize(after[...])
        mixed[...] = (normed * gains[1:2]).astype(bf16)
        logits = matmul(mixed[...], ws[...].reshape(width, 128))
        lane = lax.broadcasted_iota(jnp.int32, (length, 128), 1)

        def softmax(first, last):
            inside = jnp.logical_and(lane >= first, lane < last)
            top = jnp.max(jnp.where(inside, logits, -jnp.inf), axis=1, keepdims=True)
            expd = jnp.where(inside, jnp.exp(jnp.where(inside, logits, top) - top), 0.0)
            return expd / jnp.sum(expd, axis=1, keepdims=True)

        probs, coef = softmax(2, 2 + experts), softmax(2 + experts, 4 + experts)
        info[...] = probs + coef
        chosen = jnp.where(lane - 2 == route, 1.0, 0.0)
        over_lanes = lambda a: jnp.sum(a, axis=1, keepdims=True)
        gate = over_lanes(probs * chosen) * (1 - drop[:, :1]).astype(f32)
        coef_0 = over_lanes(jnp.where(lane == 2 + experts, coef, 0.0))
        coef_1 = over_lanes(jnp.where(lane == 3 + experts, coef, 0.0))
        grad = cot[...].astype(f32)
        gd[...] = (coef_0 * grad).astype(bf16)
        ge[...] = (coef_1 * gate * grad).astype(bf16)
        square = lambda d: lax.broadcasted_iota(jnp.int32, (length, length), d)
        earlier = jnp.where(square(0) > square(1), 1.0, 0.0).astype(bf16)
        position = over_lanes(chosen * matmul(earlier, chosen.astype(bf16))).astype(jnp.int32)
        turn = route[:, :1] - lax.axis_index("expert")
        target = jnp.where(turn < 0, turn + experts, turn) * self.capacity + position
        slot = lax.broadcasted_iota(jnp.int32, (length, experts * self.capacity), 1)
        disp[...] = jnp.where(slot == target, 1.0, 0.0).astype(bf16)


def attend_pair_backward(q, k, v, g, lse):
    scaling = 1.0 / math.sqrt(HD)
    qs = q * scaling
    kt = k.T
    length = q.shape[0]
    grad_k = [0.0] * (length // QB)
    grad_v = [0.0] * (length // QB)
    grad_q = []
    for h, mask in enumerate(masks()):
        kh, vh, qh, gh = k * mask, v * mask, q * mask, g * mask
        row = []
        for c, start in enumerate(range(0, length, QB)):
            end = start + QB
            scores = causal(outer_nt(kh[:end], qs[start:end]), start)
            probs = jnp.exp(scores - lse[h : h + 1, start:end])
            grad_probs = outer_nt(vh[:end], g[start:end])
            delta = jnp.sum(probs * grad_probs, axis=0, keepdims=True)
            grad_scores = (probs * (grad_probs - delta)).astype(bf16)
            more_v = matmul(probs.astype(bf16), gh[start:end])
            more_k = matmul(grad_scores, qh[start:end])
            for b in range(c + 1):
                rows = slice(b * QB, (b + 1) * QB)
                grad_v[b] = grad_v[b] + more_v[rows]
                grad_k[b] = grad_k[b] + more_k[rows]
            row.append(matmul(kt[h * HD : (h + 1) * HD, :end], grad_scores))
        grad_q.append(jnp.concatenate(row, axis=1))
    return (
        (jnp.concatenate(grad_q, axis=0).T * scaling).astype(bf16),
        (jnp.concatenate(grad_k, axis=0) * scaling).astype(bf16),
        jnp.concatenate(grad_v, axis=0).astype(bf16),
    )


def thirds(values):
    parts = []
    for _ in range(3):
        parts.append(values.astype(bf16))
        values = values - parts[-1].astype(f32)
    return parts


class Back:
    def __init__(self, length, width, experts, devices, capacity):
        self.length, self.width, self.experts, self.capacity = length, width, experts, capacity
        self.devices, self.share = devices, width // devices
        self.pairs = width // PAIR
        self.columns = 3 * PAIR
        self.firsts = width // self.columns
        self.rest = width - self.firsts * self.columns
        self.items = self.firsts + self.pairs + 1
        self.heads_at = 4
        self.last = self.heads_at + self.pairs
        self.steps = self.last + 1
        self.first_item = self.heads_at
        self.outs = [
            jax.ShapeDtypeStruct((length, width), bf16),
            jax.ShapeDtypeStruct((length, width), f32),
        ]
        slots = experts * capacity
        self.scratch = [
            pltpu.VMEM((slots, 2 * width), bf16),
            pltpu.VMEM((length, width), f32),
            pltpu.VMEM((length, width), f32),
            pltpu.VMEM((devices, self.share, 128), bf16),
            pltpu.VMEM((devices, self.share, width), bf16),
            pltpu.VMEM((2, devices, self.share, self.columns), bf16),
            pltpu.VMEM((8, width), f32),
            pltpu.VMEM((128, width), f32),
            pltpu.VMEM((width, length), bf16),
            pltpu.VMEM((length, width), bf16),
            pltpu.SemaphoreType.DMA((5 + experts,)),
            pltpu.SemaphoreType.DMA((2, 3)),
        ]

    def made(self):
        chips = (4, 2, 2, self.experts // 2) if self.devices == 8 * self.experts else (self.devices,)
        return (self.items,) + chips + (self.share, self.columns)

    def final_outs(self):
        share, width = self.share, self.width
        return [jax.ShapeDtypeStruct((share, c), f32) for c in (3 * width, width, 128)]

    def store(self, outs, i, value):
        d_qkv, d_out, d_small = outs
        final = self.items - 1

        for f in range(self.firsts):

            @when(i == f)
            def _(f=f):
                d_out[:, f * self.columns : (f + 1) * self.columns] = value

        @when(jnp.logical_and(i >= self.firsts, i < final))
        def _():
            for p in range(3):
                at = pl.multiple_of(p * self.width + (i - self.firsts) * PAIR, PAIR)
                d_qkv[:, pl.ds(at, PAIR)] = value[:, p * PAIR : (p + 1) * PAIR]

        @when(i == final)
        def _():
            d_out[:, self.firsts * self.columns :] = value[:, : self.rest]
            d_small[...] = value[:, self.rest : self.rest + 128]

    def __call__(self, now, steps, *refs):
        experts, width, length = self.experts, self.width, self.length
        refs = list(refs)
        tok, cot, routes, dropped, qkv, lse, att, mixed_in, disp, info = refs[:10]
        small_hbm, qkv_hbm, out_hbm, dense_hbm, grad_hbm, after_hbm = refs[10:16]
        came_hbm = refs[16 : 16 + experts]
        mixed, tokens_grad, *rest = refs[16 + experts :]
        if self.moves:
            made = self.moves[-1].own
        else:
            made = rest.pop(0)
        came, dense, grads, ws, wo, wq, gains, d_heads, attn_in_t, grad_att, sems, wq_sems = rest
        fetch = lambda a, b, i: pltpu.make_async_copy(a, b, sems.at[i])
        capacity = self.capacity
        loads = [fetch(came_hbm[j], came.at[pl.ds(j * capacity, capacity)], j) for j in range(experts)]
        loads += [
            fetch(a, b, experts + i)
            for i, (a, b) in enumerate(
                ((dense_hbm, dense), (grad_hbm, grads), (after_hbm, tokens_grad), (small_hbm, ws), (out_hbm, wo))
            )
        ]

        def pair_weights(pair):
            slot = lax.rem(pair, 2)
            return [
                pltpu.make_async_copy(
                    qkv_hbm.at[:, :, pl.ds(pl.multiple_of(p * width + pair * PAIR, PAIR), PAIR)],
                    wq.at[slot, :, :, pl.ds(p * PAIR, PAIR)],
                    wq_sems.at[slot, p],
                )
                for p in range(3)
            ]

        put = lambda i, columns, values: self.put(made, i, columns, values)
        lane = lax.broadcasted_iota(jnp.int32, (length, 128), 1)
        over_lanes = lambda a: jnp.sum(a, axis=1, keepdims=True)

        @when(now == 0)
        def _():
            for copy in loads + pair_weights(0):
                copy.start()

        @when(now == 1)
        def _():
            for copy in loads:
                copy.wait()
            probs = jnp.where(jnp.logical_and(lane >= 2, lane < 2 + experts), info[...], 0.0)
            coef_0 = over_lanes(jnp.where(lane == 2 + experts, info[...], 0.0))
            coef_1 = over_lanes(jnp.where(lane == 3 + experts, info[...], 0.0))
            route, drop = columns_of(routes, dropped)
            chosen = jnp.where(lane - 2 == route, 1.0, 0.0)
            kept = (1 - drop[:, :1]).astype(f32)
            gate_prob = over_lanes(probs * chosen)
            gate = gate_prob * kept
            grad = cot[...].astype(f32)
            expert_tok = matmul(disp[...], came[:, :width])
            mixed[...] = (tokens_grad[...] + coef_0 * dense[...] + (coef_1 * gate) * expert_tok).astype(bf16)
            shared = over_lanes(grad * expert_tok)
            grad_0, grad_1 = over_lanes(grad * dense[...]), shared * gate
            both = coef_0 * grad_0 + coef_1 * grad_1
            grad_gate = shared * coef_1 * kept
            logits = jnp.where(
                jnp.logical_and(lane >= 2, lane < 2 + experts), (grad_gate * gate_prob) * (chosen - probs), 0.0
            )
            logits = jnp.where(lane == 2 + experts, coef_0 * (grad_0 - both), logits)
            logits = jnp.where(lane == 3 + experts, coef_1 * (grad_1 - both), logits)
            pieces = thirds(logits)
            d_heads[...] = add(*(product_tn(p, mixed_in[...]) for p in pieces))
            weights = ws[...].reshape(width, 128)
            grads[...] = (
                grads[...] + matmul(disp[...], came[:, width:]) + add(*(outer_nt(p, weights) for p in pieces))
            )
            gains[...] = weights.astype(f32).T[:8]

        @when(now == 2)
        def _():
            normed, scale = normalize(tokens_grad[...])
            d_heads[1:2] = jnp.sum(grads[...] * normed, axis=0, keepdims=True)
            grads[...] = cot[...].astype(f32) + norm_back(grads[...] * gains[1:2], normed, scale)
            normed, _ = normalize(tok[...].astype(f32))
            attn_in_t[...] = (normed * gains[0:1]).astype(bf16).T

        @when(now == 3)
        def _():
            grad_attn = grads[...].astype(bf16)
            grad_att[...] = outer_nt(grad_attn, wo[...].reshape(width, width)).astype(bf16)
            d_out = product_tn(att[...], grad_attn).astype(bf16)
            for f in range(self.firsts):
                put(f, slice(None), d_out[:, f * self.columns : (f + 1) * self.columns])
            put(self.items - 1, slice(0, self.rest), d_out[:, self.firsts * self.columns :])
            dense[...] = jnp.zeros_like(dense)

        @when(jnp.logical_and(now >= self.heads_at, now < self.last))
        def _():
            pair = now - self.heads_at
            cols = lambda part: pl.ds(pl.multiple_of(part * width + pair * PAIR, PAIR), PAIR)
            d_pair = attend_pair_backward(
                qkv[:, cols(0)], qkv[:, cols(1)], qkv[:, cols(2)], grad_att[:, cols(0)], lse[pair]
            )
            d_pair = jnp.concatenate(d_pair, axis=1)
            for copy in pair_weights(pair):
                copy.wait()

            @when(pair + 1 < self.pairs)
            def _():
                for copy in pair_weights(pair + 1):
                    copy.start()

            put(pair + self.firsts, slice(None), matmul(attn_in_t[...], d_pair).astype(bf16))
            dense[...] += outer_nt(d_pair, wq[lax.rem(pair, 2)].reshape(width, self.columns))

        @when(now == self.last)
        def _():
            normed, scale = normalize(tok[...].astype(f32))
            d_heads[0:1] = jnp.sum(dense[...] * normed, axis=0, keepdims=True)
            put(self.items - 1, slice(self.rest, self.rest + 128), d_heads[...].T.astype(bf16))
            if self.rest + 128 < self.columns:
                spare = self.columns - self.rest - 128
                put(self.items - 1, slice(self.rest + 128, None), jnp.zeros((width, spare), bf16))
            tokens_grad[...] = grads[...] + norm_back(dense[...] * gains[0:1], normed, scale)

    def put(self, made, i, columns, values):
        lead = made.shape[1:-1]
        at = (i,) + (slice(None),) * len(lead) + (columns,)
        made[at] = values.reshape(lead + values.shape[1:])


def gelu_both(v):
    c = math.sqrt(2.0 / math.pi)
    square = v * v
    t = jnp.tanh(c * (v + 0.044715 * (square * v)))
    half = 0.5 * (1.0 + t)
    slope = half + 0.5 * v * (1.0 - t * t) * (c * (1.0 + (3 * 0.044715) * square))
    return v * half, slope


def mlp_block(x, g, xt, gt, w1, w2, out_sum, back_sum):
    hidden, slope = gelu_both(matmul(x[...], w1))
    hidden = hidden.astype(bf16)
    grad_pre = (slope * outer_nt(g[...], w2)).astype(bf16)
    out_sum[...] += matmul(hidden, w2)
    back_sum[...] += outer_nt(grad_pre, w1)
    return matmul(xt[...], grad_pre).astype(bf16), matmul(gt[...], hidden).astype(bf16)


class Experts:
    TURNS = 7

    def __init__(self, pieces, blocks, width, size, chunks, back):
        self.parts, self.piece = len(pieces), pieces[0].shape
        self.blocks, self.width, self.size, self.back = blocks, width, size, back
        rows = self.parts * self.piece[0]
        if chunks:
            self.block = (2, size // 256, chunks, width // chunks, 128)
            whole = (blocks // 2, 2) + self.block
        else:
            self.block = (width, size)
            whole = (blocks,) + self.block
        piece = jax.ShapeDtypeStruct(self.piece, bf16)
        self.outs = [piece] * self.parts + [jax.ShapeDtypeStruct(whole, bf16)] * 2
        self.scratch = (
            [pltpu.VMEM(self.piece, bf16)] * self.parts
            + [pltpu.VMEM((rows, width), bf16)] * 2
            + [pltpu.VMEM((width, rows), bf16)] * 2
            + [pltpu.VMEM((rows, width), f32)] * 2
            + [pltpu.VMEM((2,) + self.block, bf16)] * 2
            + [pltpu.SemaphoreType.DMA((2, 2)), pltpu.SemaphoreType.DMA((self.parts,))]
            + [pltpu.VMEM((2, width, size), bf16), pltpu.VMEM((2, size, width), bf16)]
            + [pltpu.SemaphoreType.DMA((2, 2))]
        )

    def __call__(self, now, steps, *refs):
        refs = list(refs)
        take = lambda count: [refs.pop(0) for _ in range(count)]
        pieces, full = take(self.parts), take(2)
        kept, targets, results = take(self.parts), take(2), take(self.parts)
        x, g, xt, gt, out_sum, back_sum, stage_1, stage_2, sems, kept_sems, w1, w2, w_sems = refs
        width, size = self.width, self.piece[0]

        def flush(step):
            at = lax.rem(step, 2)
            where = (step // 2, at) if len(self.block) > 2 else (step,)
            return [
                pltpu.make_async_copy(stage.at[at], target.at[where], sems.at[at, i])
                for i, (stage, target) in enumerate(zip((stage_1, stage_2), targets))
            ]

        def weights(step):
            at = lax.rem(step, 2)
            return [
                pltpu.make_async_copy(a.at[step], b.at[at], w_sems.at[at, i])
                for i, (a, b) in enumerate(zip(full, (w1, w2)))
            ]

        @when(now == 0)
        def _():
            for copy in weights(0):
                copy.start()
            for j, piece in enumerate(pieces):
                x[j * size : (j + 1) * size] = piece[:, :width]
                g[j * size : (j + 1) * size] = piece[:, width:]
            xt[...] = x[...].T
            gt[...] = g[...].T
            out_sum[...] = jnp.zeros_like(out_sum)
            back_sum[...] = jnp.zeros_like(back_sum)

        def block(step, _):
            for copy in weights(step):
                copy.wait()

            @when(step + 1 < self.blocks)
            def _():
                for copy in weights(step + 1):
                    copy.start()

            @when(step >= 2)
            def _():
                for copy in flush(step - 2):
                    copy.wait()

            slot = lax.rem(step, 2)
            for stage, d in zip((stage_1, stage_2), mlp_block(x, g, xt, gt, w1[slot], w2[slot], out_sum, back_sum)):
                if len(self.block) == 2:
                    stage[slot] = d
                else:
                    for c in range(d.shape[1] // 128):
                        share = d[:, c * 128 : (c + 1) * 128].reshape(self.block[2:])
                        stage[slot, c // self.block[1], c % self.block[1]] = share
            for copy in flush(step):
                copy.start()
            return 0

        lax.fori_loop(now * self.blocks // steps, (now + 1) * self.blocks // steps, block, 0)

        @when(now == steps - 1)
        def _():
            for h, total in enumerate((out_sum, back_sum)):
                for j, result in enumerate(results):
                    result[:, h * width : (h + 1) * width] = total[j * size : (j + 1) * size].astype(bf16)
            keep = [pltpu.make_async_copy(a, b, kept_sems.at[j]) for j, (a, b) in enumerate(zip(results, kept))]
            for copy in keep:
                copy.start()
            for copy in keep:
                copy.wait()
            if self.back:
                self.back.send()
            for step in (self.blocks - 2, self.blocks - 1):
                for copy in flush(step):
                    copy.wait()


def finish(arrays, small, cuts):
    pieces = []
    for i, a in enumerate(arrays):
        axis = 1 if a.shape[0] == 1 else 0
        parts = 4 if a.size * a.dtype.itemsize >= MIB else 1
        size = a.shape[axis] // parts
        pieces += [(i, (0,) * axis + (pl.ds(p * size, size),)) for p in range(parts)]
    n = len(arrays)

    def kernel(*refs):
        ins, columns, outs, rows = refs[:n], refs[n], refs[n + 1 : 2 * n + 1], refs[2 * n + 1 : -n - 1]
        held, sems = refs[-n - 1 : -1], refs[-1]
        move = lambda a, b, way: [
            pltpu.make_async_copy(a[i].at[at], b[i].at[at], sems.at[way, c]) for c, (i, at) in enumerate(pieces)
        ]
        loads, copies = move(ins, held, 0), move(held, outs, 1)
        for load in loads:
            load.start()
        for load, copy in zip(loads, copies):
            load.wait()
            copy.start()
        turned = columns[...].T
        for ref, first, last in zip(rows, cuts, cuts[1:]):
            ref[...] = turned[first:last]
        for copy in copies:
            copy.wait()

    whole, hbm = pl.BlockSpec(memory_space=pltpu.VMEM), pl.BlockSpec(memory_space=pltpu.HBM)
    shapes = [jax.ShapeDtypeStruct(a.shape, a.dtype) for a in arrays]
    shapes += [jax.ShapeDtypeStruct((b - a, small.shape[0]), f32) for a, b in zip(cuts, cuts[1:])]
    results = pl.pallas_call(
        kernel,
        out_shape=shapes,
        in_specs=[hbm] * n + [whole],
        out_specs=[hbm] * n + [whole] * (len(cuts) - 1),
        scratch_shapes=[pltpu.VMEM(a.shape, a.dtype) for a in arrays] + [pltpu.SemaphoreType.DMA((2, len(pieces)))],
        compiler_params=pltpu.CompilerParams(vmem_limit_bytes=60 * MIB),
        name="finish",
    )(*arrays, small)
    return results[:n], results[n:]


def move(name, moves, collective_id, experts):
    return call(name, 1, None, [], [], [], [], [], moves, collective_id, experts, 0)


def shards(
    fast,
    tokens,
    gain_attn,
    w_qkv,
    w_out,
    gain_mix,
    w_fc,
    w_proj,
    w_router,
    w_coef,
    expert_in,
    expert_out,
    routes,
    dropped,
    cotangent,
):
    experts = lax.axis_size("expert")
    nodes = lax.axis_size("node")
    devices = nodes * experts
    width = tokens.shape[1]
    tok_rows = tokens.shape[0]
    ff = w_fc.shape[1]
    share = w_qkv.shape[0]
    small = jnp.concatenate([gain_attn[:, None], gain_mix[:, None], w_router, w_coef], axis=1)
    small = jnp.pad(small, ((0, 0), (0, 128 - small.shape[1])))
    win, wout = expert_in[0], expert_out[0]
    cut = lambda a, rows, columns, m, n: [
        [(a, i * (rows // m), rows // m, j * (columns // n), columns // n)] for i in range(m) for j in range(n)
    ]
    weights = (small, w_qkv, w_out, w_fc, w_proj)
    capacity = -(-(tok_rows * 10) // (8 * experts))
    moves, given = [], None
    if fast:
        sixth = cut(1, share, 3 * width, 1, 6)
        items = sixth[:2] + [sixth[2] + sixth[3], sixth[4] + sixth[5]] + cut(2, share, width, 1, 1)
        items += cut(3, share, ff, 1, 4) + cut(4, ff // devices, width, 4, 1)
        items[0] = cut(0, share, 128, 1, 1)[0] + items[0]
        assert len(items) == Forward.DENSE_ITEMS
        items += cut(5, width, win.shape[1], 4, 1) + cut(6, wout.shape[0], width, 4, 1)
        moves = [Gather(list(weights) + [win, wout], [True] * 5 + [False] * 2, items, nodes, experts)]
        moves.append(Exchange([], 1, experts, None, moves[0].turns, (capacity, 2 * width)))
        full = []
    else:
        full = [lax.all_gather(a, AXES, axis=0, tiled=False) for a in weights]
        win_full, wout_full = (lax.all_gather(a, "node", axis=0, tiled=False) for a in (win, wout))

    def scatter_xla(parts, axes):
        return lax.psum_scatter(parts, axes, scatter_dimension=0, tiled=False).astype(f32)

    def exchange(parts, sign):
        moved = [parts[0]]
        for j in range(1, experts):
            shift = [(s, (s + sign * j) % experts) for s in range(experts)]
            moved.append(lax.ppermute(parts[j], "expert", shift))
        return moved

    forward = Forward(tok_rows, width, experts, devices, capacity, ff, *(moves or (None, None)))
    whole, hbm = pl.BlockSpec(memory_space=pltpu.VMEM), pl.BlockSpec(memory_space=pltpu.HBM)
    routes, dropped = routes.reshape(1, tok_rows), dropped.reshape(1, tok_rows)
    if fast:

        def given(ins, os, own):
            moves[1].sources = own[: experts - 1]

    results = call(
        "forward",
        forward.steps,
        forward,
        [tokens, cotangent, routes, dropped] + full,
        [whole] * 4 + [hbm] * len(full),
        forward.outs + forward.targets,
        [whole] * len(forward.outs) + [hbm] * 2,
        forward.scratch,
        moves,
        1,
        experts,
        12 * tok_rows * width * (width + ff),
        given,
    )
    qkv_rows, lse, attended, after_attn, mixed_in, dispatch, probs, dense_out, grad_mixed = results[:9]
    results = results[9:]
    leaving, (d_fc, d_proj), moved = (
        results[: forward.kept],
        results[forward.kept : forward.kept + 2],
        results[forward.kept + 2 :],
    )
    small_full, qkv_full, out_full = (moved if fast else full)[:3]
    scatters, return_to, given = [], None, None
    chunks = 4
    step = width // chunks
    half = (experts // 2, step, 128)
    win_out = [jax.ShapeDtypeStruct(expert_in.shape, f32)]
    wout_out = [jax.ShapeDtypeStruct(expert_out.shape, f32)]

    def store_wout(out, chunk, sums):
        at = pl.ds(pl.multiple_of(chunk * step, step), step)
        for h, total in enumerate(sums):
            for c in range(half[0]):
                out[0, (h * half[0] + c) * 128 : (h * half[0] + c + 1) * 128, at] = total[c].T

    if fast:
        win_full, wout_full = moved[5:7]
        arrived = leaving + moved[7:]
        by_chip = lambda a: a.reshape(4, 2, 2, experts // 2, chunks, step, 128)

        def store(outs, i, value):
            if i < chunks:
                for q in range(step // share):
                    at = (i * (step // share) + q) * 128
                    outs[0][:, at : at + 128] = value[q * share : (q + 1) * share]
            else:
                outs[1][:, (i - chunks) * step : (i - chunks + 1) * step] = value.T

        def store_plane(outs, i, sums):
            @when(i < 2 * chunks)
            def _():
                for h, total in enumerate(sums):
                    outs[0][h * half[0] : (h + 1) * half[0], i] = total.astype(bf16)

            @when(i >= 2 * chunks)
            def _():
                at = pl.ds(pl.multiple_of((i - 2 * chunks) * step, step), step)
                for h, total in enumerate(sums):
                    for c in range(half[0]):
                        outs[1][0, at, (h * half[0] + c) * 128 : (h * half[0] + c + 1) * 128] = total[c]

        outs = [jax.ShapeDtypeStruct((experts, 2 * chunks) + half[1:], bf16)]
        parts = [(by_chip(d_fc), False, 0, chunks), (by_chip(d_proj), False, 0, chunks), (None, False, 0, chunks)]
        summing = Scatter(parts, half, experts, outs + win_out, store_plane, spread=True)
        return_to = Exchange([], -1, experts, None, summing.turns, leaving[0].shape)
        scatters = [return_to, summing]
    else:
        arrived = exchange(leaving, 1)
    blocks, size = win_full.shape[0], win_full.shape[2]
    experts_kernel = Experts(arrived, blocks, width, size, chunks if fast else None, return_to)
    if fast:

        def given(ins, os, own):
            summing.given = [os[experts]]
            return_to.sources = os[1:experts]

    results = call(
        "expert_mlp",
        experts_kernel.TURNS,
        experts_kernel,
        arrived + [win_full, wout_full],
        [whole] * experts + [hbm] * 2,
        experts_kernel.outs,
        [hbm] * len(experts_kernel.outs),
        experts_kernel.scratch,
        scatters,
        3,
        experts,
        12 * experts * capacity * width * blocks * size,
        given,
    )
    returned, (d_win, d_wout) = results[:experts], results[experts : experts + 2]
    if fast:
        results = results[experts + 2 :]
        came_back = returned[:1] + results[: experts - 1]
        plane_sums, grad_win = results[experts - 1 :]
    else:
        came_back = exchange(returned, -1)
    back = Back(tok_rows, width, experts, devices, capacity)
    back.moves = []
    if fast:
        parts = [(None, True, 0, back.items)]
        made = back.made()
        scatter_rest = Scatter(
            parts, made[4:], experts, back.final_outs(), back.store, back.first_item, made, spread=True
        )
        parts = [(d_wout, False, 0, chunks)]
        scatter_wout = Scatter(
            parts, half, experts, wout_out, lambda outs, i, sums: store_wout(outs[0], i, sums), spread=True
        )
        outs = [jax.ShapeDtypeStruct((share, ff), f32), jax.ShapeDtypeStruct((ff // devices, width), f32)]
        along = Along(plane_sums, experts, outs, store, max(scatter_rest.turns, scatter_wout.turns))
        back.moves = [along, scatter_wout, scatter_rest]
    outs = back.outs + ([] if fast else [jax.ShapeDtypeStruct((back.items, width, back.columns), bf16)])
    mixed, tokens_grad, *results = call(
        "back",
        back.steps,
        back,
        [tokens, cotangent, routes, dropped, qkv_rows, lse, attended, mixed_in, dispatch, probs]
        + [small_full, qkv_full, out_full, dense_out, grad_mixed, after_attn]
        + came_back,
        [whole] * 10 + [hbm] * (6 + experts),
        outs,
        [whole] * len(outs),
        back.scratch,
        back.moves,
        5,
        experts,
        32 * tok_rows * width * width,
    )
    if fast:
        done, (gain_1, gain_2, router, coef) = finish(
            [mixed, tokens_grad, grad_win] + results[:5], results[5], (0, 1, 2, 2 + experts, 4 + experts)
        )
        mixed, tokens_grad, grad_win, grad_fc, grad_proj, grad_wout, grad_wqkv, grad_wo = done
        small_grads = (gain_1[0], gain_2[0], router.T, coef.T)
    else:
        summed = scatter_xla(results[0].reshape(back.items, devices, share, -1).swapaxes(0, 1), AXES)
        last = summed[-1]
        grad_wo = jnp.concatenate([*summed[: back.firsts], last[:, : back.rest]], axis=1)
        grad_small = last[:, back.rest : back.rest + 128]
        small_grads = (
            grad_small[:, 0],
            grad_small[:, 1],
            grad_small[:, 2 : 2 + experts],
            grad_small[:, 2 + experts : 4 + experts],
        )
        pairs = summed[back.firsts : -1].reshape(back.pairs, share, 3, PAIR)
        grad_wqkv = pairs.transpose(1, 2, 0, 3).reshape(share, 3 * width)
        grad_fc = scatter_xla(d_fc.reshape(devices, share, ff), AXES)
        by_unit = d_proj.reshape(width, devices, ff // devices).transpose(1, 0, 2)
        grad_proj = scatter_xla(by_unit, AXES).T
        grad_win = scatter_xla(d_win, "node")[None]
        grad_wout = scatter_xla(d_wout, "node").T[None]
    return (
        mixed,
        tokens_grad,
        small_grads[0],
        grad_wqkv,
        grad_wo,
        small_grads[1],
        grad_fc,
        grad_proj,
        small_grads[2],
        small_grads[3],
        grad_win,
        grad_wout,
    )


def solution(mesh):
    rows = P(AXES, None)
    in_specs = (
        rows,
        P(AXES),
        rows,
        rows,
        P(AXES),
        rows,
        rows,
        rows,
        rows,
        P("expert", None, "node"),
        P("expert", "node", None),
        rows,
        P(AXES),
        rows,
    )
    out_specs = (
        rows,
        rows,
        P(AXES),
        rows,
        rows,
        P(AXES),
        rows,
        rows,
        rows,
        rows,
        P("expert", None, "node"),
        P("expert", "node", None),
    )
    fast = mesh.shape["node"] == 8 and mesh.shape["expert"] == 4
    return jax.shard_map(
        functools.partial(shards, fast), mesh=mesh, in_specs=in_specs, out_specs=out_specs, check_vma=False
    )
```

```python
import functools
import math

import jax
import jax.numpy as jnp
from jax import lax
from jax.experimental import pallas as pl
from jax.experimental.pallas import tpu as pltpu
from jax.sharding import PartitionSpec as P

HD = 64
PAIR = 2 * HD
SEQ = 512
QB = 256
BLOCK = 512
MIB = 1 << 20
AXES = ("node", "expert")
MESH = pl.DeviceIdType.MESH
epsilon = 1e-05
f32 = jnp.float32
bf16 = jnp.bfloat16


def normalize(values):
    centered = values - jnp.mean(values, axis=-1, keepdims=True)
    inv_scale = lax.rsqrt(jnp.mean(centered * centered, axis=-1, keepdims=True) + epsilon)
    return (centered * inv_scale, inv_scale)


def norm_back(grad_norm, normed, inv_scale):
    mean_grad = jnp.mean(grad_norm, axis=-1, keepdims=True)
    mean_cross = jnp.mean(grad_norm * normed, axis=-1, keepdims=True)
    return inv_scale * (grad_norm - mean_grad - normed * mean_cross)


def contract(left_op, right_op, left_dim, right_dim):
    return lax.dot_general(
        left_op, right_op, (((left_dim,), (right_dim,)), ((), ())), preferred_element_type=f32
    )


def matmul(left_op, right_op):
    return contract(left_op, right_op, 1, 0)


def product_tn(left_op, right_op):
    return contract(left_op, right_op, 0, 0)


def outer_nt(left_op, right_op):
    return contract(left_op, right_op, 1, 1)


class Place:
    def __init__(self, experts):
        self.experts = experts
        self.n, self.e = lax.axis_index("node"), lax.axis_index("expert")
        n = self.n
        self.k, self.x, self.y = lax.rem(n, 2), lax.rem(n // 2, 2), n // 4
        k, x, y = self.k, self.x, self.y
        self.nx, self.ny = y * 4 + (1 - x) * 2 + k, (1 - y) * 4 + x * 2 + k
        self.nd, self.nc = (1 - y) * 4 + (1 - x) * 2 + k, y * 4 + x * 2 + 1 - k

    def z(self, j):
        return (self.n, lax.rem(self.e + j, self.experts))

    def greet(self, along_z):
        barrier = pltpu.get_barrier_semaphore()
        peers = [(self.nx, self.e), (self.ny, self.e), (self.nc, self.e)]
        if along_z:
            peers += [self.z(j) for j in range(1, self.experts)]
        for peer in peers:
            pl.semaphore_signal(barrier, inc=1, device_id=peer, device_id_type=MESH)
        pl.semaphore_wait(barrier, len(peers))


def when(condition):
    return pl.when(condition)


class Gather:
    def __init__(self, args, dense, items, nodes, experts):
        self.args, self.dense, self.items, self.experts = args, dense, items, experts
        self.outs = [
            jax.ShapeDtypeStruct(((nodes * experts if d else nodes),) + a.shape, a.dtype)
            for a, d in zip(args, dense)
        ]
        hbm = pl.BlockSpec(memory_space=pltpu.HBM)
        self.in_specs, self.out_specs = [hbm] * len(args), [hbm] * len(args)
        m = sum(len(item) for item in items)
        self.scratch = [
            pltpu.SemaphoreType.DMA((m, experts + 7)),
            pltpu.SemaphoreType.DMA((m, experts + 7)),
            pltpu.SemaphoreType.DMA((m,)),
        ]
        self.along_z = any(dense)
        self.steps = [self.along, self.across, self.corner, self.over, self.end]
        self.turns = len(items) + len(self.steps) - 1

    def bind(self, ins, outs, scratch, place):
        experts = self.experts
        send, recv, loc = scratch
        p, e = place, place.e

        def remote(source, target, item, kind, device):
            return pltpu.make_async_remote_copy(
                src_ref=source,
                dst_ref=target,
                send_sem=send.at[item, kind],
                recv_sem=recv.at[item, kind],
                device_id=device,
                device_id_type=MESH,
            )

        self.full = outs
        self.bound = [[] for _ in self.items]
        pieces = [(turn, piece) for turn, item in enumerate(self.items) for piece in item]
        for i, (turn, (arg, row, rows, col, columns)) in enumerate(pieces):
            dense = self.dense[arg]
            shard, whole = ins[arg], outs[arg]
            per = experts if dense else 1
            own = p.n * per + (e if dense else 0)

            def view(ref, lead, start=0, size=None, whole_rows=rows, row=row, col=col, columns=columns):
                return ref.at[lead, pl.ds(row + start, size or whole_rows), pl.ds(col, columns)]

            def bundle(m, view=view, whole=whole, per=per):
                return view(whole, pl.ds(m * per, per))

            def half(m, h, view=view, whole=whole, per=per, dense=dense, rows=rows):
                if dense:
                    return view(whole, pl.ds(m * per + h * (per // 2), per // 2))
                return view(whole, m, h * (rows // 2), rows // 2)

            mine = shard.at[pl.ds(row, rows), pl.ds(col, columns)]
            land = view(whole, own)
            local = pltpu.make_async_copy(mine, land, loc.at[i])
            z = []
            if dense:
                z = [remote(mine, land, i, j - 1, p.z(j)) for j in range(1, experts)]
            first, last = (bundle(p.n), bundle(p.n)) if dense else (mine, land)
            b = experts - 1
            xy = [remote(first, last, i, b, (p.nx, e)), remote(first, last, i, b + 1, (p.ny, e))]
            diag = [
                remote(half(p.nx, 0), half(p.nx, 0), i, b + 2, (p.ny, e)),
                remote(half(p.ny, 1), half(p.ny, 1), i, b + 3, (p.nx, e)),
            ]
            core = [remote(first, last, i, b + 4, (p.nc, e))] + [
                remote(bundle(m), bundle(m), i, b + 5 + j, (p.nc, e)) for j, m in enumerate((p.nx, p.ny, p.nd))
            ]
            self.bound[turn].append((local, z, xy, diag, core))

    def turn(self, now):
        for t in range(self.turns):

            @when(now == t)
            def _(t=t):
                for late, step in enumerate(self.steps):
                    if 0 <= t - late < len(self.items):
                        for piece in self.bound[t - late]:
                            step(*piece)

    def finish(self, now):
        pass

    def along(self, local, z, xy, diag, core):
        local.start()
        for copy in z:
            copy.start()

    def across(self, local, z, xy, diag, core):
        for copy in z:
            copy.wait()
        local.wait()
        xy[0].start()
        xy[1].start()
        core[0].start()

    def corner(self, local, z, xy, diag, core):
        for i in range(2):
            xy[i].wait()
            diag[i].start()
            core[1 + i].start()

    def over(self, local, z, xy, diag, core):
        diag[0].wait()
        diag[1].wait()
        core[3].start()

    def end(self, local, z, xy, diag, core):
        for copy in core:
            copy.wait()


class Exchange:
    along_z = True

    def __init__(self, pieces, sign, experts, start, turns, shape):
        self.args, self.sign, self.experts, self.start, self.turns = list(pieces), sign, experts, start, turns
        self.given = None
        self.outs = [jax.ShapeDtypeStruct(shape, bf16)] * (experts - 1)
        hbm = pl.BlockSpec(memory_space=pltpu.HBM)
        self.in_specs, self.out_specs = [hbm] * len(self.args), [hbm] * (experts - 1)
        self.scratch = [pltpu.SemaphoreType.DMA((experts,)), pltpu.SemaphoreType.DMA((experts,))]

    def bind(self, ins, outs, scratch, place):
        self.out, self.sems, self.place = outs, scratch, place
        if ins:
            self.sources = ins

    def copies(self):
        return [
            pltpu.make_async_remote_copy(
                src_ref=source,
                dst_ref=self.out[j],
                send_sem=self.sems[0].at[j],
                recv_sem=self.sems[1].at[j],
                device_id=self.place.z((self.sign * (j + 1)) % self.experts),
                device_id_type=MESH,
            )
            for j, source in enumerate(self.sources)
        ]

    def send(self):
        for copy in self.copies():
            copy.start()

    def turn(self, now):
        if self.start is not None:

            @when(now == self.start)
            def _():
                self.send()

    def finish(self, now):
        @when(now == self.turns - 1)
        def _():
            for copy in self.copies():
                copy.wait()


class Scatter:
    RING, SPREAD_RING, CORE_RING = 6, 8, 4

    def __init__(self, parts, half, experts, outs, store, start=0, made=None, spread=False):
        self.experts, self.outs, self.store, self.start, self.made = experts, outs, store, start, made
        self.parts = parts
        self.given = []
        self.args = [p[0] for p in parts if p[0] is not None]
        h = half
        self.starts = [sum(p[3] for p in parts[:a]) for a in range(len(parts) + 1)]
        m = self.m = self.starts[-1]
        self.m_z = sum(p[3] for p in parts if p[1])
        unit = h[1:]
        ring = self.ring = min(self.SPREAD_RING if spread else self.RING, m)
        self.core_ring = min(self.CORE_RING, m)
        self.in_specs = [pl.BlockSpec(memory_space=pltpu.HBM)] * len(self.args)
        self.out_specs = [pl.BlockSpec(memory_space=pltpu.VMEM)] * len(outs)
        kinds = 7 + experts
        self.scratch = [
            pltpu.VMEM(made or (ring, 4, 2) + h, bf16),
            pltpu.VMEM((self.core_ring, 4, 2) + h, bf16),
            pltpu.VMEM((ring, 2) + h, bf16),
            pltpu.VMEM((ring, 2) + h, bf16),
            pltpu.VMEM((ring,) + h, bf16),
            pltpu.VMEM((ring,) + h, bf16),
            pltpu.SemaphoreType.DMA((m, kinds)),
            pltpu.SemaphoreType.DMA((m, kinds)),
            pltpu.SemaphoreType.DMA((m,)),
        ]
        if self.m_z:
            self.scratch.append(pltpu.VMEM((self.m_z, experts - 1) + unit, bf16))
            self.scratch.append(pltpu.VMEM((self.m_z, experts) + unit, bf16))
        self.stages = (0, 1, 3, 5, 7) if spread else (0, 1, 2, 3, 4)
        self.turns = start + m + self.stages[4 if self.m_z else 3]
        self.along_z = self.m_z > 0

    def bind(self, ins, outs, scratch, place):
        ins = list(ins)
        given = list(self.given)
        self.sources = [given.pop(0) if p[0] is None else ins.pop(0) for p in self.parts] if not self.made else []
        self.out, self.place = outs, place
        self.own, self.rc, self.rx, self.ry, self.lx, self.ly, self.sent, self.recv, self.loc = scratch[:9]
        self.rz, self.zs = scratch[9:] if self.m_z else (None, None)

    def slot(self, i):
        return lax.rem(i, self.ring)

    def remote(self, source, target, item, kind, device):
        return pltpu.make_async_remote_copy(
            src_ref=source,
            dst_ref=target,
            send_sem=self.sent.at[item, kind],
            recv_sem=self.recv.at[item, kind],
            device_id=device,
            device_id_type=MESH,
        )

    def at(self, i, site, *more):
        return (i, site, self.place.k) + more if self.made else (self.slot(i), site) + more

    def first(self, source, i, chunk):
        p = self.place
        land = self.rc.at[lax.rem(i, self.core_ring)]
        if self.made:
            return [self.remote(self.own.at[i, :, 1 - p.k], land, i, 0, (p.nc, p.e))]
        part = lambda core: source.at[:, core, :, :, chunk]
        local = pltpu.make_async_copy(part(p.k), self.own.at[self.slot(i)], self.loc.at[i])
        return [self.remote(part(1 - p.k), land, i, 0, (p.nc, p.e)), local]

    def sites(self):
        p = self.place
        return p.y * 2 + p.x, p.y * 2 + 1 - p.x, (1 - p.y) * 2 + p.x, (1 - p.y) * 2 + 1 - p.x

    def round_one(self, i):
        p = self.place
        b = self.slot(i)
        _, to_x, to_y, diag = self.sites()
        own = lambda *at: self.own.at[self.at(i, *at)]
        return [
            self.remote(own(diag, 0), self.rx.at[b, 0], i, 1, (p.nx, p.e)),
            self.remote(own(diag, 1), self.ry.at[b, 0], i, 2, (p.ny, p.e)),
            self.remote(own(to_x, 0), self.rx.at[b, 1], i, 3, (p.nx, p.e)),
            self.remote(own(to_y, 1), self.ry.at[b, 1], i, 4, (p.ny, p.e)),
        ]

    def round_two(self, i):
        p = self.place
        b = self.slot(i)
        _, to_x, to_y, _ = self.sites()
        return [
            self.remote(self.own.at[self.at(i, to_x, 1)], self.lx.at[b], i, 5, (p.nx, p.e)),
            self.remote(self.own.at[self.at(i, to_y, 0)], self.ly.at[b], i, 6, (p.ny, p.e)),
        ]

    def round_z(self, i):
        p = self.place
        return [
            self.remote(self.zs.at[i, lax.rem(p.e + j, self.experts)], self.rz.at[i, j - 1], i, 6 + j, p.z(j))
            for j in range(1, self.experts)
        ]

    def turn(self, now):
        limits = (self.m, self.m, self.m, self.m, self.m_z)
        steps = (self.load, self.chip, self.cross, self.plane, self.column)
        for limit, late, step in zip(limits, self.stages, steps):
            i = now - self.start - late
            if limit:

                @when(jnp.logical_and(i >= 0, i < limit))
                def _(step=step, i=i):
                    step(i)

    def finish(self, now):
        pass

    def load(self, i):
        if self.made:
            self.first(None, i, 0)[0].start()
            return
        for a, source in enumerate(self.sources):

            @when(jnp.logical_and(i >= self.starts[a], i < self.starts[a + 1]))
            def _(a=a, source=source):
                for copy in self.first(source, i, i - self.starts[a] + self.parts[a][2]):
                    copy.start()

    def chip(self, i):
        for copy in self.first(None if self.made else self.sources[0], i, 0):
            copy.wait()

        def sum_one(q, _):
            at = self.at(i, q)
            self.own[at] = add(self.own[at], self.rc[lax.rem(i, self.core_ring), q]).astype(bf16)
            return 0

        lax.fori_loop(0, 4, sum_one, 0)
        for copy in self.round_one(i):
            copy.start()

    def cross(self, i):
        one = self.round_one(i)
        two = self.round_two(i)
        b = self.slot(i)
        _, to_x, to_y, _ = self.sites()
        for copy in one:
            copy.wait()
        at_x, at_y = self.at(i, to_x, 1), self.at(i, to_y, 0)
        self.own[at_x] = add(self.own[at_x], self.ry[b, 0]).astype(bf16)
        two[0].start()
        self.own[at_y] = add(self.own[at_y], self.rx[b, 0]).astype(bf16)
        two[1].start()

    def plane(self, i):
        for copy in self.round_two(i):
            copy.wait()
        mine, _, _, _ = self.sites()
        b = self.slot(i)
        sums = lambda: (
            add(self.own[self.at(i, mine, 0)], self.rx[b, 1], self.ly[b]),
            add(self.own[self.at(i, mine, 1)], self.lx[b], self.ry[b, 1]),
        )
        if self.m_z:

            @when(i < self.m_z)
            def _():
                s = self.experts // 2
                for h, total in enumerate(sums()):
                    self.zs[i, h * s : (h + 1) * s] = total.astype(bf16)
                for copy in self.round_z(i):
                    copy.start()

        if self.m_z < self.m:

            @when(i >= self.m_z)
            def _():
                self.store(self.out, i, sums())

    def column(self, i):
        for copy in self.round_z(i):
            copy.wait()
        terms = [self.zs[i, self.place.e]] + [self.rz[i, j] for j in range(self.experts - 1)]
        self.store(self.out, i, add(*terms))


class Along:
    along_z = True

    def __init__(self, shares, experts, outs, store, turns):
        self.args, self.experts, self.outs, self.store, self.turns = [shares], experts, outs, store, turns
        self.in_specs = [pl.BlockSpec(memory_space=pltpu.HBM)]
        self.out_specs = [pl.BlockSpec(memory_space=pltpu.VMEM)] * len(outs)
        self.items = shares.shape[1]
        self.scratch = [
            pltpu.VMEM(shares.shape, bf16),
            pltpu.SemaphoreType.DMA((experts,)),
            pltpu.SemaphoreType.DMA((experts,)),
        ]

    def bind(self, ins, outs, scratch, place):
        self.source, self.out, self.place = ins[0], outs, place
        self.land, self.sent, self.recv = scratch

    def copies(self):
        p = self.place
        copies = [pltpu.make_async_copy(self.source.at[p.e], self.land.at[0], self.recv.at[0])]
        return copies + [
            pltpu.make_async_remote_copy(
                src_ref=self.source.at[lax.rem(p.e + j, self.experts)],
                dst_ref=self.land.at[j],
                send_sem=self.sent.at[j],
                recv_sem=self.recv.at[j],
                device_id=p.z(j),
                device_id_type=MESH,
            )
            for j in range(1, self.experts)
        ]

    def turn(self, now):
        @when(now == 0)
        def _():
            for copy in self.copies():
                copy.start()

    def finish(self, now):
        @when(now == self.turns - 1)
        def _():
            for copy in self.copies():
                copy.wait()
            for i in range(self.items):
                self.store(self.out, i, add(*(self.land[j, i] for j in range(self.experts))))


def add(*terms):
    return functools.reduce(jnp.add, [t.astype(f32) for t in terms])


def call(
    name, steps, body, args, in_specs, outs, out_specs, scratch, moves, collective_id, experts, flops, given=None
):
    total = max([steps] + [m.turns for m in moves])

    def hold(spec):
        if spec.block_shape is None:
            return spec
        index = spec.index_map
        return pl.BlockSpec(spec.block_shape, lambda j: index(jnp.minimum(j, steps - 1)))

    join = lambda what: [x for m in moves for x in getattr(m, what)]

    def kernel(*refs):
        refs = list(refs)
        take = lambda group: [refs.pop(0) for _ in group]
        ins, m_ins = take(args), [take(m.args) for m in moves]
        os, m_os = take(outs), [take(m.outs) for m in moves]
        own, m_own = take(scratch), [take(m.scratch) for m in moves]
        now = pl.program_id(0)
        if moves:
            place = Place(experts)
            if given is not None:
                given(ins, os, own)
            for m, a, o, r in zip(moves, m_ins, m_os, m_own):
                m.bind(a, o, r, place)

            @when(now == 0)
            def _():
                place.greet(any(m.along_z for m in moves))

            for m in moves:
                m.turn(now)
        if body is not None:

            @when(now < steps)
            def _():
                body(now, steps, *ins, *os, *own)

        for m in moves:
            m.finish(now)

    results = pl.pallas_call(
        kernel,
        grid=(total,),
        out_shape=list(outs) + join("outs"),
        in_specs=[hold(s) for s in in_specs] + join("in_specs"),
        out_specs=[hold(s) for s in out_specs] + join("out_specs"),
        scratch_shapes=list(scratch) + join("scratch"),
        cost_estimate=pl.CostEstimate(flops=flops, bytes_accessed=32 * MIB, transcendentals=0),
        compiler_params=pltpu.CompilerParams(
            vmem_limit_bytes=60 * MIB,
            **({"collective_id": collective_id, "has_side_effects": True} if moves else {}),
        ),
        name=name,
    )(*args, *join("args"))
    return list(results)


def masks():
    lanes = lax.broadcasted_iota(jnp.int32, (1, PAIR), 1)
    return [(lanes // HD == h).astype(bf16) for h in range(2)]


def causal(scores_t, start):
    keys = lax.broadcasted_iota(jnp.int32, scores_t.shape, 0)
    queries = lax.broadcasted_iota(jnp.int32, scores_t.shape, 1) + start
    return jnp.where(keys <= queries, scores_t, -jnp.inf)


def attend_pair(q, k, v):
    q = q * (1.0 / math.sqrt(HD))
    vt = v.T
    length = q.shape[0]
    outs, tops = [], []
    for h, mask in enumerate(masks()):
        kh = k * mask
        row, logs = [], []
        for start in range(0, length, QB):
            end = start + QB
            scores = causal(outer_nt(kh[:end], q[start:end]), start)
            top = jnp.max(scores, axis=0, keepdims=True)
            expd = jnp.exp(scores - top)
            total = jnp.sum(expd, axis=0, keepdims=True)
            probs = (expd / total).astype(bf16)
            row.append(matmul(vt[h * HD : (h + 1) * HD, :end], probs))
            logs.append(top + jnp.log(total))
        outs.append(jnp.concatenate(row, axis=1))
        tops.append(jnp.concatenate(logs, axis=1))
    return jnp.concatenate(outs, axis=0).T.astype(bf16), jnp.concatenate(tops, axis=0)


def columns_of(*rows):
    return [jnp.broadcast_to(r[...].astype(f32), (128, r.shape[1])).T.astype(jnp.int32) for r in rows]


class Forward:
    def __init__(self, length, width, experts, devices, capacity, ff, gather, leave):
        self.length, self.width, self.experts, self.capacity = length, width, experts, capacity
        self.gather, self.leave = gather, leave
        pairs = width // PAIR
        share = self.share = width // devices
        self.blocks = ff // BLOCK
        self.per_block = BLOCK * devices // ff
        self.at_norm, self.at_qkv = 4, 7
        self.at_heads = self.at_qkv + 1
        self.per_turn = 2
        self.at_out = self.at_heads + length // SEQ * pairs // self.per_turn
        self.at_leave = self.at_out + 1
        self.at_mlp = max(self.at_leave + 2, self.DENSE_ITEMS + 3)
        self.steps = self.at_mlp + self.blocks
        slots = experts * capacity
        rows = lambda c, t: jax.ShapeDtypeStruct((length, c), t)
        piece = (capacity, 2 * width)
        self.kept = 1 if leave else experts
        self.outs = [
            rows(3 * width, bf16),
            jax.ShapeDtypeStruct((length // SEQ * pairs, 2, SEQ), f32),
            rows(width, bf16),
            rows(width, f32),
            rows(width, bf16),
            rows(slots, bf16),
            rows(128, f32),
            rows(width, f32),
            rows(width, f32),
        ] + [jax.ShapeDtypeStruct(piece, bf16)] * self.kept
        if gather:
            stages = [(devices, self.per_block * share * devices // ff * (ff // devices // 128), 128)]
            stages = [(devices, BLOCK // 128 * share, 128), (self.per_block, width, 128)]
            targets = [(devices, width, 128)] * 2
        else:
            stages, targets = [(width, BLOCK)] * 2, [(width, ff)] * 2
        self.targets = [jax.ShapeDtypeStruct(t, bf16) for t in targets]
        self.scratch = [pltpu.VMEM(piece, bf16)] * (experts - self.kept) + [
            pltpu.VMEM((devices, share, 128), bf16),
            pltpu.VMEM((devices, share, 3 * width), bf16),
            pltpu.VMEM((devices, share, width), bf16),
            pltpu.VMEM((8, width), f32),
            pltpu.VMEM((length, width), bf16),
            pltpu.SemaphoreType.DMA((3,)),
            pltpu.VMEM((length, width), bf16),
            pltpu.VMEM((length, width), bf16),
            pltpu.VMEM((width, length), bf16),
            pltpu.VMEM((width, length), bf16),
            pltpu.VMEM((2, devices, share, BLOCK), bf16),
            pltpu.VMEM((2, self.per_block, ff // devices, width), bf16),
            pltpu.VMEM((2,) + stages[0], bf16),
            pltpu.VMEM((2,) + stages[1], bf16),
            pltpu.SemaphoreType.DMA((2, 2)),
            pltpu.SemaphoreType.DMA((2, 2)),
        ]

    DENSE_ITEMS = 13

    def __call__(self, now, steps, tok, cot, routes, dropped, *refs):
        refs = list(refs)
        take = lambda count: [refs.pop(0) for _ in range(count)]
        full = self.gather.full[:5] if self.gather else take(5)
        qkv, lse, att, after, mixed, disp, info, dense_out, grad_mixed = take(9)
        leave = take(self.kept)
        targets = take(2)
        leave += take(self.experts - self.kept)
        ws, wq, wo, gains, attn_in, sems, gd, ge, xt, gt, w1, w2, stage_1, stage_2, w_sems, d_sems = refs
        width, length = self.width, self.length
        loads = [pltpu.make_async_copy(a, b, sems.at[i]) for i, (a, b) in enumerate(zip(full, (ws, wq, wo)))]

        def weights(block):
            at = lax.rem(block, 2)
            cols = pl.ds(pl.multiple_of(block * BLOCK, BLOCK), BLOCK)
            return [
                pltpu.make_async_copy(full[3].at[:, :, cols], w1.at[at], w_sems.at[at, 0]),
                pltpu.make_async_copy(full[4].at[pl.ds(block * self.per_block, self.per_block)], w2.at[at], w_sems.at[at, 1]),
            ]

        def flush(block):
            at = lax.rem(block, 2)
            if self.gather:
                size = BLOCK // 128 * self.share
                first = targets[0].at[:, pl.ds(pl.multiple_of(block * size, size), size)]
                second = targets[1].at[pl.ds(block * self.per_block, self.per_block)]
            else:
                cols = pl.ds(pl.multiple_of(block * BLOCK, BLOCK), BLOCK)
                first, second = targets[0].at[:, cols], targets[1].at[:, cols]
            return [
                pltpu.make_async_copy(stage_1.at[at], first, d_sems.at[at, 0]),
                pltpu.make_async_copy(stage_2.at[at], second, d_sems.at[at, 1]),
            ]

        @when(now == self.at_norm)
        def _():
            loads[0].start()
            loads[0].wait()
            gains[...] = ws[...].reshape(width, 128).astype(f32).T[:8]
            normed, _ = normalize(tok[...].astype(f32))
            attn_in[...] = (normed * gains[0:1]).astype(bf16)

        @when(now == self.at_qkv)
        def _():
            loads[1].start()
            loads[1].wait()

            def columns(c, _):
                cols = pl.ds(pl.multiple_of(c * BLOCK, BLOCK), BLOCK)
                weights = wq[:, :, cols].reshape(width, BLOCK)
                qkv[:, cols] = matmul(attn_in[...], weights).astype(bf16)
                return 0

            lax.fori_loop(0, 3 * width // BLOCK, columns, 0)

        @when(jnp.logical_and(now >= self.at_heads, now < self.at_out))
        def _():
            pairs = width // PAIR

            def pair(i, _):
                at = (now - self.at_heads) * self.per_turn + i
                seq, at_pair = at // pairs, lax.rem(at, pairs)
                rows = pl.ds(pl.multiple_of(seq * SEQ, SEQ), SEQ)
                cols = lambda part: pl.ds(pl.multiple_of(part * width + at_pair * PAIR, PAIR), PAIR)
                out, tops = attend_pair(qkv[rows, cols(0)], qkv[rows, cols(1)], qkv[rows, cols(2)])
                att[rows, cols(0)] = out
                lse[at] = tops
                return 0

            lax.fori_loop(0, self.per_turn, pair, 0)

        @when(now == self.at_out)
        def _():
            loads[2].start()
            loads[2].wait()
            self.route(tok, cot, routes, dropped, att, wo, ws, gains, after, mixed, gd, ge, disp, info)

        @when(now == self.at_leave)
        def _():
            for h, values in enumerate((mixed, ge)):
                placed = product_tn(disp[...], values[...]).astype(bf16)
                for j in range(self.experts):
                    leave[j][:, h * width : (h + 1) * width] = placed[j * self.capacity : (j + 1) * self.capacity]
            if self.leave:
                self.leave.send()

        @when(now == self.at_mlp - 1)
        def _():
            xt[...] = mixed[...].T
            gt[...] = gd[...].T
            dense_out[...] = jnp.zeros_like(dense_out)
            grad_mixed[...] = jnp.zeros_like(grad_mixed)

        @when(jnp.logical_and(now >= self.at_mlp, now < self.at_mlp + self.blocks))
        def _():
            block = now - self.at_mlp
            at = lax.rem(block, 2)

            @when(block == 0)
            def _():
                for copy in weights(0):
                    copy.start()

            @when(block + 1 < self.blocks)
            def _():
                for copy in weights(block + 1):
                    copy.start()

            for copy in weights(block):
                copy.wait()

            @when(block >= 2)
            def _():
                for copy in flush(block - 2):
                    copy.wait()

            d1, d2 = mlp_block(
                mixed,
                gd,
                xt,
                gt,
                w1[at].reshape(width, BLOCK),
                w2[at].reshape(BLOCK, width),
                dense_out,
                grad_mixed,
            )
            if self.gather:
                share = self.share
                for c in range(BLOCK // 128):
                    cols = slice(c * 128, (c + 1) * 128)
                    for s in range(width // share):
                        stage_1[at, s, c * share : (c + 1) * share] = d1[s * share : (s + 1) * share, cols]
                    stage_2[at, c] = d2[:, cols]
            else:
                stage_1[at] = d1
                stage_2[at] = d2
            for copy in flush(block):
                copy.start()

            @when(block == self.blocks - 1)
            def _():
                for last in (self.blocks - 2, self.blocks - 1):
                    for copy in flush(last):
                        copy.wait()

    def route(self, tok, cot, routes, dropped, att, wo, ws, gains, after, mixed, gd, ge, disp, info):
        width, length, experts = self.width, self.length, self.experts
        route, drop = columns_of(routes, dropped)
        after[...] = tok[...].astype(f32) + matmul(att[...], wo[...].reshape(width, width))
        normed, _ = normalize(after[...])
        mixed[...] = (normed * gains[1:2]).astype(bf16)
        logits = matmul(mixed[...], ws[...].reshape(width, 128))
        lane = lax.broadcasted_iota(jnp.int32, (length, 128), 1)

        def softmax(first, last):
            inside = jnp.logical_and(lane >= first, lane < last)
            top = jnp.max(jnp.where(inside, logits, -jnp.inf), axis=1, keepdims=True)
            expd = jnp.where(inside, jnp.exp(jnp.where(inside, logits, top) - top), 0.0)
            return expd / jnp.sum(expd, axis=1, keepdims=True)

        probs, coef = softmax(2, 2 + experts), softmax(2 + experts, 4 + experts)
        info[...] = probs + coef
        chosen = jnp.where(lane - 2 == route, 1.0, 0.0)
        over_lanes = lambda a: jnp.sum(a, axis=1, keepdims=True)
        gate = over_lanes(probs * chosen) * (1 - drop[:, :1]).astype(f32)
        coef_0 = over_lanes(jnp.where(lane == 2 + experts, coef, 0.0))
        coef_1 = over_lanes(jnp.where(lane == 3 + experts, coef, 0.0))
        grad = cot[...].astype(f32)
        gd[...] = (coef_0 * grad).astype(bf16)
        ge[...] = (coef_1 * gate * grad).astype(bf16)
        square = lambda d: lax.broadcasted_iota(jnp.int32, (length, length), d)
        earlier = jnp.where(square(0) > square(1), 1.0, 0.0).astype(bf16)
        position = over_lanes(chosen * matmul(earlier, chosen.astype(bf16))).astype(jnp.int32)
        turn = route[:, :1] - lax.axis_index("expert")
        target = jnp.where(turn < 0, turn + experts, turn) * self.capacity + position
        slot = lax.broadcasted_iota(jnp.int32, (length, experts * self.capacity), 1)
        disp[...] = jnp.where(slot == target, 1.0, 0.0).astype(bf16)


def attend_pair_backward(q, k, v, g, lse):
    scaling = 1.0 / math.sqrt(HD)
    qs = q * scaling
    kt = k.T
    length = q.shape[0]
    grad_k = [0.0] * (length // QB)
    grad_v = [0.0] * (length // QB)
    grad_q = []
    for h, mask in enumerate(masks()):
        kh, vh, qh, gh = k * mask, v * mask, q * mask, g * mask
        row = []
        for c, start in enumerate(range(0, length, QB)):
            end = start + QB
            scores = causal(outer_nt(kh[:end], qs[start:end]), start)
            probs = jnp.exp(scores - lse[h : h + 1, start:end])
            grad_probs = outer_nt(vh[:end], g[start:end])
            delta = jnp.sum(probs * grad_probs, axis=0, keepdims=True)
            grad_scores = (probs * (grad_probs - delta)).astype(bf16)
            more_v = matmul(probs.astype(bf16), gh[start:end])
            more_k = matmul(grad_scores, qh[start:end])
            for b in range(c + 1):
                rows = slice(b * QB, (b + 1) * QB)
                grad_v[b] = grad_v[b] + more_v[rows]
                grad_k[b] = grad_k[b] + more_k[rows]
            row.append(matmul(kt[h * HD : (h + 1) * HD, :end], grad_scores))
        grad_q.append(jnp.concatenate(row, axis=1))
    return (
        (jnp.concatenate(grad_q, axis=0).T * scaling).astype(bf16),
        (jnp.concatenate(grad_k, axis=0) * scaling).astype(bf16),
        jnp.concatenate(grad_v, axis=0).astype(bf16),
    )


def thirds(values):
    parts = []
    for _ in range(3):
        parts.append(values.astype(bf16))
        values = values - parts[-1].astype(f32)
    return parts


class Back:
    def __init__(self, length, width, experts, devices, capacity):
        self.length, self.width, self.experts, self.capacity = length, width, experts, capacity
        self.devices, self.share = devices, width // devices
        self.pairs = width // PAIR
        self.columns = 3 * PAIR
        self.firsts = width // self.columns
        self.rest = width - self.firsts * self.columns
        self.items = self.firsts + self.pairs + 1
        self.heads_at = 4
        self.last = self.heads_at + self.pairs
        self.steps = self.last + 1
        self.first_item = self.heads_at
        self.outs = [
            jax.ShapeDtypeStruct((length, width), bf16),
            jax.ShapeDtypeStruct((length, width), f32),
        ]
        slots = experts * capacity
        self.scratch = [
            pltpu.VMEM((slots, 2 * width), bf16),
            pltpu.VMEM((length, width), f32),
            pltpu.VMEM((length, width), f32),
            pltpu.VMEM((devices, self.share, 128), bf16),
            pltpu.VMEM((devices, self.share, width), bf16),
            pltpu.VMEM((2, devices, self.share, self.columns), bf16),
            pltpu.VMEM((8, width), f32),
            pltpu.VMEM((128, width), f32),
            pltpu.VMEM((width, length), bf16),
            pltpu.VMEM((length, width), bf16),
            pltpu.SemaphoreType.DMA((5 + experts,)),
            pltpu.SemaphoreType.DMA((2, 3)),
        ]

    def made(self):
        chips = (4, 2, 2, self.experts // 2) if self.devices == 8 * self.experts else (self.devices,)
        return (self.items,) + chips + (self.share, self.columns)

    def final_outs(self):
        share, width = self.share, self.width
        return [jax.ShapeDtypeStruct((share, c), f32) for c in (3 * width, width, 128)]

    def store(self, outs, i, value):
        d_qkv, d_out, d_small = outs
        final = self.items - 1

        for f in range(self.firsts):

            @when(i == f)
            def _(f=f):
                d_out[:, f * self.columns : (f + 1) * self.columns] = value

        @when(jnp.logical_and(i >= self.firsts, i < final))
        def _():
            for p in range(3):
                at = pl.multiple_of(p * self.width + (i - self.firsts) * PAIR, PAIR)
                d_qkv[:, pl.ds(at, PAIR)] = value[:, p * PAIR : (p + 1) * PAIR]

        @when(i == final)
        def _():
            d_out[:, self.firsts * self.columns :] = value[:, : self.rest]
            d_small[...] = value[:, self.rest : self.rest + 128]

    def __call__(self, now, steps, *refs):
        experts, width, length = self.experts, self.width, self.length
        refs = list(refs)
        tok, cot, routes, dropped, qkv, lse, att, mixed_in, disp, info = refs[:10]
        small_hbm, qkv_hbm, out_hbm, dense_hbm, grad_hbm, after_hbm = refs[10:16]
        came_hbm = refs[16 : 16 + experts]
        mixed, tokens_grad, *rest = refs[16 + experts :]
        if self.moves:
            made = self.moves[-1].own
        else:
            made = rest.pop(0)
        came, dense, grads, ws, wo, wq, gains, d_heads, attn_in_t, grad_att, sems, wq_sems = rest
        fetch = lambda a, b, i: pltpu.make_async_copy(a, b, sems.at[i])
        capacity = self.capacity
        loads = [fetch(came_hbm[j], came.at[pl.ds(j * capacity, capacity)], j) for j in range(experts)]
        loads += [
            fetch(a, b, experts + i)
            for i, (a, b) in enumerate(
                ((dense_hbm, dense), (grad_hbm, grads), (after_hbm, tokens_grad), (small_hbm, ws), (out_hbm, wo))
            )
        ]

        def pair_weights(pair):
            slot = lax.rem(pair, 2)
            return [
                pltpu.make_async_copy(
                    qkv_hbm.at[:, :, pl.ds(pl.multiple_of(p * width + pair * PAIR, PAIR), PAIR)],
                    wq.at[slot, :, :, pl.ds(p * PAIR, PAIR)],
                    wq_sems.at[slot, p],
                )
                for p in range(3)
            ]

        put = lambda i, columns, values: self.put(made, i, columns, values)
        lane = lax.broadcasted_iota(jnp.int32, (length, 128), 1)
        over_lanes = lambda a: jnp.sum(a, axis=1, keepdims=True)

        @when(now == 0)
        def _():
            for copy in loads + pair_weights(0):
                copy.start()

        @when(now == 1)
        def _():
            for copy in loads:
                copy.wait()
            probs = jnp.where(jnp.logical_and(lane >= 2, lane < 2 + experts), info[...], 0.0)
            coef_0 = over_lanes(jnp.where(lane == 2 + experts, info[...], 0.0))
            coef_1 = over_lanes(jnp.where(lane == 3 + experts, info[...], 0.0))
            route, drop = columns_of(routes, dropped)
            chosen = jnp.where(lane - 2 == route, 1.0, 0.0)
            kept = (1 - drop[:, :1]).astype(f32)
            gate_prob = over_lanes(probs * chosen)
            gate = gate_prob * kept
            grad = cot[...].astype(f32)
            expert_tok = matmul(disp[...], came[:, :width])
            mixed[...] = (tokens_grad[...] + coef_0 * dense[...] + (coef_1 * gate) * expert_tok).astype(bf16)
            shared = over_lanes(grad * expert_tok)
            grad_0, grad_1 = over_lanes(grad * dense[...]), shared * gate
            both = coef_0 * grad_0 + coef_1 * grad_1
            grad_gate = shared * coef_1 * kept
            logits = jnp.where(
                jnp.logical_and(lane >= 2, lane < 2 + experts), (grad_gate * gate_prob) * (chosen - probs), 0.0
            )
            logits = jnp.where(lane == 2 + experts, coef_0 * (grad_0 - both), logits)
            logits = jnp.where(lane == 3 + experts, coef_1 * (grad_1 - both), logits)
            pieces = thirds(logits)
            d_heads[...] = add(*(product_tn(p, mixed_in[...]) for p in pieces))
            weights = ws[...].reshape(width, 128)
            grads[...] = (
                grads[...] + matmul(disp[...], came[:, width:]) + add(*(outer_nt(p, weights) for p in pieces))
            )
            gains[...] = weights.astype(f32).T[:8]

        @when(now == 2)
        def _():
            normed, scale = normalize(tokens_grad[...])
            d_heads[1:2] = jnp.sum(grads[...] * normed, axis=0, keepdims=True)
            grads[...] = cot[...].astype(f32) + norm_back(grads[...] * gains[1:2], normed, scale)
            normed, _ = normalize(tok[...].astype(f32))
            attn_in_t[...] = (normed * gains[0:1]).astype(bf16).T

        @when(now == 3)
        def _():
            grad_attn = grads[...].astype(bf16)
            grad_att[...] = outer_nt(grad_attn, wo[...].reshape(width, width)).astype(bf16)
            d_out = product_tn(att[...], grad_attn).astype(bf16)
            for f in range(self.firsts):
                put(f, slice(None), d_out[:, f * self.columns : (f + 1) * self.columns])
            put(self.items - 1, slice(0, self.rest), d_out[:, self.firsts * self.columns :])
            dense[...] = jnp.zeros_like(dense)

        @when(jnp.logical_and(now >= self.heads_at, now < self.last))
        def _():
            pair = now - self.heads_at
            cols = lambda part: pl.ds(pl.multiple_of(part * width + pair * PAIR, PAIR), PAIR)
            d_pair = attend_pair_backward(
                qkv[:, cols(0)], qkv[:, cols(1)], qkv[:, cols(2)], grad_att[:, cols(0)], lse[pair]
            )
            d_pair = jnp.concatenate(d_pair, axis=1)
            for copy in pair_weights(pair):
                copy.wait()

            @when(pair + 1 < self.pairs)
            def _():
                for copy in pair_weights(pair + 1):
                    copy.start()

            put(pair + self.firsts, slice(None), matmul(attn_in_t[...], d_pair).astype(bf16))
            dense[...] += outer_nt(d_pair, wq[lax.rem(pair, 2)].reshape(width, self.columns))

        @when(now == self.last)
        def _():
            normed, scale = normalize(tok[...].astype(f32))
            d_heads[0:1] = jnp.sum(dense[...] * normed, axis=0, keepdims=True)
            put(self.items - 1, slice(self.rest, self.rest + 128), d_heads[...].T.astype(bf16))
            if self.rest + 128 < self.columns:
                spare = self.columns - self.rest - 128
                put(self.items - 1, slice(self.rest + 128, None), jnp.zeros((width, spare), bf16))
            tokens_grad[...] = grads[...] + norm_back(dense[...] * gains[0:1], normed, scale)

    def put(self, made, i, columns, values):
        lead = made.shape[1:-1]
        at = (i,) + (slice(None),) * len(lead) + (columns,)
        made[at] = values.reshape(lead + values.shape[1:])


def gelu_both(v):
    c = math.sqrt(2.0 / math.pi)
    square = v * v
    t = jnp.tanh(c * (v + 0.044715 * (square * v)))
    half = 0.5 * (1.0 + t)
    slope = half + 0.5 * v * (1.0 - t * t) * (c * (1.0 + (3 * 0.044715) * square))
    return v * half, slope


def mlp_block(x, g, xt, gt, w1, w2, out_sum, back_sum):
    hidden, slope = gelu_both(matmul(x[...], w1))
    hidden = hidden.astype(bf16)
    grad_pre = (slope * outer_nt(g[...], w2)).astype(bf16)
    out_sum[...] += matmul(hidden, w2)
    back_sum[...] += outer_nt(grad_pre, w1)
    return matmul(xt[...], grad_pre).astype(bf16), matmul(gt[...], hidden).astype(bf16)


class Experts:
    TURNS = 8

    def __init__(self, pieces, blocks, width, size, chunks, back):
        self.parts, self.piece = len(pieces), pieces[0].shape
        self.blocks, self.width, self.size, self.back = blocks, width, size, back
        rows = self.parts * self.piece[0]
        if chunks:
            self.block = (2, size // 256, chunks, width // chunks, 128)
            whole = (blocks // 2, 2) + self.block
        else:
            self.block = (width, size)
            whole = (blocks,) + self.block
        piece = jax.ShapeDtypeStruct(self.piece, bf16)
        self.outs = [piece] * self.parts + [jax.ShapeDtypeStruct(whole, bf16)] * 2
        self.scratch = (
            [pltpu.VMEM(self.piece, bf16)] * self.parts
            + [pltpu.VMEM((rows, width), bf16)] * 2
            + [pltpu.VMEM((width, rows), bf16)] * 2
            + [pltpu.VMEM((rows, width), f32)] * 2
            + [pltpu.VMEM((2,) + self.block, bf16)] * 2
            + [pltpu.SemaphoreType.DMA((2, 2)), pltpu.SemaphoreType.DMA((self.parts,))]
            + [pltpu.VMEM((2, width, size), bf16), pltpu.VMEM((2, size, width), bf16)]
            + [pltpu.SemaphoreType.DMA((2, 2))]
        )

    def __call__(self, now, steps, *refs):
        refs = list(refs)
        take = lambda count: [refs.pop(0) for _ in range(count)]
        pieces, full = take(self.parts), take(2)
        kept, targets, results = take(self.parts), take(2), take(self.parts)
        x, g, xt, gt, out_sum, back_sum, stage_1, stage_2, sems, kept_sems, w1, w2, w_sems = refs
        width, size = self.width, self.piece[0]

        def flush(step):
            at = lax.rem(step, 2)
            where = (step // 2, at) if len(self.block) > 2 else (step,)
            return [
                pltpu.make_async_copy(stage.at[at], target.at[where], sems.at[at, i])
                for i, (stage, target) in enumerate(zip((stage_1, stage_2), targets))
            ]

        def weights(step):
            at = lax.rem(step, 2)
            return [
                pltpu.make_async_copy(a.at[step], b.at[at], w_sems.at[at, i])
                for i, (a, b) in enumerate(zip(full, (w1, w2)))
            ]

        @when(now == 0)
        def _():
            for copy in weights(0):
                copy.start()
            for j, piece in enumerate(pieces):
                x[j * size : (j + 1) * size] = piece[:, :width]
                g[j * size : (j + 1) * size] = piece[:, width:]
            xt[...] = x[...].T
            gt[...] = g[...].T
            out_sum[...] = jnp.zeros_like(out_sum)
            back_sum[...] = jnp.zeros_like(back_sum)

        def block(step, _):
            for copy in weights(step):
                copy.wait()

            @when(step + 1 < self.blocks)
            def _():
                for copy in weights(step + 1):
                    copy.start()

            @when(step >= 2)
            def _():
                for copy in flush(step - 2):
                    copy.wait()

            slot = lax.rem(step, 2)
            for stage, d in zip((stage_1, stage_2), mlp_block(x, g, xt, gt, w1[slot], w2[slot], out_sum, back_sum)):
                if len(self.block) == 2:
                    stage[slot] = d
                else:
                    for c in range(d.shape[1] // 128):
                        share = d[:, c * 128 : (c + 1) * 128].reshape(self.block[2:])
                        stage[slot, c // self.block[1], c % self.block[1]] = share
            for copy in flush(step):
                copy.start()
            return 0

        lax.fori_loop(now * self.blocks // steps, (now + 1) * self.blocks // steps, block, 0)

        @when(now == steps - 1)
        def _():
            for h, total in enumerate((out_sum, back_sum)):
                for j, result in enumerate(results):
                    result[:, h * width : (h + 1) * width] = total[j * size : (j + 1) * size].astype(bf16)
            keep = [pltpu.make_async_copy(a, b, kept_sems.at[j]) for j, (a, b) in enumerate(zip(results, kept))]
            for copy in keep:
                copy.start()
            for copy in keep:
                copy.wait()
            if self.back:
                self.back.send()
            for step in (self.blocks - 2, self.blocks - 1):
                for copy in flush(step):
                    copy.wait()


def finish(arrays, small, cuts):
    pieces = []
    for i, a in enumerate(arrays):
        axis = 1 if a.shape[0] == 1 else 0
        parts = 4 if a.size * a.dtype.itemsize >= MIB else 1
        size = a.shape[axis] // parts
        pieces += [(i, (0,) * axis + (pl.ds(p * size, size),)) for p in range(parts)]
    n = len(arrays)

    def kernel(*refs):
        ins, columns, outs, rows = refs[:n], refs[n], refs[n + 1 : 2 * n + 1], refs[2 * n + 1 : -n - 1]
        held, sems = refs[-n - 1 : -1], refs[-1]
        move = lambda a, b, way: [
            pltpu.make_async_copy(a[i].at[at], b[i].at[at], sems.at[way, c]) for c, (i, at) in enumerate(pieces)
        ]
        loads, copies = move(ins, held, 0), move(held, outs, 1)
        for load in loads:
            load.start()
        for load, copy in zip(loads, copies):
            load.wait()
            copy.start()
        turned = columns[...].T
        for ref, first, last in zip(rows, cuts, cuts[1:]):
            ref[...] = turned[first:last]
        for copy in copies:
            copy.wait()

    whole, hbm = pl.BlockSpec(memory_space=pltpu.VMEM), pl.BlockSpec(memory_space=pltpu.HBM)
    shapes = [jax.ShapeDtypeStruct(a.shape, a.dtype) for a in arrays]
    shapes += [jax.ShapeDtypeStruct((b - a, small.shape[0]), f32) for a, b in zip(cuts, cuts[1:])]
    results = pl.pallas_call(
        kernel,
        out_shape=shapes,
        in_specs=[hbm] * n + [whole],
        out_specs=[hbm] * n + [whole] * (len(cuts) - 1),
        scratch_shapes=[pltpu.VMEM(a.shape, a.dtype) for a in arrays] + [pltpu.SemaphoreType.DMA((2, len(pieces)))],
        compiler_params=pltpu.CompilerParams(vmem_limit_bytes=60 * MIB),
        name="finish",
    )(*arrays, small)
    return results[:n], results[n:]


def move(name, moves, collective_id, experts):
    return call(name, 1, None, [], [], [], [], [], moves, collective_id, experts, 0)


def shards(
    fast,
    tokens,
    gain_attn,
    w_qkv,
    w_out,
    gain_mix,
    w_fc,
    w_proj,
    w_router,
    w_coef,
    expert_in,
    expert_out,
    routes,
    dropped,
    cotangent,
):
    experts = lax.axis_size("expert")
    nodes = lax.axis_size("node")
    devices = nodes * experts
    width = tokens.shape[1]
    tok_rows = tokens.shape[0]
    ff = w_fc.shape[1]
    share = w_qkv.shape[0]
    small = jnp.concatenate([gain_attn[:, None], gain_mix[:, None], w_router, w_coef], axis=1)
    small = jnp.pad(small, ((0, 0), (0, 128 - small.shape[1])))
    win, wout = expert_in[0], expert_out[0]
    cut = lambda a, rows, columns, m, n: [
        [(a, i * (rows // m), rows // m, j * (columns // n), columns // n)] for i in range(m) for j in range(n)
    ]
    weights = (small, w_qkv, w_out, w_fc, w_proj)
    capacity = -(-(tok_rows * 10) // (8 * experts))
    moves, given = [], None
    if fast:
        sixth = cut(1, share, 3 * width, 1, 6)
        items = sixth[:2] + [sixth[2] + sixth[3], sixth[4] + sixth[5]] + cut(2, share, width, 1, 1)
        items += cut(3, share, ff, 1, 4) + cut(4, ff // devices, width, 4, 1)
        items[0] = cut(0, share, 128, 1, 1)[0] + items[0]
        assert len(items) == Forward.DENSE_ITEMS
        items += cut(5, width, win.shape[1], 4, 1) + cut(6, wout.shape[0], width, 4, 1)
        moves = [Gather(list(weights) + [win, wout], [True] * 5 + [False] * 2, items, nodes, experts)]
        moves.append(Exchange([], 1, experts, None, moves[0].turns, (capacity, 2 * width)))
        full = []
    else:
        full = [lax.all_gather(a, AXES, axis=0, tiled=False) for a in weights]
        win_full, wout_full = (lax.all_gather(a, "node", axis=0, tiled=False) for a in (win, wout))

    def scatter_xla(parts, axes):
        return lax.psum_scatter(parts, axes, scatter_dimension=0, tiled=False).astype(f32)

    def exchange(parts, sign):
        moved = [parts[0]]
        for j in range(1, experts):
            shift = [(s, (s + sign * j) % experts) for s in range(experts)]
            moved.append(lax.ppermute(parts[j], "expert", shift))
        return moved

    forward = Forward(tok_rows, width, experts, devices, capacity, ff, *(moves or (None, None)))
    whole, hbm = pl.BlockSpec(memory_space=pltpu.VMEM), pl.BlockSpec(memory_space=pltpu.HBM)
    routes, dropped = routes.reshape(1, tok_rows), dropped.reshape(1, tok_rows)
    if fast:

        def given(ins, os, own):
            moves[1].sources = own[: experts - 1]

    results = call(
        "forward",
        forward.steps,
        forward,
        [tokens, cotangent, routes, dropped] + full,
        [whole] * 4 + [hbm] * len(full),
        forward.outs + forward.targets,
        [whole] * len(forward.outs) + [hbm] * 2,
        forward.scratch,
        moves,
        1,
        experts,
        12 * tok_rows * width * (width + ff),
        given,
    )
    qkv_rows, lse, attended, after_attn, mixed_in, dispatch, probs, dense_out, grad_mixed = results[:9]
    results = results[9:]
    leaving, (d_fc, d_proj), moved = (
        results[: forward.kept],
        results[forward.kept : forward.kept + 2],
        results[forward.kept + 2 :],
    )
    small_full, qkv_full, out_full = (moved if fast else full)[:3]
    scatters, return_to, given = [], None, None
    chunks = 4
    step = width // chunks
    half = (experts // 2, step, 128)
    win_out = [jax.ShapeDtypeStruct(expert_in.shape, f32)]
    wout_out = [jax.ShapeDtypeStruct(expert_out.shape, f32)]

    def store_wout(out, chunk, sums):
        at = pl.ds(pl.multiple_of(chunk * step, step), step)
        for h, total in enumerate(sums):
            for c in range(half[0]):
                out[0, (h * half[0] + c) * 128 : (h * half[0] + c + 1) * 128, at] = total[c].T

    if fast:
        win_full, wout_full = moved[5:7]
        arrived = leaving + moved[7:]
        by_chip = lambda a: a.reshape(4, 2, 2, experts // 2, chunks, step, 128)

        def store(outs, i, value):
            if i < chunks:
                for q in range(step // share):
                    at = (i * (step // share) + q) * 128
                    outs[0][:, at : at + 128] = value[q * share : (q + 1) * share]
            else:
                outs[1][:, (i - chunks) * step : (i - chunks + 1) * step] = value.T

        def store_plane(outs, i, sums):
            @when(i < 2 * chunks)
            def _():
                for h, total in enumerate(sums):
                    outs[0][h * half[0] : (h + 1) * half[0], i] = total.astype(bf16)

            @when(i >= 2 * chunks)
            def _():
                at = pl.ds(pl.multiple_of((i - 2 * chunks) * step, step), step)
                for h, total in enumerate(sums):
                    for c in range(half[0]):
                        outs[1][0, at, (h * half[0] + c) * 128 : (h * half[0] + c + 1) * 128] = total[c]

        outs = [jax.ShapeDtypeStruct((experts, 2 * chunks) + half[1:], bf16)]
        parts = [(by_chip(d_fc), False, 0, chunks), (by_chip(d_proj), False, 0, chunks), (None, False, 0, chunks)]
        summing = Scatter(parts, half, experts, outs + win_out, store_plane, spread=True)
        return_to = Exchange([], -1, experts, None, summing.turns, leaving[0].shape)
        scatters = [return_to, summing]
    else:
        arrived = exchange(leaving, 1)
    blocks, size = win_full.shape[0], win_full.shape[2]
    experts_kernel = Experts(arrived, blocks, width, size, chunks if fast else None, return_to)
    if fast:

        def given(ins, os, own):
            summing.given = [os[experts]]
            return_to.sources = os[1:experts]

    results = call(
        "expert_mlp",
        experts_kernel.TURNS,
        experts_kernel,
        arrived + [win_full, wout_full],
        [whole] * experts + [hbm] * 2,
        experts_kernel.outs,
        [hbm] * len(experts_kernel.outs),
        experts_kernel.scratch,
        scatters,
        3,
        experts,
        12 * experts * capacity * width * blocks * size,
        given,
    )
    returned, (d_win, d_wout) = results[:experts], results[experts : experts + 2]
    if fast:
        results = results[experts + 2 :]
        came_back = returned[:1] + results[: experts - 1]
        plane_sums, grad_win = results[experts - 1 :]
    else:
        came_back = exchange(returned, -1)
    back = Back(tok_rows, width, experts, devices, capacity)
    back.moves = []
    if fast:
        parts = [(None, True, 0, back.items)]
        made = back.made()
        scatter_rest = Scatter(
            parts, made[4:], experts, back.final_outs(), back.store, back.first_item, made, spread=True
        )
        parts = [(d_wout, False, 0, chunks)]
        scatter_wout = Scatter(
            parts, half, experts, wout_out, lambda outs, i, sums: store_wout(outs[0], i, sums), spread=True
        )
        outs = [jax.ShapeDtypeStruct((share, ff), f32), jax.ShapeDtypeStruct((ff // devices, width), f32)]
        along = Along(plane_sums, experts, outs, store, max(scatter_rest.turns, scatter_wout.turns))
        back.moves = [along, scatter_wout, scatter_rest]
    outs = back.outs + ([] if fast else [jax.ShapeDtypeStruct((back.items, width, back.columns), bf16)])
    mixed, tokens_grad, *results = call(
        "back",
        back.steps,
        back,
        [tokens, cotangent, routes, dropped, qkv_rows, lse, attended, mixed_in, dispatch, probs]
        + [small_full, qkv_full, out_full, dense_out, grad_mixed, after_attn]
        + came_back,
        [whole] * 10 + [hbm] * (6 + experts),
        outs,
        [whole] * len(outs),
        back.scratch,
        back.moves,
        5,
        experts,
        32 * tok_rows * width * width,
    )
    if fast:
        done, (gain_1, gain_2, router, coef) = finish(
            [mixed, tokens_grad, grad_win] + results[:5], results[5], (0, 1, 2, 2 + experts, 4 + experts)
        )
        mixed, tokens_grad, grad_win, grad_fc, grad_proj, grad_wout, grad_wqkv, grad_wo = done
        small_grads = (gain_1[0], gain_2[0], router.T, coef.T)
    else:
        summed = scatter_xla(results[0].reshape(back.items, devices, share, -1).swapaxes(0, 1), AXES)
        last = summed[-1]
        grad_wo = jnp.concatenate([*summed[: back.firsts], last[:, : back.rest]], axis=1)
        grad_small = last[:, back.rest : back.rest + 128]
        small_grads = (
            grad_small[:, 0],
            grad_small[:, 1],
            grad_small[:, 2 : 2 + experts],
            grad_small[:, 2 + experts : 4 + experts],
        )
        pairs = summed[back.firsts : -1].reshape(back.pairs, share, 3, PAIR)
        grad_wqkv = pairs.transpose(1, 2, 0, 3).reshape(share, 3 * width)
        grad_fc = scatter_xla(d_fc.reshape(devices, share, ff), AXES)
        by_unit = d_proj.reshape(width, devices, ff // devices).transpose(1, 0, 2)
        grad_proj = scatter_xla(by_unit, AXES).T
        grad_win = scatter_xla(d_win, "node")[None]
        grad_wout = scatter_xla(d_wout, "node").T[None]
    return (
        mixed,
        tokens_grad,
        small_grads[0],
        grad_wqkv,
        grad_wo,
        small_grads[1],
        grad_fc,
        grad_proj,
        small_grads[2],
        small_grads[3],
        grad_win,
        grad_wout,
    )


def solution(mesh):
    rows = P(AXES, None)
    in_specs = (
        rows,
        P(AXES),
        rows,
        rows,
        P(AXES),
        rows,
        rows,
        rows,
        rows,
        P("expert", None, "node"),
        P("expert", "node", None),
        rows,
        P(AXES),
        rows,
    )
    out_specs = (
        rows,
        rows,
        P(AXES),
        rows,
        rows,
        P(AXES),
        rows,
        rows,
        rows,
        rows,
        P("expert", None, "node"),
        P("expert", "node", None),
    )
    fast = mesh.shape["node"] == 8 and mesh.shape["expert"] == 4
    return jax.shard_map(
        functools.partial(shards, fast), mesh=mesh, in_specs=in_specs, out_specs=out_specs, check_vma=False
    )
```
